32 devices in a mesh: group: 4 (over x, core), expert: 8 (over z, y).
Axes of the slice: x: 2, y: 2, z: 4, core: 2. Of those that a mesh axis runs over, the one named last changes fastest.
Arguments:
- tokens: bfloat16 [128, 197, 768], P(('group', 'expert')), may hold values from -6 to 6
- cotangent: bfloat16 [128, 197, 768], P(('group', 'expert')), may hold values from -6 to 6
- routes: int32 [128, 197, 2], P(('group', 'expert')), may hold values from 0 to 15, all different within a row
- order: int32 [32, 788], P(('group', 'expert')), may hold values from 0 to 787, each once within a row
- ln1_gain: float32 [768], P(('group', 'expert')), may hold values from 0.5 to 1.5
- ln1_bias: float32 [768], P(('group', 'expert')), may hold values from -0.625 to 0.625
- w_qkv: float32 [768, 2304], P(('group', 'expert')), may hold values from -0.21875 to 0.21875
- w_out: float32 [768, 768], P(('group', 'expert')), may hold values from -0.875 to 0.875
- b_out: float32 [768], P(('group', 'expert')), may hold values from -1.25 to 1.25
- ln2_gain: float32 [768], P(('group', 'expert')), may hold values from 0.5 to 1.5
- ln2_bias: float32 [768], P(('group', 'expert')), may hold values from -0.625 to 0.625
- w_router: float32 [768, 16], P(('group', 'expert')), may hold values from -0.15625 to 0.15625
- w_in: float32 [16, 768, 3072], P('expert', 'group'), may hold values from -0.21875 to 0.21875
- b_in: float32 [16, 3072], P('expert', 'group'), may hold values from -1.25 to 1.25
- w_back: float32 [16, 3072, 768], P('expert', 'group'), may hold values from -1.75 to 1.75
- b_back: float32 [16, 768], P('expert', 'group'), may hold values from -1.25 to 1.25
Outputs:
- output: bfloat16 [128, 197, 768], P(('group', 'expert'))
- grad_tokens: float32 [128, 197, 768], P(('group', 'expert'))
- grad_ln1_gain: float32 [768], P(('group', 'expert'))
- grad_ln1_bias: float32 [768], P(('group', 'expert'))
- grad_w_qkv: float32 [768, 2304], P(('group', 'expert'))
- grad_w_out: float32 [768, 768], P(('group', 'expert'))
- grad_b_out: float32 [768], P(('group', 'expert'))
- grad_ln2_gain: float32 [768], P(('group', 'expert'))
- grad_ln2_bias: float32 [768], P(('group', 'expert'))
- grad_w_router: float32 [768, 16], P(('group', 'expert'))
- grad_w_in: float32 [16, 768, 3072], P('expert', 'group')
- grad_b_in: float32 [16, 3072], P('expert', 'group')
- grad_w_back: float32 [16, 3072, 768], P('expert', 'group')
- grad_b_back: float32 [16, 768], P('expert', 'group')
The draws below stay inside these ranges and needn't reach their ends.
Inputs may be any that keep to these rules, and one draw needn't show every extreme that they name: `routes`: each row names two different experts. Each row of order holds every token number of its block once.
All inputs are finite; a program needn't handle non-finite values.
Results may differ from the reference program's by a relative error of at most 0.015.
The reference program's roundings to bfloat16 on the way count: a program that leaves them out, or rounds other values in their place, can miss the bound.
Values may be sent and summed in bfloat16 or wider, within the bound.
No kernel may reach another device: no remote copies, remote signals or barrier semaphores. Data moves between devices by JAX's collectives and lax.ppermute only.
A program may use at most 256 MiB of HBM per device.

```python
from functools import partial
import jax
import jax.numpy as jnp
from jax import lax

D = 768
HEADS = 12
HEAD_DIM = 64
HID = 3072
SEQ = 197
IMG_DEV = 4
EXPERTS = 16
BLOCKS = 32
TOK_DEV = 788
IMAGES = 128
CAP = 123


def block_scale(stream_key, dims, split, low, top_value):
    level = 1.0
    for dim, shards_of in split:
        heights = jax.random.uniform(jax.random.fold_in(jax.random.fold_in(stream_key, 6), dim), (shards_of,), jnp.float32, low / len(split), top_value / len(split))
        level = level * jnp.repeat(jnp.exp(heights), dims[dim] // shards_of).reshape((-1,) + (1,) * (len(dims) - 1 - dim))
    return level


def choose_distinct(key, rows, amount, top, lift):
    ranking = jax.random.permutation(jax.random.fold_in(key, 1), amount)
    favour = ranking
    for power in range(3):
        favour = favour * favour // amount
    favour = favour * lift // amount
    chance = jax.random.randint(jax.random.fold_in(key, 2), (rows, amount), 0, 4096) + favour
    sure = jax.random.permutation(jax.random.fold_in(key, 3), rows)[jnp.arange(amount) % rows]
    chance = jnp.where(jnp.arange(rows)[:, None] == sure[None, :], 1 << 14, chance)
    priority = chance * amount + jnp.arange(amount)
    return lax.top_k(priority.astype(jnp.int32), top)[1].astype(jnp.int32)


def scatter_about(rng, dims, scale, bound, split=(), held_as=jnp.bfloat16):
    values = scale * jax.random.normal(rng, dims, jnp.float32)
    if split:
        values = values * block_scale(rng, dims, split, -0.22, 0.18)
    return jnp.clip(values, -bound, bound).astype(held_as)


def setup_inputs(seed: int = 0) -> dict:
    seeds = jax.random.split(jax.random.key(seed), 17)
    return {
        "tokens": scatter_about(seeds[0], (IMAGES, SEQ, D), 1.0, 6.0, ((0, 32),)),
        "cotangent": scatter_about(seeds[1], (IMAGES, SEQ, D), 1.0, 6.0, ((0, 32),)),
        "routes": choose_distinct(seeds[2], IMAGES * SEQ, EXPERTS, 2, 1024).reshape((IMAGES, SEQ, 2)),
        "order": jax.vmap(lambda own: jax.random.permutation(own, TOK_DEV))(jax.random.split(seeds[3], BLOCKS)).reshape((BLOCKS, TOK_DEV)).astype(jnp.int32),
        "ln1_gain": jnp.clip(1.0 + 0.1 * jax.random.normal(seeds[4], (D,), jnp.float32), 0.5, 1.5),
        "ln1_bias": scatter_about(seeds[5], (D,), 0.1, 0.625, ((0, 32),), jnp.float32),
        "w_qkv": scatter_about(seeds[6], (D, 3 * D), D ** -0.5, 0.21875, ((0, 32),), jnp.float32),
        "w_out": scatter_about(seeds[7], (D, D), (D // 16) ** -0.5, 0.875, ((0, 32),), jnp.float32),
        "b_out": scatter_about(seeds[8], (D,), 0.2, 1.25, ((0, 32),), jnp.float32),
        "ln2_gain": jnp.clip(1.0 + 0.1 * jax.random.normal(seeds[9], (D,), jnp.float32), 0.5, 1.5),
        "ln2_bias": scatter_about(seeds[10], (D,), 0.1, 0.625, ((0, 32),), jnp.float32),
        "w_router": scatter_about(seeds[11], (D, EXPERTS), (2 * D) ** -0.5, 0.15625, ((0, 32),), jnp.float32),
        "w_in": scatter_about(seeds[12], (EXPERTS, D, HID), D ** -0.5, 0.21875, ((0, 8), (1, 4)), jnp.float32),
        "b_in": scatter_about(seeds[13], (EXPERTS, HID), 0.2, 1.25, ((0, 8), (1, 4)), jnp.float32),
        "w_back": scatter_about(seeds[14], (EXPERTS, HID, D), (max(HID // 256, 1)) ** -0.5, 1.75, ((0, 8), (1, 4)), jnp.float32),
        "b_back": scatter_about(seeds[15], (EXPERTS, D), 0.2, 1.25, ((0, 8), (1, 4)), jnp.float32),
    }


highest = lax.Precision.HIGHEST

@jax.custom_vjp
def low(v):
    return lax.optimization_barrier(v.astype(jnp.bfloat16)).astype(jnp.float32)

@jax.custom_vjp
def low_back(v):
    return v

def low_keep(v):
    return (low(v), None)

def low_pass(kept, grad):
    return (grad,)

def back_keep(v):
    return (v, None)

def back_low(kept, grad):
    return (low(grad),)
low.defvjp(low_keep, low_pass)
low_back.defvjp(back_keep, back_low)

def layer_norm(features, gain_vec, shift_vec):
    centre = features - lax.optimization_barrier(jnp.mean(features, axis=-1, keepdims=True))
    spread = lax.optimization_barrier(jnp.mean(centre * centre, axis=-1, keepdims=True))
    return centre * lax.rsqrt(spread + 1e-06) * gain_vec + shift_vec

def place_pairs(choices, ranked, experts, capacity):
    tok_count = choices.shape[0]
    ordered = jnp.concatenate([choices[ranked, 0], choices[ranked, 1]])
    labels = jnp.arange(experts, dtype=jnp.int32)
    onehot = (ordered[:, None] == labels[None, :]).astype(jnp.int32)
    before = jnp.cumsum(onehot, axis=0, dtype=jnp.int32) - onehot
    placed = lax.optimization_barrier(jnp.sum(before * onehot, axis=1, dtype=jnp.int32))
    first = jnp.zeros((tok_count,), jnp.int32).at[ranked].set(placed[:tok_count])
    second = jnp.zeros((tok_count,), jnp.int32).at[ranked].set(placed[tok_count:])
    slot_pos = jnp.stack([first, second], axis=1)
    target = jnp.where(slot_pos < capacity, choices * capacity + slot_pos, experts * capacity).astype(jnp.int32)
    owners = jnp.repeat(jnp.arange(tok_count, dtype=jnp.int32), 2)
    source = jnp.full((experts * capacity + 1,), tok_count, jnp.int32).at[target.reshape(-1)].set(owners)
    return (target, source[:experts * capacity])

def attend(block_part, qkv_low, out_low):
    images, length, model_width = block_part.shape
    projected = jnp.dot(block_part.reshape(-1, model_width), qkv_low, precision=highest)
    projected = low(low_back(projected)).reshape(images, length, 3, HEADS, HEAD_DIM)
    queries, all_keys, values = (projected[:, :, 0], projected[:, :, 1], projected[:, :, 2])
    scores = jnp.einsum('bqhd,bkhd->bhqk', queries, all_keys, precision=highest) * HEAD_DIM ** (-0.5)
    scores = low_back(scores)
    weights = jax.nn.softmax(scores, axis=-1)
    mixed_rows = jnp.einsum('bhqk,bkhd->bqhd', low(weights), values, precision=highest)
    mixed_rows = low(low_back(mixed_rows.reshape(-1, model_width)))
    attended = low_back(jnp.dot(mixed_rows, out_low, precision=highest))
    return attended.reshape(images, length, model_width)

def expert_rows(slot_rows, w_first, b_first, w_second, b_second):
    inner_pre = low_back(jnp.dot(slot_rows, w_first, precision=highest)) + b_first
    active = low(jax.nn.gelu(inner_pre))
    return low(low_back(jnp.dot(active, w_second, precision=highest) + b_second))

def gather_rows(table_rows, slot_index):
    return table_rows[slot_index]

def forward(choices, target, source, tokens, ln1_gain, ln1_bias, w_qkv, w_out, b_out, ln2_gain, ln2_bias, w_router, w_in, b_in, w_back, b_back):
    model_width = tokens.shape[-1]
    normed = low(layer_norm(tokens, low(ln1_gain), low(ln1_bias)))
    blocks = normed.reshape(BLOCKS, IMG_DEV, SEQ, model_width)
    qkv_low = low(w_qkv)
    out_low = low(w_out)
    attended = lax.map(jax.checkpoint(lambda block_part: attend(block_part, qkv_low, out_low)), blocks)
    first_sum = tokens + attended.reshape(tokens.shape) + low(b_out)
    routed = low(layer_norm(first_sum, low(ln2_gain), low(ln2_bias))).reshape(BLOCKS, TOK_DEV, model_width)
    logits = low_back(jnp.einsum('btd,de->bte', routed, low(w_router), precision=highest))
    gates = jax.nn.softmax(logits, axis=-1)
    padded = jnp.concatenate([routed, jnp.zeros((BLOCKS, 1, model_width), jnp.float32)], axis=1)
    sent_rows = low_back(jax.vmap(gather_rows)(padded, source))
    by_expert = sent_rows.reshape(BLOCKS, EXPERTS, CAP, model_width).transpose(1, 0, 2, 3)
    by_expert = by_expert.reshape(EXPERTS, BLOCKS * CAP, model_width)
    results = lax.map(jax.checkpoint(lambda expert_pack: expert_rows(*expert_pack)), (by_expert, low(w_in), low(b_in), low(w_back), low(b_back)))
    returned = results.reshape(EXPERTS, BLOCKS, CAP, model_width).transpose(1, 0, 2, 3)
    returned = returned.reshape(BLOCKS, EXPERTS * CAP, model_width)
    returned = jnp.concatenate([returned, jnp.zeros((BLOCKS, 1, model_width), jnp.float32)], axis=1)
    picked = jax.vmap(gather_rows)(returned, target)
    chosen = jnp.take_along_axis(gates, choices, axis=-1)
    mixture = lax.optimization_barrier(jnp.sum(chosen[..., None] * picked, axis=2))
    return first_sum + mixture.reshape(tokens.shape)

def reference(tokens, cotangent, routes, order, ln1_gain, ln1_bias, w_qkv, w_out, b_out, ln2_gain, ln2_bias, w_router, w_in, b_in, w_back, b_back):
    choices = routes.reshape(BLOCKS, TOK_DEV, 2)
    target, source = jax.vmap(lambda picks, ranked: place_pairs(picks, ranked, EXPERTS, CAP))(choices, order)
    output, pullback = jax.vjp(partial(forward, choices, target, source), tokens.astype(jnp.float32), ln1_gain, ln1_bias, w_qkv, w_out, b_out, ln2_gain, ln2_bias, w_router, w_in, b_in, w_back, b_back)
    grad_tokens, grad_ln1_gain, grad_ln1_bias, grad_w_qkv, grad_w_out, grad_b_out, grad_ln2_gain, grad_ln2_bias, grad_w_router, grad_w_in, grad_b_in, grad_w_back, grad_b_back = pullback(cotangent.astype(jnp.float32))
    return (output.astype(jnp.bfloat16), grad_tokens, grad_ln1_gain, grad_ln1_bias, grad_w_qkv, grad_w_out, grad_b_out, grad_ln2_gain, grad_ln2_bias, grad_w_router, grad_w_in, grad_b_in, grad_w_back, grad_b_back)
```

```python
import functools

import jax
import jax.numpy as jnp
from jax import lax
from jax.experimental import pallas as pl
from jax.experimental.pallas import tpu as pltpu
from jax.sharding import PartitionSpec as P

HEAD_DIM = 64
LANES = 128
VECTORS = 5
f32 = jnp.float32
bf16 = jnp.bfloat16
BOTH = ("group", "expert")


def dot(a, b):
    return lax.dot_general(a, b, (((1,), (0,)), ((), ())), preferred_element_type=f32)


def dot_nt(a, b):
    return lax.dot_general(a, b, (((1,), (1,)), ((), ())), preferred_element_type=f32)


def dot_tn(a, b):
    return lax.dot_general(a, b, (((0,), (0,)), ((), ())), preferred_element_type=f32)


def iota(shape, dim):
    return lax.broadcasted_iota(jnp.int32, shape, dim)


def params(mib, grid=1):
    return pltpu.CompilerParams(
        vmem_limit_bytes=mib * 1024 * 1024, dimension_semantics=("arbitrary",) * grid
    )


def three_parts(value):
    high = value.astype(bf16).astype(f32)
    rest = value - high
    mid = rest.astype(bf16).astype(f32)
    return high, mid, rest - mid


def norm_parts(rows):
    centre = rows - jnp.mean(rows, axis=-1, keepdims=True)
    spread = jnp.mean(centre * centre, axis=-1, keepdims=True)
    scale = lax.rsqrt(spread + 1e-06)
    return centre * scale, scale


def norm_backward(grad, unit, scale, gain):
    lead = grad * gain
    first = jnp.mean(lead, axis=-1, keepdims=True)
    second = jnp.mean(lead * unit, axis=-1, keepdims=True)
    return scale * (lead - first - unit * second)


def load_weights(step, core, parts, scratch, sems):
    copies = []
    for k, (own, other) in enumerate(parts):
        copies.append(pltpu.make_async_copy(own, scratch[k].at[:, core], sems.at[2 * k]))
        copies.append(pltpu.make_async_copy(other, scratch[k].at[:, 1 - core], sems.at[2 * k + 1]))

    @pl.when(step == 0)
    def _():
        for copy in copies:
            copy.start()
        for copy in copies:
            copy.wait()


def route_kernel(labels, cap, capp, routes_ref, order_ref, rows_ref, cols_ref):
    images, _, length = routes_ref.shape
    tok_count = order_ref.shape[1]
    order = order_ref[...]
    label = iota((labels, length), 0)
    perms, hots = [], []
    counts = jnp.zeros((2 * labels, tok_count), f32)
    for i in range(images):
        perm = jnp.where(iota((length, tok_count), 0) + i * length == order, 1.0, 0.0).astype(bf16)
        hot = jnp.concatenate(
            [
                jnp.where(label == routes_ref[i, 0:1, :], 1.0, 0.0),
                jnp.where(label == routes_ref[i, 1:2, :], 1.0, 0.0),
            ],
            axis=0,
        )
        perms.append(perm)
        hots.append(hot)
        counts = counts + dot(hot.astype(bf16), perm)
    earlier = jnp.where(
        iota((tok_count, tok_count), 0) < iota((tok_count, tok_count), 1), 1.0, 0.0
    ).astype(bf16)
    before = dot(counts.astype(bf16), earlier)
    total = jnp.sum(counts[:labels], axis=1, keepdims=True)
    before = jnp.concatenate([before[:labels], before[labels:] + total], axis=0)
    before = jnp.minimum(before, float(cap)).astype(bf16)
    same = jnp.where(iota((length, length), 0) == iota((length, length), 1), 1.0, 0.0).astype(bf16)
    for i in range(images):
        back = dot_nt(before, perms[i]) * hots[i]
        slot_one = jnp.sum(back[:labels], axis=0, keepdims=True)
        slot_two = jnp.sum(back[labels:], axis=0, keepdims=True)
        one = routes_ref[i, 0:1, :].astype(f32)
        two = routes_ref[i, 1:2, :].astype(f32)
        kept_one = jnp.where(slot_one < cap, one, -1.0)
        kept_two = jnp.where(slot_two < cap, two, -1.0)
        slot_one = jnp.where(slot_one < cap, slot_one, 0.0)
        slot_two = jnp.where(slot_two < cap, slot_two, 0.0)
        aim_one = (kept_one * capp + slot_one).astype(jnp.int32)
        aim_two = (kept_two * capp + slot_two).astype(jnp.int32)
        rows_ref[i] = jnp.concatenate(
            [aim_one, aim_two, jnp.zeros((6, length), jnp.int32)], axis=0
        )
        stacked = jnp.concatenate(
            [kept_one, slot_one, kept_two, slot_two, one, two, one, two], axis=0
        ).astype(bf16)
        turned = dot_nt(same, stacked)
        cols_ref[i] = jnp.concatenate(
            [
                turned[:, 0:1] * capp + turned[:, 1:2],
                turned[:, 2:3] * capp + turned[:, 3:4],
                turned[:, 4:5],
                turned[:, 5:6],
                turned[:, 4:8],
            ],
            axis=1,
        ).astype(jnp.int32)


def route(routes, order, labels, cap, capp):
    images, _, length = routes.shape
    return pl.pallas_call(
        functools.partial(route_kernel, labels, cap, capp),
        out_shape=(
            jax.ShapeDtypeStruct((images, 8, length), jnp.int32),
            jax.ShapeDtypeStruct((images, length, 8), jnp.int32),
        ),
        compiler_params=pltpu.CompilerParams(vmem_limit_bytes=40 * 1024 * 1024),
        name="route_tokens",
    )(routes, order)


def dispatch_kernel(cap, capp, owners, local, gated, joint, rows_ref, value_ref, *refs):
    images, length, width = value_ref.shape
    outs = refs[1:] if gated else refs
    span = owners * capp
    for l in range(local):
        slots = iota((span, length), 0) + l * span
        total = None
        gate_rows = None
        for i in range(images):
            one = slots == rows_ref[i, 0:1, :]
            two = slots == rows_ref[i, 1:2, :]
            both = jnp.where(one | two, 1.0, 0.0).astype(bf16)
            part = dot(both, value_ref[i])
            total = part if total is None else total + part
            if gated:
                gates = refs[0][i]
                first = dot_nt(gates[0:8], jnp.where(one, 1.0, 0.0).astype(bf16))
                second = dot_nt(gates[8:16], jnp.where(two, 1.0, 0.0).astype(bf16))
                part = first + second
                gate_rows = part if gate_rows is None else gate_rows + part
        for o in range(owners):
            block = total[o * capp : (o + 1) * capp]
            if joint:
                outs[0][o, l * capp : (l + 1) * capp, :] = block.astype(bf16)
            else:
                outs[l][o] = block.astype(bf16)
            if gated:
                tail = block[capp - 16 :, 0:capp]
                spare = gate_rows[:, o * capp : (o + 1) * capp]
                line = iota((16, capp), 0) - (cap - (capp - 16))
                for k in range(3):
                    tail = jnp.where(line == k, spare[k : k + 1], tail)
                outs[l][o, capp - 16 :, 0:capp] = tail.astype(bf16)


def dispatch(rows, values, gates, cap, capp, owners, local):
    width = values.shape[2]
    joint = gates is None
    operands = (rows, values) if joint else (rows, values, gates)
    out_shape = [jax.ShapeDtypeStruct((owners, capp, width), bf16)] * local
    if joint:
        out_shape = [jax.ShapeDtypeStruct((owners, local * capp, width), bf16)]
    return pl.pallas_call(
        functools.partial(dispatch_kernel, cap, capp, owners, local, not joint, joint),
        out_shape=out_shape,
        compiler_params=pltpu.CompilerParams(vmem_limit_bytes=40 * 1024 * 1024),
        name="fill_slots",
    )(*operands)


def forward_kernel(
    labels,
    core_ref,
    tokens_ref,
    routes_ref,
    one_own,
    one_other,
    two_own,
    two_other,
    qkv_ref,
    mixed_ref,
    lse_ref,
    first_ref,
    routed_ref,
    gates_ref,
    gate_rows_ref,
    total_ref,
    one_ref,
    two_ref,
    misc_ref,
    sems,
):
    _, length, width = tokens_ref.shape
    step = pl.program_id(0)
    parts = ((one_own, one_other), (two_own, two_other))
    load_weights(step, core_ref[0], parts, (one_ref, two_ref), sems)

    @pl.when(step == 0)
    def _():
        misc_ref[...] = jnp.transpose(two_ref[..., 2 * width :].reshape(width, LANES))

    vec = [misc_ref[labels + k : labels + k + 1, :].astype(f32) for k in range(VECTORS)]
    rows = tokens_ref[0].astype(f32)
    unit, _ = norm_parts(rows)
    normed = (unit * vec[0] + vec[1]).astype(bf16)
    projected = jnp.concatenate(
        [
            dot(normed, one_ref[...].reshape(width, 2 * width)).astype(bf16),
            dot(normed, two_ref[..., 0:width].reshape(width, width)).astype(bf16),
        ],
        axis=1,
    )
    qkv_ref[0] = projected
    lane = iota((length, LANES), 1)
    low_half = lane < HEAD_DIM
    pieces = []
    for pair in range(width // LANES):
        at = pair * LANES
        query = projected[:, at : at + LANES] * jnp.asarray(HEAD_DIM**-0.5, bf16)
        keys = projected[:, width + at : width + at + LANES]
        values = projected[:, 2 * width + at : 2 * width + at + LANES]
        mixed = None
        for half in range(2):
            own = low_half if half == 0 else jnp.logical_not(low_half)
            scores = dot_nt(jnp.where(own, query, jnp.zeros_like(query)), keys)
            top = jnp.max(scores, axis=-1, keepdims=True)
            shifted = jnp.exp(scores - top)
            total = jnp.sum(shifted, axis=-1, keepdims=True)
            head = 2 * pair + half
            total_ref[0:length, :] = jnp.where(
                lane == head, top + jnp.log(total), total_ref[0:length, :]
            )
            low = (shifted * (1.0 / total)).astype(bf16)
            part = dot(low, jnp.where(own, values, jnp.zeros_like(values)))
            mixed = part if mixed is None else mixed + part
        pieces.append(mixed.astype(bf16))
    mixed = jnp.concatenate(pieces, axis=1)
    mixed_ref[0] = mixed
    lse_ref[0] = jnp.transpose(total_ref[...])[0:16]
    w_out = two_ref[..., width : 2 * width].reshape(width, width)
    first = rows + dot(mixed, w_out) + vec[2]
    first_ref[0] = first
    unit, _ = norm_parts(first)
    routed = (unit * vec[3] + vec[4]).astype(bf16)
    routed_ref[0] = routed
    router = misc_ref[0:labels, :]
    logits = dot_nt(routed, router)
    shifted = jnp.exp(logits - jnp.max(logits, axis=1, keepdims=True))
    gates_ref[0] = shifted / jnp.sum(shifted, axis=1, keepdims=True)
    logits = dot_nt(router, routed)
    shifted = jnp.exp(logits - jnp.max(logits, axis=0, keepdims=True))
    gates = shifted / jnp.sum(shifted, axis=0, keepdims=True)
    label = iota((labels, length), 0)
    blank = jnp.zeros((5, length), f32)
    stack = []
    for k in range(2):
        chosen = jnp.where(label == routes_ref[0, k : k + 1, :], gates, 0.0)
        stack += [*three_parts(jnp.sum(chosen, axis=0, keepdims=True)), blank]
    gate_rows_ref[0] = jnp.concatenate(stack, axis=0).astype(bf16)


def weight_scratch(packed):
    return [
        pltpu.VMEM((part[0].shape[0], 2, *part[0].shape[1:]), part[0].dtype) for part in packed
    ]


def forward(core, tokens, routes, packed, labels):
    images, length, width = tokens.shape
    whole = lambda *tail: pl.BlockSpec((1, *tail), lambda i: (i, 0, 0))
    lanes = -(-length // LANES) * LANES
    return pl.pallas_call(
        functools.partial(forward_kernel, labels),
        grid=(images,),
        in_specs=[
            pl.BlockSpec(memory_space=pltpu.SMEM),
            whole(length, width),
            whole(2, length),
            *[pl.BlockSpec(memory_space=pl.ANY)] * 4,
        ],
        out_specs=[
            whole(length, 3 * width),
            whole(length, width),
            whole(16, lanes),
            whole(length, width),
            whole(length, width),
            whole(length, labels),
            whole(16, length),
        ],
        out_shape=[
            jax.ShapeDtypeStruct((images, length, 3 * width), bf16),
            jax.ShapeDtypeStruct((images, length, width), bf16),
            jax.ShapeDtypeStruct((images, 16, lanes), f32),
            jax.ShapeDtypeStruct((images, length, width), f32),
            jax.ShapeDtypeStruct((images, length, width), bf16),
            jax.ShapeDtypeStruct((images, length, labels), f32),
            jax.ShapeDtypeStruct((images, 16, length), bf16),
        ],
        scratch_shapes=[
            pltpu.VMEM((lanes, LANES), f32),
            *weight_scratch(packed),
            pltpu.VMEM((LANES, width), bf16),
            pltpu.SemaphoreType.DMA((4,)),
        ],
        compiler_params=params(40),
        cost_estimate=pl.CostEstimate(
            flops=16_000_000_000, bytes_accessed=20_000_000, transcendentals=2_000_000
        ),
        name="attention_forward",
    )(core, tokens, routes, *packed[0], *packed[1])


def expert_kernel(
    cap,
    rows_ref,
    cot_ref,
    win_ref,
    wback_ref,
    bback_ref,
    out_ref,
    grad_ref,
    gwin_ref,
    gwback_ref,
    turned_ref,
    grad_out_ref,
    out_acc_ref,
    grad_acc_ref,
    active_ref,
    inner_ref,
    bias_ref,
):
    owners, capp, width = rows_ref.shape
    hidden = win_ref.shape[-1]
    total = owners * capp
    spare = cap - (capp - 16)
    step = pl.program_id(0)
    last = pl.num_programs(0) - 1

    @pl.when(step == 0)
    def _():
        summed = jnp.zeros((1, width), f32)
        for b in range(owners):
            tail = rows_ref[b, capp - 16 :, 0:capp].astype(f32)
            gate = (
                tail[spare : spare + 1] + tail[spare + 1 : spare + 2] + tail[spare + 2 : spare + 3]
            )
            gate = jnp.transpose(jnp.broadcast_to(gate, (LANES, capp)))[:, 0:1]
            part = (cot_ref[b].astype(f32) * gate).astype(bf16)
            grad_out_ref[b * capp : (b + 1) * capp, :] = part
            summed = summed + jnp.sum(part.astype(f32), axis=0, keepdims=True)
            turned_ref[:, b * capp : (b + 1) * capp] = jnp.transpose(rows_ref[b])
        bias_ref[...] = jnp.broadcast_to(summed, bias_ref.shape)
        out_acc_ref[...] = jnp.zeros_like(out_acc_ref)
        grad_acc_ref[...] = jnp.zeros_like(grad_acc_ref)

    first = win_ref[...].reshape(width, hidden)
    second = wback_ref[0, 0, 0:hidden, :]
    bias = wback_ref[0, 0, hidden : hidden + 16, :].astype(f32)[0:1, 0:hidden]
    bias_sum = jnp.zeros((1, hidden), f32)
    per = max(1, 256 // capp)
    k0 = 0.7978845608028654
    k1 = 0.044715
    for c in range(owners // per):
        at = slice(c * per * capp, (c + 1) * per * capp)
        block = rows_ref[c * per : (c + 1) * per].reshape(per * capp, width)
        inner = dot(block, first) + bias
        square = inner * inner
        curve = jnp.tanh(inner * (k0 + (k0 * k1) * square))
        half = 0.5 * (1.0 + curve)
        low = (inner * half).astype(bf16)
        active_ref[at, :] = low
        slope = half + (0.5 * inner) * (1.0 - curve * curve) * (k0 + (3.0 * k0 * k1) * square)
        grad_inner = dot_nt(grad_out_ref[at, :], second) * slope
        bias_sum = bias_sum + jnp.sum(grad_inner, axis=0, keepdims=True)
        grad_low = grad_inner.astype(bf16)
        inner_ref[at, :] = grad_low
        out_acc_ref[at, :] += dot(low, second)
        grad_acc_ref[at, :] += dot_nt(grad_low, first)
    gwin_ref[...] = dot(turned_ref[...], inner_ref[...]).astype(bf16).reshape(gwin_ref.shape)
    gwback_ref[0, 0:hidden, :] = dot_tn(active_ref[...], grad_out_ref[...]).astype(bf16)
    row = iota((16, width), 0)
    if hidden < width:
        bias_sum = jnp.concatenate([bias_sum, jnp.zeros((1, width - hidden), f32)], axis=1)
    pad = jnp.where(row == 0, bias_sum, jnp.where(row == 1, bias_ref[0:1, :], 0.0))
    gwback_ref[0, hidden : hidden + 16, :] = pad.astype(bf16)

    @pl.when(step == last)
    def _():
        for b in range(owners):
            at = slice(b * capp, (b + 1) * capp)
            result = (out_acc_ref[at, :] + bback_ref[...].astype(f32)).astype(bf16)
            out_ref[b] = result
            score = jnp.sum(result.astype(f32) * cot_ref[b].astype(f32), axis=1, keepdims=True)
            score = jnp.transpose(jnp.broadcast_to(score, (capp, LANES)))[0:1, :]
            back = grad_acc_ref[at, :]
            grad_ref[b] = back.astype(bf16)
            tail = back[capp - 16 :, 0:capp]
            line = iota((16, capp), 0) - spare
            for k, part in enumerate(three_parts(score)):
                tail = jnp.where(line == k, part, tail)
            grad_ref[b, capp - 16 :, 0:capp] = tail.astype(bf16)


def expert(rows, cots, win, wback, bback, which, cap):
    owners, capp, width = rows.shape
    groups, _, depth, wide = win.shape
    hidden = wide // groups
    total = owners * capp
    full = lambda shape: pl.BlockSpec(shape, lambda j: (0,) * len(shape))
    flops = 2 * 6 * total * width * wide
    return pl.pallas_call(
        functools.partial(expert_kernel, cap),
        grid=(groups,),
        in_specs=[
            full((owners, capp, width)),
            pl.BlockSpec((owners, capp, width), lambda j: (0, which, 0)),
            pl.BlockSpec((groups, 1, depth, hidden), lambda j: (0, which, 0, j)),
            pl.BlockSpec((1, 1, hidden + 16, width), lambda j: (j, which, 0, 0)),
            full((1, width)),
        ],
        out_specs=[
            full((owners, capp, width)),
            full((owners, capp, width)),
            pl.BlockSpec((groups, depth, hidden), lambda j: (0, 0, j)),
            pl.BlockSpec((1, hidden + 16, width), lambda j: (j, 0, 0)),
        ],
        out_shape=[
            jax.ShapeDtypeStruct((owners, capp, width), bf16),
            jax.ShapeDtypeStruct((owners, capp, width), bf16),
            jax.ShapeDtypeStruct((groups, depth, wide), bf16),
            jax.ShapeDtypeStruct((groups, hidden + 16, width), bf16),
        ],
        scratch_shapes=[
            pltpu.VMEM((width, total), bf16),
            pltpu.VMEM((total, width), bf16),
            pltpu.VMEM((total, width), f32),
            pltpu.VMEM((total, width), f32),
            pltpu.VMEM((total, hidden), bf16),
            pltpu.VMEM((total, hidden), bf16),
            pltpu.VMEM((8, width), f32),
        ],
        compiler_params=params(56),
        cost_estimate=pl.CostEstimate(
            flops=flops, bytes_accessed=30_000_000, transcendentals=total * wide
        ),
        name="expert_rows",
    )(rows, cots, win, wback, bback)


def add_to(ref, columns, value):
    shape = (*ref.shape[:-1], value.shape[-1])
    ref[..., columns] += value.reshape(shape)


def backward_kernel(
    labels,
    local,
    cap,
    core_ref,
    tokens_ref,
    cot_ref,
    cols_ref,
    qkv_ref,
    mixed_ref,
    lse_ref,
    first_ref,
    routed_ref,
    gates_ref,
    one_own,
    one_other,
    two_own,
    two_other,
    *refs,
):
    slots = refs[:local]
    (
        grad_tokens_ref,
        keep_one_ref,
        send_one_ref,
        keep_two_ref,
        send_two_ref,
        grad_one_ref,
        grad_two_ref,
        stack_ref,
        vec_ref,
        score_ref,
        one_ref,
        two_ref,
        misc_ref,
        sems,
    ) = refs[local:]
    _, length, width = tokens_ref.shape
    owners, capp, _ = slots[0].shape
    spare = cap - (capp - 16)
    span = owners * capp
    step = pl.program_id(0)
    parts = ((one_own, one_other), (two_own, two_other))
    load_weights(step, core_ref[0], parts, (one_ref, two_ref), sems)

    @pl.when(step == 0)
    def _():
        misc_ref[...] = jnp.transpose(two_ref[..., 2 * width :].reshape(width, LANES))

    vec = [misc_ref[labels + k : labels + k + 1, :].astype(f32) for k in range(VECTORS)]

    @pl.when(step == 0)
    def _():
        grad_one_ref[...] = jnp.zeros_like(grad_one_ref)
        grad_two_ref[...] = jnp.zeros_like(grad_two_ref)
        vec_ref[...] = jnp.zeros_like(vec_ref)
        stack_ref[...] = jnp.zeros_like(stack_ref)
        for l in range(local):
            for o in range(owners):
                score_ref[:, l * span + o * capp : l * span + (o + 1) * capp] = slots[l][
                    o, capp - 16 :, 0:capp
                ]

    cot = cot_ref[0].astype(f32)
    aim_one, aim_two = cols_ref[0, :, 0:1], cols_ref[0, :, 1:2]
    route_one, route_two = cols_ref[0, :, 2:3], cols_ref[0, :, 3:4]
    picked = None
    gate_one = None
    gate_two = None
    for l in range(local):
        lane = iota((length, span), 1) + l * span
        one = jnp.where(lane == aim_one, 1.0, 0.0)
        two = jnp.where(lane == aim_two, 1.0, 0.0)
        part = dot((one + two).astype(bf16), slots[l][...].reshape(span, width))
        picked = part if picked is None else picked + part
        score = score_ref[:, l * span : (l + 1) * span]
        part_one = dot_nt(one.astype(bf16), score)
        part_two = dot_nt(two.astype(bf16), score)
        gate_one = part_one if gate_one is None else gate_one + part_one
        gate_two = part_two if gate_two is None else gate_two + part_two
    line = iota((length, 16), 1)
    mine = (line >= spare) & (line < spare + 3)
    gate_one = jnp.sum(jnp.where(mine, gate_one, 0.0), axis=1, keepdims=True)
    gate_two = jnp.sum(jnp.where(mine, gate_two, 0.0), axis=1, keepdims=True)
    label = iota((length, labels), 1)
    grad_gates = jnp.where(label == route_one, gate_one, 0.0) + jnp.where(
        label == route_two, gate_two, 0.0
    )
    gates = gates_ref[0]
    inner = jnp.sum(grad_gates * gates, axis=1, keepdims=True)
    grad_logits = (gates * (grad_gates - inner)).astype(bf16)
    router = misc_ref[0:labels, :]
    routed = routed_ref[0]
    stack_ref[0:labels, :] += dot_tn(grad_logits, routed)
    grad_routed = dot(grad_logits, router) + picked
    unit, scale = norm_parts(first_ref[0])
    vec_ref[3:4, :] += jnp.sum(grad_routed * unit, axis=0, keepdims=True)
    vec_ref[4:5, :] += jnp.sum(grad_routed, axis=0, keepdims=True)
    grad_first = cot + norm_backward(grad_routed, unit, scale, vec[3])
    vec_ref[2:3, :] += jnp.sum(grad_first, axis=0, keepdims=True)
    first_low = grad_first.astype(bf16)
    add_to(grad_two_ref, slice(width, 2 * width), dot_tn(mixed_ref[0], first_low))
    w_out = two_ref[..., width : 2 * width].reshape(width, width)
    grad_mixed = dot_nt(first_low, w_out).astype(bf16)
    low_half = iota((length, LANES), 1) < HEAD_DIM
    rate = jnp.asarray(HEAD_DIM**-0.5, bf16)
    grads = [[], [], []]
    for pair in range(width // LANES):
        at = pair * LANES
        query = qkv_ref[0, :, at : at + LANES] * rate
        keys = qkv_ref[0, :, width + at : width + at + LANES]
        values = qkv_ref[0, :, 2 * width + at : 2 * width + at + LANES]
        mix = grad_mixed[:, at : at + LANES]
        grad_q = grad_k = grad_v = None
        for half in range(2):
            own = low_half if half == 0 else jnp.logical_not(low_half)
            none = jnp.zeros_like(query)
            query_own = jnp.where(own, query, none)
            mix_own = jnp.where(own, mix, none)
            head = 2 * pair + half
            probs = jnp.exp(dot_nt(keys, query_own) - lse_ref[0, head : head + 1, 0:length])
            grad_probs = dot_nt(values, mix_own)
            inner = jnp.sum(grad_probs * probs, axis=0, keepdims=True)
            scores = (probs * (grad_probs - inner)).astype(bf16)
            part = dot(probs.astype(bf16), mix_own)
            grad_v = part if grad_v is None else grad_v + part
            part = dot(scores, query_own)
            grad_k = part if grad_k is None else grad_k + part
            part = dot_tn(scores, jnp.where(own, keys, none))
            grad_q = part if grad_q is None else grad_q + part
        grads[0].append((grad_q * HEAD_DIM**-0.5).astype(bf16))
        grads[1].append(grad_k.astype(bf16))
        grads[2].append(grad_v.astype(bf16))
    grad_one = jnp.concatenate(grads[0] + grads[1], axis=1)
    grad_two = jnp.concatenate(grads[2], axis=1)
    rows = tokens_ref[0].astype(f32)
    unit, scale = norm_parts(rows)
    normed = (unit * vec[0] + vec[1]).astype(bf16)
    add_to(grad_one_ref, slice(None), dot_tn(normed, grad_one))
    add_to(grad_two_ref, slice(0, width), dot_tn(normed, grad_two))
    grad_normed = dot_nt(grad_one, one_ref[...].reshape(width, 2 * width))
    grad_normed += dot_nt(grad_two, two_ref[..., 0:width].reshape(width, width))
    vec_ref[0:1, :] += jnp.sum(grad_normed * unit, axis=0, keepdims=True)
    vec_ref[1:2, :] += jnp.sum(grad_normed, axis=0, keepdims=True)
    grad_tokens_ref[0] = grad_first + norm_backward(grad_normed, unit, scale, vec[0])

    @pl.when(step == pl.num_programs(0) - 1)
    def _():
        stack_ref[labels : labels + 8, :] = vec_ref[...]
        add_to(grad_two_ref, slice(2 * width, None), jnp.transpose(stack_ref[...]))
        mine, other = core_ref[0], 1 - core_ref[0]
        keep_one_ref[...] = grad_one_ref[:, mine]
        keep_two_ref[...] = grad_two_ref[:, mine]
        send_one_ref[...] = grad_one_ref[:, other].astype(bf16)
        send_two_ref[...] = grad_two_ref[:, other].astype(bf16)


def backward(
    core, tokens, cot, cols, qkv, mixed, lse, first, routed, gates, cap, packed, slots, labels
):
    images, length, width = tokens.shape
    local = len(slots)
    owners, capp, _ = slots[0].shape
    whole = lambda *tail: pl.BlockSpec((1, *tail), lambda i: (i, 0, 0))
    shapes = [part[0].shape for part in packed]
    still = lambda shape: pl.BlockSpec(shape, lambda i: (0, 0, 0))
    return pl.pallas_call(
        functools.partial(backward_kernel, labels, local, cap),
        grid=(images,),
        in_specs=[
            pl.BlockSpec(memory_space=pltpu.SMEM),
            whole(length, width),
            whole(length, width),
            whole(length, 8),
            whole(length, 3 * width),
            whole(length, width),
            whole(*lse.shape[1:]),
            whole(length, width),
            whole(length, width),
            whole(length, labels),
            *[pl.BlockSpec(memory_space=pl.ANY)] * 4,
            *[pl.BlockSpec((owners, capp, width), lambda i: (0, 0, 0))] * local,
        ],
        out_specs=[
            whole(length, width),
            *[still(shape) for shape in shapes for _ in range(2)],
        ],
        out_shape=[
            jax.ShapeDtypeStruct((images, length, width), f32),
            *[jax.ShapeDtypeStruct(shape, kind) for shape in shapes for kind in (f32, bf16)],
        ],
        scratch_shapes=[
            *[pltpu.VMEM((shape[0], 2, *shape[1:]), f32) for shape in shapes],
            pltpu.VMEM((LANES, width), f32),
            pltpu.VMEM((8, width), f32),
            pltpu.VMEM((16, local * owners * capp), bf16),
            *weight_scratch(packed),
            pltpu.VMEM((LANES, width), bf16),
            pltpu.SemaphoreType.DMA((4,)),
        ],
        compiler_params=params(58),
        cost_estimate=pl.CostEstimate(
            flops=40_000_000_000, bytes_accessed=40_000_000, transcendentals=2_000_000
        ),
        name="attention_backward",
    )(
        core,
        tokens,
        cot,
        cols,
        qkv,
        mixed,
        lse,
        first,
        routed,
        gates,
        *packed[0],
        *packed[1],
        *slots,
    )


def output_kernel(labels, local, first_ref, cols_ref, gates_ref, slots_ref, out_ref):
    _, length, width = first_ref.shape
    owners, capp, _ = slots_ref.shape
    capp = capp // local
    span = owners * capp
    label = iota((length, labels), 1)
    total = first_ref[0]
    for k in range(2):
        picked = None
        for l in range(local):
            lane = iota((length, span), 1) + l * span
            hot = jnp.where(lane == cols_ref[0, :, k : k + 1], 1.0, 0.0).astype(bf16)
            part = dot(hot, slots_ref[:, l * capp : (l + 1) * capp, :].reshape(span, width))
            picked = part if picked is None else picked + part
        chosen = jnp.where(label == cols_ref[0, :, k + 2 : k + 3], gates_ref[0], 0.0)
        total = total + jnp.sum(chosen, axis=1, keepdims=True) * picked
    out_ref[0] = total.astype(bf16)


def combine(first, cols, gates, slots, local):
    images, length, width = first.shape
    labels = gates.shape[2]
    whole = lambda *tail: pl.BlockSpec((1, *tail), lambda i: (i, 0, 0))
    return pl.pallas_call(
        functools.partial(output_kernel, labels, local),
        grid=(images,),
        in_specs=[
            whole(length, width),
            whole(length, 8),
            whole(length, labels),
            pl.BlockSpec(slots.shape, lambda i: (0, 0, 0)),
        ],
        out_specs=whole(length, width),
        out_shape=jax.ShapeDtypeStruct((images, length, width), bf16),
        compiler_params=params(40),
        name="combine_outputs",
    )(first, cols, gates, slots)


def bits_of(groups, owners):
    outer = [("group", k) for k in reversed(range(1, groups.bit_length() - 1))]
    inner = [("expert", k) for k in reversed(range(owners.bit_length() - 1))]
    return outer, inner


def swap(block, hop, sizes):
    axis, bit = hop
    return lax.ppermute(block, axis, [(d, d ^ (1 << bit)) for d in range(sizes[axis])])


def own_bit(hop):
    return lax.rem(lax.axis_index(hop[0]) >> hop[1], 2)


def spread(block, have, hops, order, sizes):
    for hop in hops:
        other = swap(block, hop, sizes)
        have = sorted([*have, hop], key=order.index)
        at = have.index(hop)
        mine = own_bit(hop) == 0
        block = jnp.stack(
            [jnp.where(mine, block, other), jnp.where(mine, other, block)], axis=at
        )
    return block, have


def gather_back(total, hops, order, sizes):
    have = list(order)
    for hop in hops:
        at = have.index(hop)
        have.remove(hop)
        bit = own_bit(hop)
        away = lax.dynamic_index_in_dim(total, 1 - bit, at, keepdims=False)
        stay = lax.dynamic_index_in_dim(total, bit, at, keepdims=False)
        total = stay + swap(away.astype(bf16), hop, sizes).astype(f32)
    return total


def per_device(
    groups,
    owners,
    tokens,
    cotangent,
    routes,
    order,
    ln1_gain,
    ln1_bias,
    w_qkv,
    w_out,
    b_out,
    ln2_gain,
    ln2_bias,
    w_router,
    w_in,
    b_in,
    w_back,
    b_back,
):
    images, length, width = tokens.shape
    tok_count = images * length
    labels = w_router.shape[1]
    local = labels // owners
    depth = w_in.shape[1]
    hidden = w_back.shape[1]
    cap = max(2, 5 * tok_count // (2 * labels))
    capp = -(-(cap + 3) // 16) * 16

    own = width // (groups * owners)
    sizes = {"group": groups, "expert": owners}
    outer, inner = bits_of(groups, owners)
    order_of_hops = [*outer, *inner]
    sibling = ("group", 0)
    core = own_bit(sibling).astype(jnp.int32).reshape(1)
    routes_one = [*inner, *outer]
    routes_two = [*inner[:-1], *outer, *inner[-1:]]
    router = w_router.reshape(own, owners, local).swapaxes(1, 2).reshape(own, labels)
    vectors = jnp.stack([ln1_gain, ln1_bias, b_out, ln2_gain, ln2_bias], axis=1)
    blank = jnp.zeros((own, LANES - labels - VECTORS), f32)
    slices = [
        w_qkv[:, : 2 * width].astype(bf16),
        jnp.concatenate([w_qkv[:, 2 * width :], w_out, router, vectors, blank], axis=1).astype(bf16),
    ]
    near = inner[:-1]
    slices = [spread(block, [], near, order_of_hops, sizes) for block in slices]

    marks = (routes % local) * owners + routes // local
    marks = marks.swapaxes(1, 2)
    rows, cols = route(marks, order, labels, cap, capp)
    cots = dispatch(rows, cotangent, None, cap, capp, owners, local)[0]
    exchange = lambda block: lax.all_to_all(block, "expert", 0, 0, tiled=True)
    cots, one, two = lax.optimization_barrier((cots, slices[0][0], slices[1][0]))
    cots = exchange(cots)
    packed = []
    for block, (_, have), path in ((one, slices[0], routes_one), (two, slices[1], routes_two)):
        half, _ = spread(block, have, path[len(near) :], order_of_hops, sizes)
        half = half.reshape(groups // 2, owners * own, block.shape[-1])
        packed.append((half, swap(half, sibling, sizes)))

    biases = jnp.zeros((local, 16, width), f32)
    biases = biases.at[:, 0, :hidden].set(b_in).at[:, 1, :depth].set(b_back)
    wback = jnp.concatenate([w_back, biases], axis=1).astype(bf16)
    win = lax.all_gather(w_in.astype(bf16), "group")
    wback = lax.all_gather(wback, "group")

    qkv, mixed, lse, first, routed, gates, gate_rows = forward(core, tokens, marks, packed, labels)
    sent = dispatch(rows, routed, gate_rows, cap, capp, owners, local)
    cots, *sent = lax.optimization_barrier((cots, *sent))
    sent = [exchange(block) for block in sent]
    outcomes, backs, share_in, share_back = [], [], [], []
    for l in range(local):
        bias = wback[:, l, hidden + 1, :depth].reshape(1, width)
        outcome, back, grad_in, grad_back = expert(sent[l], cots, win, wback, bias, l, cap)
        if l + 1 < local:
            back, sent[l + 1] = lax.optimization_barrier((back, sent[l + 1]))
        if l:
            back, backs[-1] = lax.optimization_barrier((back, backs[-1]))
        backs.append(exchange(back))
        outcomes.append(outcome)
        share_in.append(lax.psum_scatter(grad_in, "group", scatter_dimension=0))
        share_back.append(lax.psum_scatter(grad_back, "group", scatter_dimension=0))
    joined = jnp.concatenate(outcomes, axis=1)
    joined, *backs = lax.optimization_barrier((joined, *backs))
    joined = exchange(joined)
    share_in = jnp.stack(share_in).astype(f32)
    share_back = jnp.stack(share_back).astype(f32)
    grad_tokens, *halves = backward(
        core,
        tokens,
        cotangent,
        cols,
        qkv,
        mixed,
        lse,
        first,
        routed,
        gates,
        cap,
        packed,
        backs,
        labels,
    )
    output = combine(first, cols, gates, joined, local)
    sums = []
    for keep, away, path in (
        (halves[0], halves[1], routes_one[::-1]),
        (halves[2], halves[3], routes_two[::-1]),
    ):
        total = keep + swap(away, sibling, sizes).astype(f32)
        total = total.reshape(*[2] * len(order_of_hops), own, keep.shape[2])
        first_hops = path[: len(path) - len(near)]
        sums.append(gather_back(total, first_hops, order_of_hops, sizes))
    one, two, output = lax.optimization_barrier((*sums, output))
    rest = [hop for hop in order_of_hops if hop in near]
    sums = [gather_back(part, near[::-1], rest, sizes) for part in (one, two)]
    one, two = sums
    small = two[:, 2 * width :]
    grad_router = small[:, :labels].reshape(own, local, owners).swapaxes(1, 2).reshape(own, labels)
    place = lax.axis_index("group") * depth
    return (
        output,
        grad_tokens,
        small[:, labels],
        small[:, labels + 1],
        jnp.concatenate([one, two[:, :width]], axis=1),
        two[:, width : 2 * width],
        small[:, labels + 2],
        small[:, labels + 3],
        small[:, labels + 4],
        grad_router,
        share_in,
        share_back[:, hidden, :hidden],
        share_back[:, :hidden],
        lax.dynamic_slice_in_dim(share_back[:, hidden + 1], place, depth, axis=1),
    )


def solution(mesh):
    rows = P(BOTH, None)
    line = P(BOTH)
    tall = P(BOTH, None, None)
    deep = P("expert", "group", None)
    flat = P("expert", "group")
    groups, owners = mesh.shape["group"], mesh.shape["expert"]
    return jax.shard_map(
        functools.partial(per_device, groups, owners),
        mesh=mesh,
        in_specs=(
            tall,
            tall,
            tall,
            rows,
            line,
            line,
            rows,
            rows,
            line,
            line,
            line,
            rows,
            deep,
            flat,
            deep,
            flat,
        ),
        out_specs=(
            tall,
            tall,
            line,
            line,
            rows,
            rows,
            line,
            line,
            line,
            rows,
            deep,
            flat,
            deep,
            flat,
        ),
        check_vma=False,
    )
```

```python
import functools

import jax
import jax.numpy as jnp
from jax import lax
from jax.experimental import pallas as pl
from jax.experimental.pallas import tpu as pltpu
from jax.sharding import PartitionSpec as P

HEAD_DIM = 64
LANES = 128
VECTORS = 5
f32 = jnp.float32
bf16 = jnp.bfloat16
BOTH = ("group", "expert")


def dot(a, b):
    return lax.dot_general(a, b, (((1,), (0,)), ((), ())), preferred_element_type=f32)


def dot_nt(a, b):
    return lax.dot_general(a, b, (((1,), (1,)), ((), ())), preferred_element_type=f32)


def dot_tn(a, b):
    return lax.dot_general(a, b, (((0,), (0,)), ((), ())), preferred_element_type=f32)


def iota(shape, dim):
    return lax.broadcasted_iota(jnp.int32, shape, dim)


def params(mib, grid=1):
    return pltpu.CompilerParams(
        vmem_limit_bytes=mib * 1024 * 1024, dimension_semantics=("arbitrary",) * grid
    )


def three_parts(value):
    high = value.astype(bf16).astype(f32)
    rest = value - high
    mid = rest.astype(bf16).astype(f32)
    return high, mid, rest - mid


def norm_parts(rows):
    centre = rows - jnp.mean(rows, axis=-1, keepdims=True)
    spread = jnp.mean(centre * centre, axis=-1, keepdims=True)
    scale = lax.rsqrt(spread + 1e-06)
    return centre * scale, scale


def norm_backward(grad, unit, scale, gain):
    lead = grad * gain
    first = jnp.mean(lead, axis=-1, keepdims=True)
    second = jnp.mean(lead * unit, axis=-1, keepdims=True)
    return scale * (lead - first - unit * second)


def load_weights(step, core, parts, scratch, sems):
    copies = []
    for k, (own, other) in enumerate(parts):
        copies.append(pltpu.make_async_copy(own, scratch[k].at[:, core], sems.at[2 * k]))
        copies.append(pltpu.make_async_copy(other, scratch[k].at[:, 1 - core], sems.at[2 * k + 1]))

    @pl.when(step == 0)
    def _():
        for copy in copies:
            copy.start()
        for copy in copies:
            copy.wait()


def pack_kernel(owners, qkv_ref, out_ref, router_ref, vec_ref, one_ref, two_ref):
    own, width = out_ref.shape
    labels = router_ref.shape[1]
    local = labels // owners
    one_ref[...] = qkv_ref[:, 0 : 2 * width].astype(bf16)
    two_ref[:, 0:width] = qkv_ref[:, 2 * width :].astype(bf16)
    two_ref[:, width : 2 * width] = out_ref[...].astype(bf16)
    router = router_ref[...]
    columns = [
        router[:, o * local + l : o * local + l + 1] for l in range(local) for o in range(owners)
    ]
    vectors = jnp.concatenate([vec_ref[...], jnp.zeros((LANES - VECTORS, own), f32)], axis=0)
    if own < LANES:
        vectors = jnp.concatenate([vectors, jnp.zeros((LANES, LANES - own), f32)], axis=1)
    vectors = jnp.transpose(vectors)[0:own, 0:VECTORS]
    blank = jnp.zeros((own, LANES - labels - VECTORS), f32)
    two_ref[:, 2 * width :] = jnp.concatenate([*columns, vectors, blank], axis=1).astype(bf16)


def pack(w_qkv, w_out, w_router, vectors, owners):
    own, width = w_out.shape
    return pl.pallas_call(
        functools.partial(pack_kernel, owners),
        out_shape=[
            jax.ShapeDtypeStruct((own, 2 * width), bf16),
            jax.ShapeDtypeStruct((own, 2 * width + LANES), bf16),
        ],
        name="pack_weights",
    )(w_qkv, w_out, w_router, vectors)


def dense_out_kernel(owners, one_ref, one_in, two_ref, two_in, qkv_ref, out_ref, router_ref, vec_ref):
    own, width = out_ref.shape
    labels = router_ref.shape[1]
    local = labels // owners
    one = one_ref[...] + one_in[...].astype(f32)
    two = two_ref[...] + two_in[...].astype(f32)
    qkv_ref[:, 0 : 2 * width] = one
    qkv_ref[:, 2 * width :] = two[:, 0:width]
    out_ref[...] = two[:, width : 2 * width]
    small = two[:, 2 * width :]
    columns = [
        small[:, l * owners + o : l * owners + o + 1] for o in range(owners) for l in range(local)
    ]
    router_ref[...] = jnp.concatenate(columns, axis=1)
    if own < LANES:
        small = jnp.concatenate([small, jnp.zeros((LANES - own, LANES), f32)], axis=0)
    vec_ref[...] = jnp.transpose(small)[labels : labels + 8, 0:own]


def dense_out(one, two, labels, owners):
    own = one[0].shape[0]
    width = one[0].shape[1] // 2
    return pl.pallas_call(
        functools.partial(dense_out_kernel, owners),
        out_shape=[
            jax.ShapeDtypeStruct((own, 3 * width), f32),
            jax.ShapeDtypeStruct((own, width), f32),
            jax.ShapeDtypeStruct((own, labels), f32),
            jax.ShapeDtypeStruct((8, own), f32),
        ],
        name="dense_gradients",
    )(*one, *two)


def route_kernel(labels, cap, capp, routes_ref, order_ref, rows_ref, cols_ref):
    images, _, length = routes_ref.shape
    tok_count = order_ref.shape[1]
    order = order_ref[...]
    label = iota((labels, length), 0)
    perms, hots = [], []
    counts = jnp.zeros((2 * labels, tok_count), f32)
    for i in range(images):
        perm = jnp.where(iota((length, tok_count), 0) + i * length == order, 1.0, 0.0).astype(bf16)
        hot = jnp.concatenate(
            [
                jnp.where(label == routes_ref[i, 0:1, :], 1.0, 0.0),
                jnp.where(label == routes_ref[i, 1:2, :], 1.0, 0.0),
            ],
            axis=0,
        )
        perms.append(perm)
        hots.append(hot)
        counts = counts + dot(hot.astype(bf16), perm)
    earlier = jnp.where(
        iota((tok_count, tok_count), 0) < iota((tok_count, tok_count), 1), 1.0, 0.0
    ).astype(bf16)
    before = dot(counts.astype(bf16), earlier)
    total = jnp.sum(counts[:labels], axis=1, keepdims=True)
    before = jnp.concatenate([before[:labels], before[labels:] + total], axis=0)
    before = jnp.minimum(before, float(cap)).astype(bf16)
    same = jnp.where(iota((length, length), 0) == iota((length, length), 1), 1.0, 0.0).astype(bf16)
    for i in range(images):
        back = dot_nt(before, perms[i]) * hots[i]
        slot_one = jnp.sum(back[:labels], axis=0, keepdims=True)
        slot_two = jnp.sum(back[labels:], axis=0, keepdims=True)
        one = routes_ref[i, 0:1, :].astype(f32)
        two = routes_ref[i, 1:2, :].astype(f32)
        kept_one = jnp.where(slot_one < cap, one, -1.0)
        kept_two = jnp.where(slot_two < cap, two, -1.0)
        slot_one = jnp.where(slot_one < cap, slot_one, 0.0)
        slot_two = jnp.where(slot_two < cap, slot_two, 0.0)
        aim_one = (kept_one * capp + slot_one).astype(jnp.int32)
        aim_two = (kept_two * capp + slot_two).astype(jnp.int32)
        rows_ref[i] = jnp.concatenate(
            [aim_one, aim_two, jnp.zeros((6, length), jnp.int32)], axis=0
        )
        stacked = jnp.concatenate(
            [kept_one, slot_one, kept_two, slot_two, one, two, one, two], axis=0
        ).astype(bf16)
        turned = dot_nt(same, stacked)
        cols_ref[i] = jnp.concatenate(
            [
                turned[:, 0:1] * capp + turned[:, 1:2],
                turned[:, 2:3] * capp + turned[:, 3:4],
                turned[:, 4:5],
                turned[:, 5:6],
                turned[:, 4:8],
            ],
            axis=1,
        ).astype(jnp.int32)


def route(routes, order, labels, cap, capp):
    images, _, length = routes.shape
    return pl.pallas_call(
        functools.partial(route_kernel, labels, cap, capp),
        out_shape=(
            jax.ShapeDtypeStruct((images, 8, length), jnp.int32),
            jax.ShapeDtypeStruct((images, length, 8), jnp.int32),
        ),
        compiler_params=pltpu.CompilerParams(vmem_limit_bytes=40 * 1024 * 1024),
        name="route_tokens",
    )(routes, order)


def dispatch_kernel(cap, capp, owners, which, gated, joint, rows_ref, value_ref, *refs):
    images, length, width = value_ref.shape
    outs = refs[1:] if gated else refs
    span = owners * capp
    for place, l in enumerate(which):
        slots = iota((span, length), 0) + l * span
        total = None
        gate_rows = None
        for i in range(images):
            one = slots == rows_ref[i, 0:1, :]
            two = slots == rows_ref[i, 1:2, :]
            both = jnp.where(one | two, 1.0, 0.0).astype(bf16)
            part = dot(both, value_ref[i])
            total = part if total is None else total + part
            if gated:
                gates = refs[0][i]
                first = dot_nt(gates[0:8], jnp.where(one, 1.0, 0.0).astype(bf16))
                second = dot_nt(gates[8:16], jnp.where(two, 1.0, 0.0).astype(bf16))
                part = first + second
                gate_rows = part if gate_rows is None else gate_rows + part
        for o in range(owners):
            block = total[o * capp : (o + 1) * capp]
            if joint:
                outs[0][o, place * capp : (place + 1) * capp, :] = block.astype(bf16)
            else:
                outs[0][o] = block.astype(bf16)
            if gated:
                tail = block[capp - 16 :, 0:capp]
                spare = gate_rows[:, o * capp : (o + 1) * capp]
                line = iota((16, capp), 0) - (cap - (capp - 16))
                for k in range(3):
                    tail = jnp.where(line == k, spare[k : k + 1], tail)
                outs[0][o, capp - 16 :, 0:capp] = tail.astype(bf16)


def dispatch(rows, values, gates, cap, capp, owners, which):
    width = values.shape[2]
    joint = gates is None
    operands = (rows, values) if joint else (rows, values, gates)
    out_shape = jax.ShapeDtypeStruct((owners, len(which) * capp, width), bf16)
    return pl.pallas_call(
        functools.partial(dispatch_kernel, cap, capp, owners, tuple(which), not joint, joint),
        out_shape=out_shape,
        compiler_params=pltpu.CompilerParams(vmem_limit_bytes=40 * 1024 * 1024),
        name="fill_slots",
    )(*operands)


def forward_kernel(
    labels,
    core_ref,
    tokens_ref,
    routes_ref,
    one_own,
    one_other,
    two_own,
    two_other,
    qkv_ref,
    mixed_ref,
    lse_ref,
    first_ref,
    routed_ref,
    gates_ref,
    gate_rows_ref,
    total_ref,
    one_ref,
    two_ref,
    misc_ref,
    sems,
):
    _, length, width = tokens_ref.shape
    step = pl.program_id(0)
    parts = ((one_own, one_other), (two_own, two_other))
    load_weights(step, core_ref[0], parts, (one_ref, two_ref), sems)

    @pl.when(step == 0)
    def _():
        misc_ref[...] = jnp.transpose(two_ref[..., 2 * width :].reshape(width, LANES))

    vec = [misc_ref[labels + k : labels + k + 1, :].astype(f32) for k in range(VECTORS)]
    rows = tokens_ref[0].astype(f32)
    unit, _ = norm_parts(rows)
    normed = (unit * vec[0] + vec[1]).astype(bf16)
    projected = jnp.concatenate(
        [
            dot(normed, one_ref[...].reshape(width, 2 * width)).astype(bf16),
            dot(normed, two_ref[..., 0:width].reshape(width, width)).astype(bf16),
        ],
        axis=1,
    )
    qkv_ref[0] = projected
    lane = iota((length, LANES), 1)
    low_half = lane < HEAD_DIM
    pieces = []
    for pair in range(width // LANES):
        at = pair * LANES
        query = projected[:, at : at + LANES] * jnp.asarray(HEAD_DIM**-0.5, bf16)
        keys = projected[:, width + at : width + at + LANES]
        values = projected[:, 2 * width + at : 2 * width + at + LANES]
        mixed = None
        for half in range(2):
            own = low_half if half == 0 else jnp.logical_not(low_half)
            scores = dot_nt(jnp.where(own, query, jnp.zeros_like(query)), keys)
            top = jnp.max(scores, axis=-1, keepdims=True)
            shifted = jnp.exp(scores - top)
            total = jnp.sum(shifted, axis=-1, keepdims=True)
            head = 2 * pair + half
            total_ref[0:length, :] = jnp.where(
                lane == head, top + jnp.log(total), total_ref[0:length, :]
            )
            low = (shifted * (1.0 / total)).astype(bf16)
            part = dot(low, jnp.where(own, values, jnp.zeros_like(values)))
            mixed = part if mixed is None else mixed + part
        pieces.append(mixed.astype(bf16))
    mixed = jnp.concatenate(pieces, axis=1)
    mixed_ref[0] = mixed
    lse_ref[0] = jnp.transpose(total_ref[...])[0:16]
    w_out = two_ref[..., width : 2 * width].reshape(width, width)
    first = rows + dot(mixed, w_out) + vec[2]
    first_ref[0] = first
    unit, _ = norm_parts(first)
    routed = (unit * vec[3] + vec[4]).astype(bf16)
    routed_ref[0] = routed
    router = misc_ref[0:labels, :]
    logits = dot_nt(routed, router)
    shifted = jnp.exp(logits - jnp.max(logits, axis=1, keepdims=True))
    gates_ref[0] = shifted / jnp.sum(shifted, axis=1, keepdims=True)
    logits = dot_nt(router, routed)
    shifted = jnp.exp(logits - jnp.max(logits, axis=0, keepdims=True))
    gates = shifted / jnp.sum(shifted, axis=0, keepdims=True)
    label = iota((labels, length), 0)
    blank = jnp.zeros((5, length), f32)
    stack = []
    for k in range(2):
        chosen = jnp.where(label == routes_ref[0, k : k + 1, :], gates, 0.0)
        stack += [*three_parts(jnp.sum(chosen, axis=0, keepdims=True)), blank]
    gate_rows_ref[0] = jnp.concatenate(stack, axis=0).astype(bf16)


def weight_scratch(packed):
    return [
        pltpu.VMEM((part[0].shape[0], 2, *part[0].shape[1:]), part[0].dtype) for part in packed
    ]


def forward(core, tokens, routes, packed, labels):
    images, length, width = tokens.shape
    whole = lambda *tail: pl.BlockSpec((1, *tail), lambda i: (i, 0, 0))
    lanes = -(-length // LANES) * LANES
    return pl.pallas_call(
        functools.partial(forward_kernel, labels),
        grid=(images,),
        in_specs=[
            pl.BlockSpec(memory_space=pltpu.SMEM),
            whole(length, width),
            whole(2, length),
            *[pl.BlockSpec(memory_space=pl.ANY)] * 4,
        ],
        out_specs=[
            whole(length, 3 * width),
            whole(length, width),
            whole(16, lanes),
            whole(length, width),
            whole(length, width),
            whole(length, labels),
            whole(16, length),
        ],
        out_shape=[
            jax.ShapeDtypeStruct((images, length, 3 * width), bf16),
            jax.ShapeDtypeStruct((images, length, width), bf16),
            jax.ShapeDtypeStruct((images, 16, lanes), f32),
            jax.ShapeDtypeStruct((images, length, width), f32),
            jax.ShapeDtypeStruct((images, length, width), bf16),
            jax.ShapeDtypeStruct((images, length, labels), f32),
            jax.ShapeDtypeStruct((images, 16, length), bf16),
        ],
        scratch_shapes=[
            pltpu.VMEM((lanes, LANES), f32),
            *weight_scratch(packed),
            pltpu.VMEM((LANES, width), bf16),
            pltpu.SemaphoreType.DMA((4,)),
        ],
        compiler_params=params(40),
        cost_estimate=pl.CostEstimate(
            flops=16_000_000_000, bytes_accessed=20_000_000, transcendentals=2_000_000
        ),
        name="attention_forward",
    )(core, tokens, routes, *packed[0], *packed[1])


def expert_kernel(
    cap,
    rows_ref,
    cot_ref,
    win_ref,
    wback_ref,
    biases_ref,
    *refs,
):
    (
        out_ref,
        grad_ref,
        weights_ref,
        turned_ref,
        grad_out_ref,
        out_acc_ref,
        grad_acc_ref,
        active_ref,
        inner_ref,
        bias_ref,
        gwin_ref,
        gwback_ref,
        gbias_ref,
        sems,
    ) = refs[-14:]
    owners, capp, width = rows_ref.shape
    groups, depth, hidden = win_ref.shape
    spare = cap - (capp - 16)
    step = pl.program_id(0)
    last = pl.num_programs(0) - 1
    slot = lax.rem(step, 2)
    across = width // hidden

    def copies(step, slot):
        at = pl.multiple_of(hidden + lax.div(step, across) * depth, 16)
        start = pl.multiple_of(lax.rem(step, across) * hidden, LANES)
        return (
            pltpu.make_async_copy(
                gwback_ref.at[slot], weights_ref.at[step, pl.ds(0, hidden)], sems.at[0, slot]
            ),
            pltpu.make_async_copy(
                gwin_ref.at[slot],
                weights_ref.at[:, pl.ds(at, depth), pl.ds(start, hidden)],
                sems.at[1, slot],
            ),
        )

    @pl.when(step >= 2)
    def _():
        for copy in copies(step - 2, slot):
            copy.wait()

    @pl.when(step == 0)
    def _():
        summed = jnp.zeros((1, width), f32)
        for b in range(owners):
            tail = rows_ref[b, capp - 16 :, 0:capp].astype(f32)
            gate = (
                tail[spare : spare + 1] + tail[spare + 1 : spare + 2] + tail[spare + 2 : spare + 3]
            )
            gate = jnp.transpose(jnp.broadcast_to(gate, (LANES, capp)))[:, 0:1]
            part = (cot_ref[b].astype(f32) * gate).astype(bf16)
            grad_out_ref[b * capp : (b + 1) * capp, :] = part
            summed = summed + jnp.sum(part.astype(f32), axis=0, keepdims=True)
            turned_ref[:, b * capp : (b + 1) * capp] = jnp.transpose(rows_ref[b])
        bias_ref[...] = jnp.broadcast_to(summed, bias_ref.shape)
        out_acc_ref[...] = jnp.zeros_like(out_acc_ref)
        grad_acc_ref[...] = jnp.zeros_like(grad_acc_ref)

    first = win_ref[...].reshape(width, hidden)
    second = wback_ref[0]
    bias = biases_ref[step].astype(f32)[0:1, 0:hidden]
    bias_sum = jnp.zeros((1, hidden), f32)
    per = max(1, 256 // capp)
    k0 = 0.7978845608028654
    k1 = 0.044715
    for c in range(owners // per):
        at = slice(c * per * capp, (c + 1) * per * capp)
        block = rows_ref[c * per : (c + 1) * per].reshape(per * capp, width)
        inner = dot(block, first) + bias
        square = inner * inner
        curve = jnp.tanh(inner * (k0 + (k0 * k1) * square))
        half = 0.5 * (1.0 + curve)
        low = (inner * half).astype(bf16)
        active_ref[at, :] = low
        slope = half + (0.5 * inner) * (1.0 - curve * curve) * (k0 + (3.0 * k0 * k1) * square)
        grad_inner = dot_nt(grad_out_ref[at, :], second) * slope
        bias_sum = bias_sum + jnp.sum(grad_inner, axis=0, keepdims=True)
        grad_low = grad_inner.astype(bf16)
        inner_ref[at, :] = grad_low
        out_acc_ref[at, :] += dot(low, second)
        grad_acc_ref[at, :] += dot_nt(grad_low, first)
    gwin_ref[slot] = dot(turned_ref[...], inner_ref[...]).astype(bf16).reshape(win_ref.shape)
    gwback_ref[slot] = dot_tn(active_ref[...], grad_out_ref[...]).astype(bf16)
    row = iota((16, width), 0)
    if hidden < width:
        bias_sum = jnp.concatenate([bias_sum, jnp.zeros((1, width - hidden), f32)], axis=1)
    pad = jnp.where(row == 0, bias_sum, jnp.where(row == 1, bias_ref[0:1, :], 0.0))
    gbias_ref[step] = pad.astype(bf16)
    for copy in copies(step, slot):
        copy.start()

    @pl.when(step == last)
    def _():
        end = pltpu.make_async_copy(
            gbias_ref, weights_ref.at[:, pl.ds(weights_ref.shape[1] - 16, 16)], sems.at[2, 0]
        )
        end.start()
        whole = jnp.concatenate(
            [biases_ref[g].astype(f32)[1:2, 0:depth] for g in range(groups)], axis=1
        )
        for b in range(owners):
            at = slice(b * capp, (b + 1) * capp)
            result = (out_acc_ref[at, :] + whole).astype(bf16)
            out_ref[b] = result
            score = jnp.sum(result.astype(f32) * cot_ref[b].astype(f32), axis=1, keepdims=True)
            score = jnp.transpose(jnp.broadcast_to(score, (capp, LANES)))[0:1, :]
            back = grad_acc_ref[at, :]
            grad_ref[b] = back.astype(bf16)
            tail = back[capp - 16 :, 0:capp]
            line = iota((16, capp), 0) - spare
            for k, part in enumerate(three_parts(score)):
                tail = jnp.where(line == k, part, tail)
            grad_ref[b, capp - 16 :, 0:capp] = tail.astype(bf16)
        for back in range(2):
            for copy in copies(step - back, lax.rem(step + back, 2)):
                copy.wait()
        end.wait()


def expert(rows, cots, weights, outcomes, which, local, cap):
    owners, capp, width = rows.shape
    groups, height, _ = weights.shape
    depth = width // groups
    hidden = height - 16 - (height - 16) // 2
    across = width // hidden
    total = owners * capp
    full = lambda shape: pl.BlockSpec(shape, lambda j: (0,) * len(shape))
    anywhere = pl.BlockSpec(memory_space=pl.ANY)
    extra = [] if outcomes is None else [outcomes]
    return pl.pallas_call(
        functools.partial(expert_kernel, cap),
        grid=(groups,),
        in_specs=[
            full((owners, capp, width)),
            full((owners, capp, width)),
            pl.BlockSpec(
                (groups, depth, hidden), lambda j: (0, hidden // depth + j // across, j % across)
            ),
            pl.BlockSpec((1, hidden, width), lambda j: (j, 0, 0)),
            pl.BlockSpec((groups, 16, width), lambda j: (0, (height - 16) // 16, 0)),
            *[anywhere] * len(extra),
        ],
        out_specs=[
            pl.BlockSpec((owners, capp, width), lambda j: (0, which, 0)),
            full((owners, capp, width)),
            anywhere,
        ],
        out_shape=[
            jax.ShapeDtypeStruct((owners, local * capp, width), bf16),
            jax.ShapeDtypeStruct((owners, capp, width), bf16),
            jax.ShapeDtypeStruct(weights.shape, bf16),
        ],
        input_output_aliases={5: 0} if extra else {},
        scratch_shapes=[
            pltpu.VMEM((width, total), bf16),
            pltpu.VMEM((total, width), bf16),
            pltpu.VMEM((total, width), f32),
            pltpu.VMEM((total, width), f32),
            pltpu.VMEM((total, hidden), bf16),
            pltpu.VMEM((total, hidden), bf16),
            pltpu.VMEM((8, width), f32),
            pltpu.VMEM((2, groups, depth, hidden), bf16),
            pltpu.VMEM((2, hidden, width), bf16),
            pltpu.VMEM((groups, 16, width), bf16),
            pltpu.SemaphoreType.DMA((3, 2)),
        ],
        compiler_params=params(56),
        cost_estimate=pl.CostEstimate(
            flops=2 * 6 * total * width * hidden * groups,
            bytes_accessed=30_000_000,
            transcendentals=total * hidden * groups,
        ),
        name="expert_rows",
    )(rows, cots, weights, weights, weights, *extra)


def share_kernel(*refs):
    parts, (back_ref, in_ref, bias_ref) = refs[:3], refs[-3:]
    value = [part[...] for part in parts]
    back_ref[0] = value[0].astype(f32)
    in_ref[0] = value[1].astype(f32)
    bias_ref[0] = value[2].astype(f32)


def share_out(share, outs, which, local, depth):
    height, width = share.shape
    hidden = (height - 16) // 2
    steps = hidden // depth
    extra = [] if outs is None else list(outs)
    return pl.pallas_call(
        share_kernel,
        grid=(steps,),
        in_specs=[
            pl.BlockSpec((depth, width), lambda j: (j, 0)),
            pl.BlockSpec((depth, width), lambda j: (steps + j, 0)),
            pl.BlockSpec((16, width), lambda j: (2 * hidden // 16, 0)),
            *[pl.BlockSpec(memory_space=pl.ANY)] * len(extra),
        ],
        out_specs=[
            pl.BlockSpec((1, depth, width), lambda j: (which, j, 0)),
            pl.BlockSpec((1, depth, width), lambda j: (which, 0, j)),
            pl.BlockSpec((1, 16, width), lambda j: (which, 0, 0)),
        ],
        out_shape=[
            jax.ShapeDtypeStruct((local, hidden, width), f32),
            jax.ShapeDtypeStruct((local, depth, steps * width), f32),
            jax.ShapeDtypeStruct((local, 16, width), f32),
        ],
        input_output_aliases={3 + k: k for k in range(len(extra))},
        compiler_params=params(32),
        name="expert_gradients",
    )(share, share, share, *extra)


def add_to(ref, columns, value):
    shape = (*ref.shape[:-1], value.shape[-1])
    ref[..., columns] += value.reshape(shape)


def backward_kernel(
    labels,
    local,
    cap,
    core_ref,
    tokens_ref,
    cot_ref,
    cols_ref,
    qkv_ref,
    mixed_ref,
    lse_ref,
    first_ref,
    routed_ref,
    gates_ref,
    one_own,
    one_other,
    two_own,
    two_other,
    *refs,
):
    slots = refs[:local]
    (
        grad_tokens_ref,
        keep_one_ref,
        send_one_ref,
        keep_two_ref,
        send_two_ref,
        grad_one_ref,
        grad_two_ref,
        stack_ref,
        vec_ref,
        score_ref,
        one_ref,
        two_ref,
        misc_ref,
        sems,
    ) = refs[local:]
    _, length, width = tokens_ref.shape
    owners, capp, _ = slots[0].shape
    spare = cap - (capp - 16)
    span = owners * capp
    step = pl.program_id(0)
    parts = ((one_own, one_other), (two_own, two_other))
    load_weights(step, core_ref[0], parts, (one_ref, two_ref), sems)

    @pl.when(step == 0)
    def _():
        misc_ref[...] = jnp.transpose(two_ref[..., 2 * width :].reshape(width, LANES))

    vec = [misc_ref[labels + k : labels + k + 1, :].astype(f32) for k in range(VECTORS)]

    @pl.when(step == 0)
    def _():
        grad_one_ref[...] = jnp.zeros_like(grad_one_ref)
        grad_two_ref[...] = jnp.zeros_like(grad_two_ref)
        vec_ref[...] = jnp.zeros_like(vec_ref)
        stack_ref[...] = jnp.zeros_like(stack_ref)
        for l in range(local):
            for o in range(owners):
                score_ref[:, l * span + o * capp : l * span + (o + 1) * capp] = slots[l][
                    o, capp - 16 :, 0:capp
                ]

    cot = cot_ref[0].astype(f32)
    aim_one, aim_two = cols_ref[0, :, 0:1], cols_ref[0, :, 1:2]
    route_one, route_two = cols_ref[0, :, 2:3], cols_ref[0, :, 3:4]
    picked = None
    gate_one = None
    gate_two = None
    for l in range(local):
        lane = iota((length, span), 1) + l * span
        one = jnp.where(lane == aim_one, 1.0, 0.0)
        two = jnp.where(lane == aim_two, 1.0, 0.0)
        part = dot((one + two).astype(bf16), slots[l][...].reshape(span, width))
        picked = part if picked is None else picked + part
        score = score_ref[:, l * span : (l + 1) * span]
        part_one = dot_nt(one.astype(bf16), score)
        part_two = dot_nt(two.astype(bf16), score)
        gate_one = part_one if gate_one is None else gate_one + part_one
        gate_two = part_two if gate_two is None else gate_two + part_two
    line = iota((length, 16), 1)
    mine = (line >= spare) & (line < spare + 3)
    gate_one = jnp.sum(jnp.where(mine, gate_one, 0.0), axis=1, keepdims=True)
    gate_two = jnp.sum(jnp.where(mine, gate_two, 0.0), axis=1, keepdims=True)
    label = iota((length, labels), 1)
    grad_gates = jnp.where(label == route_one, gate_one, 0.0) + jnp.where(
        label == route_two, gate_two, 0.0
    )
    gates = gates_ref[0]
    inner = jnp.sum(grad_gates * gates, axis=1, keepdims=True)
    grad_logits = (gates * (grad_gates - inner)).astype(bf16)
    router = misc_ref[0:labels, :]
    routed = routed_ref[0]
    stack_ref[0:labels, :] += dot_tn(grad_logits, routed)
    grad_routed = dot(grad_logits, router) + picked
    unit, scale = norm_parts(first_ref[0])
    vec_ref[3:4, :] += jnp.sum(grad_routed * unit, axis=0, keepdims=True)
    vec_ref[4:5, :] += jnp.sum(grad_routed, axis=0, keepdims=True)
    grad_first = cot + norm_backward(grad_routed, unit, scale, vec[3])
    vec_ref[2:3, :] += jnp.sum(grad_first, axis=0, keepdims=True)
    first_low = grad_first.astype(bf16)
    add_to(grad_two_ref, slice(width, 2 * width), dot_tn(mixed_ref[0], first_low))
    w_out = two_ref[..., width : 2 * width].reshape(width, width)
    grad_mixed = dot_nt(first_low, w_out).astype(bf16)
    low_half = iota((length, LANES), 1) < HEAD_DIM
    rate = jnp.asarray(HEAD_DIM**-0.5, bf16)
    grads = [[], [], []]
    for pair in range(width // LANES):
        at = pair * LANES
        query = qkv_ref[0, :, at : at + LANES] * rate
        keys = qkv_ref[0, :, width + at : width + at + LANES]
        values = qkv_ref[0, :, 2 * width + at : 2 * width + at + LANES]
        mix = grad_mixed[:, at : at + LANES]
        grad_q = grad_k = grad_v = None
        for half in range(2):
            own = low_half if half == 0 else jnp.logical_not(low_half)
            none = jnp.zeros_like(query)
            query_own = jnp.where(own, query, none)
            mix_own = jnp.where(own, mix, none)
            head = 2 * pair + half
            probs = jnp.exp(dot_nt(keys, query_own) - lse_ref[0, head : head + 1, 0:length])
            grad_probs = dot_nt(values, mix_own)
            inner = jnp.sum(grad_probs * probs, axis=0, keepdims=True)
            scores = (probs * (grad_probs - inner)).astype(bf16)
            part = dot(probs.astype(bf16), mix_own)
            grad_v = part if grad_v is None else grad_v + part
            part = dot(scores, query_own)
            grad_k = part if grad_k is None else grad_k + part
            part = dot_tn(scores, jnp.where(own, keys, none))
            grad_q = part if grad_q is None else grad_q + part
        grads[0].append((grad_q * HEAD_DIM**-0.5).astype(bf16))
        grads[1].append(grad_k.astype(bf16))
        grads[2].append(grad_v.astype(bf16))
    grad_one = jnp.concatenate(grads[0] + grads[1], axis=1)
    grad_two = jnp.concatenate(grads[2], axis=1)
    rows = tokens_ref[0].astype(f32)
    unit, scale = norm_parts(rows)
    normed = (unit * vec[0] + vec[1]).astype(bf16)
    add_to(grad_one_ref, slice(None), dot_tn(normed, grad_one))
    add_to(grad_two_ref, slice(0, width), dot_tn(normed, grad_two))
    grad_normed = dot_nt(grad_one, one_ref[...].reshape(width, 2 * width))
    grad_normed += dot_nt(grad_two, two_ref[..., 0:width].reshape(width, width))
    vec_ref[0:1, :] += jnp.sum(grad_normed * unit, axis=0, keepdims=True)
    vec_ref[1:2, :] += jnp.sum(grad_normed, axis=0, keepdims=True)
    grad_tokens_ref[0] = grad_first + norm_backward(grad_normed, unit, scale, vec[0])

    @pl.when(step == pl.num_programs(0) - 1)
    def _():
        stack_ref[labels : labels + 8, :] = vec_ref[...]
        add_to(grad_two_ref, slice(2 * width, None), jnp.transpose(stack_ref[...]))
        mine, other = core_ref[0], 1 - core_ref[0]
        keep_one_ref[...] = grad_one_ref[:, mine].astype(bf16)
        keep_two_ref[...] = grad_two_ref[:, mine].astype(bf16)
        send_one_ref[...] = grad_one_ref[:, other].astype(bf16)
        send_two_ref[...] = grad_two_ref[:, other].astype(bf16)


def backward(
    core, tokens, cot, cols, qkv, mixed, lse, first, routed, gates, cap, packed, slots, labels
):
    images, length, width = tokens.shape
    local = len(slots)
    owners, capp, _ = slots[0].shape
    whole = lambda *tail: pl.BlockSpec((1, *tail), lambda i: (i, 0, 0))
    shapes = [part[0].shape for part in packed]
    still = lambda shape: pl.BlockSpec(shape, lambda i: (0, 0, 0))
    return pl.pallas_call(
        functools.partial(backward_kernel, labels, local, cap),
        grid=(images,),
        in_specs=[
            pl.BlockSpec(memory_space=pltpu.SMEM),
            whole(length, width),
            whole(length, width),
            whole(length, 8),
            whole(length, 3 * width),
            whole(length, width),
            whole(*lse.shape[1:]),
            whole(length, width),
            whole(length, width),
            whole(length, labels),
            *[pl.BlockSpec(memory_space=pl.ANY)] * 4,
            *[pl.BlockSpec((owners, capp, width), lambda i: (0, 0, 0))] * local,
        ],
        out_specs=[
            whole(length, width),
            *[still(shape) for shape in shapes for _ in range(2)],
        ],
        out_shape=[
            jax.ShapeDtypeStruct((images, length, width), f32),
            *[jax.ShapeDtypeStruct(shape, bf16) for shape in shapes for _ in range(2)],
        ],
        scratch_shapes=[
            *[pltpu.VMEM((shape[0], 2, *shape[1:]), f32) for shape in shapes],
            pltpu.VMEM((LANES, width), f32),
            pltpu.VMEM((8, width), f32),
            pltpu.VMEM((16, local * owners * capp), bf16),
            *weight_scratch(packed),
            pltpu.VMEM((LANES, width), bf16),
            pltpu.SemaphoreType.DMA((4,)),
        ],
        compiler_params=params(58),
        cost_estimate=pl.CostEstimate(
            flops=40_000_000_000, bytes_accessed=40_000_000, transcendentals=2_000_000
        ),
        name="attention_backward",
    )(
        core,
        tokens,
        cot,
        cols,
        qkv,
        mixed,
        lse,
        first,
        routed,
        gates,
        *packed[0],
        *packed[1],
        *slots,
    )


def output_kernel(labels, local, first_ref, cols_ref, gates_ref, slots_ref, out_ref):
    _, length, width = first_ref.shape
    owners, capp, _ = slots_ref.shape
    capp = capp // local
    span = owners * capp
    label = iota((length, labels), 1)
    total = first_ref[0]
    for k in range(2):
        picked = None
        for l in range(local):
            lane = iota((length, span), 1) + l * span
            hot = jnp.where(lane == cols_ref[0, :, k : k + 1], 1.0, 0.0).astype(bf16)
            part = dot(hot, slots_ref[:, l * capp : (l + 1) * capp, :].reshape(span, width))
            picked = part if picked is None else picked + part
        chosen = jnp.where(label == cols_ref[0, :, k + 2 : k + 3], gates_ref[0], 0.0)
        total = total + jnp.sum(chosen, axis=1, keepdims=True) * picked
    out_ref[0] = total.astype(bf16)


def combine(first, cols, gates, slots, local):
    images, length, width = first.shape
    labels = gates.shape[2]
    whole = lambda *tail: pl.BlockSpec((1, *tail), lambda i: (i, 0, 0))
    return pl.pallas_call(
        functools.partial(output_kernel, labels, local),
        grid=(images,),
        in_specs=[
            whole(length, width),
            whole(length, 8),
            whole(length, labels),
            pl.BlockSpec(slots.shape, lambda i: (0, 0, 0)),
        ],
        out_specs=whole(length, width),
        out_shape=jax.ShapeDtypeStruct((images, length, width), bf16),
        compiler_params=params(40),
        name="combine_outputs",
    )(first, cols, gates, slots)


def bits_of(groups, owners):
    outer = [("group", k) for k in reversed(range(1, groups.bit_length() - 1))]
    inner = [("expert", k) for k in reversed(range(owners.bit_length() - 1))]
    return outer, inner


def swap(block, hop, sizes):
    axis, bit = hop
    return lax.ppermute(block, axis, [(d, d ^ (1 << bit)) for d in range(sizes[axis])])


def own_bit(hop):
    return lax.rem(lax.axis_index(hop[0]) >> hop[1], 2)


def spread(block, have, hops, order, sizes):
    for hop in hops:
        other = swap(block, hop, sizes)
        have = sorted([*have, hop], key=order.index)
        at = have.index(hop)
        mine = own_bit(hop) == 0
        block = jnp.stack(
            [jnp.where(mine, block, other), jnp.where(mine, other, block)], axis=at
        )
    return block, have


def halve(total, hop, at, sizes):
    bit = own_bit(hop)
    away = lax.dynamic_index_in_dim(total, 1 - bit, at, keepdims=False)
    stay = lax.dynamic_index_in_dim(total, bit, at, keepdims=False)
    return stay, swap(away.astype(bf16), hop, sizes)


def gather_back(total, hops, order, sizes):
    have = list(order)
    for hop in hops:
        at = have.index(hop)
        have.remove(hop)
        stay, other = halve(total, hop, at, sizes)
        total = stay + other.astype(f32)
    return total


def per_device(
    groups,
    owners,
    tokens,
    cotangent,
    routes,
    order,
    ln1_gain,
    ln1_bias,
    w_qkv,
    w_out,
    b_out,
    ln2_gain,
    ln2_bias,
    w_router,
    w_in,
    b_in,
    w_back,
    b_back,
):
    images, length, width = tokens.shape
    tok_count = images * length
    labels = w_router.shape[1]
    local = labels // owners
    depth = w_in.shape[1]
    hidden = w_back.shape[1]
    cap = max(2, 5 * tok_count // (2 * labels))
    capp = -(-(cap + 3) // 16) * 16

    own = width // (groups * owners)
    sizes = {"group": groups, "expert": owners}
    outer, inner = bits_of(groups, owners)
    order_of_hops = [*outer, *inner]
    sibling = ("group", 0)
    core = own_bit(sibling).astype(jnp.int32).reshape(1)
    routes_one = [*inner, *outer]
    routes_two = [*inner[:-1], *outer, *inner[-1:]]
    vectors = jnp.stack([ln1_gain, ln1_bias, b_out, ln2_gain, ln2_bias])
    slices = pack(w_qkv, w_out, w_router, vectors, owners)
    near = inner[:-1]
    marks = (routes % local) * owners + routes // local
    marks = marks.swapaxes(1, 2)
    rows, cols = route(marks, order, labels, cap, capp)
    exchange = lambda block: lax.all_to_all(block, "expert", 0, 0, tiled=True)
    slices = [spread(block, [], near[:1], order_of_hops, sizes)[0] for block in slices]
    rows, one, two = lax.optimization_barrier((rows, *slices))
    slices = [spread(block, near[:1], near[1:], order_of_hops, sizes) for block in (one, two)]
    cots = [dispatch(rows, cotangent, None, cap, capp, owners, [l]) for l in range(local)]
    cots[0], w_in, w_back, one, two = lax.optimization_barrier(
        (cots[0], w_in, w_back, slices[0][0], slices[1][0])
    )
    cots[0] = exchange(cots[0])
    halves = []
    for block, (_, have), path in ((one, slices[0], routes_one), (two, slices[1], routes_two)):
        half, _ = spread(block, have, path[len(near) :], order_of_hops, sizes)
        halves.append(half.reshape(groups // 2, owners * own, block.shape[-1]))
    biases = jnp.zeros((local, 16, width), f32)
    biases = biases.at[:, 0, :hidden].set(b_in).at[:, 1, :depth].set(b_back)
    wide = w_in.reshape(local, depth, -1, width).swapaxes(1, 2).reshape(local, -1, width)
    height = hidden + wide.shape[1] + 16
    experts = [
        jnp.concatenate([w_back[l], wide[l], biases[l]], axis=0).astype(bf16)
        for l in range(local)
    ]
    cots[0], cots[-1], *moved = lax.optimization_barrier((cots[0], cots[-1], *experts, *halves))
    experts, halves = moved[:local], moved[local:]
    cots[1:] = [exchange(block) for block in cots[1:]]
    experts = [lax.all_gather(block, "group") for block in experts]
    packed = [(half, swap(half, sibling, sizes)) for half in halves]
    qkv, mixed, lse, first, routed, gates, gate_rows = forward(core, tokens, marks, packed, labels)
    sent = [dispatch(rows, routed, gate_rows, cap, capp, owners, [l]) for l in range(local)]
    cots[-1], sent[0] = lax.optimization_barrier((cots[-1], sent[0]))
    sent[0] = exchange(sent[0])
    for l in range(1, local):
        sent[l - 1], sent[l] = lax.optimization_barrier((sent[l - 1], sent[l]))
        sent[l] = exchange(sent[l])
    joined, backs, shares = None, [], []
    for l in range(local):
        joined, back, grads = expert(sent[l], cots[l], experts[l], joined, l, local, cap)
        if l:
            back, backs[-1] = lax.optimization_barrier((back, backs[-1]))
        if l + 1 < local:
            back, sent[l + 1] = lax.optimization_barrier((back, sent[l + 1]))
            grads, sent[l + 1] = lax.optimization_barrier((grads, sent[l + 1]))
            back = exchange(back)
        else:
            back = exchange(back)
            grads, back = lax.optimization_barrier((grads, back))
        backs.append(back)
        shares.append(lax.psum_scatter(grads, "group", scatter_dimension=0))
    joined, *backs = lax.optimization_barrier((joined, *backs))
    joined = exchange(joined)
    grad_tokens, *halves = backward(
        core,
        tokens,
        cotangent,
        cols,
        qkv,
        mixed,
        lse,
        first,
        routed,
        gates,
        cap,
        packed,
        backs,
        labels,
    )
    sums, later = [], []
    for keep, away, path in (
        (halves[0], halves[1], routes_one[::-1]),
        (halves[2], halves[3], routes_two[::-1]),
    ):
        total = keep.astype(f32) + swap(away, sibling, sizes).astype(f32)
        total = total.reshape(*[2] * len(order_of_hops), own, keep.shape[2])
        sums.append(gather_back(total, path[:1], order_of_hops, sizes))
        later.append((path[1 : len(path) - len(near)], [h for h in order_of_hops if h != path[0]]))
    share = list(share_out(shares[0], None, 0, local, depth))
    *sums, joined, grad_tokens, share[0] = lax.optimization_barrier(
        (*sums, joined, grad_tokens, share[0])
    )
    one, two = [gather_back(part, *where, sizes) for part, where in zip(sums, later)]
    output = combine(first, cols, gates, joined, local)
    one, two, output = lax.optimization_barrier((one, two, output))
    rest = [hop for hop in order_of_hops if hop in near]
    one, two = [gather_back(part, near[:0:-1], rest, sizes) for part in (one, two)]
    for l in range(1, local):
        share = share_out(shares[l], share, l, local, depth)
    one, two, *share = lax.optimization_barrier((one, two, *share))
    one, two = [halve(part, near[0], 0, sizes) for part in (one, two)]
    share_back, share_in, share_bias = share
    grad_qkv, grad_out, grad_router, small = dense_out(one, two, labels, owners)
    place = lax.axis_index("group") * depth
    return (
        output,
        grad_tokens,
        small[0],
        small[1],
        grad_qkv,
        grad_out,
        small[2],
        small[3],
        small[4],
        grad_router,
        share_in,
        share_bias[:, 0, :hidden],
        share_back,
        lax.dynamic_slice_in_dim(share_bias[:, 1], place, depth, axis=1),
    )


def solution(mesh):
    rows = P(BOTH, None)
    line = P(BOTH)
    tall = P(BOTH, None, None)
    deep = P("expert", "group", None)
    flat = P("expert", "group")
    groups, owners = mesh.shape["group"], mesh.shape["expert"]
    return jax.shard_map(
        functools.partial(per_device, groups, owners),
        mesh=mesh,
        in_specs=(
            tall,
            tall,
            tall,
            rows,
            line,
            line,
            rows,
            rows,
            line,
            line,
            line,
            rows,
            deep,
            flat,
            deep,
            flat,
        ),
        out_specs=(
            tall,
            tall,
            line,
            line,
            rows,
            rows,
            line,
            line,
            line,
            rows,
            deep,
            flat,
            deep,
            flat,
        ),
        check_vma=False,
    )
```

```python
import functools

import jax
import jax.numpy as jnp
from jax import lax
from jax.experimental import pallas as pl
from jax.experimental.pallas import tpu as pltpu
from jax.sharding import PartitionSpec as P

HEAD_DIM = 64
LANES = 128
VECTORS = 5
f32 = jnp.float32
bf16 = jnp.bfloat16
BOTH = ("group", "expert")


def dot(a, b):
    return lax.dot_general(a, b, (((1,), (0,)), ((), ())), preferred_element_type=f32)


def dot_nt(a, b):
    return lax.dot_general(a, b, (((1,), (1,)), ((), ())), preferred_element_type=f32)


def dot_tn(a, b):
    return lax.dot_general(a, b, (((0,), (0,)), ((), ())), preferred_element_type=f32)


def iota(shape, dim):
    return lax.broadcasted_iota(jnp.int32, shape, dim)


def params(mib, grid=1):
    return pltpu.CompilerParams(
        vmem_limit_bytes=mib * 1024 * 1024, dimension_semantics=("arbitrary",) * grid
    )


def three_parts(value):
    high = value.astype(bf16).astype(f32)
    rest = value - high
    mid = rest.astype(bf16).astype(f32)
    return high, mid, rest - mid


def norm_parts(rows):
    centre = rows - jnp.mean(rows, axis=-1, keepdims=True)
    spread = jnp.mean(centre * centre, axis=-1, keepdims=True)
    scale = lax.rsqrt(spread + 1e-06)
    return centre * scale, scale


def norm_backward(grad, unit, scale, gain):
    lead = grad * gain
    first = jnp.mean(lead, axis=-1, keepdims=True)
    second = jnp.mean(lead * unit, axis=-1, keepdims=True)
    return scale * (lead - first - unit * second)


def load_weights(step, core, parts, scratch, sems):
    copies = []
    for k, (own, other) in enumerate(parts):
        copies.append(pltpu.make_async_copy(own, scratch[k].at[:, core], sems.at[2 * k]))
        copies.append(pltpu.make_async_copy(other, scratch[k].at[:, 1 - core], sems.at[2 * k + 1]))

    @pl.when(step == 0)
    def _():
        for copy in copies:
            copy.start()
        for copy in copies:
            copy.wait()


def pack_kernel(owners, qkv_ref, out_ref, router_ref, *refs):
    vec_refs, (one_ref, two_ref) = refs[:VECTORS], refs[VECTORS:]
    own, width = out_ref.shape
    labels = router_ref.shape[0]
    local = labels // owners
    one_ref[...] = qkv_ref[:, 0 : 2 * width].astype(bf16)
    two_ref[:, 0:width] = qkv_ref[:, 2 * width :].astype(bf16)
    two_ref[:, width : 2 * width] = out_ref[...].astype(bf16)
    lines = [
        router_ref[o * local + l : o * local + l + 1, :] for l in range(local) for o in range(owners)
    ]
    lines += [vec_ref[...] for vec_ref in vec_refs]
    lines.append(jnp.zeros((LANES - labels - VECTORS, own), f32))
    small = jnp.concatenate(lines, axis=0)
    if own < LANES:
        small = jnp.concatenate([small, jnp.zeros((LANES, LANES - own), f32)], axis=1)
    two_ref[:, 2 * width :] = jnp.transpose(small)[0:own].astype(bf16)


def pack(w_qkv, w_out, w_router, vectors, owners):
    own, width = w_out.shape
    return pl.pallas_call(
        functools.partial(pack_kernel, owners),
        out_shape=[
            jax.ShapeDtypeStruct((own, 2 * width), bf16),
            jax.ShapeDtypeStruct((own, 2 * width + LANES), bf16),
        ],
        name="pack_weights",
    )(w_qkv, w_out, w_router.T, *[vector.reshape(1, own) for vector in vectors])


def dense_out_kernel(
    owners, one_ref, one_in, two_ref, two_in, qkv_ref, out_ref, router_ref, *vec_refs
):
    own, width = out_ref.shape
    labels = router_ref.shape[0]
    local = labels // owners
    one = one_ref[...] + one_in[...].astype(f32)
    two = two_ref[...] + two_in[...].astype(f32)
    qkv_ref[:, 0 : 2 * width] = one
    qkv_ref[:, 2 * width :] = two[:, 0:width]
    out_ref[...] = two[:, width : 2 * width]
    small = two[:, 2 * width :]
    if own < LANES:
        small = jnp.concatenate([small, jnp.zeros((LANES - own, LANES), f32)], axis=0)
    small = jnp.transpose(small)[:, 0:own]
    for o in range(owners):
        for l in range(local):
            at = o * local + l
            router_ref[at : at + 1, :] = small[l * owners + o : l * owners + o + 1]
    for k, vec_ref in enumerate(vec_refs):
        vec_ref[...] = small[labels + k : labels + k + 1]


def dense_out(one, two, labels, owners):
    own = one[0].shape[0]
    width = one[0].shape[1] // 2
    return pl.pallas_call(
        functools.partial(dense_out_kernel, owners),
        out_shape=[
            jax.ShapeDtypeStruct((own, 3 * width), f32),
            jax.ShapeDtypeStruct((own, width), f32),
            jax.ShapeDtypeStruct((labels, own), f32),
            *[jax.ShapeDtypeStruct((1, own), f32)] * VECTORS,
        ],
        name="dense_gradients",
    )(*one, *two)


def route_kernel(labels, cap, capp, routes_ref, order_ref, rows_ref, cols_ref):
    images, _, length = routes_ref.shape
    tok_count = order_ref.shape[1]
    order = order_ref[...]
    label = iota((labels, length), 0)
    perms, hots = [], []
    counts = jnp.zeros((2 * labels, tok_count), f32)
    for i in range(images):
        perm = jnp.where(iota((length, tok_count), 0) + i * length == order, 1.0, 0.0).astype(bf16)
        hot = jnp.concatenate(
            [
                jnp.where(label == routes_ref[i, 0:1, :], 1.0, 0.0),
                jnp.where(label == routes_ref[i, 1:2, :], 1.0, 0.0),
            ],
            axis=0,
        )
        perms.append(perm)
        hots.append(hot)
        counts = counts + dot(hot.astype(bf16), perm)
    earlier = jnp.where(
        iota((tok_count, tok_count), 0) < iota((tok_count, tok_count), 1), 1.0, 0.0
    ).astype(bf16)
    before = dot(counts.astype(bf16), earlier)
    total = jnp.sum(counts[:labels], axis=1, keepdims=True)
    before = jnp.concatenate([before[:labels], before[labels:] + total], axis=0)
    before = jnp.minimum(before, float(cap)).astype(bf16)
    same = jnp.where(iota((length, length), 0) == iota((length, length), 1), 1.0, 0.0).astype(bf16)
    for i in range(images):
        back = dot_nt(before, perms[i]) * hots[i]
        slot_one = jnp.sum(back[:labels], axis=0, keepdims=True)
        slot_two = jnp.sum(back[labels:], axis=0, keepdims=True)
        one = routes_ref[i, 0:1, :].astype(f32)
        two = routes_ref[i, 1:2, :].astype(f32)
        kept_one = jnp.where(slot_one < cap, one, -1.0)
        kept_two = jnp.where(slot_two < cap, two, -1.0)
        slot_one = jnp.where(slot_one < cap, slot_one, 0.0)
        slot_two = jnp.where(slot_two < cap, slot_two, 0.0)
        aim_one = (kept_one * capp + slot_one).astype(jnp.int32)
        aim_two = (kept_two * capp + slot_two).astype(jnp.int32)
        rows_ref[i] = jnp.concatenate(
            [aim_one, aim_two, jnp.zeros((6, length), jnp.int32)], axis=0
        )
        stacked = jnp.concatenate(
            [kept_one, slot_one, kept_two, slot_two, one, two, one, two], axis=0
        ).astype(bf16)
        turned = dot_nt(same, stacked)
        cols_ref[i] = jnp.concatenate(
            [
                turned[:, 0:1] * capp + turned[:, 1:2],
                turned[:, 2:3] * capp + turned[:, 3:4],
                turned[:, 4:5],
                turned[:, 5:6],
                turned[:, 4:8],
            ],
            axis=1,
        ).astype(jnp.int32)


def route(routes, order, labels, cap, capp):
    images, _, length = routes.shape
    return pl.pallas_call(
        functools.partial(route_kernel, labels, cap, capp),
        out_shape=(
            jax.ShapeDtypeStruct((images, 8, length), jnp.int32),
            jax.ShapeDtypeStruct((images, length, 8), jnp.int32),
        ),
        compiler_params=pltpu.CompilerParams(vmem_limit_bytes=40 * 1024 * 1024),
        name="route_tokens",
    )(routes, order)


def dispatch_kernel(cap, capp, owners, which, gated, joint, rows_ref, value_ref, *refs):
    images, length, width = value_ref.shape
    outs = refs[1:] if gated else refs
    span = owners * capp
    for place, l in enumerate(which):
        slots = iota((span, length), 0) + l * span
        total = None
        gate_rows = None
        for i in range(images):
            one = slots == rows_ref[i, 0:1, :]
            two = slots == rows_ref[i, 1:2, :]
            both = jnp.where(one | two, 1.0, 0.0).astype(bf16)
            part = dot(both, value_ref[i])
            total = part if total is None else total + part
            if gated:
                gates = refs[0][i]
                first = dot_nt(gates[0:8], jnp.where(one, 1.0, 0.0).astype(bf16))
                second = dot_nt(gates[8:16], jnp.where(two, 1.0, 0.0).astype(bf16))
                part = first + second
                gate_rows = part if gate_rows is None else gate_rows + part
        for o in range(owners):
            block = total[o * capp : (o + 1) * capp]
            if joint:
                outs[0][o, place * capp : (place + 1) * capp, :] = block.astype(bf16)
            else:
                outs[0][o] = block.astype(bf16)
            if gated:
                tail = block[capp - 16 :, 0:capp]
                spare = gate_rows[:, o * capp : (o + 1) * capp]
                line = iota((16, capp), 0) - (cap - (capp - 16))
                for k in range(3):
                    tail = jnp.where(line == k, spare[k : k + 1], tail)
                outs[0][o, capp - 16 :, 0:capp] = tail.astype(bf16)


def dispatch(rows, values, gates, cap, capp, owners, which):
    width = values.shape[2]
    joint = gates is None
    operands = (rows, values) if joint else (rows, values, gates)
    out_shape = jax.ShapeDtypeStruct((owners, len(which) * capp, width), bf16)
    return pl.pallas_call(
        functools.partial(dispatch_kernel, cap, capp, owners, tuple(which), not joint, joint),
        out_shape=out_shape,
        compiler_params=pltpu.CompilerParams(vmem_limit_bytes=40 * 1024 * 1024),
        name="fill_slots",
    )(*operands)


def forward_kernel(
    labels,
    core_ref,
    tokens_ref,
    routes_ref,
    one_own,
    one_other,
    two_own,
    two_other,
    qkv_ref,
    mixed_ref,
    lse_ref,
    first_ref,
    routed_ref,
    gates_ref,
    gate_rows_ref,
    total_ref,
    one_ref,
    two_ref,
    misc_ref,
    sems,
):
    _, length, width = tokens_ref.shape
    step = pl.program_id(0)
    parts = ((one_own, one_other), (two_own, two_other))
    load_weights(step, core_ref[0], parts, (one_ref, two_ref), sems)

    @pl.when(step == 0)
    def _():
        misc_ref[...] = jnp.transpose(two_ref[..., 2 * width :].reshape(width, LANES))

    vec = [misc_ref[labels + k : labels + k + 1, :].astype(f32) for k in range(VECTORS)]
    rows = tokens_ref[0].astype(f32)
    unit, _ = norm_parts(rows)
    normed = (unit * vec[0] + vec[1]).astype(bf16)
    projected = jnp.concatenate(
        [
            dot(normed, one_ref[...].reshape(width, 2 * width)).astype(bf16),
            dot(normed, two_ref[..., 0:width].reshape(width, width)).astype(bf16),
        ],
        axis=1,
    )
    qkv_ref[0] = projected
    lane = iota((length, LANES), 1)
    low_half = lane < HEAD_DIM
    pieces = []
    for pair in range(width // LANES):
        at = pair * LANES
        query = projected[:, at : at + LANES] * jnp.asarray(HEAD_DIM**-0.5, bf16)
        keys = projected[:, width + at : width + at + LANES]
        values = projected[:, 2 * width + at : 2 * width + at + LANES]
        mixed = None
        for half in range(2):
            own = low_half if half == 0 else jnp.logical_not(low_half)
            scores = dot_nt(jnp.where(own, query, jnp.zeros_like(query)), keys)
            top = jnp.max(scores, axis=-1, keepdims=True)
            shifted = jnp.exp(scores - top)
            total = jnp.sum(shifted, axis=-1, keepdims=True)
            head = 2 * pair + half
            total_ref[0:length, :] = jnp.where(
                lane == head, top + jnp.log(total), total_ref[0:length, :]
            )
            low = (shifted * (1.0 / total)).astype(bf16)
            part = dot(low, jnp.where(own, values, jnp.zeros_like(values)))
            mixed = part if mixed is None else mixed + part
        pieces.append(mixed.astype(bf16))
    mixed = jnp.concatenate(pieces, axis=1)
    mixed_ref[0] = mixed
    lse_ref[0] = jnp.transpose(total_ref[...])[0:16]
    w_out = two_ref[..., width : 2 * width].reshape(width, width)
    first = rows + dot(mixed, w_out) + vec[2]
    first_ref[0] = first
    unit, _ = norm_parts(first)
    routed = (unit * vec[3] + vec[4]).astype(bf16)
    routed_ref[0] = routed
    router = misc_ref[0:labels, :]
    logits = dot_nt(routed, router)
    shifted = jnp.exp(logits - jnp.max(logits, axis=1, keepdims=True))
    gates_ref[0] = shifted / jnp.sum(shifted, axis=1, keepdims=True)
    logits = dot_nt(router, routed)
    shifted = jnp.exp(logits - jnp.max(logits, axis=0, keepdims=True))
    gates = shifted / jnp.sum(shifted, axis=0, keepdims=True)
    label = iota((labels, length), 0)
    blank = jnp.zeros((5, length), f32)
    stack = []
    for k in range(2):
        chosen = jnp.where(label == routes_ref[0, k : k + 1, :], gates, 0.0)
        stack += [*three_parts(jnp.sum(chosen, axis=0, keepdims=True)), blank]
    gate_rows_ref[0] = jnp.concatenate(stack, axis=0).astype(bf16)


def weight_scratch(packed):
    return [
        pltpu.VMEM((part[0].shape[0], 2, *part[0].shape[1:]), part[0].dtype) for part in packed
    ]


def forward(core, tokens, routes, packed, labels):
    images, length, width = tokens.shape
    whole = lambda *tail: pl.BlockSpec((1, *tail), lambda i: (i, 0, 0))
    lanes = -(-length // LANES) * LANES
    return pl.pallas_call(
        functools.partial(forward_kernel, labels),
        grid=(images,),
        in_specs=[
            pl.BlockSpec(memory_space=pltpu.SMEM),
            whole(length, width),
            whole(2, length),
            *[pl.BlockSpec(memory_space=pl.ANY)] * 4,
        ],
        out_specs=[
            whole(length, 3 * width),
            whole(length, width),
            whole(16, lanes),
            whole(length, width),
            whole(length, width),
            whole(length, labels),
            whole(16, length),
        ],
        out_shape=[
            jax.ShapeDtypeStruct((images, length, 3 * width), bf16),
            jax.ShapeDtypeStruct((images, length, width), bf16),
            jax.ShapeDtypeStruct((images, 16, lanes), f32),
            jax.ShapeDtypeStruct((images, length, width), f32),
            jax.ShapeDtypeStruct((images, length, width), bf16),
            jax.ShapeDtypeStruct((images, length, labels), f32),
            jax.ShapeDtypeStruct((images, 16, length), bf16),
        ],
        scratch_shapes=[
            pltpu.VMEM((lanes, LANES), f32),
            *weight_scratch(packed),
            pltpu.VMEM((LANES, width), bf16),
            pltpu.SemaphoreType.DMA((4,)),
        ],
        compiler_params=params(40),
        cost_estimate=pl.CostEstimate(
            flops=16_000_000_000, bytes_accessed=20_000_000, transcendentals=2_000_000
        ),
        name="attention_forward",
    )(core, tokens, routes, *packed[0], *packed[1])


def expert_kernel(
    cap,
    rows_ref,
    cot_ref,
    win_ref,
    wback_ref,
    biases_ref,
    *refs,
):
    (
        out_ref,
        grad_ref,
        weights_ref,
        turned_ref,
        grad_out_ref,
        out_acc_ref,
        grad_acc_ref,
        active_ref,
        inner_ref,
        bias_ref,
        gwin_ref,
        gwback_ref,
        gbias_ref,
        sems,
    ) = refs[-14:]
    owners, capp, width = rows_ref.shape
    groups, depth, hidden = win_ref.shape
    spare = cap - (capp - 16)
    step = pl.program_id(0)
    last = pl.num_programs(0) - 1
    slot = lax.rem(step, 2)
    across = width // hidden

    def copies(step, slot):
        at = pl.multiple_of(hidden + lax.div(step, across) * depth, 16)
        start = pl.multiple_of(lax.rem(step, across) * hidden, LANES)
        return (
            pltpu.make_async_copy(
                gwback_ref.at[slot], weights_ref.at[step, pl.ds(0, hidden)], sems.at[0, slot]
            ),
            pltpu.make_async_copy(
                gwin_ref.at[slot],
                weights_ref.at[:, pl.ds(at, depth), pl.ds(start, hidden)],
                sems.at[1, slot],
            ),
        )

    @pl.when(step >= 2)
    def _():
        for copy in copies(step - 2, slot):
            copy.wait()

    @pl.when(step == 0)
    def _():
        summed = jnp.zeros((1, width), f32)
        for b in range(owners):
            tail = rows_ref[b, capp - 16 :, 0:capp].astype(f32)
            gate = (
                tail[spare : spare + 1] + tail[spare + 1 : spare + 2] + tail[spare + 2 : spare + 3]
            )
            gate = jnp.transpose(jnp.broadcast_to(gate, (LANES, capp)))[:, 0:1]
            part = (cot_ref[b].astype(f32) * gate).astype(bf16)
            grad_out_ref[b * capp : (b + 1) * capp, :] = part
            summed = summed + jnp.sum(part.astype(f32), axis=0, keepdims=True)
            turned_ref[:, b * capp : (b + 1) * capp] = jnp.transpose(rows_ref[b])
        bias_ref[...] = jnp.broadcast_to(summed, bias_ref.shape)
        out_acc_ref[...] = jnp.zeros_like(out_acc_ref)
        grad_acc_ref[...] = jnp.zeros_like(grad_acc_ref)

    first = win_ref[...].reshape(width, hidden)
    second = wback_ref[0]
    bias = biases_ref[step].astype(f32)[0:1, 0:hidden]
    bias_sum = jnp.zeros((1, hidden), f32)
    per = max(1, 256 // capp)
    k0 = 0.7978845608028654
    k1 = 0.044715
    for c in range(owners // per):
        at = slice(c * per * capp, (c + 1) * per * capp)
        block = rows_ref[c * per : (c + 1) * per].reshape(per * capp, width)
        inner = dot(block, first) + bias
        square = inner * inner
        curve = jnp.tanh(inner * (k0 + (k0 * k1) * square))
        half = 0.5 * (1.0 + curve)
        low = (inner * half).astype(bf16)
        active_ref[at, :] = low
        slope = half + (0.5 * inner) * (1.0 - curve * curve) * (k0 + (3.0 * k0 * k1) * square)
        grad_inner = dot_nt(grad_out_ref[at, :], second) * slope
        bias_sum = bias_sum + jnp.sum(grad_inner, axis=0, keepdims=True)
        grad_low = grad_inner.astype(bf16)
        inner_ref[at, :] = grad_low
        out_acc_ref[at, :] += dot(low, second)
        grad_acc_ref[at, :] += dot_nt(grad_low, first)
    gwin_ref[slot] = dot(turned_ref[...], inner_ref[...]).astype(bf16).reshape(win_ref.shape)
    gwback_ref[slot] = dot_tn(active_ref[...], grad_out_ref[...]).astype(bf16)
    row = iota((16, width), 0)
    if hidden < width:
        bias_sum = jnp.concatenate([bias_sum, jnp.zeros((1, width - hidden), f32)], axis=1)
    pad = jnp.where(row == 0, bias_sum, 0.0)
    gbias_ref[step] = pad.astype(bf16)
    for copy in copies(step, slot):
        copy.start()

    @pl.when(step == last)
    def _():
        for g in range(groups):
            part = bias_ref[0:1, g * depth : (g + 1) * depth]
            part = jnp.concatenate([part, jnp.zeros((1, width - depth), f32)], axis=1)
            block = gbias_ref[g].astype(f32)
            gbias_ref[g] = jnp.where(row == 1, part, block).astype(bf16)
        end = pltpu.make_async_copy(
            gbias_ref, weights_ref.at[:, pl.ds(weights_ref.shape[1] - 16, 16)], sems.at[2, 0]
        )
        end.start()
        whole = jnp.concatenate(
            [biases_ref[g].astype(f32)[1:2, 0:depth] for g in range(groups)], axis=1
        )
        for b in range(owners):
            at = slice(b * capp, (b + 1) * capp)
            result = (out_acc_ref[at, :] + whole).astype(bf16)
            out_ref[b] = result
            score = jnp.sum(result.astype(f32) * cot_ref[b].astype(f32), axis=1, keepdims=True)
            score = jnp.transpose(jnp.broadcast_to(score, (capp, LANES)))[0:1, :]
            back = grad_acc_ref[at, :]
            grad_ref[b] = back.astype(bf16)
            tail = back[capp - 16 :, 0:capp]
            line = iota((16, capp), 0) - spare
            for k, part in enumerate(three_parts(score)):
                tail = jnp.where(line == k, part, tail)
            grad_ref[b, capp - 16 :, 0:capp] = tail.astype(bf16)
        for back in range(2):
            for copy in copies(step - back, lax.rem(step + back, 2)):
                copy.wait()
        end.wait()


def expert(rows, cots, weights, outcomes, which, local, cap):
    owners, capp, width = rows.shape
    groups, height, _ = weights.shape
    depth = width // groups
    hidden = height - 16 - (height - 16) // 2
    across = width // hidden
    total = owners * capp
    full = lambda shape: pl.BlockSpec(shape, lambda j: (0,) * len(shape))
    anywhere = pl.BlockSpec(memory_space=pl.ANY)
    extra = [] if outcomes is None else [outcomes]
    return pl.pallas_call(
        functools.partial(expert_kernel, cap),
        grid=(groups,),
        in_specs=[
            full((owners, capp, width)),
            full((owners, capp, width)),
            pl.BlockSpec(
                (groups, depth, hidden), lambda j: (0, hidden // depth + j // across, j % across)
            ),
            pl.BlockSpec((1, hidden, width), lambda j: (j, 0, 0)),
            pl.BlockSpec((groups, 16, width), lambda j: (0, (height - 16) // 16, 0)),
            *[anywhere] * len(extra),
        ],
        out_specs=[
            pl.BlockSpec((owners, capp, width), lambda j: (0, which, 0)),
            full((owners, capp, width)),
            anywhere,
        ],
        out_shape=[
            jax.ShapeDtypeStruct((owners, local * capp, width), bf16),
            jax.ShapeDtypeStruct((owners, capp, width), bf16),
            jax.ShapeDtypeStruct(weights.shape, bf16),
        ],
        input_output_aliases={5: 0} if extra else {},
        scratch_shapes=[
            pltpu.VMEM((width, total), bf16),
            pltpu.VMEM((total, width), bf16),
            pltpu.VMEM((total, width), f32),
            pltpu.VMEM((total, width), f32),
            pltpu.VMEM((total, hidden), bf16),
            pltpu.VMEM((total, hidden), bf16),
            pltpu.VMEM((8, width), f32),
            pltpu.VMEM((2, groups, depth, hidden), bf16),
            pltpu.VMEM((2, hidden, width), bf16),
            pltpu.VMEM((groups, 16, width), bf16),
            pltpu.SemaphoreType.DMA((3, 2)),
        ],
        compiler_params=params(56),
        cost_estimate=pl.CostEstimate(
            flops=2 * 6 * total * width * hidden * groups,
            bytes_accessed=30_000_000,
            transcendentals=total * hidden * groups,
        ),
        name="expert_rows",
    )(rows, cots, weights, weights, weights, *extra)


def parted_kernel(
    cap,
    core_ref,
    rows_ref,
    cot_ref,
    win_ref,
    wback_ref,
    biases_ref,
    *refs,
):
    (
        out_ref,
        grad_ref,
        keep_ref,
        away_ref,
        turned_ref,
        grad_out_ref,
        out_acc_ref,
        grad_acc_ref,
        active_ref,
        inner_ref,
        bias_ref,
        gwin_ref,
        gwback_ref,
        gbias_ref,
        sems,
    ) = refs[-15:]
    owners, capp, width = rows_ref.shape
    groups, depth, hidden = win_ref.shape
    spare = cap - (capp - 16)
    step = pl.program_id(0)
    last = pl.num_programs(0) - 1
    slot = lax.rem(step, 2)
    across = width // hidden

    mine = core_ref[0]
    targets = ((keep_ref, mine, 0), (away_ref, 1 - mine, 1))

    def copies(step, slot):
        at = pl.multiple_of(hidden + lax.div(step, across) * depth, 16)
        start = pl.multiple_of(lax.rem(step, across) * hidden, LANES)
        return [
            pltpu.make_async_copy(
                gwin_ref.at[slot, :, part],
                target.at[:, pl.ds(at, depth), pl.ds(start, hidden)],
                sems.at[1 + k, slot],
            )
            for target, part, k in targets
        ]

    def whole_chunk(step, slot, act):
        for target, part, _ in targets:

            @pl.when(lax.rem(step, 2) == part)
            def _():
                act(
                    pltpu.make_async_copy(
                        gwback_ref.at[slot],
                        target.at[lax.div(step, 2), pl.ds(0, hidden)],
                        sems.at[0, slot],
                    )
                )

    def finish(step, slot):
        for copy in copies(step, slot):
            copy.wait()
        whole_chunk(step, slot, lambda copy: copy.wait())

    @pl.when(step >= 2)
    def _():
        finish(step - 2, slot)

    @pl.when(step == 0)
    def _():
        summed = jnp.zeros((1, width), f32)
        for b in range(owners):
            tail = rows_ref[b, capp - 16 :, 0:capp].astype(f32)
            gate = (
                tail[spare : spare + 1] + tail[spare + 1 : spare + 2] + tail[spare + 2 : spare + 3]
            )
            gate = jnp.transpose(jnp.broadcast_to(gate, (LANES, capp)))[:, 0:1]
            part = (cot_ref[b].astype(f32) * gate).astype(bf16)
            grad_out_ref[b * capp : (b + 1) * capp, :] = part
            summed = summed + jnp.sum(part.astype(f32), axis=0, keepdims=True)
            turned_ref[:, b * capp : (b + 1) * capp] = jnp.transpose(rows_ref[b])
        bias_ref[...] = jnp.broadcast_to(summed, bias_ref.shape)
        out_acc_ref[...] = jnp.zeros_like(out_acc_ref)
        grad_acc_ref[...] = jnp.zeros_like(grad_acc_ref)

    first = win_ref[...].reshape(width, hidden)
    second = wback_ref[0]
    bias = biases_ref[step].astype(f32)[0:1, 0:hidden]
    bias_sum = jnp.zeros((1, hidden), f32)
    per = max(1, 256 // capp)
    k0 = 0.7978845608028654
    k1 = 0.044715
    for c in range(owners // per):
        at = slice(c * per * capp, (c + 1) * per * capp)
        block = rows_ref[c * per : (c + 1) * per].reshape(per * capp, width)
        inner = dot(block, first) + bias
        square = inner * inner
        curve = jnp.tanh(inner * (k0 + (k0 * k1) * square))
        half = 0.5 * (1.0 + curve)
        low = (inner * half).astype(bf16)
        active_ref[at, :] = low
        slope = half + (0.5 * inner) * (1.0 - curve * curve) * (k0 + (3.0 * k0 * k1) * square)
        grad_inner = dot_nt(grad_out_ref[at, :], second) * slope
        bias_sum = bias_sum + jnp.sum(grad_inner, axis=0, keepdims=True)
        grad_low = grad_inner.astype(bf16)
        inner_ref[at, :] = grad_low
        out_acc_ref[at, :] += dot(low, second)
        grad_acc_ref[at, :] += dot_nt(grad_low, first)
    gwin_ref[slot] = dot(turned_ref[...], inner_ref[...]).astype(bf16).reshape(gwin_ref.shape[1:])
    gwback_ref[slot] = dot_tn(active_ref[...], grad_out_ref[...]).astype(bf16)
    row = iota((16, width), 0)
    if hidden < width:
        bias_sum = jnp.concatenate([bias_sum, jnp.zeros((1, width - hidden), f32)], axis=1)
    pad = jnp.where(row == 0, bias_sum, 0.0)
    gbias_ref[lax.div(step, 2), lax.rem(step, 2)] = pad.astype(bf16)
    for copy in copies(step, slot):
        copy.start()
    whole_chunk(step, slot, lambda copy: copy.start())

    @pl.when(step == last)
    def _():
        for g in range(groups):
            part = bias_ref[0:1, g * depth : (g + 1) * depth]
            part = jnp.concatenate([part, jnp.zeros((1, width - depth), f32)], axis=1)
            block = gbias_ref[g // 2, g % 2].astype(f32)
            gbias_ref[g // 2, g % 2] = jnp.where(row == 1, part, block).astype(bf16)
        ends = [
            pltpu.make_async_copy(
                gbias_ref.at[:, part],
                target.at[:, pl.ds(target.shape[1] - 16, 16)],
                sems.at[3, k],
            )
            for target, part, k in targets
        ]
        for end in ends:
            end.start()
        whole = jnp.concatenate(
            [biases_ref[g].astype(f32)[1:2, 0:depth] for g in range(groups)], axis=1
        )
        for b in range(owners):
            at = slice(b * capp, (b + 1) * capp)
            result = (out_acc_ref[at, :] + whole).astype(bf16)
            out_ref[b] = result
            score = jnp.sum(result.astype(f32) * cot_ref[b].astype(f32), axis=1, keepdims=True)
            score = jnp.transpose(jnp.broadcast_to(score, (capp, LANES)))[0:1, :]
            back = grad_acc_ref[at, :]
            grad_ref[b] = back.astype(bf16)
            tail = back[capp - 16 :, 0:capp]
            line = iota((16, capp), 0) - spare
            for k, part in enumerate(three_parts(score)):
                tail = jnp.where(line == k, part, tail)
            grad_ref[b, capp - 16 :, 0:capp] = tail.astype(bf16)
        finish(step - 1, 1 - slot)
        finish(step, slot)
        for end in ends:
            end.wait()


def parted_expert(core, rows, cots, weights, outcomes, which, local, cap):
    owners, capp, width = rows.shape
    groups, height, _ = weights.shape
    depth = width // groups
    hidden = height - 16 - (height - 16) // 2
    across = width // hidden
    total = owners * capp
    full = lambda shape: pl.BlockSpec(shape, lambda j: (0,) * len(shape))
    anywhere = pl.BlockSpec(memory_space=pl.ANY)
    extra = [] if outcomes is None else [outcomes]
    return pl.pallas_call(
        functools.partial(parted_kernel, cap),
        grid=(groups,),
        in_specs=[
            pl.BlockSpec(memory_space=pltpu.SMEM),
            full((owners, capp, width)),
            full((owners, capp, width)),
            pl.BlockSpec(
                (groups, depth, hidden), lambda j: (0, hidden // depth + j // across, j % across)
            ),
            pl.BlockSpec((1, hidden, width), lambda j: (j, 0, 0)),
            pl.BlockSpec((groups, 16, width), lambda j: (0, (height - 16) // 16, 0)),
            *[anywhere] * len(extra),
        ],
        out_specs=[
            pl.BlockSpec((owners, capp, width), lambda j: (0, which, 0)),
            full((owners, capp, width)),
            anywhere,
            anywhere,
        ],
        out_shape=[
            jax.ShapeDtypeStruct((owners, local * capp, width), bf16),
            jax.ShapeDtypeStruct((owners, capp, width), bf16),
            jax.ShapeDtypeStruct((groups // 2, height, width), bf16),
            jax.ShapeDtypeStruct((groups // 2, height, width), bf16),
        ],
        input_output_aliases={6: 0} if extra else {},
        scratch_shapes=[
            pltpu.VMEM((width, total), bf16),
            pltpu.VMEM((total, width), bf16),
            pltpu.VMEM((total, width), f32),
            pltpu.VMEM((total, width), f32),
            pltpu.VMEM((total, hidden), bf16),
            pltpu.VMEM((total, hidden), bf16),
            pltpu.VMEM((8, width), f32),
            pltpu.VMEM((2, groups // 2, 2, depth, hidden), bf16),
            pltpu.VMEM((2, hidden, width), bf16),
            pltpu.VMEM((groups // 2, 2, 16, width), bf16),
            pltpu.SemaphoreType.DMA((4, 2)),
        ],
        compiler_params=params(56),
        cost_estimate=pl.CostEstimate(
            flops=2 * 6 * total * width * hidden * groups,
            bytes_accessed=30_000_000,
            transcendentals=total * hidden * groups,
        ),
        name="expert_rows_parted",
    )(core, rows, cots, weights, weights, weights, *extra)


def share_kernel(addends, *refs):
    back_ref, in_ref, bias_ref = refs[-3:]
    value = [refs[k][...].astype(f32) for k in range(3)]
    if addends > 1:
        value = [part + refs[3 + k][...].astype(f32) for k, part in enumerate(value)]
    back_ref[0] = value[0]
    in_ref[0] = value[1]
    bias_ref[0] = value[2]


def share_out(shares, outs, which, local, depth):
    height, width = shares[0].shape
    hidden = (height - 16) // 2
    steps = hidden // depth
    extra = [] if outs is None else list(outs)
    operands = [share for share in shares for _ in range(3)]
    return pl.pallas_call(
        functools.partial(share_kernel, len(shares)),
        grid=(steps,),
        in_specs=[
            *[
                pl.BlockSpec((depth, width), lambda j: (j, 0)),
                pl.BlockSpec((depth, width), lambda j: (steps + j, 0)),
                pl.BlockSpec((16, width), lambda j: (2 * hidden // 16, 0)),
            ]
            * len(shares),
            *[pl.BlockSpec(memory_space=pl.ANY)] * len(extra),
        ],
        out_specs=[
            pl.BlockSpec((1, depth, width), lambda j: (which, j, 0)),
            pl.BlockSpec((1, depth, width), lambda j: (which, 0, j)),
            pl.BlockSpec((1, 16, width), lambda j: (which, 0, 0)),
        ],
        out_shape=[
            jax.ShapeDtypeStruct((local, hidden, width), f32),
            jax.ShapeDtypeStruct((local, depth, steps * width), f32),
            jax.ShapeDtypeStruct((local, 16, width), f32),
        ],
        input_output_aliases={len(operands) + k: k for k in range(len(extra))},
        compiler_params=params(32),
        name="expert_gradients",
    )(*operands, *extra)


def stage_kernel(own_rows, *refs):
    bits, refs = refs[: len(own_rows)], refs[len(own_rows) :]
    for k, rows in enumerate(own_rows):
        keep_ref, other_ref = refs[2 * k : 2 * k + 2]
        stay_ref, away_ref = refs[2 * (len(own_rows) + k) : 2 * (len(own_rows) + k) + 2]
        mine = bits[k][0] == 0
        total = keep_ref[...].astype(f32) + other_ref[...].astype(f32)
        if total.ndim == 3:
            pairs = [(total[0], total[1])]
        else:
            pairs = [
                (total[at : at + rows], total[at + rows : at + 2 * rows])
                for at in range(0, total.shape[0], 2 * rows)
            ]
        stay = [jnp.where(mine, one, two) for one, two in pairs]
        away = [jnp.where(mine, two, one) for one, two in pairs]
        stay_ref[...] = jnp.concatenate(stay, axis=0)
        away_ref[...] = jnp.concatenate(away, axis=0).astype(bf16)


def stage(pairs, lengths, bits):
    rows = [pair[0].size // pair[0].shape[-1] for pair in pairs]
    turns = [count // (2 * length) for count, length in zip(rows, lengths)]

    def fits(steps):
        return all(
            length % (16 * steps) == 0
            if turn == 1
            else turn % steps == 0 and length * (turn // steps) % 16 == 0
            for turn, length in zip(turns, lengths)
        )

    steps = next((count for count in (4, 2) if fits(count)), 1)
    operands, in_specs, out_specs, out_shape = [], [], [], []
    for pair, count, length, turn in zip(pairs, rows, lengths, turns):
        columns = pair[0].shape[-1]
        if turn == 1 and length % 16 == 0:
            shape, block = (2, length, columns), (2, length // steps, columns)
            where = lambda j: (0, j, 0)
        else:
            shape, block = (count, columns), (count // steps, columns)
            where = lambda j: (j, 0)
        operands += [part.reshape(shape) for part in pair]
        in_specs += [pl.BlockSpec(block, where)] * 2
        half = pl.BlockSpec((count // 2 // steps, columns), lambda j: (j, 0))
        out_specs += [half, half]
        out_shape += [jax.ShapeDtypeStruct((count // 2, columns), kind) for kind in (f32, bf16)]
    results = pl.pallas_call(
        functools.partial(stage_kernel, tuple(lengths)),
        grid=(steps,),
        in_specs=[*[pl.BlockSpec(memory_space=pltpu.SMEM)] * len(pairs), *in_specs],
        out_specs=out_specs,
        out_shape=out_shape,
        compiler_params=params(40),
        name="add_and_halve",
    )(*[bit.astype(jnp.int32).reshape(1) for bit in bits], *operands)
    return [results[2 * k : 2 * k + 2] for k in range(len(pairs))]


def add_to(ref, columns, value):
    shape = (*ref.shape[:-1], value.shape[-1])
    ref[..., columns] += value.reshape(shape)


def pick(which, cap, cols_ref, slots, score_ref):
    length = cols_ref.shape[1]
    owners, capp, width = slots[0].shape
    spare = cap - (capp - 16)
    span = owners * capp
    picked = gate_one = gate_two = None
    for k, l in enumerate(which):
        lane = iota((length, span), 1) + l * span
        one = jnp.where(lane == cols_ref[0, :, 0:1], 1.0, 0.0)
        two = jnp.where(lane == cols_ref[0, :, 1:2], 1.0, 0.0)
        part = dot((one + two).astype(bf16), slots[k][...].reshape(span, width))
        picked = part if picked is None else picked + part
        score = score_ref[:, k * span : (k + 1) * span]
        part_one = dot_nt(one.astype(bf16), score)
        part_two = dot_nt(two.astype(bf16), score)
        gate_one = part_one if gate_one is None else gate_one + part_one
        gate_two = part_two if gate_two is None else gate_two + part_two
    line = iota((length, 16), 1)
    mine = (line >= spare) & (line < spare + 3)
    gate_one = jnp.sum(jnp.where(mine, gate_one, 0.0), axis=1, keepdims=True)
    gate_two = jnp.sum(jnp.where(mine, gate_two, 0.0), axis=1, keepdims=True)
    return picked, gate_one, gate_two


def load_scores(slots, score_ref):
    owners, capp, _ = slots[0].shape
    span = owners * capp
    for k, block in enumerate(slots):
        for o in range(owners):
            at = k * span + o * capp
            score_ref[:, at : at + capp] = block[o, capp - 16 :, 0:capp]


def early_kernel(local, cap, cols_ref, qkv_ref, lse_ref, *refs):
    slots = refs[:local]
    picked_ref, gate_ref, probs_ref, score_ref = refs[local:]
    _, length, width = picked_ref.shape

    @pl.when(pl.program_id(0) == 0)
    def _():
        load_scores(slots, score_ref)

    picked, gate_one, gate_two = pick(range(local), cap, cols_ref, slots, score_ref)
    picked_ref[0] = picked
    lane = iota((length, 8), 1)
    gate_ref[0] = jnp.where(lane == 0, gate_one, jnp.where(lane == 1, gate_two, 0.0))
    low_half = iota((length, LANES), 1) < HEAD_DIM
    rate = jnp.asarray(HEAD_DIM**-0.5, bf16)
    for pair in range(width // LANES):
        at = pair * LANES
        query = qkv_ref[0, :, at : at + LANES] * rate
        keys = qkv_ref[0, :, width + at : width + at + LANES]
        for half in range(2):
            own = low_half if half == 0 else jnp.logical_not(low_half)
            head = 2 * pair + half
            scores = dot_nt(keys, jnp.where(own, query, jnp.zeros_like(query)))
            probs = jnp.exp(scores - lse_ref[0, head : head + 1, 0:length])
            probs_ref[0, head] = probs.astype(bf16)


def early(cols, qkv, lse, slots, cap):
    images, length, wide = qkv.shape
    width = wide // 3
    heads = width // HEAD_DIM
    owners, capp, _ = slots[0].shape
    whole = lambda *tail: pl.BlockSpec((1, *tail), lambda i: (i, *[0] * len(tail)))
    return pl.pallas_call(
        functools.partial(early_kernel, len(slots), cap),
        grid=(images,),
        in_specs=[
            whole(length, 8),
            whole(length, wide),
            whole(*lse.shape[1:]),
            *[pl.BlockSpec((owners, capp, width), lambda i: (0, 0, 0))] * len(slots),
        ],
        out_specs=[whole(length, width), whole(length, 8), whole(heads, length, length)],
        out_shape=[
            jax.ShapeDtypeStruct((images, length, width), f32),
            jax.ShapeDtypeStruct((images, length, 8), f32),
            jax.ShapeDtypeStruct((images, heads, length, length), bf16),
        ],
        scratch_shapes=[pltpu.VMEM((16, len(slots) * owners * capp), bf16)],
        compiler_params=params(40),
        cost_estimate=pl.CostEstimate(
            flops=10_000_000_000, bytes_accessed=20_000_000, transcendentals=2_000_000
        ),
        name="attention_again",
    )(cols, qkv, lse, *slots)


def backward_kernel(
    labels,
    local,
    cap,
    core_ref,
    tokens_ref,
    cot_ref,
    cols_ref,
    qkv_ref,
    mixed_ref,
    picked_ref,
    scores_ref,
    probs_ref,
    first_ref,
    routed_ref,
    gates_ref,
    one_own,
    one_other,
    two_own,
    two_other,
    *refs,
):
    slots = refs[:1]
    (
        grad_tokens_ref,
        keep_one_ref,
        send_one_ref,
        keep_two_ref,
        send_two_ref,
        grad_one_ref,
        grad_two_ref,
        stack_ref,
        vec_ref,
        score_ref,
        one_ref,
        two_ref,
        misc_ref,
        sems,
    ) = refs[1:]
    _, length, width = tokens_ref.shape
    step = pl.program_id(0)
    parts = ((one_own, one_other), (two_own, two_other))
    load_weights(step, core_ref[0], parts, (one_ref, two_ref), sems)

    @pl.when(step == 0)
    def _():
        misc_ref[...] = jnp.transpose(two_ref[..., 2 * width :].reshape(width, LANES))

    vec = [misc_ref[labels + k : labels + k + 1, :].astype(f32) for k in range(VECTORS)]

    @pl.when(step == 0)
    def _():
        grad_one_ref[...] = jnp.zeros_like(grad_one_ref)
        grad_two_ref[...] = jnp.zeros_like(grad_two_ref)
        vec_ref[...] = jnp.zeros_like(vec_ref)
        stack_ref[...] = jnp.zeros_like(stack_ref)
        load_scores(slots, score_ref)

    cot = cot_ref[0].astype(f32)
    route_one, route_two = cols_ref[0, :, 2:3], cols_ref[0, :, 3:4]
    picked, gate_one, gate_two = pick([local - 1], cap, cols_ref, slots, score_ref)
    picked = picked + picked_ref[0]
    gate_one = gate_one + scores_ref[0, :, 0:1]
    gate_two = gate_two + scores_ref[0, :, 1:2]
    label = iota((length, labels), 1)
    grad_gates = jnp.where(label == route_one, gate_one, 0.0) + jnp.where(
        label == route_two, gate_two, 0.0
    )
    gates = gates_ref[0]
    inner = jnp.sum(grad_gates * gates, axis=1, keepdims=True)
    grad_logits = (gates * (grad_gates - inner)).astype(bf16)
    router = misc_ref[0:labels, :]
    routed = routed_ref[0]
    stack_ref[0:labels, :] += dot_tn(grad_logits, routed)
    grad_routed = dot(grad_logits, router) + picked
    unit, scale = norm_parts(first_ref[0])
    vec_ref[3:4, :] += jnp.sum(grad_routed * unit, axis=0, keepdims=True)
    vec_ref[4:5, :] += jnp.sum(grad_routed, axis=0, keepdims=True)
    grad_first = cot + norm_backward(grad_routed, unit, scale, vec[3])
    vec_ref[2:3, :] += jnp.sum(grad_first, axis=0, keepdims=True)
    first_low = grad_first.astype(bf16)
    add_to(grad_two_ref, slice(width, 2 * width), dot_tn(mixed_ref[0], first_low))
    w_out = two_ref[..., width : 2 * width].reshape(width, width)
    grad_mixed = dot_nt(first_low, w_out).astype(bf16)
    low_half = iota((length, LANES), 1) < HEAD_DIM
    rate = jnp.asarray(HEAD_DIM**-0.5, bf16)
    grads = [[], [], []]
    for pair in range(width // LANES):
        at = pair * LANES
        query = qkv_ref[0, :, at : at + LANES] * rate
        keys = qkv_ref[0, :, width + at : width + at + LANES]
        values = qkv_ref[0, :, 2 * width + at : 2 * width + at + LANES]
        mix = grad_mixed[:, at : at + LANES]
        grad_q = grad_k = grad_v = None
        for half in range(2):
            own = low_half if half == 0 else jnp.logical_not(low_half)
            none = jnp.zeros_like(query)
            query_own = jnp.where(own, query, none)
            mix_own = jnp.where(own, mix, none)
            head = 2 * pair + half
            low = probs_ref[0, head]
            probs = low.astype(f32)
            grad_probs = dot_nt(values, mix_own)
            inner = jnp.sum(grad_probs * probs, axis=0, keepdims=True)
            scores = (probs * (grad_probs - inner)).astype(bf16)
            part = dot(low, mix_own)
            grad_v = part if grad_v is None else grad_v + part
            part = dot(scores, query_own)
            grad_k = part if grad_k is None else grad_k + part
            part = dot_tn(scores, jnp.where(own, keys, none))
            grad_q = part if grad_q is None else grad_q + part
        grads[0].append((grad_q * HEAD_DIM**-0.5).astype(bf16))
        grads[1].append(grad_k.astype(bf16))
        grads[2].append(grad_v.astype(bf16))
    grad_one = jnp.concatenate(grads[0] + grads[1], axis=1)
    grad_two = jnp.concatenate(grads[2], axis=1)
    rows = tokens_ref[0].astype(f32)
    unit, scale = norm_parts(rows)
    normed = (unit * vec[0] + vec[1]).astype(bf16)
    add_to(grad_one_ref, slice(None), dot_tn(normed, grad_one))
    add_to(grad_two_ref, slice(0, width), dot_tn(normed, grad_two))
    grad_normed = dot_nt(grad_one, one_ref[...].reshape(width, 2 * width))
    grad_normed += dot_nt(grad_two, two_ref[..., 0:width].reshape(width, width))
    vec_ref[0:1, :] += jnp.sum(grad_normed * unit, axis=0, keepdims=True)
    vec_ref[1:2, :] += jnp.sum(grad_normed, axis=0, keepdims=True)
    grad_tokens_ref[0] = grad_first + norm_backward(grad_normed, unit, scale, vec[0])

    @pl.when(step == pl.num_programs(0) - 1)
    def _():
        stack_ref[labels : labels + 8, :] = vec_ref[...]
        add_to(grad_two_ref, slice(2 * width, None), jnp.transpose(stack_ref[...]))
        mine, other = core_ref[0], 1 - core_ref[0]
        keep_one_ref[...] = grad_one_ref[:, mine].astype(bf16)
        keep_two_ref[...] = grad_two_ref[:, mine].astype(bf16)
        send_one_ref[...] = grad_one_ref[:, other].astype(bf16)
        send_two_ref[...] = grad_two_ref[:, other].astype(bf16)


def backward(
    core, tokens, cot, cols, qkv, mixed, ahead, first, routed, gates, cap, packed, slots, local, labels
):
    images, length, width = tokens.shape
    owners, capp, _ = slots.shape
    whole = lambda *tail: pl.BlockSpec((1, *tail), lambda i: (i, *[0] * len(tail)))
    shapes = [part[0].shape for part in packed]
    still = lambda shape: pl.BlockSpec(shape, lambda i: (0, 0, 0))
    return pl.pallas_call(
        functools.partial(backward_kernel, labels, local, cap),
        grid=(images,),
        in_specs=[
            pl.BlockSpec(memory_space=pltpu.SMEM),
            whole(length, width),
            whole(length, width),
            whole(length, 8),
            whole(length, 3 * width),
            whole(length, width),
            *[whole(*part.shape[1:]) for part in ahead],
            whole(length, width),
            whole(length, width),
            whole(length, labels),
            *[pl.BlockSpec(memory_space=pl.ANY)] * 4,
            pl.BlockSpec((owners, capp, width), lambda i: (0, 0, 0)),
        ],
        out_specs=[
            whole(length, width),
            *[still(shape) for shape in shapes for _ in range(2)],
        ],
        out_shape=[
            jax.ShapeDtypeStruct((images, length, width), f32),
            *[jax.ShapeDtypeStruct(shape, bf16) for shape in shapes for _ in range(2)],
        ],
        scratch_shapes=[
            *[pltpu.VMEM((shape[0], 2, *shape[1:]), f32) for shape in shapes],
            pltpu.VMEM((LANES, width), f32),
            pltpu.VMEM((8, width), f32),
            pltpu.VMEM((16, owners * capp), bf16),
            *weight_scratch(packed),
            pltpu.VMEM((LANES, width), bf16),
            pltpu.SemaphoreType.DMA((4,)),
        ],
        compiler_params=params(58),
        cost_estimate=pl.CostEstimate(
            flops=40_000_000_000, bytes_accessed=40_000_000, transcendentals=2_000_000
        ),
        name="attention_backward",
    )(
        core,
        tokens,
        cot,
        cols,
        qkv,
        mixed,
        *ahead,
        first,
        routed,
        gates,
        *packed[0],
        *packed[1],
        slots,
    )


def output_kernel(labels, local, first_ref, cols_ref, gates_ref, slots_ref, out_ref):
    _, length, width = first_ref.shape
    owners, capp, _ = slots_ref.shape
    capp = capp // local
    span = owners * capp
    label = iota((length, labels), 1)
    total = first_ref[0]
    for k in range(2):
        picked = None
        for l in range(local):
            lane = iota((length, span), 1) + l * span
            hot = jnp.where(lane == cols_ref[0, :, k : k + 1], 1.0, 0.0).astype(bf16)
            part = dot(hot, slots_ref[:, l * capp : (l + 1) * capp, :].reshape(span, width))
            picked = part if picked is None else picked + part
        chosen = jnp.where(label == cols_ref[0, :, k + 2 : k + 3], gates_ref[0], 0.0)
        total = total + jnp.sum(chosen, axis=1, keepdims=True) * picked
    out_ref[0] = total.astype(bf16)


def combine(first, cols, gates, slots, local):
    images, length, width = first.shape
    labels = gates.shape[2]
    whole = lambda *tail: pl.BlockSpec((1, *tail), lambda i: (i, 0, 0))
    return pl.pallas_call(
        functools.partial(output_kernel, labels, local),
        grid=(images,),
        in_specs=[
            whole(length, width),
            whole(length, 8),
            whole(length, labels),
            pl.BlockSpec(slots.shape, lambda i: (0, 0, 0)),
        ],
        out_specs=whole(length, width),
        out_shape=jax.ShapeDtypeStruct((images, length, width), bf16),
        compiler_params=params(40),
        name="combine_outputs",
    )(first, cols, gates, slots)


def bits_of(groups, owners):
    outer = [("group", k) for k in reversed(range(1, groups.bit_length() - 1))]
    inner = [("expert", k) for k in reversed(range(owners.bit_length() - 1))]
    return outer, inner


def swap(block, hop, sizes):
    axis, bit = hop
    return lax.ppermute(block, axis, [(d, d ^ (1 << bit)) for d in range(sizes[axis])])


def own_bit(hop):
    return lax.rem(lax.axis_index(hop[0]) >> hop[1], 2)


def spread(block, have, hops, order, sizes):
    for hop in hops:
        other = swap(block, hop, sizes)
        have = sorted([*have, hop], key=order.index)
        at = have.index(hop)
        mine = own_bit(hop) == 0
        block = jnp.stack(
            [jnp.where(mine, block, other), jnp.where(mine, other, block)], axis=at
        )
    return block, have


def halve(total, hop, at, sizes):
    bit = own_bit(hop)
    away = lax.dynamic_index_in_dim(total, 1 - bit, at, keepdims=False)
    stay = lax.dynamic_index_in_dim(total, bit, at, keepdims=False)
    return stay, swap(away.astype(bf16), hop, sizes)


def gather_back(total, hops, order, sizes):
    have = list(order)
    for hop in hops:
        at = have.index(hop)
        have.remove(hop)
        stay, other = halve(total, hop, at, sizes)
        total = stay + other.astype(f32)
    return total


def per_device(
    groups,
    owners,
    tokens,
    cotangent,
    routes,
    order,
    ln1_gain,
    ln1_bias,
    w_qkv,
    w_out,
    b_out,
    ln2_gain,
    ln2_bias,
    w_router,
    w_in,
    b_in,
    w_back,
    b_back,
):
    images, length, width = tokens.shape
    tok_count = images * length
    labels = w_router.shape[1]
    local = labels // owners
    depth = w_in.shape[1]
    hidden = w_back.shape[1]
    cap = max(2, 5 * tok_count // (2 * labels))
    capp = -(-(cap + 3) // 16) * 16

    own = width // (groups * owners)
    sizes = {"group": groups, "expert": owners}
    outer, inner = bits_of(groups, owners)
    order_of_hops = [*outer, *inner]
    sibling = ("group", 0)
    core = own_bit(sibling).astype(jnp.int32).reshape(1)
    routes_one = [*inner, *outer]
    routes_two = [*inner[:-1], *outer, *inner[-1:]]
    vectors = (ln1_gain, ln1_bias, b_out, ln2_gain, ln2_bias)
    slices = pack(w_qkv, w_out, w_router, vectors, owners)
    near = inner[:-1]
    marks = (routes % local) * owners + routes // local
    marks = marks.swapaxes(1, 2)
    rows, cols = route(marks, order, labels, cap, capp)
    exchange = lambda block: lax.all_to_all(block, "expert", 0, 0, tiled=True)
    slices = [spread(block, [], near[:1], order_of_hops, sizes)[0] for block in slices]
    slices = [spread(block, near[:1], near[1:], order_of_hops, sizes) for block in slices]
    haves = [have for _, have in slices]
    rows, *slices = lax.optimization_barrier((rows, *[block for block, _ in slices]))
    cots = [dispatch(rows, cotangent, None, cap, capp, owners, [l]) for l in range(local)]
    cots[0] = exchange(cots[0])
    columns = [block.shape[-1] for block in slices]
    halves = []
    for turn in range(len(outer) + 1):
        moved = []
        for k, path in enumerate((routes_one, routes_two)):
            hop = path[len(near) + turn]
            block, haves[k] = spread(slices[k], haves[k], [hop], order_of_hops, sizes)
            moved.append(block)
        if turn == 0:
            w_in, w_back, *moved = lax.optimization_barrier((w_in, w_back, *moved))
        slices = moved
    halves = [
        block.reshape(groups // 2, owners * own, count) for block, count in zip(slices, columns)
    ]
    biases = jnp.zeros((local, 16, width), f32)
    biases = biases.at[:, 0, :hidden].set(b_in).at[:, 1, :depth].set(b_back)
    wide = w_in.reshape(local, depth, -1, width).swapaxes(1, 2).reshape(local, -1, width)
    height = hidden + wide.shape[1] + 16
    experts = [
        jnp.concatenate([w_back[l], wide[l], biases[l]], axis=0).astype(bf16)
        for l in range(local)
    ]
    cots[0], cots[-1], *moved = lax.optimization_barrier((cots[0], cots[-1], *experts, *halves))
    experts, halves = moved[:local], moved[local:]
    cots[1:] = [exchange(block) for block in cots[1:]]
    experts = [lax.all_gather(block, "group") for block in experts]
    packed = [(half, swap(half, sibling, sizes)) for half in halves]
    qkv, mixed, lse, first, routed, gates, gate_rows = forward(core, tokens, marks, packed, labels)
    sent = [dispatch(rows, routed, gate_rows, cap, capp, owners, [l]) for l in range(local)]
    cots[-1], sent[0] = lax.optimization_barrier((cots[-1], sent[0]))
    sent[0] = exchange(sent[0])
    for l in range(1, local):
        sent[l - 1], sent[l] = lax.optimization_barrier((sent[l - 1], sent[l]))
        sent[l] = exchange(sent[l])
    joined, backs, shares = None, [], []
    for l in range(local):
        if l + 1 < local:
            joined, back, grads = expert(sent[l], cots[l], experts[l], joined, l, local, cap)
        else:
            joined, back, keep, away = parted_expert(
                core, sent[l], cots[l], experts[l], joined, l, local, cap
            )
        if l:
            back, backs[-1] = lax.optimization_barrier((back, backs[-1]))
        if l + 1 < local:
            back, sent[l + 1] = lax.optimization_barrier((back, sent[l + 1]))
            grads, sent[l + 1] = lax.optimization_barrier((grads, sent[l + 1]))
            shares.append([lax.psum_scatter(grads, "group", scatter_dimension=0)])
        else:
            if l:
                away, backs[-1] = lax.optimization_barrier((away, backs[-1]))
            total = keep.astype(f32) + swap(away, sibling, sizes).astype(f32)
            total = total.reshape(*[2] * len(outer), height, width)
            total = gather_back(total, outer[:-1], outer, sizes)
            bit = own_bit(outer[-1])
            stay = lax.dynamic_index_in_dim(total, bit, 0, keepdims=False).astype(bf16)
            away = lax.dynamic_index_in_dim(total, 1 - bit, 0, keepdims=False).astype(bf16)
        back = exchange(back)
        if l == local - 1:
            stay, away, back = lax.optimization_barrier((stay, away, back))
            shares.append([stay, swap(away, outer[-1], sizes)])
        backs.append(back)
    joined, backs[-1] = lax.optimization_barrier((joined, backs[-1]))
    joined = exchange(joined)
    grad_tokens, *halves = backward(
        core,
        tokens,
        cotangent,
        cols,
        qkv,
        mixed,
        early(cols, qkv, lse, backs[:-1], cap),
        first,
        routed,
        gates,
        cap,
        packed,
        backs[-1],
        local,
        labels,
    )
    sums = []
    for keep, away in (halves[:2], halves[2:]):
        sums.append((keep, swap(away, sibling, sizes)))
    left = [list(order_of_hops), list(order_of_hops)]
    paths = [routes_one[::-1], routes_two[::-1]]
    share = output = None
    for turn, hops in enumerate(zip(*paths)):
        lengths = [own << (len(have) - 1 - have.index(hop)) for have, hop in zip(left, hops)]
        sums = stage(sums, lengths, [own_bit(hop) for hop in hops])
        sums = [(stay, swap(away, hop, sizes)) for (stay, away), hop in zip(sums, hops)]
        for have, hop in zip(left, hops):
            have.remove(hop)
        if turn == 0:
            share = share_out(shares[0], None, 0, local, depth)
            beside = [shares[-1][1], *share]
        elif turn == 1:
            output = combine(first, cols, gates, joined, local)
            beside = [output]
        elif turn == 2:
            for l in range(1, local):
                share = share_out(shares[l], share, l, local, depth)
            beside = [*share, grad_tokens]
        else:
            continue
        one, two, *beside = lax.optimization_barrier((sums[0][1], sums[1][1], *beside))
        sums = [(sums[0][0], one), (sums[1][0], two)]
        if turn == 0:
            shares[-1][1], *share = beside
        elif turn == 1:
            output = beside[0]
        else:
            *share, grad_tokens = beside
    one, two = sums
    share_back, share_in, share_bias = share
    grad_qkv, grad_out, grad_router, *small = dense_out(one, two, labels, owners)
    return (
        output,
        grad_tokens,
        small[0].reshape(own),
        small[1].reshape(own),
        grad_qkv,
        grad_out,
        small[2].reshape(own),
        small[3].reshape(own),
        small[4].reshape(own),
        grad_router.T,
        share_in,
        share_bias[:, 0, :hidden],
        share_back,
        share_bias[:, 1, :depth],
    )


def solution(mesh):
    rows = P(BOTH, None)
    line = P(BOTH)
    tall = P(BOTH, None, None)
    deep = P("expert", "group", None)
    flat = P("expert", "group")
    groups, owners = mesh.shape["group"], mesh.shape["expert"]
    return jax.shard_map(
        functools.partial(per_device, groups, owners),
        mesh=mesh,
        in_specs=(
            tall,
            tall,
            tall,
            rows,
            line,
            line,
            rows,
            rows,
            line,
            line,
            line,
            rows,
            deep,
            flat,
            deep,
            flat,
        ),
        out_specs=(
            tall,
            tall,
            line,
            line,
            rows,
            rows,
            line,
            line,
            line,
            rows,
            deep,
            flat,
            deep,
            flat,
        ),
        check_vma=False,
    )
```

```python
import functools

import jax
import jax.numpy as jnp
from jax import lax
from jax.experimental import pallas as pl
from jax.experimental.pallas import tpu as pltpu
from jax.sharding import PartitionSpec as P

HEAD_DIM = 64
LANES = 128
VECTORS = 5
f32 = jnp.float32
bf16 = jnp.bfloat16
BOTH = ("group", "expert")


def dot(a, b):
    return lax.dot_general(a, b, (((1,), (0,)), ((), ())), preferred_element_type=f32)


def dot_nt(a, b):
    return lax.dot_general(a, b, (((1,), (1,)), ((), ())), preferred_element_type=f32)


def dot_tn(a, b):
    return lax.dot_general(a, b, (((0,), (0,)), ((), ())), preferred_element_type=f32)


def iota(shape, dim):
    return lax.broadcasted_iota(jnp.int32, shape, dim)


def params(mib, grid=1):
    return pltpu.CompilerParams(
        vmem_limit_bytes=mib * 1024 * 1024, dimension_semantics=("arbitrary",) * grid
    )


def three_parts(value):
    high = value.astype(bf16).astype(f32)
    rest = value - high
    mid = rest.astype(bf16).astype(f32)
    return high, mid, rest - mid


def norm_parts(rows):
    centre = rows - jnp.mean(rows, axis=-1, keepdims=True)
    spread = jnp.mean(centre * centre, axis=-1, keepdims=True)
    scale = lax.rsqrt(spread + 1e-06)
    return centre * scale, scale


def norm_backward(grad, unit, scale, gain):
    lead = grad * gain
    first = jnp.mean(lead, axis=-1, keepdims=True)
    second = jnp.mean(lead * unit, axis=-1, keepdims=True)
    return scale * (lead - first - unit * second)


def load_weights(step, core, parts, scratch, sems):
    copies = []
    for k, (own, other) in enumerate(parts):
        copies.append(
            [
                pltpu.make_async_copy(own, scratch[k].at[:, core], sems.at[2 * k]),
                pltpu.make_async_copy(other, scratch[k].at[:, 1 - core], sems.at[2 * k + 1]),
            ]
        )

    @pl.when(step == 0)
    def _():
        for pair in reversed(copies):
            for copy in pair:
                copy.start()

    return copies


def arrive(step, copies):
    @pl.when(step == 0)
    def _():
        for copy in copies:
            copy.wait()


def pack_kernel(owners, qkv_ref, out_ref, router_ref, *refs):
    vec_refs, (one_ref, two_ref) = refs[:VECTORS], refs[VECTORS:]
    own, width = out_ref.shape
    labels = router_ref.shape[0]
    local = labels // owners
    cut = one_ref.shape[1]
    rest = 3 * width - cut
    one_ref[...] = qkv_ref[:, 0:cut].astype(bf16)
    two_ref[:, 0:rest] = qkv_ref[:, cut:].astype(bf16)
    two_ref[:, rest : rest + width] = out_ref[...].astype(bf16)
    lines = [
        router_ref[o * local + l : o * local + l + 1, :] for l in range(local) for o in range(owners)
    ]
    lines += [vec_ref[...] for vec_ref in vec_refs]
    lines.append(jnp.zeros((LANES - labels - VECTORS, own), f32))
    small = jnp.concatenate(lines, axis=0)
    if own < LANES:
        small = jnp.concatenate([small, jnp.zeros((LANES, LANES - own), f32)], axis=1)
    two_ref[:, rest + width :] = jnp.transpose(small)[0:own].astype(bf16)


def pack(w_qkv, w_out, w_router, vectors, owners):
    own, width = w_out.shape
    cut = 2 * width
    return pl.pallas_call(
        functools.partial(pack_kernel, owners),
        out_shape=[
            jax.ShapeDtypeStruct((own, cut), bf16),
            jax.ShapeDtypeStruct((own, 4 * width - cut + LANES), bf16),
        ],
        name="pack_weights",
    )(w_qkv, w_out, w_router.T, *[vector.reshape(1, own) for vector in vectors])


def dense_out_kernel(
    owners, one_ref, one_in, two_ref, two_in, qkv_ref, out_ref, router_ref, *vec_refs
):
    own, width = out_ref.shape
    labels = router_ref.shape[0]
    local = labels // owners
    one = one_ref[...] + one_in[...].astype(f32)
    two = two_ref[...] + two_in[...].astype(f32)
    cut = one.shape[1]
    rest = 3 * width - cut
    qkv_ref[:, 0:cut] = one
    qkv_ref[:, cut:] = two[:, 0:rest]
    out_ref[...] = two[:, rest : rest + width]
    small = two[:, rest + width :]
    if own < LANES:
        small = jnp.concatenate([small, jnp.zeros((LANES - own, LANES), f32)], axis=0)
    small = jnp.transpose(small)[:, 0:own]
    for o in range(owners):
        for l in range(local):
            at = o * local + l
            router_ref[at : at + 1, :] = small[l * owners + o : l * owners + o + 1]
    for k, vec_ref in enumerate(vec_refs):
        vec_ref[...] = small[labels + k : labels + k + 1]


def dense_out(one, two, labels, owners):
    own = one[0].shape[0]
    width = (one[0].shape[1] + two[0].shape[1] - LANES) // 4
    return pl.pallas_call(
        functools.partial(dense_out_kernel, owners),
        out_shape=[
            jax.ShapeDtypeStruct((own, 3 * width), f32),
            jax.ShapeDtypeStruct((own, width), f32),
            jax.ShapeDtypeStruct((labels, own), f32),
            *[jax.ShapeDtypeStruct((1, own), f32)] * VECTORS,
        ],
        name="dense_gradients",
    )(*one, *two)


def route_kernel(labels, cap, capp, routes_ref, order_ref, rows_ref, cols_ref):
    images, _, length = routes_ref.shape
    tok_count = order_ref.shape[1]
    order = order_ref[...]
    label = iota((labels, length), 0)
    perms, hots = [], []
    counts = jnp.zeros((2 * labels, tok_count), f32)
    for i in range(images):
        perm = jnp.where(iota((length, tok_count), 0) + i * length == order, 1.0, 0.0).astype(bf16)
        hot = jnp.concatenate(
            [
                jnp.where(label == routes_ref[i, 0:1, :], 1.0, 0.0),
                jnp.where(label == routes_ref[i, 1:2, :], 1.0, 0.0),
            ],
            axis=0,
        )
        perms.append(perm)
        hots.append(hot)
        counts = counts + dot(hot.astype(bf16), perm)
    earlier = jnp.where(
        iota((tok_count, tok_count), 0) < iota((tok_count, tok_count), 1), 1.0, 0.0
    ).astype(bf16)
    before = dot(counts.astype(bf16), earlier)
    total = jnp.sum(counts[:labels], axis=1, keepdims=True)
    before = jnp.concatenate([before[:labels], before[labels:] + total], axis=0)
    before = jnp.minimum(before, float(cap)).astype(bf16)
    same = jnp.where(iota((length, length), 0) == iota((length, length), 1), 1.0, 0.0).astype(bf16)
    for i in range(images):
        back = dot_nt(before, perms[i]) * hots[i]
        slot_one = jnp.sum(back[:labels], axis=0, keepdims=True)
        slot_two = jnp.sum(back[labels:], axis=0, keepdims=True)
        one = routes_ref[i, 0:1, :].astype(f32)
        two = routes_ref[i, 1:2, :].astype(f32)
        kept_one = jnp.where(slot_one < cap, one, -1.0)
        kept_two = jnp.where(slot_two < cap, two, -1.0)
        slot_one = jnp.where(slot_one < cap, slot_one, 0.0)
        slot_two = jnp.where(slot_two < cap, slot_two, 0.0)
        aim_one = (kept_one * capp + slot_one).astype(jnp.int32)
        aim_two = (kept_two * capp + slot_two).astype(jnp.int32)
        rows_ref[i] = jnp.concatenate(
            [aim_one, aim_two, jnp.zeros((6, length), jnp.int32)], axis=0
        )
        stacked = jnp.concatenate(
            [kept_one, slot_one, kept_two, slot_two, one, two, one, two], axis=0
        ).astype(bf16)
        turned = dot_nt(same, stacked)
        cols_ref[i] = jnp.concatenate(
            [
                turned[:, 0:1] * capp + turned[:, 1:2],
                turned[:, 2:3] * capp + turned[:, 3:4],
                turned[:, 4:5],
                turned[:, 5:6],
                turned[:, 4:8],
            ],
            axis=1,
        ).astype(jnp.int32)


def route(routes, order, labels, cap, capp):
    images, _, length = routes.shape
    return pl.pallas_call(
        functools.partial(route_kernel, labels, cap, capp),
        out_shape=(
            jax.ShapeDtypeStruct((images, 8, length), jnp.int32),
            jax.ShapeDtypeStruct((images, length, 8), jnp.int32),
        ),
        compiler_params=pltpu.CompilerParams(vmem_limit_bytes=40 * 1024 * 1024),
        name="route_tokens",
    )(routes, order)


def dispatch_kernel(cap, capp, owners, which, gated, joint, rows_ref, value_ref, *refs):
    images, length, width = value_ref.shape
    outs = refs[1:] if gated else refs
    span = owners * capp
    for place, l in enumerate(which):
        slots = iota((span, length), 0) + l * span
        total = None
        gate_rows = None
        for i in range(images):
            one = slots == rows_ref[i, 0:1, :]
            two = slots == rows_ref[i, 1:2, :]
            both = jnp.where(one | two, 1.0, 0.0).astype(bf16)
            part = dot(both, value_ref[i])
            total = part if total is None else total + part
            if gated:
                gates = refs[0][i]
                first = dot_nt(gates[0:8], jnp.where(one, 1.0, 0.0).astype(bf16))
                second = dot_nt(gates[8:16], jnp.where(two, 1.0, 0.0).astype(bf16))
                part = first + second
                gate_rows = part if gate_rows is None else gate_rows + part
        for o in range(owners):
            block = total[o * capp : (o + 1) * capp]
            if joint:
                outs[0][o, place * capp : (place + 1) * capp, :] = block.astype(bf16)
            else:
                outs[0][o] = block.astype(bf16)
            if gated:
                tail = block[capp - 16 :, 0:capp]
                spare = gate_rows[:, o * capp : (o + 1) * capp]
                line = iota((16, capp), 0) - (cap - (capp - 16))
                for k in range(3):
                    tail = jnp.where(line == k, spare[k : k + 1], tail)
                outs[0][o, capp - 16 :, 0:capp] = tail.astype(bf16)


def dispatch(rows, values, gates, cap, capp, owners, which):
    width = values.shape[2]
    joint = gates is None
    operands = (rows, values) if joint else (rows, values, gates)
    out_shape = jax.ShapeDtypeStruct((owners, len(which) * capp, width), bf16)
    return pl.pallas_call(
        functools.partial(dispatch_kernel, cap, capp, owners, tuple(which), not joint, joint),
        out_shape=out_shape,
        compiler_params=pltpu.CompilerParams(vmem_limit_bytes=40 * 1024 * 1024),
        name="fill_slots",
    )(*operands)


def forward_kernel(
    labels,
    core_ref,
    tokens_ref,
    routes_ref,
    one_own,
    one_other,
    two_own,
    two_other,
    qkv_ref,
    mixed_ref,
    lse_ref,
    first_ref,
    routed_ref,
    gates_ref,
    gate_rows_ref,
    total_ref,
    one_ref,
    two_ref,
    misc_ref,
    sems,
):
    _, length, width = tokens_ref.shape
    step = pl.program_id(0)
    parts = ((one_own, one_other), (two_own, two_other))
    copies = load_weights(step, core_ref[0], parts, (one_ref, two_ref), sems)
    cut = one_ref.shape[-1]
    rest = 3 * width - cut
    rows = tokens_ref[0].astype(f32)
    unit, _ = norm_parts(rows)
    arrive(step, copies[1])

    @pl.when(step == 0)
    def _():
        misc_ref[...] = jnp.transpose(two_ref[..., rest + width :].reshape(width, LANES))

    vec = [misc_ref[labels + k : labels + k + 1, :].astype(f32) for k in range(VECTORS)]
    normed = (unit * vec[0] + vec[1]).astype(bf16)
    arrive(step, copies[0])
    projected = jnp.concatenate(
        [
            dot(normed, one_ref[...].reshape(width, cut)).astype(bf16),
            dot(normed, two_ref[..., 0:rest].reshape(width, rest)).astype(bf16),
        ],
        axis=1,
    )
    qkv_ref[0] = projected
    lane = iota((length, LANES), 1)
    low_half = lane < HEAD_DIM
    pieces = []
    for pair in range(width // LANES):
        at = pair * LANES
        query = projected[:, at : at + LANES] * jnp.asarray(HEAD_DIM**-0.5, bf16)
        keys = projected[:, width + at : width + at + LANES]
        values = projected[:, 2 * width + at : 2 * width + at + LANES]
        mixed = None
        for half in range(2):
            own = low_half if half == 0 else jnp.logical_not(low_half)
            scores = dot_nt(jnp.where(own, query, jnp.zeros_like(query)), keys)
            top = jnp.max(scores, axis=-1, keepdims=True)
            shifted = jnp.exp(scores - top)
            total = jnp.sum(shifted, axis=-1, keepdims=True)
            head = 2 * pair + half
            total_ref[0:length, :] = jnp.where(
                lane == head, top + jnp.log(total), total_ref[0:length, :]
            )
            low = (shifted * (1.0 / total)).astype(bf16)
            part = dot(low, jnp.where(own, values, jnp.zeros_like(values)))
            mixed = part if mixed is None else mixed + part
        pieces.append(mixed.astype(bf16))
    mixed = jnp.concatenate(pieces, axis=1)
    mixed_ref[0] = mixed
    lse_ref[0] = jnp.transpose(total_ref[...])[0:16]
    w_out = two_ref[..., rest : rest + width].reshape(width, width)
    first = rows + dot(mixed, w_out) + vec[2]
    first_ref[0] = first
    unit, _ = norm_parts(first)
    routed = (unit * vec[3] + vec[4]).astype(bf16)
    routed_ref[0] = routed
    router = misc_ref[0:labels, :]
    logits = dot_nt(routed, router)
    shifted = jnp.exp(logits - jnp.max(logits, axis=1, keepdims=True))
    gates_ref[0] = shifted / jnp.sum(shifted, axis=1, keepdims=True)
    logits = dot_nt(router, routed)
    shifted = jnp.exp(logits - jnp.max(logits, axis=0, keepdims=True))
    gates = shifted / jnp.sum(shifted, axis=0, keepdims=True)
    label = iota((labels, length), 0)
    blank = jnp.zeros((5, length), f32)
    stack = []
    for k in range(2):
        chosen = jnp.where(label == routes_ref[0, k : k + 1, :], gates, 0.0)
        stack += [*three_parts(jnp.sum(chosen, axis=0, keepdims=True)), blank]
    gate_rows_ref[0] = jnp.concatenate(stack, axis=0).astype(bf16)


def weight_scratch(packed):
    return [
        pltpu.VMEM((part[0].shape[0], 2, *part[0].shape[1:]), part[0].dtype) for part in packed
    ]


def forward(core, tokens, routes, packed, labels):
    images, length, width = tokens.shape
    whole = lambda *tail: pl.BlockSpec((1, *tail), lambda i: (i, 0, 0))
    lanes = -(-length // LANES) * LANES
    return pl.pallas_call(
        functools.partial(forward_kernel, labels),
        grid=(images,),
        in_specs=[
            pl.BlockSpec(memory_space=pltpu.SMEM),
            whole(length, width),
            whole(2, length),
            *[pl.BlockSpec(memory_space=pl.ANY)] * 4,
        ],
        out_specs=[
            whole(length, 3 * width),
            whole(length, width),
            whole(16, lanes),
            whole(length, width),
            whole(length, width),
            whole(length, labels),
            whole(16, length),
        ],
        out_shape=[
            jax.ShapeDtypeStruct((images, length, 3 * width), bf16),
            jax.ShapeDtypeStruct((images, length, width), bf16),
            jax.ShapeDtypeStruct((images, 16, lanes), f32),
            jax.ShapeDtypeStruct((images, length, width), f32),
            jax.ShapeDtypeStruct((images, length, width), bf16),
            jax.ShapeDtypeStruct((images, length, labels), f32),
            jax.ShapeDtypeStruct((images, 16, length), bf16),
        ],
        scratch_shapes=[
            pltpu.VMEM((lanes, LANES), f32),
            *weight_scratch(packed),
            pltpu.VMEM((LANES, width), bf16),
            pltpu.SemaphoreType.DMA((4,)),
        ],
        compiler_params=params(40),
        cost_estimate=pl.CostEstimate(
            flops=16_000_000_000, bytes_accessed=20_000_000, transcendentals=2_000_000
        ),
        name="attention_forward",
    )(core, tokens, routes, *packed[0], *packed[1])


def expert_kernel(
    cap,
    rows_ref,
    cot_ref,
    win_ref,
    wback_ref,
    biases_ref,
    *refs,
):
    (
        out_ref,
        grad_ref,
        weights_ref,
        turned_ref,
        grad_out_ref,
        out_acc_ref,
        grad_acc_ref,
        active_ref,
        inner_ref,
        bias_ref,
        gwin_ref,
        gwback_ref,
        gbias_ref,
        sems,
    ) = refs[-14:]
    owners, capp, width = rows_ref.shape
    groups, depth, hidden = win_ref.shape
    spare = cap - (capp - 16)
    step = pl.program_id(0)
    last = pl.num_programs(0) - 1
    slot = lax.rem(step, 2)
    across = width // hidden

    def copies(step, slot):
        at = pl.multiple_of(hidden + lax.div(step, across) * depth, 16)
        start = pl.multiple_of(lax.rem(step, across) * hidden, LANES)
        return (
            pltpu.make_async_copy(
                gwback_ref.at[slot], weights_ref.at[step, pl.ds(0, hidden)], sems.at[0, slot]
            ),
            pltpu.make_async_copy(
                gwin_ref.at[slot],
                weights_ref.at[:, pl.ds(at, depth), pl.ds(start, hidden)],
                sems.at[1, slot],
            ),
        )

    @pl.when(step >= 2)
    def _():
        for copy in copies(step - 2, slot):
            copy.wait()

    @pl.when(step == 0)
    def _():
        summed = jnp.zeros((1, width), f32)
        for b in range(owners):
            tail = rows_ref[b, capp - 16 :, 0:capp].astype(f32)
            gate = (
                tail[spare : spare + 1] + tail[spare + 1 : spare + 2] + tail[spare + 2 : spare + 3]
            )
            gate = jnp.transpose(jnp.broadcast_to(gate, (LANES, capp)))[:, 0:1]
            part = (cot_ref[b].astype(f32) * gate).astype(bf16)
            grad_out_ref[b * capp : (b + 1) * capp, :] = part
            summed = summed + jnp.sum(part.astype(f32), axis=0, keepdims=True)
            turned_ref[:, b * capp : (b + 1) * capp] = jnp.transpose(rows_ref[b])
        bias_ref[...] = jnp.broadcast_to(summed, bias_ref.shape)
        out_acc_ref[...] = jnp.zeros_like(out_acc_ref)
        grad_acc_ref[...] = jnp.zeros_like(grad_acc_ref)

    first = win_ref[...].reshape(width, hidden)
    second = wback_ref[0]
    bias = biases_ref[step].astype(f32)[0:1, 0:hidden]
    bias_sum = jnp.zeros((1, hidden), f32)
    per = max(1, 256 // capp)
    k0 = 0.7978845608028654
    k1 = 0.044715
    for c in range(owners // per):
        at = slice(c * per * capp, (c + 1) * per * capp)
        block = rows_ref[c * per : (c + 1) * per].reshape(per * capp, width)
        inner = dot(block, first) + bias
        square = inner * inner
        curve = jnp.tanh(inner * (k0 + (k0 * k1) * square))
        half = 0.5 * (1.0 + curve)
        low = (inner * half).astype(bf16)
        active_ref[at, :] = low
        slope = half + (0.5 * inner) * (1.0 - curve * curve) * (k0 + (3.0 * k0 * k1) * square)
        grad_inner = dot_nt(grad_out_ref[at, :], second) * slope
        bias_sum = bias_sum + jnp.sum(grad_inner, axis=0, keepdims=True)
        grad_low = grad_inner.astype(bf16)
        inner_ref[at, :] = grad_low
        out_acc_ref[at, :] += dot(low, second)
        grad_acc_ref[at, :] += dot_nt(grad_low, first)
    gwin_ref[slot] = dot(turned_ref[...], inner_ref[...]).astype(bf16).reshape(win_ref.shape)
    gwback_ref[slot] = dot_tn(active_ref[...], grad_out_ref[...]).astype(bf16)
    row = iota((16, width), 0)
    if hidden < width:
        bias_sum = jnp.concatenate([bias_sum, jnp.zeros((1, width - hidden), f32)], axis=1)
    pad = jnp.where(row == 0, bias_sum, 0.0)
    gbias_ref[step] = pad.astype(bf16)
    for copy in copies(step, slot):
        copy.start()

    @pl.when(step == last)
    def _():
        for g in range(groups):
            part = bias_ref[0:1, g * depth : (g + 1) * depth]
            part = jnp.concatenate([part, jnp.zeros((1, width - depth), f32)], axis=1)
            block = gbias_ref[g].astype(f32)
            gbias_ref[g] = jnp.where(row == 1, part, block).astype(bf16)
        end = pltpu.make_async_copy(
            gbias_ref, weights_ref.at[:, pl.ds(weights_ref.shape[1] - 16, 16)], sems.at[2, 0]
        )
        end.start()
        whole = jnp.concatenate(
            [biases_ref[g].astype(f32)[1:2, 0:depth] for g in range(groups)], axis=1
        )
        for b in range(owners):
            at = slice(b * capp, (b + 1) * capp)
            result = (out_acc_ref[at, :] + whole).astype(bf16)
            out_ref[b] = result
            score = jnp.sum(result.astype(f32) * cot_ref[b].astype(f32), axis=1, keepdims=True)
            score = jnp.transpose(jnp.broadcast_to(score, (capp, LANES)))[0:1, :]
            back = grad_acc_ref[at, :]
            grad_ref[b] = back.astype(bf16)
            tail = back[capp - 16 :, 0:capp]
            line = iota((16, capp), 0) - spare
            for k, part in enumerate(three_parts(score)):
                tail = jnp.where(line == k, part, tail)
            grad_ref[b, capp - 16 :, 0:capp] = tail.astype(bf16)
        for back in range(2):
            for copy in copies(step - back, lax.rem(step + back, 2)):
                copy.wait()
        end.wait()


def expert(rows, cots, weights, outcomes, which, local, cap):
    owners, capp, width = rows.shape
    groups, height, _ = weights.shape
    depth = width // groups
    hidden = height - 16 - (height - 16) // 2
    across = width // hidden
    total = owners * capp
    full = lambda shape: pl.BlockSpec(shape, lambda j: (0,) * len(shape))
    anywhere = pl.BlockSpec(memory_space=pl.ANY)
    extra = [] if outcomes is None else [outcomes]
    return pl.pallas_call(
        functools.partial(expert_kernel, cap),
        grid=(groups,),
        in_specs=[
            full((owners, capp, width)),
            full((owners, capp, width)),
            pl.BlockSpec(
                (groups, depth, hidden), lambda j: (0, hidden // depth + j // across, j % across)
            ),
            pl.BlockSpec((1, hidden, width), lambda j: (j, 0, 0)),
            pl.BlockSpec((groups, 16, width), lambda j: (0, (height - 16) // 16, 0)),
            *[anywhere] * len(extra),
        ],
        out_specs=[
            pl.BlockSpec((owners, capp, width), lambda j: (0, which, 0)),
            full((owners, capp, width)),
            anywhere,
        ],
        out_shape=[
            jax.ShapeDtypeStruct((owners, local * capp, width), bf16),
            jax.ShapeDtypeStruct((owners, capp, width), bf16),
            jax.ShapeDtypeStruct(weights.shape, bf16),
        ],
        input_output_aliases={5: 0} if extra else {},
        scratch_shapes=[
            pltpu.VMEM((width, total), bf16),
            pltpu.VMEM((total, width), bf16),
            pltpu.VMEM((total, width), f32),
            pltpu.VMEM((total, width), f32),
            pltpu.VMEM((total, hidden), bf16),
            pltpu.VMEM((total, hidden), bf16),
            pltpu.VMEM((8, width), f32),
            pltpu.VMEM((2, groups, depth, hidden), bf16),
            pltpu.VMEM((2, hidden, width), bf16),
            pltpu.VMEM((groups, 16, width), bf16),
            pltpu.SemaphoreType.DMA((3, 2)),
        ],
        compiler_params=params(56),
        cost_estimate=pl.CostEstimate(
            flops=2 * 6 * total * width * hidden * groups,
            bytes_accessed=30_000_000,
            transcendentals=total * hidden * groups,
        ),
        name="expert_rows",
    )(rows, cots, weights, weights, weights, *extra)


def parted_kernel(
    cap,
    core_ref,
    rows_ref,
    cot_ref,
    win_ref,
    wback_ref,
    biases_ref,
    *refs,
):
    (
        out_ref,
        grad_ref,
        keep_ref,
        away_ref,
        turned_ref,
        grad_out_ref,
        out_acc_ref,
        grad_acc_ref,
        active_ref,
        inner_ref,
        bias_ref,
        gwin_ref,
        gwback_ref,
        gbias_ref,
        sems,
    ) = refs[-15:]
    owners, capp, width = rows_ref.shape
    groups, depth, hidden = win_ref.shape
    spare = cap - (capp - 16)
    step = pl.program_id(0)
    last = pl.num_programs(0) - 1
    slot = lax.rem(step, 2)
    across = width // hidden

    mine = core_ref[0]
    targets = ((keep_ref, mine, 0), (away_ref, 1 - mine, 1))

    def copies(step, slot):
        at = pl.multiple_of(hidden + lax.div(step, across) * depth, 16)
        start = pl.multiple_of(lax.rem(step, across) * hidden, LANES)
        return [
            pltpu.make_async_copy(
                gwin_ref.at[slot, :, part],
                target.at[:, pl.ds(at, depth), pl.ds(start, hidden)],
                sems.at[1 + k, slot],
            )
            for target, part, k in targets
        ]

    def whole_chunk(step, slot, act):
        for target, part, _ in targets:

            @pl.when(lax.rem(step, 2) == part)
            def _():
                act(
                    pltpu.make_async_copy(
                        gwback_ref.at[slot],
                        target.at[lax.div(step, 2), pl.ds(0, hidden)],
                        sems.at[0, slot],
                    )
                )

    def finish(step, slot):
        for copy in copies(step, slot):
            copy.wait()
        whole_chunk(step, slot, lambda copy: copy.wait())

    @pl.when(step >= 2)
    def _():
        finish(step - 2, slot)

    @pl.when(step == 0)
    def _():
        summed = jnp.zeros((1, width), f32)
        for b in range(owners):
            tail = rows_ref[b, capp - 16 :, 0:capp].astype(f32)
            gate = (
                tail[spare : spare + 1] + tail[spare + 1 : spare + 2] + tail[spare + 2 : spare + 3]
            )
            gate = jnp.transpose(jnp.broadcast_to(gate, (LANES, capp)))[:, 0:1]
            part = (cot_ref[b].astype(f32) * gate).astype(bf16)
            grad_out_ref[b * capp : (b + 1) * capp, :] = part
            summed = summed + jnp.sum(part.astype(f32), axis=0, keepdims=True)
            turned_ref[:, b * capp : (b + 1) * capp] = jnp.transpose(rows_ref[b])
        bias_ref[...] = jnp.broadcast_to(summed, bias_ref.shape)
        out_acc_ref[...] = jnp.zeros_like(out_acc_ref)
        grad_acc_ref[...] = jnp.zeros_like(grad_acc_ref)

    first = win_ref[...].reshape(width, hidden)
    second = wback_ref[0]
    bias = biases_ref[step].astype(f32)[0:1, 0:hidden]
    bias_sum = jnp.zeros((1, hidden), f32)
    per = max(1, 256 // capp)
    k0 = 0.7978845608028654
    k1 = 0.044715
    for c in range(owners // per):
        at = slice(c * per * capp, (c + 1) * per * capp)
        block = rows_ref[c * per : (c + 1) * per].reshape(per * capp, width)
        inner = dot(block, first) + bias
        square = inner * inner
        curve = jnp.tanh(inner * (k0 + (k0 * k1) * square))
        half = 0.5 * (1.0 + curve)
        low = (inner * half).astype(bf16)
        active_ref[at, :] = low
        slope = half + (0.5 * inner) * (1.0 - curve * curve) * (k0 + (3.0 * k0 * k1) * square)
        grad_inner = dot_nt(grad_out_ref[at, :], second) * slope
        bias_sum = bias_sum + jnp.sum(grad_inner, axis=0, keepdims=True)
        grad_low = grad_inner.astype(bf16)
        inner_ref[at, :] = grad_low
        out_acc_ref[at, :] += dot(low, second)
        grad_acc_ref[at, :] += dot_nt(grad_low, first)
    gwin_ref[slot] = dot(turned_ref[...], inner_ref[...]).astype(bf16).reshape(gwin_ref.shape[1:])
    gwback_ref[slot] = dot_tn(active_ref[...], grad_out_ref[...]).astype(bf16)
    row = iota((16, width), 0)
    if hidden < width:
        bias_sum = jnp.concatenate([bias_sum, jnp.zeros((1, width - hidden), f32)], axis=1)
    pad = jnp.where(row == 0, bias_sum, 0.0)
    gbias_ref[lax.div(step, 2), lax.rem(step, 2)] = pad.astype(bf16)
    for copy in copies(step, slot):
        copy.start()
    whole_chunk(step, slot, lambda copy: copy.start())

    @pl.when(step == last)
    def _():
        for g in range(groups):
            part = bias_ref[0:1, g * depth : (g + 1) * depth]
            part = jnp.concatenate([part, jnp.zeros((1, width - depth), f32)], axis=1)
            block = gbias_ref[g // 2, g % 2].astype(f32)
            gbias_ref[g // 2, g % 2] = jnp.where(row == 1, part, block).astype(bf16)
        ends = [
            pltpu.make_async_copy(
                gbias_ref.at[:, part],
                target.at[:, pl.ds(target.shape[1] - 16, 16)],
                sems.at[3, k],
            )
            for target, part, k in targets
        ]
        for end in ends:
            end.start()
        whole = jnp.concatenate(
            [biases_ref[g].astype(f32)[1:2, 0:depth] for g in range(groups)], axis=1
        )
        for b in range(owners):
            at = slice(b * capp, (b + 1) * capp)
            result = (out_acc_ref[at, :] + whole).astype(bf16)
            out_ref[b] = result
            score = jnp.sum(result.astype(f32) * cot_ref[b].astype(f32), axis=1, keepdims=True)
            score = jnp.transpose(jnp.broadcast_to(score, (capp, LANES)))[0:1, :]
            back = grad_acc_ref[at, :]
            grad_ref[b] = back.astype(bf16)
            tail = back[capp - 16 :, 0:capp]
            line = iota((16, capp), 0) - spare
            for k, part in enumerate(three_parts(score)):
                tail = jnp.where(line == k, part, tail)
            grad_ref[b, capp - 16 :, 0:capp] = tail.astype(bf16)
        finish(step - 1, 1 - slot)
        finish(step, slot)
        for end in ends:
            end.wait()


def parted_expert(core, rows, cots, weights, outcomes, which, local, cap):
    owners, capp, width = rows.shape
    groups, height, _ = weights.shape
    depth = width // groups
    hidden = height - 16 - (height - 16) // 2
    across = width // hidden
    total = owners * capp
    full = lambda shape: pl.BlockSpec(shape, lambda j: (0,) * len(shape))
    anywhere = pl.BlockSpec(memory_space=pl.ANY)
    extra = [] if outcomes is None else [outcomes]
    return pl.pallas_call(
        functools.partial(parted_kernel, cap),
        grid=(groups,),
        in_specs=[
            pl.BlockSpec(memory_space=pltpu.SMEM),
            full((owners, capp, width)),
            full((owners, capp, width)),
            pl.BlockSpec(
                (groups, depth, hidden), lambda j: (0, hidden // depth + j // across, j % across)
            ),
            pl.BlockSpec((1, hidden, width), lambda j: (j, 0, 0)),
            pl.BlockSpec((groups, 16, width), lambda j: (0, (height - 16) // 16, 0)),
            *[anywhere] * len(extra),
        ],
        out_specs=[
            pl.BlockSpec((owners, capp, width), lambda j: (0, which, 0)),
            full((owners, capp, width)),
            anywhere,
            anywhere,
        ],
        out_shape=[
            jax.ShapeDtypeStruct((owners, local * capp, width), bf16),
            jax.ShapeDtypeStruct((owners, capp, width), bf16),
            jax.ShapeDtypeStruct((groups // 2, height, width), bf16),
            jax.ShapeDtypeStruct((groups // 2, height, width), bf16),
        ],
        input_output_aliases={6: 0} if extra else {},
        scratch_shapes=[
            pltpu.VMEM((width, total), bf16),
            pltpu.VMEM((total, width), bf16),
            pltpu.VMEM((total, width), f32),
            pltpu.VMEM((total, width), f32),
            pltpu.VMEM((total, hidden), bf16),
            pltpu.VMEM((total, hidden), bf16),
            pltpu.VMEM((8, width), f32),
            pltpu.VMEM((2, groups // 2, 2, depth, hidden), bf16),
            pltpu.VMEM((2, hidden, width), bf16),
            pltpu.VMEM((groups // 2, 2, 16, width), bf16),
            pltpu.SemaphoreType.DMA((4, 2)),
        ],
        compiler_params=params(56),
        cost_estimate=pl.CostEstimate(
            flops=2 * 6 * total * width * hidden * groups,
            bytes_accessed=30_000_000,
            transcendentals=total * hidden * groups,
        ),
        name="expert_rows_parted",
    )(core, rows, cots, weights, weights, weights, *extra)


def share_kernel(addends, *refs):
    back_ref, in_ref, bias_ref = refs[-3:]
    value = [refs[k][...].astype(f32) for k in range(3)]
    if addends > 1:
        value = [part + refs[3 + k][...].astype(f32) for k, part in enumerate(value)]
    back_ref[0] = value[0]
    in_ref[0] = value[1]
    bias_ref[0] = value[2]


def share_out(shares, outs, which, local, depth):
    height, width = shares[0].shape
    hidden = (height - 16) // 2
    steps = hidden // depth
    extra = [] if outs is None else list(outs)
    operands = [share for share in shares for _ in range(3)]
    return pl.pallas_call(
        functools.partial(share_kernel, len(shares)),
        grid=(steps,),
        in_specs=[
            *[
                pl.BlockSpec((depth, width), lambda j: (j, 0)),
                pl.BlockSpec((depth, width), lambda j: (steps + j, 0)),
                pl.BlockSpec((16, width), lambda j: (2 * hidden // 16, 0)),
            ]
            * len(shares),
            *[pl.BlockSpec(memory_space=pl.ANY)] * len(extra),
        ],
        out_specs=[
            pl.BlockSpec((1, depth, width), lambda j: (which, j, 0)),
            pl.BlockSpec((1, depth, width), lambda j: (which, 0, j)),
            pl.BlockSpec((1, 16, width), lambda j: (which, 0, 0)),
        ],
        out_shape=[
            jax.ShapeDtypeStruct((local, hidden, width), f32),
            jax.ShapeDtypeStruct((local, depth, steps * width), f32),
            jax.ShapeDtypeStruct((local, 16, width), f32),
        ],
        input_output_aliases={len(operands) + k: k for k in range(len(extra))},
        compiler_params=params(32),
        name="expert_gradients",
    )(*operands, *extra)


def stage_kernel(own_rows, *refs):
    bits, refs = refs[: len(own_rows)], refs[len(own_rows) :]
    for k, rows in enumerate(own_rows):
        keep_ref, other_ref = refs[2 * k : 2 * k + 2]
        stay_ref, away_ref = refs[2 * (len(own_rows) + k) : 2 * (len(own_rows) + k) + 2]
        mine = bits[k][0] == 0
        total = keep_ref[...].astype(f32) + other_ref[...].astype(f32)
        if total.ndim == 3:
            pairs = [(total[0], total[1])]
        else:
            pairs = [
                (total[at : at + rows], total[at + rows : at + 2 * rows])
                for at in range(0, total.shape[0], 2 * rows)
            ]
        stay = [jnp.where(mine, one, two) for one, two in pairs]
        away = [jnp.where(mine, two, one) for one, two in pairs]
        stay_ref[...] = jnp.concatenate(stay, axis=0)
        away_ref[...] = jnp.concatenate(away, axis=0).astype(bf16)


def stage(pairs, lengths, bits):
    rows = [pair[0].size // pair[0].shape[-1] for pair in pairs]
    turns = [count // (2 * length) for count, length in zip(rows, lengths)]

    def fits(steps):
        return all(
            length % (16 * steps) == 0
            if turn == 1
            else turn % steps == 0 and length * (turn // steps) % 16 == 0
            for turn, length in zip(turns, lengths)
        )

    steps = next((count for count in (4, 2) if fits(count)), 1)
    operands, in_specs, out_specs, out_shape = [], [], [], []
    for pair, count, length, turn in zip(pairs, rows, lengths, turns):
        columns = pair[0].shape[-1]
        if turn == 1 and length % 16 == 0:
            shape, block = (2, length, columns), (2, length // steps, columns)
            where = lambda j: (0, j, 0)
        else:
            shape, block = (count, columns), (count // steps, columns)
            where = lambda j: (j, 0)
        operands += [part.reshape(shape) for part in pair]
        in_specs += [pl.BlockSpec(block, where)] * 2
        half = pl.BlockSpec((count // 2 // steps, columns), lambda j: (j, 0))
        out_specs += [half, half]
        out_shape += [jax.ShapeDtypeStruct((count // 2, columns), kind) for kind in (f32, bf16)]
    results = pl.pallas_call(
        functools.partial(stage_kernel, tuple(lengths)),
        grid=(steps,),
        in_specs=[*[pl.BlockSpec(memory_space=pltpu.SMEM)] * len(pairs), *in_specs],
        out_specs=out_specs,
        out_shape=out_shape,
        compiler_params=params(40),
        name="add_and_halve",
    )(*[bit.astype(jnp.int32).reshape(1) for bit in bits], *operands)
    return [results[2 * k : 2 * k + 2] for k in range(len(pairs))]


def add_to(ref, columns, value):
    shape = (*ref.shape[:-1], value.shape[-1])
    ref[..., columns] += value.reshape(shape)


def pick(which, cap, cols_ref, slots, score_ref):
    length = cols_ref.shape[1]
    owners, capp, width = slots[0].shape
    spare = cap - (capp - 16)
    span = owners * capp
    picked = gate_one = gate_two = None
    for k, l in enumerate(which):
        lane = iota((length, span), 1) + l * span
        one = jnp.where(lane == cols_ref[0, :, 0:1], 1.0, 0.0)
        two = jnp.where(lane == cols_ref[0, :, 1:2], 1.0, 0.0)
        part = dot((one + two).astype(bf16), slots[k][...].reshape(span, width))
        picked = part if picked is None else picked + part
        score = score_ref[:, k * span : (k + 1) * span]
        part_one = dot_nt(one.astype(bf16), score)
        part_two = dot_nt(two.astype(bf16), score)
        gate_one = part_one if gate_one is None else gate_one + part_one
        gate_two = part_two if gate_two is None else gate_two + part_two
    line = iota((length, 16), 1)
    mine = (line >= spare) & (line < spare + 3)
    gate_one = jnp.sum(jnp.where(mine, gate_one, 0.0), axis=1, keepdims=True)
    gate_two = jnp.sum(jnp.where(mine, gate_two, 0.0), axis=1, keepdims=True)
    return picked, gate_one, gate_two


def load_scores(slots, score_ref):
    owners, capp, _ = slots[0].shape
    span = owners * capp
    for k, block in enumerate(slots):
        for o in range(owners):
            at = k * span + o * capp
            score_ref[:, at : at + capp] = block[o, capp - 16 :, 0:capp]


def early_kernel(local, cap, cols_ref, qkv_ref, lse_ref, *refs):
    slots = refs[:local]
    picked_ref, gate_ref, probs_ref, score_ref = refs[local:]
    _, length, width = picked_ref.shape

    @pl.when(pl.program_id(0) == 0)
    def _():
        load_scores(slots, score_ref)

    picked, gate_one, gate_two = pick(range(local), cap, cols_ref, slots, score_ref)
    picked_ref[0] = picked
    lane = iota((length, 8), 1)
    gate_ref[0] = jnp.where(lane == 0, gate_one, jnp.where(lane == 1, gate_two, 0.0))
    low_half = iota((length, LANES), 1) < HEAD_DIM
    rate = jnp.asarray(HEAD_DIM**-0.5, bf16)
    for pair in range(width // LANES):
        at = pair * LANES
        query = qkv_ref[0, :, at : at + LANES] * rate
        keys = qkv_ref[0, :, width + at : width + at + LANES]
        for half in range(2):
            own = low_half if half == 0 else jnp.logical_not(low_half)
            head = 2 * pair + half
            scores = dot_nt(keys, jnp.where(own, query, jnp.zeros_like(query)))
            probs = jnp.exp(scores - lse_ref[0, head : head + 1, 0:length])
            probs_ref[0, head] = probs.astype(bf16)


def early(cols, qkv, lse, slots, cap):
    images, length, wide = qkv.shape
    width = wide // 3
    heads = width // HEAD_DIM
    owners, capp, _ = slots[0].shape
    whole = lambda *tail: pl.BlockSpec((1, *tail), lambda i: (i, *[0] * len(tail)))
    return pl.pallas_call(
        functools.partial(early_kernel, len(slots), cap),
        grid=(images,),
        in_specs=[
            whole(length, 8),
            whole(length, wide),
            whole(*lse.shape[1:]),
            *[pl.BlockSpec((owners, capp, width), lambda i: (0, 0, 0))] * len(slots),
        ],
        out_specs=[whole(length, width), whole(length, 8), whole(heads, length, length)],
        out_shape=[
            jax.ShapeDtypeStruct((images, length, width), f32),
            jax.ShapeDtypeStruct((images, length, 8), f32),
            jax.ShapeDtypeStruct((images, heads, length, length), bf16),
        ],
        scratch_shapes=[pltpu.VMEM((16, len(slots) * owners * capp), bf16)],
        compiler_params=params(40),
        cost_estimate=pl.CostEstimate(
            flops=10_000_000_000, bytes_accessed=20_000_000, transcendentals=2_000_000
        ),
        name="attention_again",
    )(cols, qkv, lse, *slots)


def backward_kernel(
    labels,
    local,
    cap,
    core_ref,
    tokens_ref,
    cot_ref,
    cols_ref,
    qkv_ref,
    mixed_ref,
    picked_ref,
    scores_ref,
    probs_ref,
    first_ref,
    routed_ref,
    gates_ref,
    one_own,
    one_other,
    two_own,
    two_other,
    *refs,
):
    slots = refs[:1]
    (
        grad_tokens_ref,
        keep_one_ref,
        send_one_ref,
        keep_two_ref,
        send_two_ref,
        grad_one_ref,
        grad_two_ref,
        stack_ref,
        vec_ref,
        score_ref,
        one_ref,
        two_ref,
        misc_ref,
        sems,
    ) = refs[1:]
    _, length, width = tokens_ref.shape
    step = pl.program_id(0)
    parts = ((one_own, one_other), (two_own, two_other))
    copies = load_weights(step, core_ref[0], parts, (one_ref, two_ref), sems)
    cut = one_ref.shape[-1]
    rest = 3 * width - cut
    grad_cut = grad_one_ref.shape[-1]
    grad_rest = 3 * width - grad_cut

    @pl.when(step == 0)
    def _():
        grad_one_ref[...] = jnp.zeros_like(grad_one_ref)
        grad_two_ref[...] = jnp.zeros_like(grad_two_ref)
        vec_ref[...] = jnp.zeros_like(vec_ref)
        stack_ref[...] = jnp.zeros_like(stack_ref)
        load_scores(slots, score_ref)

    cot = cot_ref[0].astype(f32)
    route_one, route_two = cols_ref[0, :, 2:3], cols_ref[0, :, 3:4]
    picked, gate_one, gate_two = pick([local - 1], cap, cols_ref, slots, score_ref)
    picked = picked + picked_ref[0]
    gate_one = gate_one + scores_ref[0, :, 0:1]
    gate_two = gate_two + scores_ref[0, :, 1:2]
    arrive(step, copies[1])

    @pl.when(step == 0)
    def _():
        misc_ref[...] = jnp.transpose(two_ref[..., rest + width :].reshape(width, LANES))

    vec = [misc_ref[labels + k : labels + k + 1, :].astype(f32) for k in range(VECTORS)]
    label = iota((length, labels), 1)
    grad_gates = jnp.where(label == route_one, gate_one, 0.0) + jnp.where(
        label == route_two, gate_two, 0.0
    )
    gates = gates_ref[0]
    inner = jnp.sum(grad_gates * gates, axis=1, keepdims=True)
    grad_logits = (gates * (grad_gates - inner)).astype(bf16)
    router = misc_ref[0:labels, :]
    routed = routed_ref[0]
    stack_ref[0:labels, :] += dot_tn(grad_logits, routed)
    grad_routed = dot(grad_logits, router) + picked
    unit, scale = norm_parts(first_ref[0])
    vec_ref[3:4, :] += jnp.sum(grad_routed * unit, axis=0, keepdims=True)
    vec_ref[4:5, :] += jnp.sum(grad_routed, axis=0, keepdims=True)
    grad_first = cot + norm_backward(grad_routed, unit, scale, vec[3])
    vec_ref[2:3, :] += jnp.sum(grad_first, axis=0, keepdims=True)
    first_low = grad_first.astype(bf16)
    add_to(grad_two_ref, slice(grad_rest, grad_rest + width), dot_tn(mixed_ref[0], first_low))
    w_out = two_ref[..., rest : rest + width].reshape(width, width)
    grad_mixed = dot_nt(first_low, w_out).astype(bf16)
    low_half = iota((length, LANES), 1) < HEAD_DIM
    rate = jnp.asarray(HEAD_DIM**-0.5, bf16)
    grads = [[], [], []]
    for pair in range(width // LANES):
        at = pair * LANES
        query = qkv_ref[0, :, at : at + LANES] * rate
        keys = qkv_ref[0, :, width + at : width + at + LANES]
        values = qkv_ref[0, :, 2 * width + at : 2 * width + at + LANES]
        mix = grad_mixed[:, at : at + LANES]
        grad_q = grad_k = grad_v = None
        for half in range(2):
            own = low_half if half == 0 else jnp.logical_not(low_half)
            none = jnp.zeros_like(query)
            query_own = jnp.where(own, query, none)
            mix_own = jnp.where(own, mix, none)
            head = 2 * pair + half
            low = probs_ref[0, head]
            probs = low.astype(f32)
            grad_probs = dot_nt(values, mix_own)
            inner = jnp.sum(grad_probs * probs, axis=0, keepdims=True)
            scores = (probs * (grad_probs - inner)).astype(bf16)
            part = dot(low, mix_own)
            grad_v = part if grad_v is None else grad_v + part
            part = dot(scores, query_own)
            grad_k = part if grad_k is None else grad_k + part
            part = dot_tn(scores, jnp.where(own, keys, none))
            grad_q = part if grad_q is None else grad_q + part
        grads[0].append((grad_q * HEAD_DIM**-0.5).astype(bf16))
        grads[1].append(grad_k.astype(bf16))
        grads[2].append(grad_v.astype(bf16))
    grad_qkv = jnp.concatenate(grads[0] + grads[1] + grads[2], axis=1)
    rows = tokens_ref[0].astype(f32)
    unit, scale = norm_parts(rows)
    normed = (unit * vec[0] + vec[1]).astype(bf16)
    add_to(grad_one_ref, slice(None), dot_tn(normed, grad_qkv[:, 0:grad_cut]))
    add_to(grad_two_ref, slice(0, grad_rest), dot_tn(normed, grad_qkv[:, grad_cut:]))
    arrive(step, copies[0])
    grad_normed = dot_nt(grad_qkv[:, 0:cut], one_ref[...].reshape(width, cut))
    grad_normed += dot_nt(grad_qkv[:, cut:], two_ref[..., 0:rest].reshape(width, rest))
    vec_ref[0:1, :] += jnp.sum(grad_normed * unit, axis=0, keepdims=True)
    vec_ref[1:2, :] += jnp.sum(grad_normed, axis=0, keepdims=True)
    grad_tokens_ref[0] = grad_first + norm_backward(grad_normed, unit, scale, vec[0])

    @pl.when(step == pl.num_programs(0) - 1)
    def _():
        stack_ref[labels : labels + 8, :] = vec_ref[...]
        add_to(grad_two_ref, slice(grad_rest + width, None), jnp.transpose(stack_ref[...]))
        mine, other = core_ref[0], 1 - core_ref[0]
        keep_one_ref[...] = grad_one_ref[:, mine].astype(bf16)
        keep_two_ref[...] = grad_two_ref[:, mine].astype(bf16)
        send_one_ref[...] = grad_one_ref[:, other].astype(bf16)
        send_two_ref[...] = grad_two_ref[:, other].astype(bf16)


def backward(
    core, tokens, cot, cols, qkv, mixed, ahead, first, routed, gates, cap, packed, slots, local, labels
):
    images, length, width = tokens.shape
    owners, capp, _ = slots.shape
    whole = lambda *tail: pl.BlockSpec((1, *tail), lambda i: (i, *[0] * len(tail)))
    spare = sum(part[0].shape[2] for part in packed)
    grad_cut = 2 * width + width // 3 // LANES * LANES
    shapes = [(*packed[0][0].shape[:2], count) for count in (grad_cut, spare - grad_cut)]
    still = lambda shape: pl.BlockSpec(shape, lambda i: (0, 0, 0))
    return pl.pallas_call(
        functools.partial(backward_kernel, labels, local, cap),
        grid=(images,),
        in_specs=[
            pl.BlockSpec(memory_space=pltpu.SMEM),
            whole(length, width),
            whole(length, width),
            whole(length, 8),
            whole(length, 3 * width),
            whole(length, width),
            *[whole(*part.shape[1:]) for part in ahead],
            whole(length, width),
            whole(length, width),
            whole(length, labels),
            *[pl.BlockSpec(memory_space=pl.ANY)] * 4,
            pl.BlockSpec((owners, capp, width), lambda i: (0, 0, 0)),
        ],
        out_specs=[
            whole(length, width),
            *[still(shape) for shape in shapes for _ in range(2)],
        ],
        out_shape=[
            jax.ShapeDtypeStruct((images, length, width), f32),
            *[jax.ShapeDtypeStruct(shape, bf16) for shape in shapes for _ in range(2)],
        ],
        scratch_shapes=[
            *[pltpu.VMEM((shape[0], 2, *shape[1:]), f32) for shape in shapes],
            pltpu.VMEM((LANES, width), f32),
            pltpu.VMEM((8, width), f32),
            pltpu.VMEM((16, owners * capp), bf16),
            *weight_scratch(packed),
            pltpu.VMEM((LANES, width), bf16),
            pltpu.SemaphoreType.DMA((4,)),
        ],
        compiler_params=params(58),
        cost_estimate=pl.CostEstimate(
            flops=40_000_000_000, bytes_accessed=40_000_000, transcendentals=2_000_000
        ),
        name="attention_backward",
    )(
        core,
        tokens,
        cot,
        cols,
        qkv,
        mixed,
        *ahead,
        first,
        routed,
        gates,
        *packed[0],
        *packed[1],
        slots,
    )


def output_kernel(labels, local, first_ref, cols_ref, gates_ref, slots_ref, out_ref):
    _, length, width = first_ref.shape
    owners, capp, _ = slots_ref.shape
    capp = capp // local
    span = owners * capp
    label = iota((length, labels), 1)
    total = first_ref[0]
    for k in range(2):
        picked = None
        for l in range(local):
            lane = iota((length, span), 1) + l * span
            hot = jnp.where(lane == cols_ref[0, :, k : k + 1], 1.0, 0.0).astype(bf16)
            part = dot(hot, slots_ref[:, l * capp : (l + 1) * capp, :].reshape(span, width))
            picked = part if picked is None else picked + part
        chosen = jnp.where(label == cols_ref[0, :, k + 2 : k + 3], gates_ref[0], 0.0)
        total = total + jnp.sum(chosen, axis=1, keepdims=True) * picked
    out_ref[0] = total.astype(bf16)


def combine(first, cols, gates, slots, local):
    images, length, width = first.shape
    labels = gates.shape[2]
    whole = lambda *tail: pl.BlockSpec((1, *tail), lambda i: (i, 0, 0))
    return pl.pallas_call(
        functools.partial(output_kernel, labels, local),
        grid=(images,),
        in_specs=[
            whole(length, width),
            whole(length, 8),
            whole(length, labels),
            pl.BlockSpec(slots.shape, lambda i: (0, 0, 0)),
        ],
        out_specs=whole(length, width),
        out_shape=jax.ShapeDtypeStruct((images, length, width), bf16),
        compiler_params=params(40),
        name="combine_outputs",
    )(first, cols, gates, slots)


def bits_of(groups, owners):
    outer = [("group", k) for k in reversed(range(1, groups.bit_length() - 1))]
    inner = [("expert", k) for k in reversed(range(owners.bit_length() - 1))]
    return outer, inner


def swap(block, hop, sizes):
    axis, bit = hop
    return lax.ppermute(block, axis, [(d, d ^ (1 << bit)) for d in range(sizes[axis])])


def own_bit(hop):
    return lax.rem(lax.axis_index(hop[0]) >> hop[1], 2)


def spread(block, have, hops, order, sizes):
    for hop in hops:
        other = swap(block, hop, sizes)
        have = sorted([*have, hop], key=order.index)
        at = have.index(hop)
        mine = own_bit(hop) == 0
        block = jnp.stack(
            [jnp.where(mine, block, other), jnp.where(mine, other, block)], axis=at
        )
    return block, have


def halve(total, hop, at, sizes):
    bit = own_bit(hop)
    away = lax.dynamic_index_in_dim(total, 1 - bit, at, keepdims=False)
    stay = lax.dynamic_index_in_dim(total, bit, at, keepdims=False)
    return stay, swap(away.astype(bf16), hop, sizes)


def gather_back(total, hops, order, sizes):
    have = list(order)
    for hop in hops:
        at = have.index(hop)
        have.remove(hop)
        stay, other = halve(total, hop, at, sizes)
        total = stay + other.astype(f32)
    return total


def per_device(
    groups,
    owners,
    tokens,
    cotangent,
    routes,
    order,
    ln1_gain,
    ln1_bias,
    w_qkv,
    w_out,
    b_out,
    ln2_gain,
    ln2_bias,
    w_router,
    w_in,
    b_in,
    w_back,
    b_back,
):
    images, length, width = tokens.shape
    tok_count = images * length
    labels = w_router.shape[1]
    local = labels // owners
    depth = w_in.shape[1]
    hidden = w_back.shape[1]
    cap = max(2, 5 * tok_count // (2 * labels))
    capp = -(-(cap + 3) // 16) * 16

    own = width // (groups * owners)
    sizes = {"group": groups, "expert": owners}
    outer, inner = bits_of(groups, owners)
    order_of_hops = [*outer, *inner]
    sibling = ("group", 0)
    core = own_bit(sibling).astype(jnp.int32).reshape(1)
    routes_one = [*inner, *outer]
    routes_two = [*inner[:-1], *outer, *inner[-1:]]
    vectors = (ln1_gain, ln1_bias, b_out, ln2_gain, ln2_bias)
    slices = pack(w_qkv, w_out, w_router, vectors, owners)
    near = inner[:-1]
    marks = (routes % local) * owners + routes // local
    marks = marks.swapaxes(1, 2)
    rows, cols = route(marks, order, labels, cap, capp)
    exchange = lambda block: lax.all_to_all(block, "expert", 0, 0, tiled=True)
    slices = [spread(block, [], near[:1], order_of_hops, sizes)[0] for block in slices]
    slices = [spread(block, near[:1], near[1:], order_of_hops, sizes) for block in slices]
    haves = [have for _, have in slices]
    rows, *slices = lax.optimization_barrier((rows, *[block for block, _ in slices]))
    cots = [exchange(dispatch(rows, cotangent, None, cap, capp, owners, [0]))]
    columns = [block.shape[-1] for block in slices]
    halves = []
    for turn in range(len(outer) + 1):
        moved = []
        for k, path in enumerate((routes_one, routes_two)):
            hop = path[len(near) + turn]
            block, haves[k] = spread(slices[k], haves[k], [hop], order_of_hops, sizes)
            moved.append(block)
        if turn == 0:
            w_in, w_back, rows, *moved = lax.optimization_barrier((w_in, w_back, rows, *moved))
            cots += [
                dispatch(rows, cotangent, None, cap, capp, owners, [l]) for l in range(1, local)
            ]
        slices = moved
    halves = [
        block.reshape(groups // 2, owners * own, count) for block, count in zip(slices, columns)
    ]
    biases = jnp.zeros((local, 16, width), f32)
    biases = biases.at[:, 0, :hidden].set(b_in).at[:, 1, :depth].set(b_back)
    wide = w_in.reshape(local, depth, -1, width).swapaxes(1, 2).reshape(local, -1, width)
    height = hidden + wide.shape[1] + 16
    experts = [
        jnp.concatenate([w_back[l], wide[l], biases[l]], axis=0).astype(bf16)
        for l in range(local)
    ]
    cots[0], cots[-1], *moved = lax.optimization_barrier((cots[0], cots[-1], *experts, *halves))
    experts, halves = moved[:local], moved[local:]
    cots[1:] = [exchange(block) for block in cots[1:]]
    experts = [lax.all_gather(block, "group") for block in experts]
    packed = [(half, swap(half, sibling, sizes)) for half in halves]
    qkv, mixed, lse, first, routed, gates, gate_rows = forward(core, tokens, marks, packed, labels)
    sent = [dispatch(rows, routed, gate_rows, cap, capp, owners, [l]) for l in range(local)]
    cots[-1], sent[0] = lax.optimization_barrier((cots[-1], sent[0]))
    sent[0] = exchange(sent[0])
    for l in range(1, local):
        sent[l - 1], sent[l] = lax.optimization_barrier((sent[l - 1], sent[l]))
        sent[l] = exchange(sent[l])
    joined, backs, shares = None, [], []
    for l in range(local):
        if l + 1 < local:
            joined, back, grads = expert(sent[l], cots[l], experts[l], joined, l, local, cap)
        else:
            joined, back, keep, away = parted_expert(
                core, sent[l], cots[l], experts[l], joined, l, local, cap
            )
        if l:
            back, backs[-1] = lax.optimization_barrier((back, backs[-1]))
        if l + 1 < local:
            back, sent[l + 1] = lax.optimization_barrier((back, sent[l + 1]))
            grads, sent[l + 1] = lax.optimization_barrier((grads, sent[l + 1]))
            shares.append([lax.psum_scatter(grads, "group", scatter_dimension=0)])
        else:
            if l:
                away, backs[-1] = lax.optimization_barrier((away, backs[-1]))
            total = keep.astype(f32) + swap(away, sibling, sizes).astype(f32)
            total = total.reshape(*[2] * len(outer), height, width)
            total = gather_back(total, outer[:-1], outer, sizes)
            bit = own_bit(outer[-1])
            stay = lax.dynamic_index_in_dim(total, bit, 0, keepdims=False).astype(bf16)
            away = lax.dynamic_index_in_dim(total, 1 - bit, 0, keepdims=False).astype(bf16)
        back = exchange(back)
        if l == local - 1:
            stay, away, back = lax.optimization_barrier((stay, away, back))
            shares.append([stay, swap(away, outer[-1], sizes)])
        backs.append(back)
    joined, backs[-1] = lax.optimization_barrier((joined, backs[-1]))
    joined = exchange(joined)
    grad_tokens, *halves = backward(
        core,
        tokens,
        cotangent,
        cols,
        qkv,
        mixed,
        early(cols, qkv, lse, backs[:-1], cap),
        first,
        routed,
        gates,
        cap,
        packed,
        backs[-1],
        local,
        labels,
    )
    sums = []
    for keep, away in (halves[:2], halves[2:]):
        sums.append((keep, swap(away, sibling, sizes)))
    left = [list(order_of_hops), list(order_of_hops)]
    paths = [routes_one[::-1], routes_two[::-1]]
    share = output = None
    for turn, hops in enumerate(zip(*paths)):
        lengths = [own << (len(have) - 1 - have.index(hop)) for have, hop in zip(left, hops)]
        sums = stage(sums, lengths, [own_bit(hop) for hop in hops])
        sums = [(stay, swap(away, hop, sizes)) for (stay, away), hop in zip(sums, hops)]
        for have, hop in zip(left, hops):
            have.remove(hop)
        if turn == 0:
            share = share_out(shares[0], None, 0, local, depth)
            beside = [shares[-1][1], *share]
        elif turn == 1:
            output = combine(first, cols, gates, joined, local)
            beside = [output]
        elif turn == 2:
            for l in range(1, local):
                share = share_out(shares[l], share, l, local, depth)
            beside = [*share, grad_tokens]
        else:
            continue
        one, two, *beside = lax.optimization_barrier((sums[0][1], sums[1][1], *beside))
        sums = [(sums[0][0], one), (sums[1][0], two)]
        if turn == 0:
            shares[-1][1], *share = beside
        elif turn == 1:
            output = beside[0]
        else:
            *share, grad_tokens = beside
    one, two = sums
    share_back, share_in, share_bias = share
    grad_qkv, grad_out, grad_router, *small = dense_out(one, two, labels, owners)
    return (
        output,
        grad_tokens,
        small[0].reshape(own),
        small[1].reshape(own),
        grad_qkv,
        grad_out,
        small[2].reshape(own),
        small[3].reshape(own),
        small[4].reshape(own),
        grad_router.T,
        share_in,
        share_bias[:, 0, :hidden],
        share_back,
        share_bias[:, 1, :depth],
    )


def solution(mesh):
    rows = P(BOTH, None)
    line = P(BOTH)
    tall = P(BOTH, None, None)
    deep = P("expert", "group", None)
    flat = P("expert", "group")
    groups, owners = mesh.shape["group"], mesh.shape["expert"]
    return jax.shard_map(
        functools.partial(per_device, groups, owners),
        mesh=mesh,
        in_specs=(
            tall,
            tall,
            tall,
            rows,
            line,
            line,
            rows,
            rows,
            line,
            line,
            line,
            rows,
            deep,
            flat,
            deep,
            flat,
        ),
        out_specs=(
            tall,
            tall,
            line,
            line,
            rows,
            rows,
            line,
            line,
            line,
            rows,
            deep,
            flat,
            deep,
            flat,
        ),
        check_vma=False,
    )
```

```python
import functools

import jax
import jax.numpy as jnp
from jax import lax
from jax.experimental import pallas as pl
from jax.experimental.layout import Layout, with_layout_constraint
from jax.experimental.pallas import tpu as pltpu
from jax.sharding import PartitionSpec as P

HEAD_DIM = 64
LANES = 128
VECTORS = 5
f32 = jnp.float32
bf16 = jnp.bfloat16
BOTH = ("group", "expert")


def dot(a, b):
    return lax.dot_general(a, b, (((1,), (0,)), ((), ())), preferred_element_type=f32)


def dot_nt(a, b):
    return lax.dot_general(a, b, (((1,), (1,)), ((), ())), preferred_element_type=f32)


def dot_tn(a, b):
    return lax.dot_general(a, b, (((0,), (0,)), ((), ())), preferred_element_type=f32)


def iota(shape, dim):
    return lax.broadcasted_iota(jnp.int32, shape, dim)


def params(mib, grid=1):
    return pltpu.CompilerParams(
        vmem_limit_bytes=mib * 1024 * 1024, dimension_semantics=("arbitrary",) * grid
    )


def three_parts(value):
    high = value.astype(bf16).astype(f32)
    rest = value - high
    mid = rest.astype(bf16).astype(f32)
    return high, mid, rest - mid


def norm_parts(rows):
    centre = rows - jnp.mean(rows, axis=-1, keepdims=True)
    spread = jnp.mean(centre * centre, axis=-1, keepdims=True)
    scale = lax.rsqrt(spread + 1e-06)
    return centre * scale, scale


def norm_backward(grad, unit, scale, gain):
    lead = grad * gain
    first = jnp.mean(lead, axis=-1, keepdims=True)
    second = jnp.mean(lead * unit, axis=-1, keepdims=True)
    return scale * (lead - first - unit * second)


def load_weights(step, core, parts, scratch, sems):
    copies = []
    for k, (own, other) in enumerate(parts):
        copies.append(
            [
                pltpu.make_async_copy(own, scratch[k].at[:, core], sems.at[2 * k]),
                pltpu.make_async_copy(other, scratch[k].at[:, 1 - core], sems.at[2 * k + 1]),
            ]
        )

    @pl.when(step == 0)
    def _():
        for pair in reversed(copies):
            for copy in pair:
                copy.start()

    return copies


def arrive(step, copies, turn=0):
    @pl.when(step == turn)
    def _():
        for copy in copies:
            copy.wait()


def pack_kernel(owners, qkv_ref, out_ref, router_ref, *refs):
    vec_refs, (one_ref, two_ref) = refs[:VECTORS], refs[VECTORS:]
    own, width = out_ref.shape
    labels = router_ref.shape[0]
    local = labels // owners
    cut = one_ref.shape[1]
    rest = 3 * width - cut
    one_ref[...] = qkv_ref[:, 0:cut].astype(bf16)
    two_ref[:, 0:rest] = qkv_ref[:, cut:].astype(bf16)
    two_ref[:, rest : rest + width] = out_ref[...].astype(bf16)
    lines = [
        router_ref[o * local + l : o * local + l + 1, :] for l in range(local) for o in range(owners)
    ]
    lines += [vec_ref[...] for vec_ref in vec_refs]
    lines.append(jnp.zeros((LANES - labels - VECTORS, own), f32))
    small = jnp.concatenate(lines, axis=0)
    if own < LANES:
        small = jnp.concatenate([small, jnp.zeros((LANES, LANES - own), f32)], axis=1)
    two_ref[:, rest + width :] = jnp.transpose(small)[0:own].astype(bf16)


def pack(w_qkv, w_out, w_router, vectors, owners):
    own, width = w_out.shape
    cut = 2 * width
    return pl.pallas_call(
        functools.partial(pack_kernel, owners),
        out_shape=[
            jax.ShapeDtypeStruct((own, cut), bf16),
            jax.ShapeDtypeStruct((own, 4 * width - cut + LANES), bf16),
        ],
        name="pack_weights",
    )(w_qkv, w_out, w_router.T, *[vector.reshape(1, own) for vector in vectors])


def dense_out_kernel(
    owners, one_ref, one_in, two_ref, two_in, qkv_ref, out_ref, router_ref, *vec_refs
):
    own, width = out_ref.shape
    labels = router_ref.shape[0]
    local = labels // owners
    one = one_ref[...] + one_in[...].astype(f32)
    two = two_ref[...] + two_in[...].astype(f32)
    cut = one.shape[1]
    rest = 3 * width - cut
    qkv_ref[:, 0:cut] = one
    qkv_ref[:, cut:] = two[:, 0:rest]
    out_ref[...] = two[:, rest : rest + width]
    small = two[:, rest + width :]
    if own < LANES:
        small = jnp.concatenate([small, jnp.zeros((LANES - own, LANES), f32)], axis=0)
    small = jnp.transpose(small)[:, 0:own]
    for o in range(owners):
        for l in range(local):
            at = o * local + l
            router_ref[at : at + 1, :] = small[l * owners + o : l * owners + o + 1]
    for k, vec_ref in enumerate(vec_refs):
        vec_ref[...] = small[labels + k : labels + k + 1]


def dense_out(one, two, labels, owners):
    own = one[0].shape[0]
    width = (one[0].shape[1] + two[0].shape[1] - LANES) // 4
    return pl.pallas_call(
        functools.partial(dense_out_kernel, owners),
        out_shape=[
            jax.ShapeDtypeStruct((own, 3 * width), f32),
            jax.ShapeDtypeStruct((own, width), f32),
            jax.ShapeDtypeStruct((labels, own), f32),
            *[jax.ShapeDtypeStruct((1, own), f32)] * VECTORS,
        ],
        name="dense_gradients",
    )(*one, *two)


def route_kernel(labels, cap, capp, routes_ref, order_ref, rows_ref, cols_ref):
    images, _, length = routes_ref.shape
    tok_count = order_ref.shape[1]
    order = order_ref[...]
    label = iota((labels, length), 0)
    perms, hots = [], []
    counts = jnp.zeros((2 * labels, tok_count), f32)
    for i in range(images):
        perm = jnp.where(iota((length, tok_count), 0) + i * length == order, 1.0, 0.0).astype(bf16)
        hot = jnp.concatenate(
            [
                jnp.where(label == routes_ref[i, 0:1, :], 1.0, 0.0),
                jnp.where(label == routes_ref[i, 1:2, :], 1.0, 0.0),
            ],
            axis=0,
        )
        perms.append(perm)
        hots.append(hot)
        counts = counts + dot(hot.astype(bf16), perm)
    earlier = jnp.where(
        iota((tok_count, tok_count), 0) < iota((tok_count, tok_count), 1), 1.0, 0.0
    ).astype(bf16)
    before = dot(counts.astype(bf16), earlier)
    total = jnp.sum(counts[:labels], axis=1, keepdims=True)
    before = jnp.concatenate([before[:labels], before[labels:] + total], axis=0)
    before = jnp.minimum(before, float(cap)).astype(bf16)
    same = jnp.where(iota((length, length), 0) == iota((length, length), 1), 1.0, 0.0).astype(bf16)
    for i in range(images):
        back = dot_nt(before, perms[i]) * hots[i]
        slot_one = jnp.sum(back[:labels], axis=0, keepdims=True)
        slot_two = jnp.sum(back[labels:], axis=0, keepdims=True)
        one = routes_ref[i, 0:1, :].astype(f32)
        two = routes_ref[i, 1:2, :].astype(f32)
        kept_one = jnp.where(slot_one < cap, one, -1.0)
        kept_two = jnp.where(slot_two < cap, two, -1.0)
        slot_one = jnp.where(slot_one < cap, slot_one, 0.0)
        slot_two = jnp.where(slot_two < cap, slot_two, 0.0)
        aim_one = (kept_one * capp + slot_one).astype(jnp.int32)
        aim_two = (kept_two * capp + slot_two).astype(jnp.int32)
        rows_ref[i] = jnp.concatenate(
            [aim_one, aim_two, jnp.zeros((6, length), jnp.int32)], axis=0
        )
        stacked = jnp.concatenate(
            [kept_one, slot_one, kept_two, slot_two, one, two, one, two], axis=0
        ).astype(bf16)
        turned = dot_nt(same, stacked)
        cols_ref[i] = jnp.concatenate(
            [
                turned[:, 0:1] * capp + turned[:, 1:2],
                turned[:, 2:3] * capp + turned[:, 3:4],
                turned[:, 4:5],
                turned[:, 5:6],
                turned[:, 4:8],
            ],
            axis=1,
        ).astype(jnp.int32)


def route(routes, order, labels, cap, capp):
    images, _, length = routes.shape
    return pl.pallas_call(
        functools.partial(route_kernel, labels, cap, capp),
        out_shape=(
            jax.ShapeDtypeStruct((images, 8, length), jnp.int32),
            jax.ShapeDtypeStruct((images, length, 8), jnp.int32),
        ),
        compiler_params=pltpu.CompilerParams(vmem_limit_bytes=40 * 1024 * 1024),
        name="route_tokens",
    )(routes, order)


def dispatch_kernel(cap, capp, owners, which, gated, joint, rows_ref, value_ref, *refs):
    images, length, width = value_ref.shape
    outs = refs[1:] if gated else refs
    span = owners * capp
    for place, l in enumerate(which):
        slots = iota((span, length), 0) + l * span
        total = None
        gate_rows = None
        for i in range(images):
            one = slots == rows_ref[i, 0:1, :]
            two = slots == rows_ref[i, 1:2, :]
            both = jnp.where(one | two, 1.0, 0.0).astype(bf16)
            part = dot(both, value_ref[i])
            total = part if total is None else total + part
            if gated:
                gates = refs[0][i]
                first = dot_nt(gates[0:8], jnp.where(one, 1.0, 0.0).astype(bf16))
                second = dot_nt(gates[8:16], jnp.where(two, 1.0, 0.0).astype(bf16))
                part = first + second
                gate_rows = part if gate_rows is None else gate_rows + part
        for o in range(owners):
            block = total[o * capp : (o + 1) * capp]
            if joint:
                outs[0][o, place * capp : (place + 1) * capp, :] = block.astype(bf16)
            else:
                outs[0][o] = block.astype(bf16)
            if gated:
                tail = block[capp - 16 :, 0:capp]
                spare = gate_rows[:, o * capp : (o + 1) * capp]
                line = iota((16, capp), 0) - (cap - (capp - 16))
                for k in range(3):
                    tail = jnp.where(line == k, spare[k : k + 1], tail)
                outs[0][o, capp - 16 :, 0:capp] = tail.astype(bf16)


def dispatch(rows, values, gates, cap, capp, owners, which):
    width = values.shape[2]
    joint = gates is None
    operands = (rows, values) if joint else (rows, values, gates)
    out_shape = jax.ShapeDtypeStruct((owners, len(which) * capp, width), bf16)
    return pl.pallas_call(
        functools.partial(dispatch_kernel, cap, capp, owners, tuple(which), not joint, joint),
        out_shape=out_shape,
        compiler_params=pltpu.CompilerParams(vmem_limit_bytes=40 * 1024 * 1024),
        name="fill_slots",
    )(*operands)


def forward_kernel(
    labels,
    core_ref,
    tokens_ref,
    routes_ref,
    one_own,
    one_other,
    two_own,
    two_other,
    qkv_ref,
    mixed_ref,
    lse_ref,
    first_ref,
    routed_ref,
    gates_ref,
    gate_rows_ref,
    total_ref,
    one_ref,
    two_ref,
    misc_ref,
    sems,
):
    _, length, width = tokens_ref.shape
    step = pl.program_id(0)
    parts = ((one_own, one_other), (two_own, two_other))
    copies = load_weights(step, core_ref[0], parts, (one_ref, two_ref), sems)
    cut = one_ref.shape[-1]
    rest = 3 * width - cut
    rows = tokens_ref[0].astype(f32)
    unit, _ = norm_parts(rows)
    arrive(step, copies[1])

    @pl.when(step == 0)
    def _():
        misc_ref[...] = jnp.transpose(two_ref[..., rest + width :].reshape(width, LANES))

    vec = [misc_ref[labels + k : labels + k + 1, :].astype(f32) for k in range(VECTORS)]
    normed = (unit * vec[0] + vec[1]).astype(bf16)
    arrive(step, copies[0])
    projected = jnp.concatenate(
        [
            dot(normed, one_ref[...].reshape(width, cut)).astype(bf16),
            dot(normed, two_ref[..., 0:rest].reshape(width, rest)).astype(bf16),
        ],
        axis=1,
    )
    qkv_ref[0] = projected
    lane = iota((length, LANES), 1)
    low_half = lane < HEAD_DIM
    pieces = []
    for pair in range(width // LANES):
        at = pair * LANES
        query = projected[:, at : at + LANES] * jnp.asarray(HEAD_DIM**-0.5, bf16)
        keys = projected[:, width + at : width + at + LANES]
        values = projected[:, 2 * width + at : 2 * width + at + LANES]
        mixed = None
        for half in range(2):
            own = low_half if half == 0 else jnp.logical_not(low_half)
            scores = dot_nt(jnp.where(own, query, jnp.zeros_like(query)), keys)
            top = jnp.max(scores, axis=-1, keepdims=True)
            shifted = jnp.exp(scores - top)
            total = jnp.sum(shifted, axis=-1, keepdims=True)
            head = 2 * pair + half
            total_ref[0:length, :] = jnp.where(
                lane == head, top + jnp.log(total), total_ref[0:length, :]
            )
            low = (shifted * (1.0 / total)).astype(bf16)
            part = dot(low, jnp.where(own, values, jnp.zeros_like(values)))
            mixed = part if mixed is None else mixed + part
        pieces.append(mixed.astype(bf16))
    mixed = jnp.concatenate(pieces, axis=1)
    mixed_ref[0] = mixed
    lse_ref[0] = jnp.transpose(total_ref[...])[0:16]
    w_out = two_ref[..., rest : rest + width].reshape(width, width)
    first = rows + dot(mixed, w_out) + vec[2]
    first_ref[0] = first
    unit, _ = norm_parts(first)
    routed = (unit * vec[3] + vec[4]).astype(bf16)
    routed_ref[0] = routed
    router = misc_ref[0:labels, :]
    logits = dot_nt(routed, router)
    shifted = jnp.exp(logits - jnp.max(logits, axis=1, keepdims=True))
    gates_ref[0] = shifted / jnp.sum(shifted, axis=1, keepdims=True)
    logits = dot_nt(router, routed)
    shifted = jnp.exp(logits - jnp.max(logits, axis=0, keepdims=True))
    gates = shifted / jnp.sum(shifted, axis=0, keepdims=True)
    label = iota((labels, length), 0)
    blank = jnp.zeros((5, length), f32)
    stack = []
    for k in range(2):
        chosen = jnp.where(label == routes_ref[0, k : k + 1, :], gates, 0.0)
        stack += [*three_parts(jnp.sum(chosen, axis=0, keepdims=True)), blank]
    gate_rows_ref[0] = jnp.concatenate(stack, axis=0).astype(bf16)


def weight_scratch(packed):
    return [
        pltpu.VMEM((part[0].shape[0], 2, *part[0].shape[1:]), part[0].dtype) for part in packed
    ]


def forward(core, tokens, routes, packed, labels):
    images, length, width = tokens.shape
    whole = lambda *tail: pl.BlockSpec((1, *tail), lambda i: (i, 0, 0))
    lanes = -(-length // LANES) * LANES
    return pl.pallas_call(
        functools.partial(forward_kernel, labels),
        grid=(images,),
        in_specs=[
            pl.BlockSpec(memory_space=pltpu.SMEM),
            whole(length, width),
            whole(2, length),
            *[pl.BlockSpec(memory_space=pl.ANY)] * 4,
        ],
        out_specs=[
            whole(length, 3 * width),
            whole(length, width),
            whole(16, lanes),
            whole(length, width),
            whole(length, width),
            whole(length, labels),
            whole(16, length),
        ],
        out_shape=[
            jax.ShapeDtypeStruct((images, length, 3 * width), bf16),
            jax.ShapeDtypeStruct((images, length, width), bf16),
            jax.ShapeDtypeStruct((images, 16, lanes), f32),
            jax.ShapeDtypeStruct((images, length, width), f32),
            jax.ShapeDtypeStruct((images, length, width), bf16),
            jax.ShapeDtypeStruct((images, length, labels), f32),
            jax.ShapeDtypeStruct((images, 16, length), bf16),
        ],
        scratch_shapes=[
            pltpu.VMEM((lanes, LANES), f32),
            *weight_scratch(packed),
            pltpu.VMEM((LANES, width), bf16),
            pltpu.SemaphoreType.DMA((4,)),
        ],
        compiler_params=params(40),
        cost_estimate=pl.CostEstimate(
            flops=16_000_000_000, bytes_accessed=20_000_000, transcendentals=2_000_000
        ),
        name="attention_forward",
    )(core, tokens, routes, *packed[0], *packed[1])


def expert_kernel(
    cap,
    rows_ref,
    cot_ref,
    win_ref,
    wback_ref,
    biases_ref,
    *refs,
):
    (
        out_ref,
        grad_ref,
        weights_ref,
        turned_ref,
        grad_out_ref,
        out_acc_ref,
        grad_acc_ref,
        active_ref,
        inner_ref,
        bias_ref,
        gwin_ref,
        gwback_ref,
        gbias_ref,
        sems,
    ) = refs[-14:]
    owners, capp, width = rows_ref.shape
    groups, depth, hidden = win_ref.shape
    spare = cap - (capp - 16)
    step = pl.program_id(0)
    last = pl.num_programs(0) - 1
    slot = lax.rem(step, 2)
    across = width // hidden

    def copies(step, slot):
        at = pl.multiple_of(hidden + lax.div(step, across) * depth, 16)
        start = pl.multiple_of(lax.rem(step, across) * hidden, LANES)
        return (
            pltpu.make_async_copy(
                gwback_ref.at[slot], weights_ref.at[step, pl.ds(0, hidden)], sems.at[0, slot]
            ),
            pltpu.make_async_copy(
                gwin_ref.at[slot],
                weights_ref.at[:, pl.ds(at, depth), pl.ds(start, hidden)],
                sems.at[1, slot],
            ),
        )

    @pl.when(step >= 2)
    def _():
        for copy in copies(step - 2, slot):
            copy.wait()

    @pl.when(step == 0)
    def _():
        summed = jnp.zeros((1, width), f32)
        for b in range(owners):
            tail = rows_ref[b, capp - 16 :, 0:capp].astype(f32)
            gate = (
                tail[spare : spare + 1] + tail[spare + 1 : spare + 2] + tail[spare + 2 : spare + 3]
            )
            gate = jnp.transpose(jnp.broadcast_to(gate, (LANES, capp)))[:, 0:1]
            part = (cot_ref[b].astype(f32) * gate).astype(bf16)
            grad_out_ref[b * capp : (b + 1) * capp, :] = part
            summed = summed + jnp.sum(part.astype(f32), axis=0, keepdims=True)
            turned_ref[:, b * capp : (b + 1) * capp] = jnp.transpose(rows_ref[b])
        bias_ref[...] = jnp.broadcast_to(summed, bias_ref.shape)
        out_acc_ref[...] = jnp.zeros_like(out_acc_ref)
        grad_acc_ref[...] = jnp.zeros_like(grad_acc_ref)

    first = win_ref[...].reshape(width, hidden)
    second = wback_ref[0]
    bias = biases_ref[step].astype(f32)[0:1, 0:hidden]
    bias_sum = jnp.zeros((1, hidden), f32)
    per = max(1, 256 // capp)
    k0 = 0.7978845608028654
    k1 = 0.044715
    for c in range(owners // per):
        at = slice(c * per * capp, (c + 1) * per * capp)
        block = rows_ref[c * per : (c + 1) * per].reshape(per * capp, width)
        inner = dot(block, first) + bias
        square = inner * inner
        curve = jnp.tanh(inner * (k0 + (k0 * k1) * square))
        half = 0.5 * (1.0 + curve)
        low = (inner * half).astype(bf16)
        active_ref[at, :] = low
        slope = half + (0.5 * inner) * (1.0 - curve * curve) * (k0 + (3.0 * k0 * k1) * square)
        grad_inner = dot_nt(grad_out_ref[at, :], second) * slope
        bias_sum = bias_sum + jnp.sum(grad_inner, axis=0, keepdims=True)
        grad_low = grad_inner.astype(bf16)
        inner_ref[at, :] = grad_low
        out_acc_ref[at, :] += dot(low, second)
        grad_acc_ref[at, :] += dot_nt(grad_low, first)
    gwin_ref[slot] = dot(turned_ref[...], inner_ref[...]).astype(bf16).reshape(win_ref.shape)
    gwback_ref[slot] = dot_tn(active_ref[...], grad_out_ref[...]).astype(bf16)
    row = iota((16, width), 0)
    if hidden < width:
        bias_sum = jnp.concatenate([bias_sum, jnp.zeros((1, width - hidden), f32)], axis=1)
    pad = jnp.where(row == 0, bias_sum, 0.0)
    gbias_ref[step] = pad.astype(bf16)
    for copy in copies(step, slot):
        copy.start()

    @pl.when(step == last)
    def _():
        for g in range(groups):
            part = bias_ref[0:1, g * depth : (g + 1) * depth]
            part = jnp.concatenate([part, jnp.zeros((1, width - depth), f32)], axis=1)
            block = gbias_ref[g].astype(f32)
            gbias_ref[g] = jnp.where(row == 1, part, block).astype(bf16)
        end = pltpu.make_async_copy(
            gbias_ref, weights_ref.at[:, pl.ds(weights_ref.shape[1] - 16, 16)], sems.at[2, 0]
        )
        end.start()
        whole = jnp.concatenate(
            [biases_ref[g].astype(f32)[1:2, 0:depth] for g in range(groups)], axis=1
        )
        for b in range(owners):
            at = slice(b * capp, (b + 1) * capp)
            result = (out_acc_ref[at, :] + whole).astype(bf16)
            out_ref[b] = result
            score = jnp.sum(result.astype(f32) * cot_ref[b].astype(f32), axis=1, keepdims=True)
            score = jnp.transpose(jnp.broadcast_to(score, (capp, LANES)))[0:1, :]
            back = grad_acc_ref[at, :]
            grad_ref[b] = back.astype(bf16)
            tail = back[capp - 16 :, 0:capp]
            line = iota((16, capp), 0) - spare
            for k, part in enumerate(three_parts(score)):
                tail = jnp.where(line == k, part, tail)
            grad_ref[b, capp - 16 :, 0:capp] = tail.astype(bf16)
        for back in range(2):
            for copy in copies(step - back, lax.rem(step + back, 2)):
                copy.wait()
        end.wait()


def expert(rows, cots, weights, outcomes, which, local, cap):
    owners, capp, width = rows.shape
    groups, height, _ = weights.shape
    depth = width // groups
    hidden = height - 16 - (height - 16) // 2
    across = width // hidden
    total = owners * capp
    full = lambda shape: pl.BlockSpec(shape, lambda j: (0,) * len(shape))
    anywhere = pl.BlockSpec(memory_space=pl.ANY)
    extra = [] if outcomes is None else [outcomes]
    return pl.pallas_call(
        functools.partial(expert_kernel, cap),
        grid=(groups,),
        in_specs=[
            full((owners, capp, width)),
            full((owners, capp, width)),
            pl.BlockSpec(
                (groups, depth, hidden), lambda j: (0, hidden // depth + j // across, j % across)
            ),
            pl.BlockSpec((1, hidden, width), lambda j: (j, 0, 0)),
            pl.BlockSpec((groups, 16, width), lambda j: (0, (height - 16) // 16, 0)),
            *[anywhere] * len(extra),
        ],
        out_specs=[
            pl.BlockSpec((owners, capp, width), lambda j: (0, which, 0)),
            full((owners, capp, width)),
            anywhere,
        ],
        out_shape=[
            jax.ShapeDtypeStruct((owners, local * capp, width), bf16),
            jax.ShapeDtypeStruct((owners, capp, width), bf16),
            jax.ShapeDtypeStruct(weights.shape, bf16),
        ],
        input_output_aliases={5: 0} if extra else {},
        scratch_shapes=[
            pltpu.VMEM((width, total), bf16),
            pltpu.VMEM((total, width), bf16),
            pltpu.VMEM((total, width), f32),
            pltpu.VMEM((total, width), f32),
            pltpu.VMEM((total, hidden), bf16),
            pltpu.VMEM((total, hidden), bf16),
            pltpu.VMEM((8, width), f32),
            pltpu.VMEM((2, groups, depth, hidden), bf16),
            pltpu.VMEM((2, hidden, width), bf16),
            pltpu.VMEM((groups, 16, width), bf16),
            pltpu.SemaphoreType.DMA((3, 2)),
        ],
        compiler_params=params(56),
        cost_estimate=pl.CostEstimate(
            flops=2 * 6 * total * width * hidden * groups,
            bytes_accessed=30_000_000,
            transcendentals=total * hidden * groups,
        ),
        name="expert_rows",
    )(rows, cots, weights, weights, weights, *extra)


def parted_kernel(
    cap,
    core_ref,
    rows_ref,
    cot_ref,
    win_ref,
    wback_ref,
    biases_ref,
    *refs,
):
    (
        out_ref,
        grad_ref,
        keep_ref,
        away_ref,
        turned_ref,
        grad_out_ref,
        out_acc_ref,
        grad_acc_ref,
        active_ref,
        inner_ref,
        bias_ref,
        gwin_ref,
        gwback_ref,
        gbias_ref,
        sems,
    ) = refs[-15:]
    owners, capp, width = rows_ref.shape
    groups, depth, hidden = win_ref.shape
    spare = cap - (capp - 16)
    step = pl.program_id(0)
    last = pl.num_programs(0) - 1
    slot = lax.rem(step, 2)
    across = width // hidden

    mine = core_ref[0]
    targets = ((keep_ref, mine, 0), (away_ref, 1 - mine, 1))

    def copies(step, slot):
        at = pl.multiple_of(hidden + lax.div(step, across) * depth, 16)
        start = pl.multiple_of(lax.rem(step, across) * hidden, LANES)
        return [
            pltpu.make_async_copy(
                gwin_ref.at[slot, :, part],
                target.at[:, pl.ds(at, depth), pl.ds(start, hidden)],
                sems.at[1 + k, slot],
            )
            for target, part, k in targets
        ]

    def whole_chunk(step, slot, act):
        for target, part, _ in targets:

            @pl.when(lax.rem(step, 2) == part)
            def _():
                act(
                    pltpu.make_async_copy(
                        gwback_ref.at[slot],
                        target.at[lax.div(step, 2), pl.ds(0, hidden)],
                        sems.at[0, slot],
                    )
                )

    def finish(step, slot):
        for copy in copies(step, slot):
            copy.wait()
        whole_chunk(step, slot, lambda copy: copy.wait())

    @pl.when(step >= 2)
    def _():
        finish(step - 2, slot)

    @pl.when(step == 0)
    def _():
        summed = jnp.zeros((1, width), f32)
        for b in range(owners):
            tail = rows_ref[b, capp - 16 :, 0:capp].astype(f32)
            gate = (
                tail[spare : spare + 1] + tail[spare + 1 : spare + 2] + tail[spare + 2 : spare + 3]
            )
            gate = jnp.transpose(jnp.broadcast_to(gate, (LANES, capp)))[:, 0:1]
            part = (cot_ref[b].astype(f32) * gate).astype(bf16)
            grad_out_ref[b * capp : (b + 1) * capp, :] = part
            summed = summed + jnp.sum(part.astype(f32), axis=0, keepdims=True)
            turned_ref[:, b * capp : (b + 1) * capp] = jnp.transpose(rows_ref[b])
        bias_ref[...] = jnp.broadcast_to(summed, bias_ref.shape)
        out_acc_ref[...] = jnp.zeros_like(out_acc_ref)
        grad_acc_ref[...] = jnp.zeros_like(grad_acc_ref)

    first = win_ref[...].reshape(width, hidden)
    second = wback_ref[0]
    bias = biases_ref[step].astype(f32)[0:1, 0:hidden]
    bias_sum = jnp.zeros((1, hidden), f32)
    per = max(1, 256 // capp)
    k0 = 0.7978845608028654
    k1 = 0.044715
    for c in range(owners // per):
        at = slice(c * per * capp, (c + 1) * per * capp)
        block = rows_ref[c * per : (c + 1) * per].reshape(per * capp, width)
        inner = dot(block, first) + bias
        square = inner * inner
        curve = jnp.tanh(inner * (k0 + (k0 * k1) * square))
        half = 0.5 * (1.0 + curve)
        low = (inner * half).astype(bf16)
        active_ref[at, :] = low
        slope = half + (0.5 * inner) * (1.0 - curve * curve) * (k0 + (3.0 * k0 * k1) * square)
        grad_inner = dot_nt(grad_out_ref[at, :], second) * slope
        bias_sum = bias_sum + jnp.sum(grad_inner, axis=0, keepdims=True)
        grad_low = grad_inner.astype(bf16)
        inner_ref[at, :] = grad_low
        out_acc_ref[at, :] += dot(low, second)
        grad_acc_ref[at, :] += dot_nt(grad_low, first)
    gwin_ref[slot] = dot(turned_ref[...], inner_ref[...]).astype(bf16).reshape(gwin_ref.shape[1:])
    gwback_ref[slot] = dot_tn(active_ref[...], grad_out_ref[...]).astype(bf16)
    row = iota((16, width), 0)
    if hidden < width:
        bias_sum = jnp.concatenate([bias_sum, jnp.zeros((1, width - hidden), f32)], axis=1)
    pad = jnp.where(row == 0, bias_sum, 0.0)
    gbias_ref[lax.div(step, 2), lax.rem(step, 2)] = pad.astype(bf16)
    for copy in copies(step, slot):
        copy.start()
    whole_chunk(step, slot, lambda copy: copy.start())

    @pl.when(step == last)
    def _():
        for g in range(groups):
            part = bias_ref[0:1, g * depth : (g + 1) * depth]
            part = jnp.concatenate([part, jnp.zeros((1, width - depth), f32)], axis=1)
            block = gbias_ref[g // 2, g % 2].astype(f32)
            gbias_ref[g // 2, g % 2] = jnp.where(row == 1, part, block).astype(bf16)
        ends = [
            pltpu.make_async_copy(
                gbias_ref.at[:, part],
                target.at[:, pl.ds(target.shape[1] - 16, 16)],
                sems.at[3, k],
            )
            for target, part, k in targets
        ]
        for end in ends:
            end.start()
        whole = jnp.concatenate(
            [biases_ref[g].astype(f32)[1:2, 0:depth] for g in range(groups)], axis=1
        )
        for b in range(owners):
            at = slice(b * capp, (b + 1) * capp)
            result = (out_acc_ref[at, :] + whole).astype(bf16)
            out_ref[b] = result
            score = jnp.sum(result.astype(f32) * cot_ref[b].astype(f32), axis=1, keepdims=True)
            score = jnp.transpose(jnp.broadcast_to(score, (capp, LANES)))[0:1, :]
            back = grad_acc_ref[at, :]
            grad_ref[b] = back.astype(bf16)
            tail = back[capp - 16 :, 0:capp]
            line = iota((16, capp), 0) - spare
            for k, part in enumerate(three_parts(score)):
                tail = jnp.where(line == k, part, tail)
            grad_ref[b, capp - 16 :, 0:capp] = tail.astype(bf16)
        finish(step - 1, 1 - slot)
        finish(step, slot)
        for end in ends:
            end.wait()


def parted_expert(core, rows, cots, weights, outcomes, which, local, cap):
    owners, capp, width = rows.shape
    groups, height, _ = weights.shape
    depth = width // groups
    hidden = height - 16 - (height - 16) // 2
    across = width // hidden
    total = owners * capp
    full = lambda shape: pl.BlockSpec(shape, lambda j: (0,) * len(shape))
    anywhere = pl.BlockSpec(memory_space=pl.ANY)
    extra = [] if outcomes is None else [outcomes]
    return pl.pallas_call(
        functools.partial(parted_kernel, cap),
        grid=(groups,),
        in_specs=[
            pl.BlockSpec(memory_space=pltpu.SMEM),
            full((owners, capp, width)),
            full((owners, capp, width)),
            pl.BlockSpec(
                (groups, depth, hidden), lambda j: (0, hidden // depth + j // across, j % across)
            ),
            pl.BlockSpec((1, hidden, width), lambda j: (j, 0, 0)),
            pl.BlockSpec((groups, 16, width), lambda j: (0, (height - 16) // 16, 0)),
            *[anywhere] * len(extra),
        ],
        out_specs=[
            pl.BlockSpec((owners, capp, width), lambda j: (0, which, 0)),
            full((owners, capp, width)),
            anywhere,
            anywhere,
        ],
        out_shape=[
            jax.ShapeDtypeStruct((owners, local * capp, width), bf16),
            jax.ShapeDtypeStruct((owners, capp, width), bf16),
            jax.ShapeDtypeStruct((groups // 2, height, width), bf16),
            jax.ShapeDtypeStruct((groups // 2, height, width), bf16),
        ],
        input_output_aliases={6: 0} if extra else {},
        scratch_shapes=[
            pltpu.VMEM((width, total), bf16),
            pltpu.VMEM((total, width), bf16),
            pltpu.VMEM((total, width), f32),
            pltpu.VMEM((total, width), f32),
            pltpu.VMEM((total, hidden), bf16),
            pltpu.VMEM((total, hidden), bf16),
            pltpu.VMEM((8, width), f32),
            pltpu.VMEM((2, groups // 2, 2, depth, hidden), bf16),
            pltpu.VMEM((2, hidden, width), bf16),
            pltpu.VMEM((groups // 2, 2, 16, width), bf16),
            pltpu.SemaphoreType.DMA((4, 2)),
        ],
        compiler_params=params(56),
        cost_estimate=pl.CostEstimate(
            flops=2 * 6 * total * width * hidden * groups,
            bytes_accessed=30_000_000,
            transcendentals=total * hidden * groups,
        ),
        name="expert_rows_parted",
    )(core, rows, cots, weights, weights, weights, *extra)


def share_kernel(addends, *refs):
    back_ref, in_ref, bias_ref = refs[-3:]
    value = [refs[k][...].astype(f32) for k in range(3)]
    if addends > 1:
        value = [part + refs[3 + k][...].astype(f32) for k, part in enumerate(value)]
    back_ref[0] = value[0]
    in_ref[0] = value[1]
    bias_ref[0] = value[2]


def share_out(shares, outs, which, local, depth):
    height, width = shares[0].shape
    hidden = (height - 16) // 2
    steps = hidden // depth
    extra = [] if outs is None else list(outs)
    operands = [share for share in shares for _ in range(3)]
    return pl.pallas_call(
        functools.partial(share_kernel, len(shares)),
        grid=(steps,),
        in_specs=[
            *[
                pl.BlockSpec((depth, width), lambda j: (j, 0)),
                pl.BlockSpec((depth, width), lambda j: (steps + j, 0)),
                pl.BlockSpec((16, width), lambda j: (2 * hidden // 16, 0)),
            ]
            * len(shares),
            *[pl.BlockSpec(memory_space=pl.ANY)] * len(extra),
        ],
        out_specs=[
            pl.BlockSpec((1, depth, width), lambda j: (which, j, 0)),
            pl.BlockSpec((1, depth, width), lambda j: (which, 0, j)),
            pl.BlockSpec((1, 16, width), lambda j: (which, 0, 0)),
        ],
        out_shape=[
            jax.ShapeDtypeStruct((local, hidden, width), f32),
            jax.ShapeDtypeStruct((local, depth, steps * width), f32),
            jax.ShapeDtypeStruct((local, 16, width), f32),
        ],
        input_output_aliases={len(operands) + k: k for k in range(len(extra))},
        compiler_params=params(32),
        name="expert_gradients",
    )(*operands, *extra)


def stage_kernel(own_rows, *refs):
    bits, refs = refs[: len(own_rows)], refs[len(own_rows) :]
    for k, rows in enumerate(own_rows):
        keep_ref, other_ref = refs[2 * k : 2 * k + 2]
        stay_ref, away_ref = refs[2 * (len(own_rows) + k) : 2 * (len(own_rows) + k) + 2]
        mine = bits[k][0] == 0
        total = keep_ref[...].astype(f32) + other_ref[...].astype(f32)
        if total.ndim == 3:
            pairs = [(total[0], total[1])]
        else:
            pairs = [
                (total[at : at + rows], total[at + rows : at + 2 * rows])
                for at in range(0, total.shape[0], 2 * rows)
            ]
        stay = [jnp.where(mine, one, two) for one, two in pairs]
        away = [jnp.where(mine, two, one) for one, two in pairs]
        stay_ref[...] = jnp.concatenate(stay, axis=0)
        away_ref[...] = jnp.concatenate(away, axis=0).astype(bf16)


def stage(pairs, lengths, bits):
    rows = [pair[0].size // pair[0].shape[-1] for pair in pairs]
    turns = [count // (2 * length) for count, length in zip(rows, lengths)]

    def fits(steps):
        return all(
            length % (16 * steps) == 0
            if turn == 1
            else turn % steps == 0 and length * (turn // steps) % 16 == 0
            for turn, length in zip(turns, lengths)
        )

    steps = next((count for count in (4, 2) if fits(count)), 1)
    operands, in_specs, out_specs, out_shape = [], [], [], []
    for pair, count, length, turn in zip(pairs, rows, lengths, turns):
        columns = pair[0].shape[-1]
        if turn == 1 and length % 16 == 0:
            shape, block = (2, length, columns), (2, length // steps, columns)
            where = lambda j: (0, j, 0)
        else:
            shape, block = (count, columns), (count // steps, columns)
            where = lambda j: (j, 0)
        operands += [part.reshape(shape) for part in pair]
        in_specs += [pl.BlockSpec(block, where)] * 2
        half = pl.BlockSpec((count // 2 // steps, columns), lambda j: (j, 0))
        out_specs += [half, half]
        out_shape += [jax.ShapeDtypeStruct((count // 2, columns), kind) for kind in (f32, bf16)]
    results = pl.pallas_call(
        functools.partial(stage_kernel, tuple(lengths)),
        grid=(steps,),
        in_specs=[*[pl.BlockSpec(memory_space=pltpu.SMEM)] * len(pairs), *in_specs],
        out_specs=out_specs,
        out_shape=out_shape,
        compiler_params=params(40),
        name="add_and_halve",
    )(*[bit.astype(jnp.int32).reshape(1) for bit in bits], *operands)
    return [results[2 * k : 2 * k + 2] for k in range(len(pairs))]


def add_to(ref, columns, value):
    shape = (*ref.shape[:-1], value.shape[-1])
    ref[..., columns] += value.reshape(shape)


def pick(which, cap, cols_ref, slots, score_ref):
    length = cols_ref.shape[1]
    owners, capp, width = slots[0].shape
    spare = cap - (capp - 16)
    span = owners * capp
    picked = gate_one = gate_two = None
    for k, l in enumerate(which):
        lane = iota((length, span), 1) + l * span
        one = jnp.where(lane == cols_ref[0, :, 0:1], 1.0, 0.0)
        two = jnp.where(lane == cols_ref[0, :, 1:2], 1.0, 0.0)
        part = dot((one + two).astype(bf16), slots[k][...].reshape(span, width))
        picked = part if picked is None else picked + part
        score = score_ref[:, k * span : (k + 1) * span]
        part_one = dot_nt(one.astype(bf16), score)
        part_two = dot_nt(two.astype(bf16), score)
        gate_one = part_one if gate_one is None else gate_one + part_one
        gate_two = part_two if gate_two is None else gate_two + part_two
    line = iota((length, 16), 1)
    mine = (line >= spare) & (line < spare + 3)
    gate_one = jnp.sum(jnp.where(mine, gate_one, 0.0), axis=1, keepdims=True)
    gate_two = jnp.sum(jnp.where(mine, gate_two, 0.0), axis=1, keepdims=True)
    return picked, gate_one, gate_two


def load_scores(slots, score_ref):
    owners, capp, _ = slots[0].shape
    span = owners * capp
    for k, block in enumerate(slots):
        for o in range(owners):
            at = k * span + o * capp
            score_ref[:, at : at + capp] = block[o, capp - 16 :, 0:capp]


def early_kernel(local, cap, cols_ref, qkv_ref, lse_ref, *refs):
    slots = refs[:local]
    picked_ref, gate_ref, probs_ref, score_ref = refs[local:]
    _, length, width = picked_ref.shape

    @pl.when(pl.program_id(0) == 0)
    def _():
        load_scores(slots, score_ref)

    picked, gate_one, gate_two = pick(range(local), cap, cols_ref, slots, score_ref)
    picked_ref[0] = picked
    lane = iota((length, 8), 1)
    gate_ref[0] = jnp.where(lane == 0, gate_one, jnp.where(lane == 1, gate_two, 0.0))
    low_half = iota((length, LANES), 1) < HEAD_DIM
    rate = jnp.asarray(HEAD_DIM**-0.5, bf16)
    for pair in range(width // LANES):
        at = pair * LANES
        query = qkv_ref[0, :, at : at + LANES] * rate
        keys = qkv_ref[0, :, width + at : width + at + LANES]
        for half in range(2):
            own = low_half if half == 0 else jnp.logical_not(low_half)
            head = 2 * pair + half
            scores = dot_nt(keys, jnp.where(own, query, jnp.zeros_like(query)))
            probs = jnp.exp(scores - lse_ref[0, head : head + 1, 0:length])
            probs_ref[0, head] = probs.astype(bf16)


def early(cols, qkv, lse, slots, cap):
    images, length, wide = qkv.shape
    width = wide // 3
    heads = width // HEAD_DIM
    owners, capp, _ = slots[0].shape
    whole = lambda *tail: pl.BlockSpec((1, *tail), lambda i: (i, *[0] * len(tail)))
    return pl.pallas_call(
        functools.partial(early_kernel, len(slots), cap),
        grid=(images,),
        in_specs=[
            whole(length, 8),
            whole(length, wide),
            whole(*lse.shape[1:]),
            *[pl.BlockSpec((owners, capp, width), lambda i: (0, 0, 0))] * len(slots),
        ],
        out_specs=[whole(length, width), whole(length, 8), whole(heads, length, length)],
        out_shape=[
            jax.ShapeDtypeStruct((images, length, width), f32),
            jax.ShapeDtypeStruct((images, length, 8), f32),
            jax.ShapeDtypeStruct((images, heads, length, length), bf16),
        ],
        scratch_shapes=[pltpu.VMEM((16, len(slots) * owners * capp), bf16)],
        compiler_params=params(40),
        cost_estimate=pl.CostEstimate(
            flops=10_000_000_000, bytes_accessed=20_000_000, transcendentals=2_000_000
        ),
        name="attention_again",
    )(cols, qkv, lse, *slots)


def backward_kernel(
    labels,
    local,
    cap,
    core_ref,
    tokens_ref,
    cot_ref,
    cols_ref,
    qkv_ref,
    mixed_ref,
    picked_ref,
    scores_ref,
    probs_ref,
    first_ref,
    routed_ref,
    gates_ref,
    one_own,
    one_other,
    two_own,
    two_other,
    *refs,
):
    slots = refs[:1]
    (
        grad_tokens_ref,
        keep_one_ref,
        send_one_ref,
        keep_two_ref,
        send_two_ref,
        grad_one_ref,
        grad_two_ref,
        stack_ref,
        vec_ref,
        score_ref,
        one_ref,
        two_ref,
        misc_ref,
        normed_ref,
        pair_ref,
        first_keep_ref,
        sems,
    ) = refs[1:]
    _, length, width = tokens_ref.shape
    step = pl.program_id(0)
    place = lax.rem(step, 2)
    pitch = normed_ref.shape[0] // 2
    parts = ((one_own, one_other), (two_own, two_other))
    copies = load_weights(step, core_ref[0], parts, (one_ref, two_ref), sems)
    cut = one_ref.shape[-1]
    rest = 3 * width - cut
    grad_cut = grad_one_ref.shape[-1]
    grad_rest = 3 * width - grad_cut

    @pl.when(step == 0)
    def _():
        grad_one_ref[...] = jnp.zeros_like(grad_one_ref)
        grad_two_ref[...] = jnp.zeros_like(grad_two_ref)
        vec_ref[...] = jnp.zeros_like(vec_ref)
        stack_ref[...] = jnp.zeros_like(stack_ref)
        normed_ref[...] = jnp.zeros_like(normed_ref)
        pair_ref[...] = jnp.zeros_like(pair_ref)
        load_scores(slots, score_ref)

    cot = cot_ref[0].astype(f32)
    route_one, route_two = cols_ref[0, :, 2:3], cols_ref[0, :, 3:4]
    picked, gate_one, gate_two = pick([local - 1], cap, cols_ref, slots, score_ref)
    picked = picked + picked_ref[0]
    gate_one = gate_one + scores_ref[0, :, 0:1]
    gate_two = gate_two + scores_ref[0, :, 1:2]
    arrive(step, copies[1])

    @pl.when(step == 0)
    def _():
        misc_ref[...] = jnp.transpose(two_ref[..., rest + width :].reshape(width, LANES))

    vec = [misc_ref[labels + k : labels + k + 1, :].astype(f32) for k in range(VECTORS)]
    label = iota((length, labels), 1)
    grad_gates = jnp.where(label == route_one, gate_one, 0.0) + jnp.where(
        label == route_two, gate_two, 0.0
    )
    gates = gates_ref[0]
    inner = jnp.sum(grad_gates * gates, axis=1, keepdims=True)
    grad_logits = (gates * (grad_gates - inner)).astype(bf16)
    router = misc_ref[0:labels, :]
    routed = routed_ref[0]
    stack_ref[0:labels, :] += dot_tn(grad_logits, routed)
    grad_routed = dot(grad_logits, router) + picked
    unit, scale = norm_parts(first_ref[0])
    vec_ref[3:4, :] += jnp.sum(grad_routed * unit, axis=0, keepdims=True)
    vec_ref[4:5, :] += jnp.sum(grad_routed, axis=0, keepdims=True)
    grad_first = cot + norm_backward(grad_routed, unit, scale, vec[3])
    vec_ref[2:3, :] += jnp.sum(grad_first, axis=0, keepdims=True)
    first_low = grad_first.astype(bf16)
    add_to(grad_two_ref, slice(grad_rest, grad_rest + width), dot_tn(mixed_ref[0], first_low))
    w_out = two_ref[..., rest : rest + width].reshape(width, width)
    grad_mixed = dot_nt(first_low, w_out).astype(bf16)
    low_half = iota((length, LANES), 1) < HEAD_DIM
    rate = jnp.asarray(HEAD_DIM**-0.5, bf16)
    grads = [[], [], []]
    for pair in range(width // LANES):
        at = pair * LANES
        query = qkv_ref[0, :, at : at + LANES] * rate
        keys = qkv_ref[0, :, width + at : width + at + LANES]
        values = qkv_ref[0, :, 2 * width + at : 2 * width + at + LANES]
        mix = grad_mixed[:, at : at + LANES]
        grad_q = grad_k = grad_v = None
        for half in range(2):
            own = low_half if half == 0 else jnp.logical_not(low_half)
            none = jnp.zeros_like(query)
            query_own = jnp.where(own, query, none)
            mix_own = jnp.where(own, mix, none)
            head = 2 * pair + half
            low = probs_ref[0, head]
            probs = low.astype(f32)
            grad_probs = dot_nt(values, mix_own)
            inner = jnp.sum(grad_probs * probs, axis=0, keepdims=True)
            scores = (probs * (grad_probs - inner)).astype(bf16)
            part = dot(low, mix_own)
            grad_v = part if grad_v is None else grad_v + part
            part = dot(scores, query_own)
            grad_k = part if grad_k is None else grad_k + part
            part = dot_tn(scores, jnp.where(own, keys, none))
            grad_q = part if grad_q is None else grad_q + part
        grads[0].append((grad_q * HEAD_DIM**-0.5).astype(bf16))
        grads[1].append(grad_k.astype(bf16))
        grads[2].append(grad_v.astype(bf16))
    grad_qkv = jnp.concatenate(grads[0] + grads[1] + grads[2], axis=1)
    pair_ref[pl.ds(pl.multiple_of(place * pitch, 16), length), :] = grad_qkv
    first_keep_ref[place] = grad_first
    arrive(step, copies[0], 1)

    @pl.when(place == 1)
    def _():
        units = []
        for k in range(2):
            unit, scale = norm_parts(tokens_ref[k].astype(f32))
            units.append((unit, scale))
            normed_ref[k * pitch : k * pitch + length, :] = (unit * vec[0] + vec[1]).astype(bf16)
        pair = pair_ref[...]
        normed = normed_ref[...]
        add_to(grad_one_ref, slice(None), dot_tn(normed, pair[:, 0:grad_cut]))
        add_to(grad_two_ref, slice(0, grad_rest), dot_tn(normed, pair[:, grad_cut:]))
        grad_both = dot_nt(pair[:, 0:cut], one_ref[...].reshape(width, cut))
        grad_both += dot_nt(pair[:, cut:], two_ref[..., 0:rest].reshape(width, rest))
        for k, (unit, scale) in enumerate(units):
            grad_normed = grad_both[k * pitch : k * pitch + length]
            vec_ref[0:1, :] += jnp.sum(grad_normed * unit, axis=0, keepdims=True)
            vec_ref[1:2, :] += jnp.sum(grad_normed, axis=0, keepdims=True)
            grad_tokens_ref[k] = first_keep_ref[k] + norm_backward(grad_normed, unit, scale, vec[0])

    @pl.when(step == pl.num_programs(0) - 1)
    def _():
        stack_ref[labels : labels + 8, :] = vec_ref[...]
        add_to(grad_two_ref, slice(grad_rest + width, None), jnp.transpose(stack_ref[...]))
        mine, other = core_ref[0], 1 - core_ref[0]
        keep_one_ref[...] = grad_one_ref[:, mine].astype(bf16)
        keep_two_ref[...] = grad_two_ref[:, mine].astype(bf16)
        send_one_ref[...] = grad_one_ref[:, other].astype(bf16)
        send_two_ref[...] = grad_two_ref[:, other].astype(bf16)


def backward(
    core, tokens, cot, cols, qkv, mixed, ahead, first, routed, gates, cap, packed, slots, local, labels
):
    images, length, width = tokens.shape
    owners, capp, _ = slots.shape
    whole = lambda *tail: pl.BlockSpec((1, *tail), lambda i: (i, *[0] * len(tail)))
    spare = sum(part[0].shape[2] for part in packed)
    grad_cut = 2 * width + width // 3 // LANES * LANES
    shapes = [(*packed[0][0].shape[:2], count) for count in (grad_cut, spare - grad_cut)]
    still = lambda shape: pl.BlockSpec(shape, lambda i: (0, 0, 0))
    assert images % 2 == 0
    both = pl.BlockSpec((2, length, width), lambda i: (i // 2, 0, 0))
    pitch = -(-length // 16) * 16
    return pl.pallas_call(
        functools.partial(backward_kernel, labels, local, cap),
        grid=(images,),
        in_specs=[
            pl.BlockSpec(memory_space=pltpu.SMEM),
            both,
            whole(length, width),
            whole(length, 8),
            whole(length, 3 * width),
            whole(length, width),
            *[whole(*part.shape[1:]) for part in ahead],
            whole(length, width),
            whole(length, width),
            whole(length, labels),
            *[pl.BlockSpec(memory_space=pl.ANY)] * 4,
            pl.BlockSpec((owners, capp, width), lambda i: (0, 0, 0)),
        ],
        out_specs=[
            both,
            *[still(shape) for shape in shapes for _ in range(2)],
        ],
        out_shape=[
            jax.ShapeDtypeStruct((images, length, width), f32),
            *[jax.ShapeDtypeStruct(shape, bf16) for shape in shapes for _ in range(2)],
        ],
        scratch_shapes=[
            *[pltpu.VMEM((shape[0], 2, *shape[1:]), f32) for shape in shapes],
            pltpu.VMEM((LANES, width), f32),
            pltpu.VMEM((8, width), f32),
            pltpu.VMEM((16, owners * capp), bf16),
            *weight_scratch(packed),
            pltpu.VMEM((LANES, width), bf16),
            pltpu.VMEM((2 * pitch, width), bf16),
            pltpu.VMEM((2 * pitch, 3 * width), bf16),
            pltpu.VMEM((2, length, width), f32),
            pltpu.SemaphoreType.DMA((4,)),
        ],
        compiler_params=params(60),
        cost_estimate=pl.CostEstimate(
            flops=40_000_000_000, bytes_accessed=40_000_000, transcendentals=2_000_000
        ),
        name="attention_backward",
    )(
        core,
        tokens,
        cot,
        cols,
        qkv,
        mixed,
        *ahead,
        first,
        routed,
        gates,
        *packed[0],
        *packed[1],
        slots,
    )


def output_kernel(labels, local, first_ref, cols_ref, gates_ref, slots_ref, out_ref):
    _, length, width = first_ref.shape
    owners, capp, _ = slots_ref.shape
    capp = capp // local
    span = owners * capp
    label = iota((length, labels), 1)
    total = first_ref[0]
    for k in range(2):
        picked = None
        for l in range(local):
            lane = iota((length, span), 1) + l * span
            hot = jnp.where(lane == cols_ref[0, :, k : k + 1], 1.0, 0.0).astype(bf16)
            part = dot(hot, slots_ref[:, l * capp : (l + 1) * capp, :].reshape(span, width))
            picked = part if picked is None else picked + part
        chosen = jnp.where(label == cols_ref[0, :, k + 2 : k + 3], gates_ref[0], 0.0)
        total = total + jnp.sum(chosen, axis=1, keepdims=True) * picked
    out_ref[0] = total.astype(bf16)


def combine(first, cols, gates, slots, local):
    images, length, width = first.shape
    labels = gates.shape[2]
    whole = lambda *tail: pl.BlockSpec((1, *tail), lambda i: (i, 0, 0))
    return pl.pallas_call(
        functools.partial(output_kernel, labels, local),
        grid=(images,),
        in_specs=[
            whole(length, width),
            whole(length, 8),
            whole(length, labels),
            pl.BlockSpec(slots.shape, lambda i: (0, 0, 0)),
        ],
        out_specs=whole(length, width),
        out_shape=jax.ShapeDtypeStruct((images, length, width), bf16),
        compiler_params=params(40),
        name="combine_outputs",
    )(first, cols, gates, slots)


def bits_of(groups, owners):
    outer = [("group", k) for k in reversed(range(1, groups.bit_length() - 1))]
    inner = [("expert", k) for k in reversed(range(owners.bit_length() - 1))]
    return outer, inner


def swap(block, hop, sizes):
    axis, bit = hop
    return lax.ppermute(block, axis, [(d, d ^ (1 << bit)) for d in range(sizes[axis])])


def own_bit(hop):
    return lax.rem(lax.axis_index(hop[0]) >> hop[1], 2)


def spread(block, have, hops, order, sizes):
    for hop in hops:
        other = swap(block, hop, sizes)
        have = sorted([*have, hop], key=order.index)
        at = have.index(hop)
        mine = own_bit(hop) == 0
        block = jnp.stack(
            [jnp.where(mine, block, other), jnp.where(mine, other, block)], axis=at
        )
    return block, have


def halve(total, hop, at, sizes):
    bit = own_bit(hop)
    away = lax.dynamic_index_in_dim(total, 1 - bit, at, keepdims=False)
    stay = lax.dynamic_index_in_dim(total, bit, at, keepdims=False)
    return stay, swap(away.astype(bf16), hop, sizes)


def gather_back(total, hops, order, sizes):
    have = list(order)
    for hop in hops:
        at = have.index(hop)
        have.remove(hop)
        stay, other = halve(total, hop, at, sizes)
        total = stay + other.astype(f32)
    return total


def per_device(
    groups,
    owners,
    tokens,
    cotangent,
    routes,
    order,
    ln1_gain,
    ln1_bias,
    w_qkv,
    w_out,
    b_out,
    ln2_gain,
    ln2_bias,
    w_router,
    w_in,
    b_in,
    w_back,
    b_back,
):
    images, length, width = tokens.shape
    tok_count = images * length
    labels = w_router.shape[1]
    local = labels // owners
    depth = w_in.shape[1]
    hidden = w_back.shape[1]
    cap = max(2, 5 * tok_count // (2 * labels))
    capp = -(-(cap + 3) // 16) * 16

    own = width // (groups * owners)
    sizes = {"group": groups, "expert": owners}
    outer, inner = bits_of(groups, owners)
    order_of_hops = [*outer, *inner]
    sibling = ("group", 0)
    core = own_bit(sibling).astype(jnp.int32).reshape(1)
    routes_one = [*inner, *outer]
    routes_two = [*inner[:-1], *outer, *inner[-1:]]
    vectors = (ln1_gain, ln1_bias, b_out, ln2_gain, ln2_bias)
    slices = pack(w_qkv, w_out, w_router, vectors, owners)
    near = inner[:-1]
    marks = (routes % local) * owners + routes // local
    marks = marks.swapaxes(1, 2)
    rows, cols = route(marks, order, labels, cap, capp)
    exchange = lambda block: lax.all_to_all(block, "expert", 0, 0, tiled=True)
    slices = [spread(block, [], near[:1], order_of_hops, sizes)[0] for block in slices]
    slices = [spread(block, near[:1], near[1:], order_of_hops, sizes) for block in slices]
    haves = [have for _, have in slices]
    rows, *slices = lax.optimization_barrier((rows, *[block for block, _ in slices]))
    cots = [exchange(dispatch(rows, cotangent, None, cap, capp, owners, [0]))]
    columns = [block.shape[-1] for block in slices]
    halves = []
    for turn in range(len(outer) + 1):
        moved = []
        for k, path in enumerate((routes_one, routes_two)):
            hop = path[len(near) + turn]
            block, haves[k] = spread(slices[k], haves[k], [hop], order_of_hops, sizes)
            moved.append(block)
        if turn == 0:
            w_in, w_back, rows, *moved = lax.optimization_barrier((w_in, w_back, rows, *moved))
            cots += [
                dispatch(rows, cotangent, None, cap, capp, owners, [l]) for l in range(1, local)
            ]
        slices = moved
    halves = [
        block.reshape(groups // 2, owners * own, count) for block, count in zip(slices, columns)
    ]
    biases = jnp.zeros((local, 16, width), f32)
    biases = biases.at[:, 0, :hidden].set(b_in).at[:, 1, :depth].set(b_back)
    wide = w_in.reshape(local, depth, -1, width).swapaxes(1, 2).reshape(local, -1, width)
    height = hidden + wide.shape[1] + 16
    experts = [
        jnp.concatenate([w_back[l], wide[l], biases[l]], axis=0).astype(bf16)
        for l in range(local)
    ]
    cots[0], cots[-1], *moved = lax.optimization_barrier((cots[0], cots[-1], *experts, *halves))
    experts, halves = moved[:local], moved[local:]
    cots[1:] = [exchange(block) for block in cots[1:]]
    experts = [lax.all_gather(block, "group") for block in experts]
    packed = [(half, swap(half, sibling, sizes)) for half in halves]
    qkv, mixed, lse, first, routed, gates, gate_rows = forward(core, tokens, marks, packed, labels)
    sent = [dispatch(rows, routed, gate_rows, cap, capp, owners, [l]) for l in range(local)]
    cots[-1], sent[0] = lax.optimization_barrier((cots[-1], sent[0]))
    sent[0] = exchange(sent[0])
    for l in range(1, local):
        sent[l - 1], sent[l] = lax.optimization_barrier((sent[l - 1], sent[l]))
        sent[l] = exchange(sent[l])
    joined, backs, shares = None, [], []
    for l in range(local):
        if l + 1 < local:
            joined, back, grads = expert(sent[l], cots[l], experts[l], joined, l, local, cap)
        else:
            joined, back, keep, away = parted_expert(
                core, sent[l], cots[l], experts[l], joined, l, local, cap
            )
        if l:
            back, backs[-1] = lax.optimization_barrier((back, backs[-1]))
        if l + 1 < local:
            back, sent[l + 1] = lax.optimization_barrier((back, sent[l + 1]))
            grads, sent[l + 1] = lax.optimization_barrier((grads, sent[l + 1]))
            shares.append([lax.psum_scatter(grads, "group", scatter_dimension=0)])
        else:
            if l:
                away, backs[-1] = lax.optimization_barrier((away, backs[-1]))
            total = keep.astype(f32) + swap(away, sibling, sizes).astype(f32)
            total = total.reshape(*[2] * len(outer), height, width)
            total = gather_back(total, outer[:-1], outer, sizes)
            bit = own_bit(outer[-1])
            stay = lax.dynamic_index_in_dim(total, bit, 0, keepdims=False).astype(bf16)
            away = lax.dynamic_index_in_dim(total, 1 - bit, 0, keepdims=False).astype(bf16)
        back = exchange(back)
        if l == local - 1:
            stay, away, back = lax.optimization_barrier((stay, away, back))
            shares.append([stay, swap(away, outer[-1], sizes)])
        backs.append(back)
    joined, backs[-1] = lax.optimization_barrier((joined, backs[-1]))
    joined = exchange(joined)
    grad_tokens, *halves = backward(
        core,
        tokens,
        cotangent,
        cols,
        qkv,
        mixed,
        early(cols, qkv, lse, backs[:-1], cap),
        first,
        routed,
        gates,
        cap,
        packed,
        backs[-1],
        local,
        labels,
    )
    sums = []
    for keep, away in (halves[:2], halves[2:]):
        sums.append((keep, swap(away, sibling, sizes)))
    left = [list(order_of_hops), list(order_of_hops)]
    paths = [routes_one[::-1], routes_two[::-1]]
    share = output = None
    for turn, hops in enumerate(zip(*paths)):
        lengths = [own << (len(have) - 1 - have.index(hop)) for have, hop in zip(left, hops)]
        sums = stage(sums, lengths, [own_bit(hop) for hop in hops])
        sums = [(stay, swap(away, hop, sizes)) for (stay, away), hop in zip(sums, hops)]
        for have, hop in zip(left, hops):
            have.remove(hop)
        if turn == 0:
            for l in range(local):
                share = share_out(shares[l], share, l, local, depth)
            grad_tokens = with_layout_constraint(grad_tokens, Layout(major_to_minor=(1, 0, 2)))
            beside = [grad_tokens, *share]
        elif turn == 1:
            output = combine(first, cols, gates, joined, local)
            beside = [output]
        else:
            continue
        one, two, *beside = lax.optimization_barrier((sums[0][1], sums[1][1], *beside))
        sums = [(sums[0][0], one), (sums[1][0], two)]
        if turn == 0:
            grad_tokens, *share = beside
        else:
            output = beside[0]
    one, two = sums
    share_back, share_in, share_bias = share
    grad_qkv, grad_out, grad_router, *small = dense_out(one, two, labels, owners)
    return (
        output,
        grad_tokens,
        small[0].reshape(own),
        small[1].reshape(own),
        grad_qkv,
        grad_out,
        small[2].reshape(own),
        small[3].reshape(own),
        small[4].reshape(own),
        grad_router.T,
        share_in,
        share_bias[:, 0, :hidden],
        share_back,
        share_bias[:, 1, :depth],
    )


def solution(mesh):
    rows = P(BOTH, None)
    line = P(BOTH)
    tall = P(BOTH, None, None)
    deep = P("expert", "group", None)
    flat = P("expert", "group")
    groups, owners = mesh.shape["group"], mesh.shape["expert"]
    return jax.shard_map(
        functools.partial(per_device, groups, owners),
        mesh=mesh,
        in_specs=(
            tall,
            tall,
            tall,
            rows,
            line,
            line,
            rows,
            rows,
            line,
            line,
            line,
            rows,
            deep,
            flat,
            deep,
            flat,
        ),
        out_specs=(
            tall,
            tall,
            line,
            line,
            rows,
            rows,
            line,
            line,
            line,
            rows,
            deep,
            flat,
            deep,
            flat,
        ),
        check_vma=False,
    )
```

```python
import functools

import jax
import jax.numpy as jnp
from jax import lax
from jax.experimental import pallas as pl
from jax.experimental.layout import Layout, with_layout_constraint
from jax.experimental.pallas import tpu as pltpu
from jax.sharding import PartitionSpec as P

HEAD_DIM = 64
LANES = 128
VECTORS = 5
f32 = jnp.float32
bf16 = jnp.bfloat16
BOTH = ("group", "expert")


def dot(a, b):
    return lax.dot_general(a, b, (((1,), (0,)), ((), ())), preferred_element_type=f32)


def dot_nt(a, b):
    return lax.dot_general(a, b, (((1,), (1,)), ((), ())), preferred_element_type=f32)


def dot_tn(a, b):
    return lax.dot_general(a, b, (((0,), (0,)), ((), ())), preferred_element_type=f32)


def iota(shape, dim):
    return lax.broadcasted_iota(jnp.int32, shape, dim)


def params(mib, grid=1):
    return pltpu.CompilerParams(
        vmem_limit_bytes=mib * 1024 * 1024, dimension_semantics=("arbitrary",) * grid
    )


def three_parts(value):
    high = value.astype(bf16).astype(f32)
    rest = value - high
    mid = rest.astype(bf16).astype(f32)
    return high, mid, rest - mid


def norm_parts(rows):
    centre = rows - jnp.mean(rows, axis=-1, keepdims=True)
    spread = jnp.mean(centre * centre, axis=-1, keepdims=True)
    scale = lax.rsqrt(spread + 1e-06)
    return centre * scale, scale


def norm_backward(grad, unit, scale, gain):
    lead = grad * gain
    first = jnp.mean(lead, axis=-1, keepdims=True)
    second = jnp.mean(lead * unit, axis=-1, keepdims=True)
    return scale * (lead - first - unit * second)


def load_weights(step, core, parts, scratch, sems):
    copies = []
    for k, (own, other) in enumerate(parts):
        copies.append(
            [
                pltpu.make_async_copy(own, scratch[k].at[:, core], sems.at[2 * k]),
                pltpu.make_async_copy(other, scratch[k].at[:, 1 - core], sems.at[2 * k + 1]),
            ]
        )

    @pl.when(step == 0)
    def _():
        for pair in reversed(copies):
            for copy in pair:
                copy.start()

    return copies


def arrive(step, copies, turn=0):
    @pl.when(step == turn)
    def _():
        for copy in copies:
            copy.wait()


def pack_kernel(owners, qkv_ref, out_ref, router_ref, *refs):
    vec_refs, (one_ref, two_ref) = refs[:VECTORS], refs[VECTORS:]
    own, width = out_ref.shape
    labels = router_ref.shape[0]
    local = labels // owners
    cut = one_ref.shape[1]
    rest = 3 * width - cut
    one_ref[...] = qkv_ref[:, 0:cut].astype(bf16)
    two_ref[:, 0:rest] = qkv_ref[:, cut:].astype(bf16)
    two_ref[:, rest : rest + width] = out_ref[...].astype(bf16)
    lines = [
        router_ref[o * local + l : o * local + l + 1, :] for l in range(local) for o in range(owners)
    ]
    lines += [vec_ref[...] for vec_ref in vec_refs]
    lines.append(jnp.zeros((LANES - labels - VECTORS, own), f32))
    small = jnp.concatenate(lines, axis=0)
    if own < LANES:
        small = jnp.concatenate([small, jnp.zeros((LANES, LANES - own), f32)], axis=1)
    two_ref[:, rest + width :] = jnp.transpose(small)[0:own].astype(bf16)


def pack(w_qkv, w_out, w_router, vectors, owners):
    own, width = w_out.shape
    cut = 2 * width
    return pl.pallas_call(
        functools.partial(pack_kernel, owners),
        out_shape=[
            jax.ShapeDtypeStruct((own, cut), bf16),
            jax.ShapeDtypeStruct((own, 4 * width - cut + LANES), bf16),
        ],
        name="pack_weights",
    )(w_qkv, w_out, w_router.T, *[vector.reshape(1, own) for vector in vectors])


def dense_out_kernel(
    owners, one_ref, one_in, two_ref, two_in, qkv_ref, out_ref, router_ref, *vec_refs
):
    own, width = out_ref.shape
    labels = router_ref.shape[0]
    local = labels // owners
    one = one_ref[...] + one_in[...].astype(f32)
    two = two_ref[...] + two_in[...].astype(f32)
    cut = one.shape[1]
    rest = 3 * width - cut
    qkv_ref[:, 0:cut] = one
    qkv_ref[:, cut:] = two[:, 0:rest]
    out_ref[...] = two[:, rest : rest + width]
    small = two[:, rest + width :]
    if own < LANES:
        small = jnp.concatenate([small, jnp.zeros((LANES - own, LANES), f32)], axis=0)
    small = jnp.transpose(small)[:, 0:own]
    for o in range(owners):
        for l in range(local):
            at = o * local + l
            router_ref[at : at + 1, :] = small[l * owners + o : l * owners + o + 1]
    for k, vec_ref in enumerate(vec_refs):
        vec_ref[...] = small[labels + k : labels + k + 1]


def dense_out(one, two, labels, owners):
    own = one[0].shape[0]
    width = (one[0].shape[1] + two[0].shape[1] - LANES) // 4
    return pl.pallas_call(
        functools.partial(dense_out_kernel, owners),
        out_shape=[
            jax.ShapeDtypeStruct((own, 3 * width), f32),
            jax.ShapeDtypeStruct((own, width), f32),
            jax.ShapeDtypeStruct((labels, own), f32),
            *[jax.ShapeDtypeStruct((1, own), f32)] * VECTORS,
        ],
        name="dense_gradients",
    )(*one, *two)


def route_kernel(labels, cap, capp, routes_ref, order_ref, rows_ref, cols_ref):
    images, _, length = routes_ref.shape
    tok_count = order_ref.shape[1]
    order = order_ref[...]
    label = iota((labels, length), 0)
    perms, hots = [], []
    counts = jnp.zeros((2 * labels, tok_count), f32)
    for i in range(images):
        perm = jnp.where(iota((length, tok_count), 0) + i * length == order, 1.0, 0.0).astype(bf16)
        hot = jnp.concatenate(
            [
                jnp.where(label == routes_ref[i, 0:1, :], 1.0, 0.0),
                jnp.where(label == routes_ref[i, 1:2, :], 1.0, 0.0),
            ],
            axis=0,
        )
        perms.append(perm)
        hots.append(hot)
        counts = counts + dot(hot.astype(bf16), perm)
    earlier = jnp.where(
        iota((tok_count, tok_count), 0) < iota((tok_count, tok_count), 1), 1.0, 0.0
    ).astype(bf16)
    before = dot(counts.astype(bf16), earlier)
    total = jnp.sum(counts[:labels], axis=1, keepdims=True)
    before = jnp.concatenate([before[:labels], before[labels:] + total], axis=0)
    before = jnp.minimum(before, float(cap)).astype(bf16)
    same = jnp.where(iota((length, length), 0) == iota((length, length), 1), 1.0, 0.0).astype(bf16)
    for i in range(images):
        back = dot_nt(before, perms[i]) * hots[i]
        slot_one = jnp.sum(back[:labels], axis=0, keepdims=True)
        slot_two = jnp.sum(back[labels:], axis=0, keepdims=True)
        one = routes_ref[i, 0:1, :].astype(f32)
        two = routes_ref[i, 1:2, :].astype(f32)
        kept_one = jnp.where(slot_one < cap, one, -1.0)
        kept_two = jnp.where(slot_two < cap, two, -1.0)
        slot_one = jnp.where(slot_one < cap, slot_one, 0.0)
        slot_two = jnp.where(slot_two < cap, slot_two, 0.0)
        aim_one = (kept_one * capp + slot_one).astype(jnp.int32)
        aim_two = (kept_two * capp + slot_two).astype(jnp.int32)
        rows_ref[i] = jnp.concatenate(
            [aim_one, aim_two, jnp.zeros((6, length), jnp.int32)], axis=0
        )
        stacked = jnp.concatenate(
            [kept_one, slot_one, kept_two, slot_two, one, two, one, two], axis=0
        ).astype(bf16)
        turned = dot_nt(same, stacked)
        cols_ref[i] = jnp.concatenate(
            [
                turned[:, 0:1] * capp + turned[:, 1:2],
                turned[:, 2:3] * capp + turned[:, 3:4],
                turned[:, 4:5],
                turned[:, 5:6],
                turned[:, 4:8],
            ],
            axis=1,
        ).astype(jnp.int32)


def route(routes, order, labels, cap, capp):
    images, _, length = routes.shape
    return pl.pallas_call(
        functools.partial(route_kernel, labels, cap, capp),
        out_shape=(
            jax.ShapeDtypeStruct((images, 8, length), jnp.int32),
            jax.ShapeDtypeStruct((images, length, 8), jnp.int32),
        ),
        compiler_params=pltpu.CompilerParams(vmem_limit_bytes=40 * 1024 * 1024),
        name="route_tokens",
    )(routes, order)


def dispatch_kernel(cap, capp, owners, which, gated, joint, rows_ref, value_ref, *refs):
    images, length, width = value_ref.shape
    outs = refs[1:] if gated else refs
    span = owners * capp
    for place, l in enumerate(which):
        slots = iota((span, length), 0) + l * span
        total = None
        gate_rows = None
        for i in range(images):
            one = slots == rows_ref[i, 0:1, :]
            two = slots == rows_ref[i, 1:2, :]
            both = jnp.where(one | two, 1.0, 0.0).astype(bf16)
            part = dot(both, value_ref[i])
            total = part if total is None else total + part
            if gated:
                gates = refs[0][i]
                first = dot_nt(gates[0:8], jnp.where(one, 1.0, 0.0).astype(bf16))
                second = dot_nt(gates[8:16], jnp.where(two, 1.0, 0.0).astype(bf16))
                part = first + second
                gate_rows = part if gate_rows is None else gate_rows + part
        for o in range(owners):
            block = total[o * capp : (o + 1) * capp]
            if joint:
                outs[0][o, place * capp : (place + 1) * capp, :] = block.astype(bf16)
            else:
                outs[0][o] = block.astype(bf16)
            if gated:
                tail = block[capp - 16 :, 0:capp]
                spare = gate_rows[:, o * capp : (o + 1) * capp]
                line = iota((16, capp), 0) - (cap - (capp - 16))
                for k in range(3):
                    tail = jnp.where(line == k, spare[k : k + 1], tail)
                outs[0][o, capp - 16 :, 0:capp] = tail.astype(bf16)


def dispatch(rows, values, gates, cap, capp, owners, which):
    width = values.shape[2]
    joint = gates is None
    operands = (rows, values) if joint else (rows, values, gates)
    out_shape = jax.ShapeDtypeStruct((owners, len(which) * capp, width), bf16)
    return pl.pallas_call(
        functools.partial(dispatch_kernel, cap, capp, owners, tuple(which), not joint, joint),
        out_shape=out_shape,
        compiler_params=pltpu.CompilerParams(vmem_limit_bytes=40 * 1024 * 1024),
        name="fill_slots",
    )(*operands)


def forward_kernel(
    labels,
    core_ref,
    tokens_ref,
    routes_ref,
    one_own,
    one_other,
    two_own,
    two_other,
    qkv_ref,
    mixed_ref,
    lse_ref,
    first_ref,
    routed_ref,
    gates_ref,
    gate_rows_ref,
    total_ref,
    one_ref,
    two_ref,
    misc_ref,
    sems,
):
    _, length, width = tokens_ref.shape
    step = pl.program_id(0)
    parts = ((one_own, one_other), (two_own, two_other))
    copies = load_weights(step, core_ref[0], parts, (one_ref, two_ref), sems)
    cut = one_ref.shape[-1]
    rest = 3 * width - cut
    rows = tokens_ref[0].astype(f32)
    unit, _ = norm_parts(rows)
    arrive(step, copies[1])

    @pl.when(step == 0)
    def _():
        misc_ref[...] = jnp.transpose(two_ref[..., rest + width :].reshape(width, LANES))

    vec = [misc_ref[labels + k : labels + k + 1, :].astype(f32) for k in range(VECTORS)]
    normed = (unit * vec[0] + vec[1]).astype(bf16)
    arrive(step, copies[0])
    projected = jnp.concatenate(
        [
            dot(normed, one_ref[...].reshape(width, cut)).astype(bf16),
            dot(normed, two_ref[..., 0:rest].reshape(width, rest)).astype(bf16),
        ],
        axis=1,
    )
    qkv_ref[0] = projected
    lane = iota((length, LANES), 1)
    low_half = lane < HEAD_DIM
    pieces = []
    for pair in range(width // LANES):
        at = pair * LANES
        query = projected[:, at : at + LANES] * jnp.asarray(HEAD_DIM**-0.5, bf16)
        keys = projected[:, width + at : width + at + LANES]
        values = projected[:, 2 * width + at : 2 * width + at + LANES]
        mixed = None
        for half in range(2):
            own = low_half if half == 0 else jnp.logical_not(low_half)
            scores = dot_nt(jnp.where(own, query, jnp.zeros_like(query)), keys)
            top = jnp.max(scores, axis=-1, keepdims=True)
            shifted = jnp.exp(scores - top)
            total = jnp.sum(shifted, axis=-1, keepdims=True)
            head = 2 * pair + half
            total_ref[0:length, :] = jnp.where(
                lane == head, top + jnp.log(total), total_ref[0:length, :]
            )
            low = (shifted * (1.0 / total)).astype(bf16)
            part = dot(low, jnp.where(own, values, jnp.zeros_like(values)))
            mixed = part if mixed is None else mixed + part
        pieces.append(mixed.astype(bf16))
    mixed = jnp.concatenate(pieces, axis=1)
    mixed_ref[0] = mixed
    lse_ref[0] = jnp.transpose(total_ref[...])[0:16]
    w_out = two_ref[..., rest : rest + width].reshape(width, width)
    first = rows + dot(mixed, w_out) + vec[2]
    first_ref[0] = first
    unit, _ = norm_parts(first)
    routed = (unit * vec[3] + vec[4]).astype(bf16)
    routed_ref[0] = routed
    router = misc_ref[0:labels, :]
    logits = dot_nt(routed, router)
    shifted = jnp.exp(logits - jnp.max(logits, axis=1, keepdims=True))
    gates_ref[0] = shifted / jnp.sum(shifted, axis=1, keepdims=True)
    logits = dot_nt(router, routed)
    shifted = jnp.exp(logits - jnp.max(logits, axis=0, keepdims=True))
    gates = shifted / jnp.sum(shifted, axis=0, keepdims=True)
    label = iota((labels, length), 0)
    blank = jnp.zeros((5, length), f32)
    stack = []
    for k in range(2):
        chosen = jnp.where(label == routes_ref[0, k : k + 1, :], gates, 0.0)
        stack += [*three_parts(jnp.sum(chosen, axis=0, keepdims=True)), blank]
    gate_rows_ref[0] = jnp.concatenate(stack, axis=0).astype(bf16)


def weight_scratch(packed):
    return [
        pltpu.VMEM((part[0].shape[0], 2, *part[0].shape[1:]), part[0].dtype) for part in packed
    ]


def forward(core, tokens, routes, packed, labels):
    images, length, width = tokens.shape
    whole = lambda *tail: pl.BlockSpec((1, *tail), lambda i: (i, 0, 0))
    lanes = -(-length // LANES) * LANES
    return pl.pallas_call(
        functools.partial(forward_kernel, labels),
        grid=(images,),
        in_specs=[
            pl.BlockSpec(memory_space=pltpu.SMEM),
            whole(length, width),
            whole(2, length),
            *[pl.BlockSpec(memory_space=pl.ANY)] * 4,
        ],
        out_specs=[
            whole(length, 3 * width),
            whole(length, width),
            whole(16, lanes),
            whole(length, width),
            whole(length, width),
            whole(length, labels),
            whole(16, length),
        ],
        out_shape=[
            jax.ShapeDtypeStruct((images, length, 3 * width), bf16),
            jax.ShapeDtypeStruct((images, length, width), bf16),
            jax.ShapeDtypeStruct((images, 16, lanes), f32),
            jax.ShapeDtypeStruct((images, length, width), f32),
            jax.ShapeDtypeStruct((images, length, width), bf16),
            jax.ShapeDtypeStruct((images, length, labels), f32),
            jax.ShapeDtypeStruct((images, 16, length), bf16),
        ],
        scratch_shapes=[
            pltpu.VMEM((lanes, LANES), f32),
            *weight_scratch(packed),
            pltpu.VMEM((LANES, width), bf16),
            pltpu.SemaphoreType.DMA((4,)),
        ],
        compiler_params=params(40),
        cost_estimate=pl.CostEstimate(
            flops=16_000_000_000, bytes_accessed=20_000_000, transcendentals=2_000_000
        ),
        name="attention_forward",
    )(core, tokens, routes, *packed[0], *packed[1])


def expert_kernel(
    cap,
    rows_ref,
    cot_ref,
    win_ref,
    wback_ref,
    biases_ref,
    *refs,
):
    (
        out_ref,
        grad_ref,
        weights_ref,
        turned_ref,
        grad_out_ref,
        out_acc_ref,
        grad_acc_ref,
        active_ref,
        inner_ref,
        bias_ref,
        gwin_ref,
        gwback_ref,
        gbias_ref,
        sems,
    ) = refs[-14:]
    owners, capp, width = rows_ref.shape
    groups, depth, hidden = win_ref.shape
    spare = cap - (capp - 16)
    step = pl.program_id(0)
    last = pl.num_programs(0) - 1
    slot = lax.rem(step, 2)
    across = width // hidden

    def copies(step, slot):
        at = pl.multiple_of(hidden + lax.div(step, across) * depth, 16)
        start = pl.multiple_of(lax.rem(step, across) * hidden, LANES)
        return (
            pltpu.make_async_copy(
                gwback_ref.at[slot], weights_ref.at[step, pl.ds(0, hidden)], sems.at[0, slot]
            ),
            pltpu.make_async_copy(
                gwin_ref.at[slot],
                weights_ref.at[:, pl.ds(at, depth), pl.ds(start, hidden)],
                sems.at[1, slot],
            ),
        )

    @pl.when(step >= 2)
    def _():
        for copy in copies(step - 2, slot):
            copy.wait()

    @pl.when(step == 0)
    def _():
        summed = jnp.zeros((1, width), f32)
        for b in range(owners):
            tail = rows_ref[b, capp - 16 :, 0:capp].astype(f32)
            gate = (
                tail[spare : spare + 1] + tail[spare + 1 : spare + 2] + tail[spare + 2 : spare + 3]
            )
            gate = jnp.transpose(jnp.broadcast_to(gate, (LANES, capp)))[:, 0:1]
            part = (cot_ref[b].astype(f32) * gate).astype(bf16)
            grad_out_ref[b * capp : (b + 1) * capp, :] = part
            summed = summed + jnp.sum(part.astype(f32), axis=0, keepdims=True)
            turned_ref[:, b * capp : (b + 1) * capp] = jnp.transpose(rows_ref[b])
        bias_ref[...] = jnp.broadcast_to(summed, bias_ref.shape)
        out_acc_ref[...] = jnp.zeros_like(out_acc_ref)
        grad_acc_ref[...] = jnp.zeros_like(grad_acc_ref)

    first = win_ref[...].reshape(width, hidden)
    second = wback_ref[0]
    bias = biases_ref[step].astype(f32)[0:1, 0:hidden]
    bias_sum = jnp.zeros((1, hidden), f32)
    per = max(1, 256 // capp)
    k0 = 0.7978845608028654
    k1 = 0.044715
    for c in range(owners // per):
        at = slice(c * per * capp, (c + 1) * per * capp)
        block = rows_ref[c * per : (c + 1) * per].reshape(per * capp, width)
        inner = dot(block, first) + bias
        square = inner * inner
        curve = jnp.tanh(inner * (k0 + (k0 * k1) * square))
        half = 0.5 * (1.0 + curve)
        low = (inner * half).astype(bf16)
        active_ref[at, :] = low
        slope = half + (0.5 * inner) * (1.0 - curve * curve) * (k0 + (3.0 * k0 * k1) * square)
        grad_inner = dot_nt(grad_out_ref[at, :], second) * slope
        bias_sum = bias_sum + jnp.sum(grad_inner, axis=0, keepdims=True)
        grad_low = grad_inner.astype(bf16)
        inner_ref[at, :] = grad_low
        out_acc_ref[at, :] += dot(low, second)
        grad_acc_ref[at, :] += dot_nt(grad_low, first)
    gwin_ref[slot] = dot(turned_ref[...], inner_ref[...]).astype(bf16).reshape(win_ref.shape)
    gwback_ref[slot] = dot_tn(active_ref[...], grad_out_ref[...]).astype(bf16)
    row = iota((16, width), 0)
    if hidden < width:
        bias_sum = jnp.concatenate([bias_sum, jnp.zeros((1, width - hidden), f32)], axis=1)
    pad = jnp.where(row == 0, bias_sum, 0.0)
    gbias_ref[step] = pad.astype(bf16)
    for copy in copies(step, slot):
        copy.start()

    @pl.when(step == last)
    def _():
        for g in range(groups):
            part = bias_ref[0:1, g * depth : (g + 1) * depth]
            part = jnp.concatenate([part, jnp.zeros((1, width - depth), f32)], axis=1)
            block = gbias_ref[g].astype(f32)
            gbias_ref[g] = jnp.where(row == 1, part, block).astype(bf16)
        end = pltpu.make_async_copy(
            gbias_ref, weights_ref.at[:, pl.ds(weights_ref.shape[1] - 16, 16)], sems.at[2, 0]
        )
        end.start()
        whole = jnp.concatenate(
            [biases_ref[g].astype(f32)[1:2, 0:depth] for g in range(groups)], axis=1
        )
        for b in range(owners):
            at = slice(b * capp, (b + 1) * capp)
            result = (out_acc_ref[at, :] + whole).astype(bf16)
            out_ref[b] = result
            score = jnp.sum(result.astype(f32) * cot_ref[b].astype(f32), axis=1, keepdims=True)
            score = jnp.transpose(jnp.broadcast_to(score, (capp, LANES)))[0:1, :]
            back = grad_acc_ref[at, :]
            grad_ref[b] = back.astype(bf16)
            tail = back[capp - 16 :, 0:capp]
            line = iota((16, capp), 0) - spare
            for k, part in enumerate(three_parts(score)):
                tail = jnp.where(line == k, part, tail)
            grad_ref[b, capp - 16 :, 0:capp] = tail.astype(bf16)
        for back in range(2):
            for copy in copies(step - back, lax.rem(step + back, 2)):
                copy.wait()
        end.wait()


def expert(rows, cots, weights, outcomes, which, local, cap):
    owners, capp, width = rows.shape
    groups, height, _ = weights.shape
    depth = width // groups
    hidden = height - 16 - (height - 16) // 2
    across = width // hidden
    total = owners * capp
    full = lambda shape: pl.BlockSpec(shape, lambda j: (0,) * len(shape))
    anywhere = pl.BlockSpec(memory_space=pl.ANY)
    extra = [] if outcomes is None else [outcomes]
    return pl.pallas_call(
        functools.partial(expert_kernel, cap),
        grid=(groups,),
        in_specs=[
            full((owners, capp, width)),
            full((owners, capp, width)),
            pl.BlockSpec(
                (groups, depth, hidden), lambda j: (0, hidden // depth + j // across, j % across)
            ),
            pl.BlockSpec((1, hidden, width), lambda j: (j, 0, 0)),
            pl.BlockSpec((groups, 16, width), lambda j: (0, (height - 16) // 16, 0)),
            *[anywhere] * len(extra),
        ],
        out_specs=[
            pl.BlockSpec((owners, capp, width), lambda j: (0, which, 0)),
            full((owners, capp, width)),
            anywhere,
        ],
        out_shape=[
            jax.ShapeDtypeStruct((owners, local * capp, width), bf16),
            jax.ShapeDtypeStruct((owners, capp, width), bf16),
            jax.ShapeDtypeStruct(weights.shape, bf16),
        ],
        input_output_aliases={5: 0} if extra else {},
        scratch_shapes=[
            pltpu.VMEM((width, total), bf16),
            pltpu.VMEM((total, width), bf16),
            pltpu.VMEM((total, width), f32),
            pltpu.VMEM((total, width), f32),
            pltpu.VMEM((total, hidden), bf16),
            pltpu.VMEM((total, hidden), bf16),
            pltpu.VMEM((8, width), f32),
            pltpu.VMEM((2, groups, depth, hidden), bf16),
            pltpu.VMEM((2, hidden, width), bf16),
            pltpu.VMEM((groups, 16, width), bf16),
            pltpu.SemaphoreType.DMA((3, 2)),
        ],
        compiler_params=params(56),
        cost_estimate=pl.CostEstimate(
            flops=2 * 6 * total * width * hidden * groups,
            bytes_accessed=30_000_000,
            transcendentals=total * hidden * groups,
        ),
        name="expert_rows",
    )(rows, cots, weights, weights, weights, *extra)


def parted_kernel(
    cap,
    core_ref,
    rows_ref,
    cot_ref,
    win_ref,
    wback_ref,
    biases_ref,
    *refs,
):
    (
        out_ref,
        grad_ref,
        keep_ref,
        away_ref,
        turned_ref,
        grad_out_ref,
        out_acc_ref,
        grad_acc_ref,
        active_ref,
        inner_ref,
        bias_ref,
        gwin_ref,
        gwback_ref,
        gbias_ref,
        sems,
    ) = refs[-15:]
    owners, capp, width = rows_ref.shape
    groups, depth, hidden = win_ref.shape
    spare = cap - (capp - 16)
    step = pl.program_id(0)
    last = pl.num_programs(0) - 1
    slot = lax.rem(step, 2)
    across = width // hidden

    mine = core_ref[0]
    targets = ((keep_ref, mine, 0), (away_ref, 1 - mine, 1))

    def copies(step, slot):
        at = pl.multiple_of(hidden + lax.div(step, across) * depth, 16)
        start = pl.multiple_of(lax.rem(step, across) * hidden, LANES)
        return [
            pltpu.make_async_copy(
                gwin_ref.at[slot, :, part],
                target.at[:, pl.ds(at, depth), pl.ds(start, hidden)],
                sems.at[1 + k, slot],
            )
            for target, part, k in targets
        ]

    def whole_chunk(step, slot, act):
        for target, part, _ in targets:

            @pl.when(lax.rem(step, 2) == part)
            def _():
                act(
                    pltpu.make_async_copy(
                        gwback_ref.at[slot],
                        target.at[lax.div(step, 2), pl.ds(0, hidden)],
                        sems.at[0, slot],
                    )
                )

    def finish(step, slot):
        for copy in copies(step, slot):
            copy.wait()
        whole_chunk(step, slot, lambda copy: copy.wait())

    @pl.when(step >= 2)
    def _():
        finish(step - 2, slot)

    @pl.when(step == 0)
    def _():
        summed = jnp.zeros((1, width), f32)
        for b in range(owners):
            tail = rows_ref[b, capp - 16 :, 0:capp].astype(f32)
            gate = (
                tail[spare : spare + 1] + tail[spare + 1 : spare + 2] + tail[spare + 2 : spare + 3]
            )
            gate = jnp.transpose(jnp.broadcast_to(gate, (LANES, capp)))[:, 0:1]
            part = (cot_ref[b].astype(f32) * gate).astype(bf16)
            grad_out_ref[b * capp : (b + 1) * capp, :] = part
            summed = summed + jnp.sum(part.astype(f32), axis=0, keepdims=True)
            turned_ref[:, b * capp : (b + 1) * capp] = jnp.transpose(rows_ref[b])
        bias_ref[...] = jnp.broadcast_to(summed, bias_ref.shape)
        out_acc_ref[...] = jnp.zeros_like(out_acc_ref)
        grad_acc_ref[...] = jnp.zeros_like(grad_acc_ref)

    first = win_ref[...].reshape(width, hidden)
    second = wback_ref[0]
    bias = biases_ref[step].astype(f32)[0:1, 0:hidden]
    bias_sum = jnp.zeros((1, hidden), f32)
    per = max(1, 256 // capp)
    k0 = 0.7978845608028654
    k1 = 0.044715
    for c in range(owners // per):
        at = slice(c * per * capp, (c + 1) * per * capp)
        block = rows_ref[c * per : (c + 1) * per].reshape(per * capp, width)
        inner = dot(block, first) + bias
        square = inner * inner
        curve = jnp.tanh(inner * (k0 + (k0 * k1) * square))
        half = 0.5 * (1.0 + curve)
        low = (inner * half).astype(bf16)
        active_ref[at, :] = low
        slope = half + (0.5 * inner) * (1.0 - curve * curve) * (k0 + (3.0 * k0 * k1) * square)
        grad_inner = dot_nt(grad_out_ref[at, :], second) * slope
        bias_sum = bias_sum + jnp.sum(grad_inner, axis=0, keepdims=True)
        grad_low = grad_inner.astype(bf16)
        inner_ref[at, :] = grad_low
        out_acc_ref[at, :] += dot(low, second)
        grad_acc_ref[at, :] += dot_nt(grad_low, first)
    gwin_ref[slot] = dot(turned_ref[...], inner_ref[...]).astype(bf16).reshape(gwin_ref.shape[1:])
    gwback_ref[slot] = dot_tn(active_ref[...], grad_out_ref[...]).astype(bf16)
    row = iota((16, width), 0)
    if hidden < width:
        bias_sum = jnp.concatenate([bias_sum, jnp.zeros((1, width - hidden), f32)], axis=1)
    pad = jnp.where(row == 0, bias_sum, 0.0)
    gbias_ref[lax.div(step, 2), lax.rem(step, 2)] = pad.astype(bf16)
    for copy in copies(step, slot):
        copy.start()
    whole_chunk(step, slot, lambda copy: copy.start())

    @pl.when(step == last)
    def _():
        for g in range(groups):
            part = bias_ref[0:1, g * depth : (g + 1) * depth]
            part = jnp.concatenate([part, jnp.zeros((1, width - depth), f32)], axis=1)
            block = gbias_ref[g // 2, g % 2].astype(f32)
            gbias_ref[g // 2, g % 2] = jnp.where(row == 1, part, block).astype(bf16)
        ends = [
            pltpu.make_async_copy(
                gbias_ref.at[:, part],
                target.at[:, pl.ds(target.shape[1] - 16, 16)],
                sems.at[3, k],
            )
            for target, part, k in targets
        ]
        for end in ends:
            end.start()
        whole = jnp.concatenate(
            [biases_ref[g].astype(f32)[1:2, 0:depth] for g in range(groups)], axis=1
        )
        for b in range(owners):
            at = slice(b * capp, (b + 1) * capp)
            result = (out_acc_ref[at, :] + whole).astype(bf16)
            out_ref[b] = result
            score = jnp.sum(result.astype(f32) * cot_ref[b].astype(f32), axis=1, keepdims=True)
            score = jnp.transpose(jnp.broadcast_to(score, (capp, LANES)))[0:1, :]
            back = grad_acc_ref[at, :]
            grad_ref[b] = back.astype(bf16)
            tail = back[capp - 16 :, 0:capp]
            line = iota((16, capp), 0) - spare
            for k, part in enumerate(three_parts(score)):
                tail = jnp.where(line == k, part, tail)
            grad_ref[b, capp - 16 :, 0:capp] = tail.astype(bf16)
        finish(step - 1, 1 - slot)
        finish(step, slot)
        for end in ends:
            end.wait()


def parted_expert(core, rows, cots, weights, outcomes, which, local, cap):
    owners, capp, width = rows.shape
    groups, height, _ = weights.shape
    depth = width // groups
    hidden = height - 16 - (height - 16) // 2
    across = width // hidden
    total = owners * capp
    full = lambda shape: pl.BlockSpec(shape, lambda j: (0,) * len(shape))
    anywhere = pl.BlockSpec(memory_space=pl.ANY)
    extra = [] if outcomes is None else [outcomes]
    return pl.pallas_call(
        functools.partial(parted_kernel, cap),
        grid=(groups,),
        in_specs=[
            pl.BlockSpec(memory_space=pltpu.SMEM),
            full((owners, capp, width)),
            full((owners, capp, width)),
            pl.BlockSpec(
                (groups, depth, hidden), lambda j: (0, hidden // depth + j // across, j % across)
            ),
            pl.BlockSpec((1, hidden, width), lambda j: (j, 0, 0)),
            pl.BlockSpec((groups, 16, width), lambda j: (0, (height - 16) // 16, 0)),
            *[anywhere] * len(extra),
        ],
        out_specs=[
            pl.BlockSpec((owners, capp, width), lambda j: (0, which, 0)),
            full((owners, capp, width)),
            anywhere,
            anywhere,
        ],
        out_shape=[
            jax.ShapeDtypeStruct((owners, local * capp, width), bf16),
            jax.ShapeDtypeStruct((owners, capp, width), bf16),
            jax.ShapeDtypeStruct((groups // 2, height, width), bf16),
            jax.ShapeDtypeStruct((groups // 2, height, width), bf16),
        ],
        input_output_aliases={6: 0} if extra else {},
        scratch_shapes=[
            pltpu.VMEM((width, total), bf16),
            pltpu.VMEM((total, width), bf16),
            pltpu.VMEM((total, width), f32),
            pltpu.VMEM((total, width), f32),
            pltpu.VMEM((total, hidden), bf16),
            pltpu.VMEM((total, hidden), bf16),
            pltpu.VMEM((8, width), f32),
            pltpu.VMEM((2, groups // 2, 2, depth, hidden), bf16),
            pltpu.VMEM((2, hidden, width), bf16),
            pltpu.VMEM((groups // 2, 2, 16, width), bf16),
            pltpu.SemaphoreType.DMA((4, 2)),
        ],
        compiler_params=params(56),
        cost_estimate=pl.CostEstimate(
            flops=2 * 6 * total * width * hidden * groups,
            bytes_accessed=30_000_000,
            transcendentals=total * hidden * groups,
        ),
        name="expert_rows_parted",
    )(core, rows, cots, weights, weights, weights, *extra)


def share_kernel(addends, *refs):
    back_ref, in_ref, bias_ref = refs[-3:]
    value = [refs[k][...].astype(f32) for k in range(3)]
    if addends > 1:
        value = [part + refs[3 + k][...].astype(f32) for k, part in enumerate(value)]
    back_ref[0] = value[0]
    in_ref[0] = value[1]
    bias_ref[0] = value[2]


def share_out(shares, outs, which, local, depth):
    height, width = shares[0].shape
    hidden = (height - 16) // 2
    steps = hidden // depth
    extra = [] if outs is None else list(outs)
    operands = [share for share in shares for _ in range(3)]
    return pl.pallas_call(
        functools.partial(share_kernel, len(shares)),
        grid=(steps,),
        in_specs=[
            *[
                pl.BlockSpec((depth, width), lambda j: (j, 0)),
                pl.BlockSpec((depth, width), lambda j: (steps + j, 0)),
                pl.BlockSpec((16, width), lambda j: (2 * hidden // 16, 0)),
            ]
            * len(shares),
            *[pl.BlockSpec(memory_space=pl.ANY)] * len(extra),
        ],
        out_specs=[
            pl.BlockSpec((1, depth, width), lambda j: (which, j, 0)),
            pl.BlockSpec((1, depth, width), lambda j: (which, 0, j)),
            pl.BlockSpec((1, 16, width), lambda j: (which, 0, 0)),
        ],
        out_shape=[
            jax.ShapeDtypeStruct((local, hidden, width), f32),
            jax.ShapeDtypeStruct((local, depth, steps * width), f32),
            jax.ShapeDtypeStruct((local, 16, width), f32),
        ],
        input_output_aliases={len(operands) + k: k for k in range(len(extra))},
        compiler_params=params(32),
        name="expert_gradients",
    )(*operands, *extra)


def stage_kernel(own_rows, *refs):
    bits, refs = refs[: len(own_rows)], refs[len(own_rows) :]
    for k, rows in enumerate(own_rows):
        keep_ref, other_ref = refs[2 * k : 2 * k + 2]
        stay_ref, away_ref = refs[2 * (len(own_rows) + k) : 2 * (len(own_rows) + k) + 2]
        mine = bits[k][0] == 0
        total = keep_ref[...].astype(f32) + other_ref[...].astype(f32)
        if total.ndim == 3:
            pairs = [(total[0], total[1])]
        else:
            pairs = [
                (total[at : at + rows], total[at + rows : at + 2 * rows])
                for at in range(0, total.shape[0], 2 * rows)
            ]
        stay = [jnp.where(mine, one, two) for one, two in pairs]
        away = [jnp.where(mine, two, one) for one, two in pairs]
        stay_ref[...] = jnp.concatenate(stay, axis=0)
        away_ref[...] = jnp.concatenate(away, axis=0).astype(bf16)


def stage(pairs, lengths, bits):
    rows = [pair[0].size // pair[0].shape[-1] for pair in pairs]
    turns = [count // (2 * length) for count, length in zip(rows, lengths)]

    def fits(steps):
        return all(
            length % (16 * steps) == 0
            if turn == 1
            else turn % steps == 0 and length * (turn // steps) % 16 == 0
            for turn, length in zip(turns, lengths)
        )

    steps = next((count for count in (4, 2) if fits(count)), 1)
    operands, in_specs, out_specs, out_shape = [], [], [], []
    for pair, count, length, turn in zip(pairs, rows, lengths, turns):
        columns = pair[0].shape[-1]
        if turn == 1 and length % 16 == 0:
            shape, block = (2, length, columns), (2, length // steps, columns)
            where = lambda j: (0, j, 0)
        else:
            shape, block = (count, columns), (count // steps, columns)
            where = lambda j: (j, 0)
        operands += [part.reshape(shape) for part in pair]
        in_specs += [pl.BlockSpec(block, where)] * 2
        half = pl.BlockSpec((count // 2 // steps, columns), lambda j: (j, 0))
        out_specs += [half, half]
        out_shape += [jax.ShapeDtypeStruct((count // 2, columns), kind) for kind in (f32, bf16)]
    results = pl.pallas_call(
        functools.partial(stage_kernel, tuple(lengths)),
        grid=(steps,),
        in_specs=[*[pl.BlockSpec(memory_space=pltpu.SMEM)] * len(pairs), *in_specs],
        out_specs=out_specs,
        out_shape=out_shape,
        compiler_params=params(40),
        name="add_and_halve",
    )(*[bit.astype(jnp.int32).reshape(1) for bit in bits], *operands)
    return [results[2 * k : 2 * k + 2] for k in range(len(pairs))]


def add_to(ref, columns, value):
    shape = (*ref.shape[:-1], value.shape[-1])
    ref[..., columns] += value.reshape(shape)


def pick(which, cap, cols_ref, slots, score_ref):
    length = cols_ref.shape[1]
    owners, capp, width = slots[0].shape
    spare = cap - (capp - 16)
    span = owners * capp
    picked = gate_one = gate_two = None
    for k, l in enumerate(which):
        lane = iota((length, span), 1) + l * span
        one = jnp.where(lane == cols_ref[0, :, 0:1], 1.0, 0.0)
        two = jnp.where(lane == cols_ref[0, :, 1:2], 1.0, 0.0)
        part = dot((one + two).astype(bf16), slots[k][...].reshape(span, width))
        picked = part if picked is None else picked + part
        score = score_ref[:, k * span : (k + 1) * span]
        part_one = dot_nt(one.astype(bf16), score)
        part_two = dot_nt(two.astype(bf16), score)
        gate_one = part_one if gate_one is None else gate_one + part_one
        gate_two = part_two if gate_two is None else gate_two + part_two
    line = iota((length, 16), 1)
    mine = (line >= spare) & (line < spare + 3)
    gate_one = jnp.sum(jnp.where(mine, gate_one, 0.0), axis=1, keepdims=True)
    gate_two = jnp.sum(jnp.where(mine, gate_two, 0.0), axis=1, keepdims=True)
    return picked, gate_one, gate_two


def load_scores(slots, score_ref):
    owners, capp, _ = slots[0].shape
    span = owners * capp
    for k, block in enumerate(slots):
        for o in range(owners):
            at = k * span + o * capp
            score_ref[:, at : at + capp] = block[o, capp - 16 :, 0:capp]


def early_kernel(local, cap, cols_ref, qkv_ref, lse_ref, *refs):
    slots = refs[:local]
    picked_ref, gate_ref, probs_ref, score_ref = refs[local:]
    _, length, width = picked_ref.shape

    @pl.when(pl.program_id(0) == 0)
    def _():
        load_scores(slots, score_ref)

    picked, gate_one, gate_two = pick(range(local), cap, cols_ref, slots, score_ref)
    picked_ref[0] = picked
    lane = iota((length, 8), 1)
    gate_ref[0] = jnp.where(lane == 0, gate_one, jnp.where(lane == 1, gate_two, 0.0))
    low_half = iota((length, LANES), 1) < HEAD_DIM
    rate = jnp.asarray(HEAD_DIM**-0.5, bf16)
    for pair in range(width // LANES):
        at = pair * LANES
        query = qkv_ref[0, :, at : at + LANES] * rate
        keys = qkv_ref[0, :, width + at : width + at + LANES]
        for half in range(2):
            own = low_half if half == 0 else jnp.logical_not(low_half)
            head = 2 * pair + half
            scores = dot_nt(keys, jnp.where(own, query, jnp.zeros_like(query)))
            probs = jnp.exp(scores - lse_ref[0, head : head + 1, 0:length])
            probs_ref[0, head] = probs.astype(bf16)


def early(cols, qkv, lse, slots, cap):
    images, length, wide = qkv.shape
    width = wide // 3
    heads = width // HEAD_DIM
    owners, capp, _ = slots[0].shape
    whole = lambda *tail: pl.BlockSpec((1, *tail), lambda i: (i, *[0] * len(tail)))
    return pl.pallas_call(
        functools.partial(early_kernel, len(slots), cap),
        grid=(images,),
        in_specs=[
            whole(length, 8),
            whole(length, wide),
            whole(*lse.shape[1:]),
            *[pl.BlockSpec((owners, capp, width), lambda i: (0, 0, 0))] * len(slots),
        ],
        out_specs=[whole(length, width), whole(length, 8), whole(heads, length, length)],
        out_shape=[
            jax.ShapeDtypeStruct((images, length, width), f32),
            jax.ShapeDtypeStruct((images, length, 8), f32),
            jax.ShapeDtypeStruct((images, heads, length, length), bf16),
        ],
        scratch_shapes=[pltpu.VMEM((16, len(slots) * owners * capp), bf16)],
        compiler_params=params(40),
        cost_estimate=pl.CostEstimate(
            flops=10_000_000_000, bytes_accessed=20_000_000, transcendentals=2_000_000
        ),
        name="attention_again",
    )(cols, qkv, lse, *slots)


def backward_kernel(
    labels,
    local,
    cap,
    core_ref,
    tokens_ref,
    cot_ref,
    cols_ref,
    qkv_ref,
    mixed_ref,
    picked_ref,
    scores_ref,
    probs_ref,
    first_ref,
    routed_ref,
    gates_ref,
    one_own,
    one_other,
    two_own,
    two_other,
    *refs,
):
    slots = refs[:1]
    (
        grad_tokens_ref,
        keep_one_ref,
        send_one_ref,
        keep_two_ref,
        send_two_ref,
        grad_one_ref,
        grad_two_ref,
        stack_ref,
        vec_ref,
        score_ref,
        one_ref,
        two_ref,
        misc_ref,
        normed_ref,
        pair_ref,
        first_keep_ref,
        sems,
    ) = refs[1:]
    _, length, width = tokens_ref.shape
    step = pl.program_id(0)
    place = lax.rem(step, 2)
    pitch = normed_ref.shape[0] // 2
    parts = ((one_own, one_other), (two_own, two_other))
    copies = load_weights(step, core_ref[0], parts, (one_ref, two_ref), sems)
    cut = one_ref.shape[-1]
    rest = 3 * width - cut
    grad_cut = grad_one_ref.shape[-1]
    grad_rest = 3 * width - grad_cut

    @pl.when(step == 0)
    def _():
        grad_one_ref[...] = jnp.zeros_like(grad_one_ref)
        grad_two_ref[...] = jnp.zeros_like(grad_two_ref)
        vec_ref[...] = jnp.zeros_like(vec_ref)
        stack_ref[...] = jnp.zeros_like(stack_ref)
        normed_ref[...] = jnp.zeros_like(normed_ref)
        pair_ref[...] = jnp.zeros_like(pair_ref)
        load_scores(slots, score_ref)

    cot = cot_ref[0].astype(f32)
    route_one, route_two = cols_ref[0, :, 2:3], cols_ref[0, :, 3:4]
    picked, gate_one, gate_two = pick([local - 1], cap, cols_ref, slots, score_ref)
    picked = picked + picked_ref[0]
    gate_one = gate_one + scores_ref[0, :, 0:1]
    gate_two = gate_two + scores_ref[0, :, 1:2]
    arrive(step, copies[1])

    @pl.when(step == 0)
    def _():
        misc_ref[...] = jnp.transpose(two_ref[..., rest + width :].reshape(width, LANES))

    vec = [misc_ref[labels + k : labels + k + 1, :].astype(f32) for k in range(VECTORS)]
    label = iota((length, labels), 1)
    grad_gates = jnp.where(label == route_one, gate_one, 0.0) + jnp.where(
        label == route_two, gate_two, 0.0
    )
    gates = gates_ref[0]
    inner = jnp.sum(grad_gates * gates, axis=1, keepdims=True)
    grad_logits = (gates * (grad_gates - inner)).astype(bf16)
    router = misc_ref[0:labels, :]
    routed = routed_ref[0]
    stack_ref[0:labels, :] += dot_tn(grad_logits, routed)
    grad_routed = dot(grad_logits, router) + picked
    unit, scale = norm_parts(first_ref[0])
    vec_ref[3:4, :] += jnp.sum(grad_routed * unit, axis=0, keepdims=True)
    vec_ref[4:5, :] += jnp.sum(grad_routed, axis=0, keepdims=True)
    grad_first = cot + norm_backward(grad_routed, unit, scale, vec[3])
    vec_ref[2:3, :] += jnp.sum(grad_first, axis=0, keepdims=True)
    first_low = grad_first.astype(bf16)
    add_to(grad_two_ref, slice(grad_rest, grad_rest + width), dot_tn(mixed_ref[0], first_low))
    w_out = two_ref[..., rest : rest + width].reshape(width, width)
    grad_mixed = dot_nt(first_low, w_out).astype(bf16)
    low_half = iota((length, LANES), 1) < HEAD_DIM
    rate = jnp.asarray(HEAD_DIM**-0.5, bf16)
    grads = [[], [], []]
    for pair in range(width // LANES):
        at = pair * LANES
        query = qkv_ref[0, :, at : at + LANES] * rate
        keys = qkv_ref[0, :, width + at : width + at + LANES]
        values = qkv_ref[0, :, 2 * width + at : 2 * width + at + LANES]
        mix = grad_mixed[:, at : at + LANES]
        grad_q = grad_k = grad_v = None
        for half in range(2):
            own = low_half if half == 0 else jnp.logical_not(low_half)
            none = jnp.zeros_like(query)
            query_own = jnp.where(own, query, none)
            mix_own = jnp.where(own, mix, none)
            head = 2 * pair + half
            low = probs_ref[0, head]
            probs = low.astype(f32)
            grad_probs = dot_nt(values, mix_own)
            inner = jnp.sum(grad_probs * probs, axis=0, keepdims=True)
            scores = (probs * (grad_probs - inner)).astype(bf16)
            part = dot(low, mix_own)
            grad_v = part if grad_v is None else grad_v + part
            part = dot(scores, query_own)
            grad_k = part if grad_k is None else grad_k + part
            part = dot_tn(scores, jnp.where(own, keys, none))
            grad_q = part if grad_q is None else grad_q + part
        grads[0].append((grad_q * HEAD_DIM**-0.5).astype(bf16))
        grads[1].append(grad_k.astype(bf16))
        grads[2].append(grad_v.astype(bf16))
    grad_qkv = jnp.concatenate(grads[0] + grads[1] + grads[2], axis=1)
    pair_ref[pl.ds(pl.multiple_of(place * pitch, 16), length), :] = grad_qkv
    first_keep_ref[place] = grad_first
    arrive(step, copies[0], 1)

    @pl.when(place == 1)
    def _():
        units = []
        for k in range(2):
            unit, scale = norm_parts(tokens_ref[k].astype(f32))
            units.append((unit, scale))
            normed_ref[k * pitch : k * pitch + length, :] = (unit * vec[0] + vec[1]).astype(bf16)
        pair = pair_ref[...]
        normed = normed_ref[...]
        add_to(grad_one_ref, slice(None), dot_tn(normed, pair[:, 0:grad_cut]))
        add_to(grad_two_ref, slice(0, grad_rest), dot_tn(normed, pair[:, grad_cut:]))
        grad_both = dot_nt(pair[:, 0:cut], one_ref[...].reshape(width, cut))
        grad_both += dot_nt(pair[:, cut:], two_ref[..., 0:rest].reshape(width, rest))
        for k, (unit, scale) in enumerate(units):
            grad_normed = grad_both[k * pitch : k * pitch + length]
            vec_ref[0:1, :] += jnp.sum(grad_normed * unit, axis=0, keepdims=True)
            vec_ref[1:2, :] += jnp.sum(grad_normed, axis=0, keepdims=True)
            grad_tokens_ref[k] = first_keep_ref[k] + norm_backward(grad_normed, unit, scale, vec[0])

    @pl.when(step == pl.num_programs(0) - 1)
    def _():
        stack_ref[labels : labels + 8, :] = vec_ref[...]
        add_to(grad_two_ref, slice(grad_rest + width, None), jnp.transpose(stack_ref[...]))
        mine, other = core_ref[0], 1 - core_ref[0]
        keep_one_ref[...] = grad_one_ref[:, mine].astype(bf16)
        keep_two_ref[...] = grad_two_ref[:, mine].astype(bf16)
        send_one_ref[...] = grad_one_ref[:, other].astype(bf16)
        send_two_ref[...] = grad_two_ref[:, other].astype(bf16)


def backward(
    core, tokens, cot, cols, qkv, mixed, ahead, first, routed, gates, cap, packed, slots, local, labels
):
    images, length, width = tokens.shape
    owners, capp, _ = slots.shape
    whole = lambda *tail: pl.BlockSpec((1, *tail), lambda i: (i, *[0] * len(tail)))
    spare = sum(part[0].shape[2] for part in packed)
    grad_cut = 2 * width + width // 3 // LANES * LANES
    shapes = [(*packed[0][0].shape[:2], count) for count in (grad_cut, spare - grad_cut)]
    still = lambda shape: pl.BlockSpec(shape, lambda i: (0, 0, 0))
    assert images % 2 == 0
    both = pl.BlockSpec((2, length, width), lambda i: (i // 2, 0, 0))
    pitch = -(-length // 16) * 16
    return pl.pallas_call(
        functools.partial(backward_kernel, labels, local, cap),
        grid=(images,),
        in_specs=[
            pl.BlockSpec(memory_space=pltpu.SMEM),
            both,
            whole(length, width),
            whole(length, 8),
            whole(length, 3 * width),
            whole(length, width),
            *[whole(*part.shape[1:]) for part in ahead],
            whole(length, width),
            whole(length, width),
            whole(length, labels),
            *[pl.BlockSpec(memory_space=pl.ANY)] * 4,
            pl.BlockSpec((owners, capp, width), lambda i: (0, 0, 0)),
        ],
        out_specs=[
            both,
            *[still(shape) for shape in shapes for _ in range(2)],
        ],
        out_shape=[
            jax.ShapeDtypeStruct((images, length, width), f32),
            *[jax.ShapeDtypeStruct(shape, bf16) for shape in shapes for _ in range(2)],
        ],
        scratch_shapes=[
            *[pltpu.VMEM((shape[0], 2, *shape[1:]), f32) for shape in shapes],
            pltpu.VMEM((LANES, width), f32),
            pltpu.VMEM((8, width), f32),
            pltpu.VMEM((16, owners * capp), bf16),
            *weight_scratch(packed),
            pltpu.VMEM((LANES, width), bf16),
            pltpu.VMEM((2 * pitch, width), bf16),
            pltpu.VMEM((2 * pitch, 3 * width), bf16),
            pltpu.VMEM((2, length, width), f32),
            pltpu.SemaphoreType.DMA((4,)),
        ],
        compiler_params=params(60),
        cost_estimate=pl.CostEstimate(
            flops=40_000_000_000, bytes_accessed=40_000_000, transcendentals=2_000_000
        ),
        name="attention_backward",
    )(
        core,
        tokens,
        cot,
        cols,
        qkv,
        mixed,
        *ahead,
        first,
        routed,
        gates,
        *packed[0],
        *packed[1],
        slots,
    )


def output_kernel(labels, local, first_ref, cols_ref, gates_ref, slots_ref, out_ref):
    _, length, width = first_ref.shape
    owners, capp, _ = slots_ref.shape
    capp = capp // local
    span = owners * capp
    label = iota((length, labels), 1)
    total = first_ref[0]
    for k in range(2):
        picked = None
        for l in range(local):
            lane = iota((length, span), 1) + l * span
            hot = jnp.where(lane == cols_ref[0, :, k : k + 1], 1.0, 0.0).astype(bf16)
            part = dot(hot, slots_ref[:, l * capp : (l + 1) * capp, :].reshape(span, width))
            picked = part if picked is None else picked + part
        chosen = jnp.where(label == cols_ref[0, :, k + 2 : k + 3], gates_ref[0], 0.0)
        total = total + jnp.sum(chosen, axis=1, keepdims=True) * picked
    out_ref[0] = total.astype(bf16)


def combine(first, cols, gates, slots, local):
    images, length, width = first.shape
    labels = gates.shape[2]
    whole = lambda *tail: pl.BlockSpec((1, *tail), lambda i: (i, 0, 0))
    return pl.pallas_call(
        functools.partial(output_kernel, labels, local),
        grid=(images,),
        in_specs=[
            whole(length, width),
            whole(length, 8),
            whole(length, labels),
            pl.BlockSpec(slots.shape, lambda i: (0, 0, 0)),
        ],
        out_specs=whole(length, width),
        out_shape=jax.ShapeDtypeStruct((images, length, width), bf16),
        compiler_params=params(40),
        name="combine_outputs",
    )(first, cols, gates, slots)


def bits_of(groups, owners):
    outer = [("group", k) for k in reversed(range(1, groups.bit_length() - 1))]
    inner = [("expert", k) for k in reversed(range(owners.bit_length() - 1))]
    return outer, inner


def swap(block, hop, sizes):
    axis, bit = hop
    return lax.ppermute(block, axis, [(d, d ^ (1 << bit)) for d in range(sizes[axis])])


def own_bit(hop):
    return lax.rem(lax.axis_index(hop[0]) >> hop[1], 2)


def spread(block, have, hops, order, sizes):
    for hop in hops:
        other = swap(block, hop, sizes)
        have = sorted([*have, hop], key=order.index)
        at = have.index(hop)
        mine = own_bit(hop) == 0
        block = jnp.stack(
            [jnp.where(mine, block, other), jnp.where(mine, other, block)], axis=at
        )
    return block, have


def halve(total, hop, at, sizes):
    bit = own_bit(hop)
    away = lax.dynamic_index_in_dim(total, 1 - bit, at, keepdims=False)
    stay = lax.dynamic_index_in_dim(total, bit, at, keepdims=False)
    return stay, swap(away.astype(bf16), hop, sizes)


def gather_back(total, hops, order, sizes):
    have = list(order)
    for hop in hops:
        at = have.index(hop)
        have.remove(hop)
        stay, other = halve(total, hop, at, sizes)
        total = stay + other.astype(f32)
    return total


def per_device(
    groups,
    owners,
    tokens,
    cotangent,
    routes,
    order,
    ln1_gain,
    ln1_bias,
    w_qkv,
    w_out,
    b_out,
    ln2_gain,
    ln2_bias,
    w_router,
    w_in,
    b_in,
    w_back,
    b_back,
):
    images, length, width = tokens.shape
    tok_count = images * length
    labels = w_router.shape[1]
    local = labels // owners
    depth = w_in.shape[1]
    hidden = w_back.shape[1]
    cap = max(2, 5 * tok_count // (2 * labels))
    capp = -(-(cap + 3) // 16) * 16

    own = width // (groups * owners)
    sizes = {"group": groups, "expert": owners}
    outer, inner = bits_of(groups, owners)
    order_of_hops = [*outer, *inner]
    sibling = ("group", 0)
    core = own_bit(sibling).astype(jnp.int32).reshape(1)
    routes_one = [*inner, *outer]
    routes_two = [*inner[:-1], *outer, *inner[-1:]]
    vectors = (ln1_gain, ln1_bias, b_out, ln2_gain, ln2_bias)
    slices = pack(w_qkv, w_out, w_router, vectors, owners)
    near = inner[:-1]
    marks = (routes % local) * owners + routes // local
    marks = marks.swapaxes(1, 2)
    rows, cols = route(marks, order, labels, cap, capp)
    exchange = lambda block: lax.all_to_all(block, "expert", 0, 0, tiled=True)
    slices = [spread(block, [], near[:1], order_of_hops, sizes)[0] for block in slices]
    rows, *slices = lax.optimization_barrier((rows, *slices))
    filled = dispatch(rows, cotangent, None, cap, capp, owners, [0])
    slices = [spread(block, near[:1], near[1:], order_of_hops, sizes) for block in slices]
    haves = [have for _, have in slices]
    rows, filled, *slices = lax.optimization_barrier(
        (rows, filled, *[block for block, _ in slices])
    )
    cots = [exchange(filled)]
    columns = [block.shape[-1] for block in slices]
    halves = []
    for turn in range(len(outer) + 1):
        moved = []
        for k, path in enumerate((routes_one, routes_two)):
            hop = path[len(near) + turn]
            block, haves[k] = spread(slices[k], haves[k], [hop], order_of_hops, sizes)
            moved.append(block)
        if turn == 0:
            w_in, w_back, rows, *moved = lax.optimization_barrier((w_in, w_back, rows, *moved))
            cots += [
                dispatch(rows, cotangent, None, cap, capp, owners, [l]) for l in range(1, local)
            ]
        slices = moved
    halves = [
        block.reshape(groups // 2, owners * own, count) for block, count in zip(slices, columns)
    ]
    biases = jnp.zeros((local, 16, width), f32)
    biases = biases.at[:, 0, :hidden].set(b_in).at[:, 1, :depth].set(b_back)
    wide = w_in.reshape(local, depth, -1, width).swapaxes(1, 2).reshape(local, -1, width)
    height = hidden + wide.shape[1] + 16
    experts = [
        jnp.concatenate([w_back[l], wide[l], biases[l]], axis=0).astype(bf16)
        for l in range(local)
    ]
    cots[0], cots[-1] = lax.optimization_barrier((cots[0], cots[-1]))
    cots[0], *moved = lax.optimization_barrier((cots[0], *experts, *halves))
    experts, halves = moved[:local], moved[local:]
    cots[1:] = [exchange(block) for block in cots[1:]]
    experts = [lax.all_gather(block, "group") for block in experts]
    packed = [(half, swap(half, sibling, sizes)) for half in halves]
    qkv, mixed, lse, first, routed, gates, gate_rows = forward(core, tokens, marks, packed, labels)
    sent = [dispatch(rows, routed, gate_rows, cap, capp, owners, [l]) for l in range(local)]
    cots[-1], sent[0] = lax.optimization_barrier((cots[-1], sent[0]))
    sent[0] = exchange(sent[0])
    for l in range(1, local):
        sent[l - 1], sent[l] = lax.optimization_barrier((sent[l - 1], sent[l]))
        sent[l] = exchange(sent[l])
    joined, backs, shares = None, [], []
    for l in range(local):
        if l + 1 < local:
            joined, back, grads = expert(sent[l], cots[l], experts[l], joined, l, local, cap)
        else:
            joined, back, keep, away = parted_expert(
                core, sent[l], cots[l], experts[l], joined, l, local, cap
            )
        if l:
            back, backs[-1] = lax.optimization_barrier((back, backs[-1]))
        if l + 1 < local:
            back, sent[l + 1] = lax.optimization_barrier((back, sent[l + 1]))
            grads, sent[l + 1] = lax.optimization_barrier((grads, sent[l + 1]))
            shares.append([lax.psum_scatter(grads, "group", scatter_dimension=0)])
        else:
            if l:
                away, backs[-1] = lax.optimization_barrier((away, backs[-1]))
            total = keep.astype(f32) + swap(away, sibling, sizes).astype(f32)
            total = total.reshape(*[2] * len(outer), height, width)
            total = gather_back(total, outer[:-1], outer, sizes)
            bit = own_bit(outer[-1])
            stay = lax.dynamic_index_in_dim(total, bit, 0, keepdims=False).astype(bf16)
            away = lax.dynamic_index_in_dim(total, 1 - bit, 0, keepdims=False).astype(bf16)
        back = exchange(back)
        if l == local - 1:
            stay, away, back = lax.optimization_barrier((stay, away, back))
            shares.append([stay, swap(away, outer[-1], sizes)])
        backs.append(back)
    joined, backs[-1] = lax.optimization_barrier((joined, backs[-1]))
    joined = exchange(joined)
    grad_tokens, *halves = backward(
        core,
        tokens,
        cotangent,
        cols,
        qkv,
        mixed,
        early(cols, qkv, lse, backs[:-1], cap),
        first,
        routed,
        gates,
        cap,
        packed,
        backs[-1],
        local,
        labels,
    )
    sums = []
    for keep, away in (halves[:2], halves[2:]):
        sums.append((keep, swap(away, sibling, sizes)))
    left = [list(order_of_hops), list(order_of_hops)]
    paths = [routes_one[::-1], routes_two[::-1]]
    share = output = None
    for turn, hops in enumerate(zip(*paths)):
        lengths = [own << (len(have) - 1 - have.index(hop)) for have, hop in zip(left, hops)]
        sums = stage(sums, lengths, [own_bit(hop) for hop in hops])
        sums = [(stay, swap(away, hop, sizes)) for (stay, away), hop in zip(sums, hops)]
        for have, hop in zip(left, hops):
            have.remove(hop)
        if turn == 0:
            for l in range(local):
                share = share_out(shares[l], share, l, local, depth)
            grad_tokens = with_layout_constraint(grad_tokens, Layout(major_to_minor=(1, 0, 2)))
            beside = [grad_tokens, *share]
        elif turn == 1:
            output = combine(first, cols, gates, joined, local)
            beside = [output]
        else:
            continue
        one, two, *beside = lax.optimization_barrier((sums[0][1], sums[1][1], *beside))
        sums = [(sums[0][0], one), (sums[1][0], two)]
        if turn == 0:
            grad_tokens, *share = beside
        else:
            output = beside[0]
    one, two = sums
    share_back, share_in, share_bias = share
    grad_qkv, grad_out, grad_router, *small = dense_out(one, two, labels, owners)
    return (
        output,
        grad_tokens,
        small[0].reshape(own),
        small[1].reshape(own),
        grad_qkv,
        grad_out,
        small[2].reshape(own),
        small[3].reshape(own),
        small[4].reshape(own),
        grad_router.T,
        share_in,
        share_bias[:, 0, :hidden],
        share_back,
        share_bias[:, 1, :depth],
    )


def solution(mesh):
    rows = P(BOTH, None)
    line = P(BOTH)
    tall = P(BOTH, None, None)
    deep = P("expert", "group", None)
    flat = P("expert", "group")
    groups, owners = mesh.shape["group"], mesh.shape["expert"]
    return jax.shard_map(
        functools.partial(per_device, groups, owners),
        mesh=mesh,
        in_specs=(
            tall,
            tall,
            tall,
            rows,
            line,
            line,
            rows,
            rows,
            line,
            line,
            line,
            rows,
            deep,
            flat,
            deep,
            flat,
        ),
        out_specs=(
            tall,
            tall,
            line,
            line,
            rows,
            rows,
            line,
            line,
            line,
            rows,
            deep,
            flat,
            deep,
            flat,
        ),
        check_vma=False,
    )
```

```python
import functools

import jax
import jax.numpy as jnp
from jax import lax
from jax.experimental import pallas as pl
from jax.experimental.layout import Layout, with_layout_constraint
from jax.experimental.pallas import tpu as pltpu
from jax.sharding import PartitionSpec as P

HEAD_DIM = 64
LANES = 128
VECTORS = 5
f32 = jnp.float32
bf16 = jnp.bfloat16
BOTH = ("group", "expert")


def dot(a, b):
    return lax.dot_general(a, b, (((1,), (0,)), ((), ())), preferred_element_type=f32)


def dot_nt(a, b):
    return lax.dot_general(a, b, (((1,), (1,)), ((), ())), preferred_element_type=f32)


def dot_tn(a, b):
    return lax.dot_general(a, b, (((0,), (0,)), ((), ())), preferred_element_type=f32)


def iota(shape, dim):
    return lax.broadcasted_iota(jnp.int32, shape, dim)


def params(mib, grid=1):
    return pltpu.CompilerParams(
        vmem_limit_bytes=mib * 1024 * 1024, dimension_semantics=("arbitrary",) * grid
    )


def three_parts(value):
    high = value.astype(bf16).astype(f32)
    rest = value - high
    mid = rest.astype(bf16).astype(f32)
    return high, mid, rest - mid


def norm_parts(rows):
    centre = rows - jnp.mean(rows, axis=-1, keepdims=True)
    spread = jnp.mean(centre * centre, axis=-1, keepdims=True)
    scale = lax.rsqrt(spread + 1e-06)
    return centre * scale, scale


def norm_backward(grad, unit, scale, gain):
    lead = grad * gain
    first = jnp.mean(lead, axis=-1, keepdims=True)
    second = jnp.mean(lead * unit, axis=-1, keepdims=True)
    return scale * (lead - first - unit * second)


def load_weights(step, core, parts, scratch, sems):
    copies = []
    for k, (own, other) in enumerate(parts):
        copies.append(
            [
                pltpu.make_async_copy(own, scratch[k].at[:, core], sems.at[2 * k]),
                pltpu.make_async_copy(other, scratch[k].at[:, 1 - core], sems.at[2 * k + 1]),
            ]
        )

    @pl.when(step == 0)
    def _():
        for pair in reversed(copies):
            for copy in pair:
                copy.start()

    return copies


def arrive(step, copies, turn=0):
    @pl.when(step == turn)
    def _():
        for copy in copies:
            copy.wait()


def pack_kernel(owners, qkv_ref, out_ref, router_ref, *refs):
    vec_refs, (one_ref, two_ref) = refs[:VECTORS], refs[VECTORS:]
    own, width = out_ref.shape
    labels = router_ref.shape[0]
    local = labels // owners
    cut = one_ref.shape[1]
    rest = 3 * width - cut
    one_ref[...] = qkv_ref[:, 0:cut].astype(bf16)
    two_ref[:, 0:rest] = qkv_ref[:, cut:].astype(bf16)
    two_ref[:, rest : rest + width] = out_ref[...].astype(bf16)
    lines = [
        router_ref[o * local + l : o * local + l + 1, :] for l in range(local) for o in range(owners)
    ]
    lines += [vec_ref[...] for vec_ref in vec_refs]
    lines.append(jnp.zeros((LANES - labels - VECTORS, own), f32))
    small = jnp.concatenate(lines, axis=0)
    if own < LANES:
        small = jnp.concatenate([small, jnp.zeros((LANES, LANES - own), f32)], axis=1)
    two_ref[:, rest + width :] = jnp.transpose(small)[0:own].astype(bf16)


def pack(w_qkv, w_out, w_router, vectors, owners):
    own, width = w_out.shape
    cut = 2 * width
    return pl.pallas_call(
        functools.partial(pack_kernel, owners),
        out_shape=[
            jax.ShapeDtypeStruct((own, cut), bf16),
            jax.ShapeDtypeStruct((own, 4 * width - cut + LANES), bf16),
        ],
        name="pack_weights",
    )(w_qkv, w_out, w_router.T, *[vector.reshape(1, own) for vector in vectors])


def dense_out_kernel(
    owners, one_ref, one_in, two_ref, two_in, qkv_ref, out_ref, router_ref, *vec_refs
):
    own, width = out_ref.shape
    labels = router_ref.shape[0]
    local = labels // owners
    one = one_ref[...] + one_in[...].astype(f32)
    two = two_ref[...] + two_in[...].astype(f32)
    cut = one.shape[1]
    rest = 3 * width - cut
    qkv_ref[:, 0:cut] = one
    qkv_ref[:, cut:] = two[:, 0:rest]
    out_ref[...] = two[:, rest : rest + width]
    small = two[:, rest + width :]
    if own < LANES:
        small = jnp.concatenate([small, jnp.zeros((LANES - own, LANES), f32)], axis=0)
    small = jnp.transpose(small)[:, 0:own]
    for o in range(owners):
        for l in range(local):
            at = o * local + l
            router_ref[at : at + 1, :] = small[l * owners + o : l * owners + o + 1]
    for k, vec_ref in enumerate(vec_refs):
        vec_ref[...] = small[labels + k : labels + k + 1]


def dense_out(one, two, labels, owners):
    own = one[0].shape[0]
    width = (one[0].shape[1] + two[0].shape[1] - LANES) // 4
    return pl.pallas_call(
        functools.partial(dense_out_kernel, owners),
        out_shape=[
            jax.ShapeDtypeStruct((own, 3 * width), f32),
            jax.ShapeDtypeStruct((own, width), f32),
            jax.ShapeDtypeStruct((labels, own), f32),
            *[jax.ShapeDtypeStruct((1, own), f32)] * VECTORS,
        ],
        name="dense_gradients",
    )(*one, *two)


def route_kernel(labels, cap, capp, routes_ref, order_ref, rows_ref, cols_ref):
    images, _, length = routes_ref.shape
    tok_count = order_ref.shape[1]
    order = order_ref[...]
    label = iota((labels, length), 0)
    perms, hots = [], []
    counts = jnp.zeros((2 * labels, tok_count), f32)
    for i in range(images):
        perm = jnp.where(iota((length, tok_count), 0) + i * length == order, 1.0, 0.0).astype(bf16)
        hot = jnp.concatenate(
            [
                jnp.where(label == routes_ref[i, 0:1, :], 1.0, 0.0),
                jnp.where(label == routes_ref[i, 1:2, :], 1.0, 0.0),
            ],
            axis=0,
        )
        perms.append(perm)
        hots.append(hot)
        counts = counts + dot(hot.astype(bf16), perm)
    earlier = jnp.where(
        iota((tok_count, tok_count), 0) < iota((tok_count, tok_count), 1), 1.0, 0.0
    ).astype(bf16)
    before = dot(counts.astype(bf16), earlier)
    total = jnp.sum(counts[:labels], axis=1, keepdims=True)
    before = jnp.concatenate([before[:labels], before[labels:] + total], axis=0)
    before = jnp.minimum(before, float(cap)).astype(bf16)
    same = jnp.where(iota((length, length), 0) == iota((length, length), 1), 1.0, 0.0).astype(bf16)
    for i in range(images):
        back = dot_nt(before, perms[i]) * hots[i]
        slot_one = jnp.sum(back[:labels], axis=0, keepdims=True)
        slot_two = jnp.sum(back[labels:], axis=0, keepdims=True)
        one = routes_ref[i, 0:1, :].astype(f32)
        two = routes_ref[i, 1:2, :].astype(f32)
        kept_one = jnp.where(slot_one < cap, one, -1.0)
        kept_two = jnp.where(slot_two < cap, two, -1.0)
        slot_one = jnp.where(slot_one < cap, slot_one, 0.0)
        slot_two = jnp.where(slot_two < cap, slot_two, 0.0)
        aim_one = (kept_one * capp + slot_one).astype(jnp.int32)
        aim_two = (kept_two * capp + slot_two).astype(jnp.int32)
        rows_ref[i] = jnp.concatenate(
            [aim_one, aim_two, jnp.zeros((6, length), jnp.int32)], axis=0
        )
        stacked = jnp.concatenate(
            [kept_one, slot_one, kept_two, slot_two, one, two, one, two], axis=0
        ).astype(bf16)
        turned = dot_nt(same, stacked)
        cols_ref[i] = jnp.concatenate(
            [
                turned[:, 0:1] * capp + turned[:, 1:2],
                turned[:, 2:3] * capp + turned[:, 3:4],
                turned[:, 4:5],
                turned[:, 5:6],
                turned[:, 4:8],
            ],
            axis=1,
        ).astype(jnp.int32)


def route(routes, order, labels, cap, capp):
    images, _, length = routes.shape
    return pl.pallas_call(
        functools.partial(route_kernel, labels, cap, capp),
        out_shape=(
            jax.ShapeDtypeStruct((images, 8, length), jnp.int32),
            jax.ShapeDtypeStruct((images, length, 8), jnp.int32),
        ),
        compiler_params=pltpu.CompilerParams(vmem_limit_bytes=40 * 1024 * 1024),
        name="route_tokens",
    )(routes, order)


def dispatch_kernel(cap, capp, owners, which, gated, joint, rows_ref, value_ref, *refs):
    images, length, width = value_ref.shape
    outs = refs[1:] if gated else refs
    span = owners * capp
    for place, l in enumerate(which):
        slots = iota((span, length), 0) + l * span
        total = None
        gate_rows = None
        for i in range(images):
            one = slots == rows_ref[i, 0:1, :]
            two = slots == rows_ref[i, 1:2, :]
            both = jnp.where(one | two, 1.0, 0.0).astype(bf16)
            part = dot(both, value_ref[i])
            total = part if total is None else total + part
            if gated:
                gates = refs[0][i]
                first = dot_nt(gates[0:8], jnp.where(one, 1.0, 0.0).astype(bf16))
                second = dot_nt(gates[8:16], jnp.where(two, 1.0, 0.0).astype(bf16))
                part = first + second
                gate_rows = part if gate_rows is None else gate_rows + part
        for o in range(owners):
            block = total[o * capp : (o + 1) * capp]
            if joint:
                outs[0][o, place * capp : (place + 1) * capp, :] = block.astype(bf16)
            else:
                outs[0][o] = block.astype(bf16)
            if gated:
                tail = block[capp - 16 :, 0:capp]
                spare = gate_rows[:, o * capp : (o + 1) * capp]
                line = iota((16, capp), 0) - (cap - (capp - 16))
                for k in range(3):
                    tail = jnp.where(line == k, spare[k : k + 1], tail)
                outs[0][o, capp - 16 :, 0:capp] = tail.astype(bf16)


def dispatch(rows, values, gates, cap, capp, owners, which):
    width = values.shape[2]
    joint = gates is None
    operands = (rows, values) if joint else (rows, values, gates)
    out_shape = jax.ShapeDtypeStruct((owners, len(which) * capp, width), bf16)
    return pl.pallas_call(
        functools.partial(dispatch_kernel, cap, capp, owners, tuple(which), not joint, joint),
        out_shape=out_shape,
        compiler_params=pltpu.CompilerParams(vmem_limit_bytes=40 * 1024 * 1024),
        name="fill_slots",
    )(*operands)


def forward_kernel(
    labels,
    core_ref,
    tokens_ref,
    routes_ref,
    one_own,
    one_other,
    two_own,
    two_other,
    qkv_ref,
    mixed_ref,
    lse_ref,
    first_ref,
    routed_ref,
    gates_ref,
    gate_rows_ref,
    total_ref,
    one_ref,
    two_ref,
    misc_ref,
    sems,
):
    _, length, width = tokens_ref.shape
    step = pl.program_id(0)
    parts = ((one_own, one_other), (two_own, two_other))
    copies = load_weights(step, core_ref[0], parts, (one_ref, two_ref), sems)
    cut = one_ref.shape[-1]
    rest = 3 * width - cut
    rows = tokens_ref[0].astype(f32)
    unit, _ = norm_parts(rows)
    arrive(step, copies[1])

    @pl.when(step == 0)
    def _():
        misc_ref[...] = jnp.transpose(two_ref[..., rest + width :].reshape(width, LANES))

    vec = [misc_ref[labels + k : labels + k + 1, :].astype(f32) for k in range(VECTORS)]
    normed = (unit * vec[0] + vec[1]).astype(bf16)
    arrive(step, copies[0])
    projected = jnp.concatenate(
        [
            dot(normed, one_ref[...].reshape(width, cut)).astype(bf16),
            dot(normed, two_ref[..., 0:rest].reshape(width, rest)).astype(bf16),
        ],
        axis=1,
    )
    qkv_ref[0] = projected
    lane = iota((length, LANES), 1)
    low_half = lane < HEAD_DIM
    pieces = []
    for pair in range(width // LANES):
        at = pair * LANES
        query = projected[:, at : at + LANES] * jnp.asarray(HEAD_DIM**-0.5, bf16)
        keys = projected[:, width + at : width + at + LANES]
        values = projected[:, 2 * width + at : 2 * width + at + LANES]
        mixed = None
        for half in range(2):
            own = low_half if half == 0 else jnp.logical_not(low_half)
            scores = dot_nt(jnp.where(own, query, jnp.zeros_like(query)), keys)
            top = jnp.max(scores, axis=-1, keepdims=True)
            shifted = jnp.exp(scores - top)
            total = jnp.sum(shifted, axis=-1, keepdims=True)
            head = 2 * pair + half
            total_ref[0:length, :] = jnp.where(
                lane == head, top + jnp.log(total), total_ref[0:length, :]
            )
            low = (shifted * (1.0 / total)).astype(bf16)
            part = dot(low, jnp.where(own, values, jnp.zeros_like(values)))
            mixed = part if mixed is None else mixed + part
        pieces.append(mixed.astype(bf16))
    mixed = jnp.concatenate(pieces, axis=1)
    mixed_ref[0] = mixed
    lse_ref[0] = jnp.transpose(total_ref[...])[0:16]
    w_out = two_ref[..., rest : rest + width].reshape(width, width)
    first = rows + dot(mixed, w_out) + vec[2]
    first_ref[0] = first
    unit, _ = norm_parts(first)
    routed = (unit * vec[3] + vec[4]).astype(bf16)
    routed_ref[0] = routed
    router = misc_ref[0:labels, :]
    logits = dot_nt(routed, router)
    shifted = jnp.exp(logits - jnp.max(logits, axis=1, keepdims=True))
    gates_ref[0] = shifted / jnp.sum(shifted, axis=1, keepdims=True)
    logits = dot_nt(router, routed)
    shifted = jnp.exp(logits - jnp.max(logits, axis=0, keepdims=True))
    gates = shifted / jnp.sum(shifted, axis=0, keepdims=True)
    label = iota((labels, length), 0)
    blank = jnp.zeros((5, length), f32)
    stack = []
    for k in range(2):
        chosen = jnp.where(label == routes_ref[0, k : k + 1, :], gates, 0.0)
        stack += [*three_parts(jnp.sum(chosen, axis=0, keepdims=True)), blank]
    gate_rows_ref[0] = jnp.concatenate(stack, axis=0).astype(bf16)


def weight_scratch(packed):
    return [
        pltpu.VMEM((part[0].shape[0], 2, *part[0].shape[1:]), part[0].dtype) for part in packed
    ]


def forward(core, tokens, routes, packed, labels):
    images, length, width = tokens.shape
    whole = lambda *tail: pl.BlockSpec((1, *tail), lambda i: (i, 0, 0))
    lanes = -(-length // LANES) * LANES
    return pl.pallas_call(
        functools.partial(forward_kernel, labels),
        grid=(images,),
        in_specs=[
            pl.BlockSpec(memory_space=pltpu.SMEM),
            whole(length, width),
            whole(2, length),
            *[pl.BlockSpec(memory_space=pl.ANY)] * 4,
        ],
        out_specs=[
            whole(length, 3 * width),
            whole(length, width),
            whole(16, lanes),
            whole(length, width),
            whole(length, width),
            whole(length, labels),
            whole(16, length),
        ],
        out_shape=[
            jax.ShapeDtypeStruct((images, length, 3 * width), bf16),
            jax.ShapeDtypeStruct((images, length, width), bf16),
            jax.ShapeDtypeStruct((images, 16, lanes), f32),
            jax.ShapeDtypeStruct((images, length, width), f32),
            jax.ShapeDtypeStruct((images, length, width), bf16),
            jax.ShapeDtypeStruct((images, length, labels), f32),
            jax.ShapeDtypeStruct((images, 16, length), bf16),
        ],
        scratch_shapes=[
            pltpu.VMEM((lanes, LANES), f32),
            *weight_scratch(packed),
            pltpu.VMEM((LANES, width), bf16),
            pltpu.SemaphoreType.DMA((4,)),
        ],
        compiler_params=params(40),
        cost_estimate=pl.CostEstimate(
            flops=16_000_000_000, bytes_accessed=20_000_000, transcendentals=2_000_000
        ),
        name="attention_forward",
    )(core, tokens, routes, *packed[0], *packed[1])


def expert_kernel(
    cap,
    rows_ref,
    cot_ref,
    win_ref,
    wback_ref,
    biases_ref,
    *refs,
):
    (
        out_ref,
        grad_ref,
        weights_ref,
        turned_ref,
        grad_out_ref,
        out_acc_ref,
        grad_acc_ref,
        active_ref,
        inner_ref,
        bias_ref,
        gwin_ref,
        gwback_ref,
        gbias_ref,
        sems,
    ) = refs[-14:]
    owners, capp, width = rows_ref.shape
    groups, depth, hidden = win_ref.shape
    spare = cap - (capp - 16)
    step = pl.program_id(0)
    last = pl.num_programs(0) - 1
    slot = lax.rem(step, 2)
    across = width // hidden

    def copies(step, slot):
        at = pl.multiple_of(hidden + lax.div(step, across) * depth, 16)
        start = pl.multiple_of(lax.rem(step, across) * hidden, LANES)
        return (
            pltpu.make_async_copy(
                gwback_ref.at[slot], weights_ref.at[step, pl.ds(0, hidden)], sems.at[0, slot]
            ),
            pltpu.make_async_copy(
                gwin_ref.at[slot],
                weights_ref.at[:, pl.ds(at, depth), pl.ds(start, hidden)],
                sems.at[1, slot],
            ),
        )

    @pl.when(step >= 2)
    def _():
        for copy in copies(step - 2, slot):
            copy.wait()

    @pl.when(step == 0)
    def _():
        summed = jnp.zeros((1, width), f32)
        for b in range(owners):
            tail = rows_ref[b, capp - 16 :, 0:capp].astype(f32)
            gate = (
                tail[spare : spare + 1] + tail[spare + 1 : spare + 2] + tail[spare + 2 : spare + 3]
            )
            gate = jnp.transpose(jnp.broadcast_to(gate, (LANES, capp)))[:, 0:1]
            part = (cot_ref[b].astype(f32) * gate).astype(bf16)
            grad_out_ref[b * capp : (b + 1) * capp, :] = part
            summed = summed + jnp.sum(part.astype(f32), axis=0, keepdims=True)
            turned_ref[:, b * capp : (b + 1) * capp] = jnp.transpose(rows_ref[b])
        bias_ref[...] = jnp.broadcast_to(summed, bias_ref.shape)
        out_acc_ref[...] = jnp.zeros_like(out_acc_ref)
        grad_acc_ref[...] = jnp.zeros_like(grad_acc_ref)

    first = win_ref[...].reshape(width, hidden)
    second = wback_ref[0]
    bias = biases_ref[step].astype(f32)[0:1, 0:hidden]
    bias_sum = jnp.zeros((1, hidden), f32)
    per = max(1, 256 // capp)
    k0 = 0.7978845608028654
    k1 = 0.044715
    for c in range(owners // per):
        at = slice(c * per * capp, (c + 1) * per * capp)
        block = rows_ref[c * per : (c + 1) * per].reshape(per * capp, width)
        inner = dot(block, first) + bias
        square = inner * inner
        curve = jnp.tanh(inner * (k0 + (k0 * k1) * square))
        half = 0.5 * (1.0 + curve)
        low = (inner * half).astype(bf16)
        active_ref[at, :] = low
        slope = half + (0.5 * inner) * (1.0 - curve * curve) * (k0 + (3.0 * k0 * k1) * square)
        grad_inner = dot_nt(grad_out_ref[at, :], second) * slope
        bias_sum = bias_sum + jnp.sum(grad_inner, axis=0, keepdims=True)
        grad_low = grad_inner.astype(bf16)
        inner_ref[at, :] = grad_low
        out_acc_ref[at, :] += dot(low, second)
        grad_acc_ref[at, :] += dot_nt(grad_low, first)
    gwin_ref[slot] = dot(turned_ref[...], inner_ref[...]).astype(bf16).reshape(win_ref.shape)
    gwback_ref[slot] = dot_tn(active_ref[...], grad_out_ref[...]).astype(bf16)
    row = iota((16, width), 0)
    if hidden < width:
        bias_sum = jnp.concatenate([bias_sum, jnp.zeros((1, width - hidden), f32)], axis=1)
    pad = jnp.where(row == 0, bias_sum, 0.0)
    gbias_ref[step] = pad.astype(bf16)
    for copy in copies(step, slot):
        copy.start()

    @pl.when(step == last)
    def _():
        for g in range(groups):
            part = bias_ref[0:1, g * depth : (g + 1) * depth]
            part = jnp.concatenate([part, jnp.zeros((1, width - depth), f32)], axis=1)
            block = gbias_ref[g].astype(f32)
            gbias_ref[g] = jnp.where(row == 1, part, block).astype(bf16)
        end = pltpu.make_async_copy(
            gbias_ref, weights_ref.at[:, pl.ds(weights_ref.shape[1] - 16, 16)], sems.at[2, 0]
        )
        end.start()
        whole = jnp.concatenate(
            [biases_ref[g].astype(f32)[1:2, 0:depth] for g in range(groups)], axis=1
        )
        for b in range(owners):
            at = slice(b * capp, (b + 1) * capp)
            result = (out_acc_ref[at, :] + whole).astype(bf16)
            out_ref[b] = result
            score = jnp.sum(result.astype(f32) * cot_ref[b].astype(f32), axis=1, keepdims=True)
            score = jnp.transpose(jnp.broadcast_to(score, (capp, LANES)))[0:1, :]
            back = grad_acc_ref[at, :]
            grad_ref[b] = back.astype(bf16)
            tail = back[capp - 16 :, 0:capp]
            line = iota((16, capp), 0) - spare
            for k, part in enumerate(three_parts(score)):
                tail = jnp.where(line == k, part, tail)
            grad_ref[b, capp - 16 :, 0:capp] = tail.astype(bf16)
        for back in range(2):
            for copy in copies(step - back, lax.rem(step + back, 2)):
                copy.wait()
        end.wait()


def expert(rows, cots, weights, outcomes, which, local, cap):
    owners, capp, width = rows.shape
    groups, height, _ = weights.shape
    depth = width // groups
    hidden = height - 16 - (height - 16) // 2
    across = width // hidden
    total = owners * capp
    full = lambda shape: pl.BlockSpec(shape, lambda j: (0,) * len(shape))
    anywhere = pl.BlockSpec(memory_space=pl.ANY)
    extra = [] if outcomes is None else [outcomes]
    return pl.pallas_call(
        functools.partial(expert_kernel, cap),
        grid=(groups,),
        in_specs=[
            full((owners, capp, width)),
            full((owners, capp, width)),
            pl.BlockSpec(
                (groups, depth, hidden), lambda j: (0, hidden // depth + j // across, j % across)
            ),
            pl.BlockSpec((1, hidden, width), lambda j: (j, 0, 0)),
            pl.BlockSpec((groups, 16, width), lambda j: (0, (height - 16) // 16, 0)),
            *[anywhere] * len(extra),
        ],
        out_specs=[
            pl.BlockSpec((owners, capp, width), lambda j: (0, which, 0)),
            full((owners, capp, width)),
            anywhere,
        ],
        out_shape=[
            jax.ShapeDtypeStruct((owners, local * capp, width), bf16),
            jax.ShapeDtypeStruct((owners, capp, width), bf16),
            jax.ShapeDtypeStruct(weights.shape, bf16),
        ],
        input_output_aliases={5: 0} if extra else {},
        scratch_shapes=[
            pltpu.VMEM((width, total), bf16),
            pltpu.VMEM((total, width), bf16),
            pltpu.VMEM((total, width), f32),
            pltpu.VMEM((total, width), f32),
            pltpu.VMEM((total, hidden), bf16),
            pltpu.VMEM((total, hidden), bf16),
            pltpu.VMEM((8, width), f32),
            pltpu.VMEM((2, groups, depth, hidden), bf16),
            pltpu.VMEM((2, hidden, width), bf16),
            pltpu.VMEM((groups, 16, width), bf16),
            pltpu.SemaphoreType.DMA((3, 2)),
        ],
        compiler_params=params(56),
        cost_estimate=pl.CostEstimate(
            flops=2 * 6 * total * width * hidden * groups,
            bytes_accessed=30_000_000,
            transcendentals=total * hidden * groups,
        ),
        name="expert_rows",
    )(rows, cots, weights, weights, weights, *extra)


def parted_kernel(
    cap,
    core_ref,
    rows_ref,
    cot_ref,
    win_ref,
    wback_ref,
    biases_ref,
    *refs,
):
    (
        out_ref,
        grad_ref,
        keep_ref,
        away_ref,
        turned_ref,
        grad_out_ref,
        out_acc_ref,
        grad_acc_ref,
        active_ref,
        inner_ref,
        bias_ref,
        gwin_ref,
        gwback_ref,
        gbias_ref,
        sems,
    ) = refs[-15:]
    owners, capp, width = rows_ref.shape
    groups, depth, hidden = win_ref.shape
    spare = cap - (capp - 16)
    step = pl.program_id(0)
    last = pl.num_programs(0) - 1
    slot = lax.rem(step, 2)
    across = width // hidden

    mine = core_ref[0]
    targets = ((keep_ref, mine, 0), (away_ref, 1 - mine, 1))

    def copies(step, slot):
        at = pl.multiple_of(hidden + lax.div(step, across) * depth, 16)
        start = pl.multiple_of(lax.rem(step, across) * hidden, LANES)
        return [
            pltpu.make_async_copy(
                gwin_ref.at[slot, :, part],
                target.at[:, pl.ds(at, depth), pl.ds(start, hidden)],
                sems.at[1 + k, slot],
            )
            for target, part, k in targets
        ]

    def whole_chunk(step, slot, act):
        for target, part, _ in targets:

            @pl.when(lax.rem(step, 2) == part)
            def _():
                act(
                    pltpu.make_async_copy(
                        gwback_ref.at[slot],
                        target.at[lax.div(step, 2), pl.ds(0, hidden)],
                        sems.at[0, slot],
                    )
                )

    def finish(step, slot):
        for copy in copies(step, slot):
            copy.wait()
        whole_chunk(step, slot, lambda copy: copy.wait())

    @pl.when(step >= 2)
    def _():
        finish(step - 2, slot)

    @pl.when(step == 0)
    def _():
        summed = jnp.zeros((1, width), f32)
        for b in range(owners):
            tail = rows_ref[b, capp - 16 :, 0:capp].astype(f32)
            gate = (
                tail[spare : spare + 1] + tail[spare + 1 : spare + 2] + tail[spare + 2 : spare + 3]
            )
            gate = jnp.transpose(jnp.broadcast_to(gate, (LANES, capp)))[:, 0:1]
            part = (cot_ref[b].astype(f32) * gate).astype(bf16)
            grad_out_ref[b * capp : (b + 1) * capp, :] = part
            summed = summed + jnp.sum(part.astype(f32), axis=0, keepdims=True)
            turned_ref[:, b * capp : (b + 1) * capp] = jnp.transpose(rows_ref[b])
        bias_ref[...] = jnp.broadcast_to(summed, bias_ref.shape)
        out_acc_ref[...] = jnp.zeros_like(out_acc_ref)
        grad_acc_ref[...] = jnp.zeros_like(grad_acc_ref)

    first = win_ref[...].reshape(width, hidden)
    second = wback_ref[0]
    bias = biases_ref[step].astype(f32)[0:1, 0:hidden]
    bias_sum = jnp.zeros((1, hidden), f32)
    per = max(1, 256 // capp)
    k0 = 0.7978845608028654
    k1 = 0.044715
    for c in range(owners // per):
        at = slice(c * per * capp, (c + 1) * per * capp)
        block = rows_ref[c * per : (c + 1) * per].reshape(per * capp, width)
        inner = dot(block, first) + bias
        square = inner * inner
        curve = jnp.tanh(inner * (k0 + (k0 * k1) * square))
        half = 0.5 * (1.0 + curve)
        low = (inner * half).astype(bf16)
        active_ref[at, :] = low
        slope = half + (0.5 * inner) * (1.0 - curve * curve) * (k0 + (3.0 * k0 * k1) * square)
        grad_inner = dot_nt(grad_out_ref[at, :], second) * slope
        bias_sum = bias_sum + jnp.sum(grad_inner, axis=0, keepdims=True)
        grad_low = grad_inner.astype(bf16)
        inner_ref[at, :] = grad_low
        out_acc_ref[at, :] += dot(low, second)
        grad_acc_ref[at, :] += dot_nt(grad_low, first)
    gwin_ref[slot] = dot(turned_ref[...], inner_ref[...]).astype(bf16).reshape(gwin_ref.shape[1:])
    gwback_ref[slot] = dot_tn(active_ref[...], grad_out_ref[...]).astype(bf16)
    row = iota((16, width), 0)
    if hidden < width:
        bias_sum = jnp.concatenate([bias_sum, jnp.zeros((1, width - hidden), f32)], axis=1)
    pad = jnp.where(row == 0, bias_sum, 0.0)
    gbias_ref[lax.div(step, 2), lax.rem(step, 2)] = pad.astype(bf16)
    for copy in copies(step, slot):
        copy.start()
    whole_chunk(step, slot, lambda copy: copy.start())

    @pl.when(step == last)
    def _():
        for g in range(groups):
            part = bias_ref[0:1, g * depth : (g + 1) * depth]
            part = jnp.concatenate([part, jnp.zeros((1, width - depth), f32)], axis=1)
            block = gbias_ref[g // 2, g % 2].astype(f32)
            gbias_ref[g // 2, g % 2] = jnp.where(row == 1, part, block).astype(bf16)
        ends = [
            pltpu.make_async_copy(
                gbias_ref.at[:, part],
                target.at[:, pl.ds(target.shape[1] - 16, 16)],
                sems.at[3, k],
            )
            for target, part, k in targets
        ]
        for end in ends:
            end.start()
        whole = jnp.concatenate(
            [biases_ref[g].astype(f32)[1:2, 0:depth] for g in range(groups)], axis=1
        )
        for b in range(owners):
            at = slice(b * capp, (b + 1) * capp)
            result = (out_acc_ref[at, :] + whole).astype(bf16)
            out_ref[b] = result
            score = jnp.sum(result.astype(f32) * cot_ref[b].astype(f32), axis=1, keepdims=True)
            score = jnp.transpose(jnp.broadcast_to(score, (capp, LANES)))[0:1, :]
            back = grad_acc_ref[at, :]
            grad_ref[b] = back.astype(bf16)
            tail = back[capp - 16 :, 0:capp]
            line = iota((16, capp), 0) - spare
            for k, part in enumerate(three_parts(score)):
                tail = jnp.where(line == k, part, tail)
            grad_ref[b, capp - 16 :, 0:capp] = tail.astype(bf16)
        finish(step - 1, 1 - slot)
        finish(step, slot)
        for end in ends:
            end.wait()


def parted_expert(core, rows, cots, weights, outcomes, which, local, cap):
    owners, capp, width = rows.shape
    groups, height, _ = weights.shape
    depth = width // groups
    hidden = height - 16 - (height - 16) // 2
    across = width // hidden
    total = owners * capp
    full = lambda shape: pl.BlockSpec(shape, lambda j: (0,) * len(shape))
    anywhere = pl.BlockSpec(memory_space=pl.ANY)
    extra = [] if outcomes is None else [outcomes]
    return pl.pallas_call(
        functools.partial(parted_kernel, cap),
        grid=(groups,),
        in_specs=[
            pl.BlockSpec(memory_space=pltpu.SMEM),
            full((owners, capp, width)),
            full((owners, capp, width)),
            pl.BlockSpec(
                (groups, depth, hidden), lambda j: (0, hidden // depth + j // across, j % across)
            ),
            pl.BlockSpec((1, hidden, width), lambda j: (j, 0, 0)),
            pl.BlockSpec((groups, 16, width), lambda j: (0, (height - 16) // 16, 0)),
            *[anywhere] * len(extra),
        ],
        out_specs=[
            pl.BlockSpec((owners, capp, width), lambda j: (0, which, 0)),
            full((owners, capp, width)),
            anywhere,
            anywhere,
        ],
        out_shape=[
            jax.ShapeDtypeStruct((owners, local * capp, width), bf16),
            jax.ShapeDtypeStruct((owners, capp, width), bf16),
            jax.ShapeDtypeStruct((groups // 2, height, width), bf16),
            jax.ShapeDtypeStruct((groups // 2, height, width), bf16),
        ],
        input_output_aliases={6: 0} if extra else {},
        scratch_shapes=[
            pltpu.VMEM((width, total), bf16),
            pltpu.VMEM((total, width), bf16),
            pltpu.VMEM((total, width), f32),
            pltpu.VMEM((total, width), f32),
            pltpu.VMEM((total, hidden), bf16),
            pltpu.VMEM((total, hidden), bf16),
            pltpu.VMEM((8, width), f32),
            pltpu.VMEM((2, groups // 2, 2, depth, hidden), bf16),
            pltpu.VMEM((2, hidden, width), bf16),
            pltpu.VMEM((groups // 2, 2, 16, width), bf16),
            pltpu.SemaphoreType.DMA((4, 2)),
        ],
        compiler_params=params(56),
        cost_estimate=pl.CostEstimate(
            flops=2 * 6 * total * width * hidden * groups,
            bytes_accessed=30_000_000,
            transcendentals=total * hidden * groups,
        ),
        name="expert_rows_parted",
    )(core, rows, cots, weights, weights, weights, *extra)


def share_kernel(addends, *refs):
    back_ref, in_ref, bias_ref = refs[-3:]
    value = [refs[k][...].astype(f32) for k in range(3)]
    if addends > 1:
        value = [part + refs[3 + k][...].astype(f32) for k, part in enumerate(value)]
    back_ref[0] = value[0]
    in_ref[0] = value[1]
    bias_ref[0] = value[2]


def share_out(shares, outs, which, local, depth):
    height, width = shares[0].shape
    hidden = (height - 16) // 2
    steps = hidden // depth
    extra = [] if outs is None else list(outs)
    operands = [share for share in shares for _ in range(3)]
    return pl.pallas_call(
        functools.partial(share_kernel, len(shares)),
        grid=(steps,),
        in_specs=[
            *[
                pl.BlockSpec((depth, width), lambda j: (j, 0)),
                pl.BlockSpec((depth, width), lambda j: (steps + j, 0)),
                pl.BlockSpec((16, width), lambda j: (2 * hidden // 16, 0)),
            ]
            * len(shares),
            *[pl.BlockSpec(memory_space=pl.ANY)] * len(extra),
        ],
        out_specs=[
            pl.BlockSpec((1, depth, width), lambda j: (which, j, 0)),
            pl.BlockSpec((1, depth, width), lambda j: (which, 0, j)),
            pl.BlockSpec((1, 16, width), lambda j: (which, 0, 0)),
        ],
        out_shape=[
            jax.ShapeDtypeStruct((local, hidden, width), f32),
            jax.ShapeDtypeStruct((local, depth, steps * width), f32),
            jax.ShapeDtypeStruct((local, 16, width), f32),
        ],
        input_output_aliases={len(operands) + k: k for k in range(len(extra))},
        compiler_params=params(32),
        name="expert_gradients",
    )(*operands, *extra)


def stage_kernel(own_rows, *refs):
    bits, refs = refs[: len(own_rows)], refs[len(own_rows) :]
    for k, rows in enumerate(own_rows):
        keep_ref, other_ref = refs[2 * k : 2 * k + 2]
        stay_ref, away_ref = refs[2 * (len(own_rows) + k) : 2 * (len(own_rows) + k) + 2]
        mine = bits[k][0] == 0
        total = keep_ref[...].astype(f32) + other_ref[...].astype(f32)
        if total.ndim == 3:
            pairs = [(total[0], total[1])]
        else:
            pairs = [
                (total[at : at + rows], total[at + rows : at + 2 * rows])
                for at in range(0, total.shape[0], 2 * rows)
            ]
        stay = [jnp.where(mine, one, two) for one, two in pairs]
        away = [jnp.where(mine, two, one) for one, two in pairs]
        stay_ref[...] = jnp.concatenate(stay, axis=0)
        away_ref[...] = jnp.concatenate(away, axis=0).astype(bf16)


def stage(pairs, lengths, bits):
    rows = [pair[0].size // pair[0].shape[-1] for pair in pairs]
    turns = [count // (2 * length) for count, length in zip(rows, lengths)]

    def fits(steps):
        return all(
            length % (16 * steps) == 0
            if turn == 1
            else turn % steps == 0 and length * (turn // steps) % 16 == 0
            for turn, length in zip(turns, lengths)
        )

    steps = next((count for count in (4, 2) if fits(count)), 1)
    operands, in_specs, out_specs, out_shape = [], [], [], []
    for pair, count, length, turn in zip(pairs, rows, lengths, turns):
        columns = pair[0].shape[-1]
        if turn == 1 and length % 16 == 0:
            shape, block = (2, length, columns), (2, length // steps, columns)
            where = lambda j: (0, j, 0)
        else:
            shape, block = (count, columns), (count // steps, columns)
            where = lambda j: (j, 0)
        operands += [part.reshape(shape) for part in pair]
        in_specs += [pl.BlockSpec(block, where)] * 2
        half = pl.BlockSpec((count // 2 // steps, columns), lambda j: (j, 0))
        out_specs += [half, half]
        out_shape += [jax.ShapeDtypeStruct((count // 2, columns), kind) for kind in (f32, bf16)]
    results = pl.pallas_call(
        functools.partial(stage_kernel, tuple(lengths)),
        grid=(steps,),
        in_specs=[*[pl.BlockSpec(memory_space=pltpu.SMEM)] * len(pairs), *in_specs],
        out_specs=out_specs,
        out_shape=out_shape,
        compiler_params=params(40),
        name="add_and_halve",
    )(*[bit.astype(jnp.int32).reshape(1) for bit in bits], *operands)
    return [results[2 * k : 2 * k + 2] for k in range(len(pairs))]


def add_to(ref, columns, value):
    shape = (*ref.shape[:-1], value.shape[-1])
    ref[..., columns] += value.reshape(shape)


def pick(which, cap, cols_ref, slots, score_ref):
    length = cols_ref.shape[1]
    owners, capp, width = slots[0].shape
    spare = cap - (capp - 16)
    span = owners * capp
    picked = gate_one = gate_two = None
    for k, l in enumerate(which):
        lane = iota((length, span), 1) + l * span
        one = jnp.where(lane == cols_ref[0, :, 0:1], 1.0, 0.0)
        two = jnp.where(lane == cols_ref[0, :, 1:2], 1.0, 0.0)
        part = dot((one + two).astype(bf16), slots[k][...].reshape(span, width))
        picked = part if picked is None else picked + part
        score = score_ref[:, k * span : (k + 1) * span]
        part_one = dot_nt(one.astype(bf16), score)
        part_two = dot_nt(two.astype(bf16), score)
        gate_one = part_one if gate_one is None else gate_one + part_one
        gate_two = part_two if gate_two is None else gate_two + part_two
    line = iota((length, 16), 1)
    mine = (line >= spare) & (line < spare + 3)
    gate_one = jnp.sum(jnp.where(mine, gate_one, 0.0), axis=1, keepdims=True)
    gate_two = jnp.sum(jnp.where(mine, gate_two, 0.0), axis=1, keepdims=True)
    return picked, gate_one, gate_two


def load_scores(slots, score_ref):
    owners, capp, _ = slots[0].shape
    span = owners * capp
    for k, block in enumerate(slots):
        for o in range(owners):
            at = k * span + o * capp
            score_ref[:, at : at + capp] = block[o, capp - 16 :, 0:capp]


def early_kernel(local, cap, cols_ref, qkv_ref, lse_ref, *refs):
    slots = refs[:local]
    picked_ref, gate_ref, probs_ref, score_ref = refs[local:]
    _, length, width = picked_ref.shape

    @pl.when(pl.program_id(0) == 0)
    def _():
        load_scores(slots, score_ref)

    picked, gate_one, gate_two = pick(range(local), cap, cols_ref, slots, score_ref)
    picked_ref[0] = picked
    lane = iota((length, 8), 1)
    gate_ref[0] = jnp.where(lane == 0, gate_one, jnp.where(lane == 1, gate_two, 0.0))
    low_half = iota((length, LANES), 1) < HEAD_DIM
    rate = jnp.asarray(HEAD_DIM**-0.5, bf16)
    for pair in range(width // LANES):
        at = pair * LANES
        query = qkv_ref[0, :, at : at + LANES] * rate
        keys = qkv_ref[0, :, width + at : width + at + LANES]
        for half in range(2):
            own = low_half if half == 0 else jnp.logical_not(low_half)
            head = 2 * pair + half
            scores = dot_nt(keys, jnp.where(own, query, jnp.zeros_like(query)))
            probs = jnp.exp(scores - lse_ref[0, head : head + 1, 0:length])
            probs_ref[0, head] = probs.astype(bf16)


def early(cols, qkv, lse, slots, cap):
    images, length, wide = qkv.shape
    width = wide // 3
    heads = width // HEAD_DIM
    owners, capp, _ = slots[0].shape
    whole = lambda *tail: pl.BlockSpec((1, *tail), lambda i: (i, *[0] * len(tail)))
    return pl.pallas_call(
        functools.partial(early_kernel, len(slots), cap),
        grid=(images,),
        in_specs=[
            whole(length, 8),
            whole(length, wide),
            whole(*lse.shape[1:]),
            *[pl.BlockSpec((owners, capp, width), lambda i: (0, 0, 0))] * len(slots),
        ],
        out_specs=[whole(length, width), whole(length, 8), whole(heads, length, length)],
        out_shape=[
            jax.ShapeDtypeStruct((images, length, width), f32),
            jax.ShapeDtypeStruct((images, length, 8), f32),
            jax.ShapeDtypeStruct((images, heads, length, length), bf16),
        ],
        scratch_shapes=[pltpu.VMEM((16, len(slots) * owners * capp), bf16)],
        compiler_params=params(40),
        cost_estimate=pl.CostEstimate(
            flops=10_000_000_000, bytes_accessed=20_000_000, transcendentals=2_000_000
        ),
        name="attention_again",
    )(cols, qkv, lse, *slots)


def backward_kernel(
    labels,
    local,
    cap,
    core_ref,
    tokens_ref,
    cot_ref,
    cols_ref,
    qkv_ref,
    mixed_ref,
    picked_ref,
    scores_ref,
    probs_ref,
    first_ref,
    routed_ref,
    gates_ref,
    one_own,
    one_other,
    two_own,
    two_other,
    *refs,
):
    slots = refs[:1]
    (
        grad_tokens_ref,
        keep_one_ref,
        send_one_ref,
        keep_two_ref,
        send_two_ref,
        grad_one_ref,
        grad_two_ref,
        stack_ref,
        vec_ref,
        score_ref,
        one_ref,
        two_ref,
        misc_ref,
        normed_ref,
        pair_ref,
        first_keep_ref,
        sems,
    ) = refs[1:]
    _, length, width = tokens_ref.shape
    step = pl.program_id(0)
    place = lax.rem(step, 2)
    pitch = normed_ref.shape[0] // 2
    parts = ((one_own, one_other), (two_own, two_other))
    copies = load_weights(step, core_ref[0], parts, (one_ref, two_ref), sems)
    cut = one_ref.shape[-1]
    rest = 3 * width - cut
    grad_cut = grad_one_ref.shape[-1]
    grad_rest = 3 * width - grad_cut

    @pl.when(step == 0)
    def _():
        grad_one_ref[...] = jnp.zeros_like(grad_one_ref)
        grad_two_ref[...] = jnp.zeros_like(grad_two_ref)
        vec_ref[...] = jnp.zeros_like(vec_ref)
        stack_ref[...] = jnp.zeros_like(stack_ref)
        normed_ref[...] = jnp.zeros_like(normed_ref)
        pair_ref[...] = jnp.zeros_like(pair_ref)
        load_scores(slots, score_ref)

    cot = cot_ref[0].astype(f32)
    route_one, route_two = cols_ref[0, :, 2:3], cols_ref[0, :, 3:4]
    picked, gate_one, gate_two = pick([local - 1], cap, cols_ref, slots, score_ref)
    picked = picked + picked_ref[0]
    gate_one = gate_one + scores_ref[0, :, 0:1]
    gate_two = gate_two + scores_ref[0, :, 1:2]
    arrive(step, copies[1])

    @pl.when(step == 0)
    def _():
        misc_ref[...] = jnp.transpose(two_ref[..., rest + width :].reshape(width, LANES))

    vec = [misc_ref[labels + k : labels + k + 1, :].astype(f32) for k in range(VECTORS)]
    label = iota((length, labels), 1)
    grad_gates = jnp.where(label == route_one, gate_one, 0.0) + jnp.where(
        label == route_two, gate_two, 0.0
    )
    gates = gates_ref[0]
    inner = jnp.sum(grad_gates * gates, axis=1, keepdims=True)
    grad_logits = (gates * (grad_gates - inner)).astype(bf16)
    router = misc_ref[0:labels, :]
    routed = routed_ref[0]
    stack_ref[0:labels, :] += dot_tn(grad_logits, routed)
    grad_routed = dot(grad_logits, router) + picked
    unit, scale = norm_parts(first_ref[0])
    vec_ref[3:4, :] += jnp.sum(grad_routed * unit, axis=0, keepdims=True)
    vec_ref[4:5, :] += jnp.sum(grad_routed, axis=0, keepdims=True)
    grad_first = cot + norm_backward(grad_routed, unit, scale, vec[3])
    vec_ref[2:3, :] += jnp.sum(grad_first, axis=0, keepdims=True)
    first_low = grad_first.astype(bf16)
    add_to(grad_two_ref, slice(grad_rest, grad_rest + width), dot_tn(mixed_ref[0], first_low))
    w_out = two_ref[..., rest : rest + width].reshape(width, width)
    grad_mixed = dot_nt(first_low, w_out).astype(bf16)
    low_half = iota((length, LANES), 1) < HEAD_DIM
    rate = jnp.asarray(HEAD_DIM**-0.5, bf16)
    grads = [[], [], []]
    for pair in range(width // LANES):
        at = pair * LANES
        query = qkv_ref[0, :, at : at + LANES] * rate
        keys = qkv_ref[0, :, width + at : width + at + LANES]
        values = qkv_ref[0, :, 2 * width + at : 2 * width + at + LANES]
        mix = grad_mixed[:, at : at + LANES]
        grad_q = grad_k = grad_v = None
        for half in range(2):
            own = low_half if half == 0 else jnp.logical_not(low_half)
            none = jnp.zeros_like(query)
            query_own = jnp.where(own, query, none)
            mix_own = jnp.where(own, mix, none)
            head = 2 * pair + half
            low = probs_ref[0, head]
            probs = low.astype(f32)
            grad_probs = dot_nt(values, mix_own)
            inner = jnp.sum(grad_probs * probs, axis=0, keepdims=True)
            scores = (probs * (grad_probs - inner)).astype(bf16)
            part = dot(low, mix_own)
            grad_v = part if grad_v is None else grad_v + part
            part = dot(scores, query_own)
            grad_k = part if grad_k is None else grad_k + part
            part = dot_tn(scores, jnp.where(own, keys, none))
            grad_q = part if grad_q is None else grad_q + part
        grads[0].append((grad_q * HEAD_DIM**-0.5).astype(bf16))
        grads[1].append(grad_k.astype(bf16))
        grads[2].append(grad_v.astype(bf16))
    grad_qkv = jnp.concatenate(grads[0] + grads[1] + grads[2], axis=1)
    pair_ref[pl.ds(pl.multiple_of(place * pitch, 16), length), :] = grad_qkv
    first_keep_ref[place] = grad_first
    arrive(step, copies[0], 1)

    @pl.when(place == 1)
    def _():
        units = []
        for k in range(2):
            unit, scale = norm_parts(tokens_ref[k].astype(f32))
            units.append((unit, scale))
            normed_ref[k * pitch : k * pitch + length, :] = (unit * vec[0] + vec[1]).astype(bf16)
        pair = pair_ref[...]
        normed = normed_ref[...]
        add_to(grad_one_ref, slice(None), dot_tn(normed, pair[:, 0:grad_cut]))
        add_to(grad_two_ref, slice(0, grad_rest), dot_tn(normed, pair[:, grad_cut:]))
        grad_both = dot_nt(pair[:, 0:cut], one_ref[...].reshape(width, cut))
        grad_both += dot_nt(pair[:, cut:], two_ref[..., 0:rest].reshape(width, rest))
        for k, (unit, scale) in enumerate(units):
            grad_normed = grad_both[k * pitch : k * pitch + length]
            vec_ref[0:1, :] += jnp.sum(grad_normed * unit, axis=0, keepdims=True)
            vec_ref[1:2, :] += jnp.sum(grad_normed, axis=0, keepdims=True)
            grad_tokens_ref[k] = first_keep_ref[k] + norm_backward(grad_normed, unit, scale, vec[0])

    @pl.when(step == pl.num_programs(0) - 1)
    def _():
        stack_ref[labels : labels + 8, :] = vec_ref[...]
        add_to(grad_two_ref, slice(grad_rest + width, None), jnp.transpose(stack_ref[...]))
        mine, other = core_ref[0], 1 - core_ref[0]
        keep_one_ref[...] = grad_one_ref[:, mine].astype(bf16)
        keep_two_ref[...] = grad_two_ref[:, mine].astype(bf16)
        send_one_ref[...] = grad_one_ref[:, other].astype(bf16)
        send_two_ref[...] = grad_two_ref[:, other].astype(bf16)


def backward(
    core, tokens, cot, cols, qkv, mixed, ahead, first, routed, gates, cap, packed, slots, local, labels
):
    images, length, width = tokens.shape
    owners, capp, _ = slots.shape
    whole = lambda *tail: pl.BlockSpec((1, *tail), lambda i: (i, *[0] * len(tail)))
    spare = sum(part[0].shape[2] for part in packed)
    grad_cut = 2 * width + width // 3 // LANES * LANES
    shapes = [(*packed[0][0].shape[:2], count) for count in (grad_cut, spare - grad_cut)]
    still = lambda shape: pl.BlockSpec(shape, lambda i: (0, 0, 0))
    assert images % 2 == 0
    both = pl.BlockSpec((2, length, width), lambda i: (i // 2, 0, 0))
    pitch = -(-length // 16) * 16
    return pl.pallas_call(
        functools.partial(backward_kernel, labels, local, cap),
        grid=(images,),
        in_specs=[
            pl.BlockSpec(memory_space=pltpu.SMEM),
            both,
            whole(length, width),
            whole(length, 8),
            whole(length, 3 * width),
            whole(length, width),
            *[whole(*part.shape[1:]) for part in ahead],
            whole(length, width),
            whole(length, width),
            whole(length, labels),
            *[pl.BlockSpec(memory_space=pl.ANY)] * 4,
            pl.BlockSpec((owners, capp, width), lambda i: (0, 0, 0)),
        ],
        out_specs=[
            both,
            *[still(shape) for shape in shapes for _ in range(2)],
        ],
        out_shape=[
            jax.ShapeDtypeStruct((images, length, width), f32),
            *[jax.ShapeDtypeStruct(shape, bf16) for shape in shapes for _ in range(2)],
        ],
        scratch_shapes=[
            *[pltpu.VMEM((shape[0], 2, *shape[1:]), f32) for shape in shapes],
            pltpu.VMEM((LANES, width), f32),
            pltpu.VMEM((8, width), f32),
            pltpu.VMEM((16, owners * capp), bf16),
            *weight_scratch(packed),
            pltpu.VMEM((LANES, width), bf16),
            pltpu.VMEM((2 * pitch, width), bf16),
            pltpu.VMEM((2 * pitch, 3 * width), bf16),
            pltpu.VMEM((2, length, width), f32),
            pltpu.SemaphoreType.DMA((4,)),
        ],
        compiler_params=params(50),
        cost_estimate=pl.CostEstimate(
            flops=40_000_000_000, bytes_accessed=40_000_000, transcendentals=2_000_000
        ),
        name="attention_backward",
    )(
        core,
        tokens,
        cot,
        cols,
        qkv,
        mixed,
        *ahead,
        first,
        routed,
        gates,
        *packed[0],
        *packed[1],
        slots,
    )


def output_kernel(labels, local, first_ref, cols_ref, gates_ref, slots_ref, out_ref):
    _, length, width = first_ref.shape
    owners, capp, _ = slots_ref.shape
    capp = capp // local
    span = owners * capp
    label = iota((length, labels), 1)
    total = first_ref[0]
    for k in range(2):
        picked = None
        for l in range(local):
            lane = iota((length, span), 1) + l * span
            hot = jnp.where(lane == cols_ref[0, :, k : k + 1], 1.0, 0.0).astype(bf16)
            part = dot(hot, slots_ref[:, l * capp : (l + 1) * capp, :].reshape(span, width))
            picked = part if picked is None else picked + part
        chosen = jnp.where(label == cols_ref[0, :, k + 2 : k + 3], gates_ref[0], 0.0)
        total = total + jnp.sum(chosen, axis=1, keepdims=True) * picked
    out_ref[0] = total.astype(bf16)


def combine(first, cols, gates, slots, local):
    images, length, width = first.shape
    labels = gates.shape[2]
    whole = lambda *tail: pl.BlockSpec((1, *tail), lambda i: (i, 0, 0))
    return pl.pallas_call(
        functools.partial(output_kernel, labels, local),
        grid=(images,),
        in_specs=[
            whole(length, width),
            whole(length, 8),
            whole(length, labels),
            pl.BlockSpec(slots.shape, lambda i: (0, 0, 0)),
        ],
        out_specs=whole(length, width),
        out_shape=jax.ShapeDtypeStruct((images, length, width), bf16),
        compiler_params=params(40),
        name="combine_outputs",
    )(first, cols, gates, slots)


def bits_of(groups, owners):
    outer = [("group", k) for k in reversed(range(1, groups.bit_length() - 1))]
    inner = [("expert", k) for k in reversed(range(owners.bit_length() - 1))]
    return outer, inner


def swap(block, hop, sizes):
    axis, bit = hop
    return lax.ppermute(block, axis, [(d, d ^ (1 << bit)) for d in range(sizes[axis])])


def own_bit(hop):
    return lax.rem(lax.axis_index(hop[0]) >> hop[1], 2)


def spread(block, have, hops, order, sizes):
    for hop in hops:
        other = swap(block, hop, sizes)
        have = sorted([*have, hop], key=order.index)
        at = have.index(hop)
        mine = own_bit(hop) == 0
        block = jnp.stack(
            [jnp.where(mine, block, other), jnp.where(mine, other, block)], axis=at
        )
    return block, have


def halve(total, hop, at, sizes):
    bit = own_bit(hop)
    away = lax.dynamic_index_in_dim(total, 1 - bit, at, keepdims=False)
    stay = lax.dynamic_index_in_dim(total, bit, at, keepdims=False)
    return stay, swap(away.astype(bf16), hop, sizes)


def gather_back(total, hops, order, sizes):
    have = list(order)
    for hop in hops:
        at = have.index(hop)
        have.remove(hop)
        stay, other = halve(total, hop, at, sizes)
        total = stay + other.astype(f32)
    return total


def per_device(
    groups,
    owners,
    tokens,
    cotangent,
    routes,
    order,
    ln1_gain,
    ln1_bias,
    w_qkv,
    w_out,
    b_out,
    ln2_gain,
    ln2_bias,
    w_router,
    w_in,
    b_in,
    w_back,
    b_back,
):
    images, length, width = tokens.shape
    tok_count = images * length
    labels = w_router.shape[1]
    local = labels // owners
    depth = w_in.shape[1]
    hidden = w_back.shape[1]
    cap = max(2, 5 * tok_count // (2 * labels))
    capp = -(-(cap + 3) // 16) * 16

    own = width // (groups * owners)
    sizes = {"group": groups, "expert": owners}
    outer, inner = bits_of(groups, owners)
    order_of_hops = [*outer, *inner]
    sibling = ("group", 0)
    core = own_bit(sibling).astype(jnp.int32).reshape(1)
    routes_one = [*inner, *outer]
    routes_two = [*inner[:-1], *outer, *inner[-1:]]
    vectors = (ln1_gain, ln1_bias, b_out, ln2_gain, ln2_bias)
    slices = pack(w_qkv, w_out, w_router, vectors, owners)
    near = inner[:-1]
    marks = (routes % local) * owners + routes // local
    marks = marks.swapaxes(1, 2)
    rows, cols = route(marks, order, labels, cap, capp)
    exchange = lambda block: lax.all_to_all(block, "expert", 0, 0, tiled=True)
    slices = [spread(block, [], near[:1], order_of_hops, sizes)[0] for block in slices]
    rows, *slices = lax.optimization_barrier((rows, *slices))
    filled = dispatch(rows, cotangent, None, cap, capp, owners, [0])
    slices = [spread(block, near[:1], near[1:], order_of_hops, sizes) for block in slices]
    haves = [have for _, have in slices]
    rows, filled, *slices = lax.optimization_barrier(
        (rows, filled, *[block for block, _ in slices])
    )
    cots = [exchange(filled)]
    columns = [block.shape[-1] for block in slices]
    halves = []
    for turn in range(len(outer) + 1):
        moved = []
        for k, path in enumerate((routes_one, routes_two)):
            hop = path[len(near) + turn]
            block, haves[k] = spread(slices[k], haves[k], [hop], order_of_hops, sizes)
            moved.append(block)
        if turn == 0:
            w_in, w_back, rows, *moved = lax.optimization_barrier((w_in, w_back, rows, *moved))
            cots += [
                dispatch(rows, cotangent, None, cap, capp, owners, [l]) for l in range(1, local)
            ]
        slices = moved
    halves = [
        block.reshape(groups // 2, owners * own, count) for block, count in zip(slices, columns)
    ]
    biases = jnp.zeros((local, 16, width), f32)
    biases = biases.at[:, 0, :hidden].set(b_in).at[:, 1, :depth].set(b_back)
    wide = w_in.reshape(local, depth, -1, width).swapaxes(1, 2).reshape(local, -1, width)
    height = hidden + wide.shape[1] + 16
    experts = [
        jnp.concatenate([w_back[l], wide[l], biases[l]], axis=0).astype(bf16)
        for l in range(local)
    ]
    cots[0], cots[-1] = lax.optimization_barrier((cots[0], cots[-1]))
    cots[0], *moved = lax.optimization_barrier((cots[0], *experts, *halves))
    experts, halves = moved[:local], moved[local:]
    cots[1:] = [exchange(block) for block in cots[1:]]
    experts = [lax.all_gather(block, "group") for block in experts]
    packed = [(half, swap(half, sibling, sizes)) for half in halves]
    qkv, mixed, lse, first, routed, gates, gate_rows = forward(core, tokens, marks, packed, labels)
    sent = [dispatch(rows, routed, gate_rows, cap, capp, owners, [l]) for l in range(local)]
    cots[-1], sent[0] = lax.optimization_barrier((cots[-1], sent[0]))
    sent[0] = exchange(sent[0])
    for l in range(1, local):
        sent[l - 1], sent[l] = lax.optimization_barrier((sent[l - 1], sent[l]))
        sent[l] = exchange(sent[l])
    joined, backs, shares = None, [], []
    for l in range(local):
        if l + 1 < local:
            joined, back, grads = expert(sent[l], cots[l], experts[l], joined, l, local, cap)
        else:
            joined, back, keep, away = parted_expert(
                core, sent[l], cots[l], experts[l], joined, l, local, cap
            )
        if l:
            back, backs[-1] = lax.optimization_barrier((back, backs[-1]))
        if l + 1 < local:
            back, sent[l + 1] = lax.optimization_barrier((back, sent[l + 1]))
            grads, sent[l + 1] = lax.optimization_barrier((grads, sent[l + 1]))
            shares.append([lax.psum_scatter(grads, "group", scatter_dimension=0)])
        else:
            if l:
                away, backs[-1] = lax.optimization_barrier((away, backs[-1]))
            total = keep.astype(f32) + swap(away, sibling, sizes).astype(f32)
            total = total.reshape(*[2] * len(outer), height, width)
            total = gather_back(total, outer[:-1], outer, sizes)
            bit = own_bit(outer[-1])
            stay = lax.dynamic_index_in_dim(total, bit, 0, keepdims=False).astype(bf16)
            away = lax.dynamic_index_in_dim(total, 1 - bit, 0, keepdims=False).astype(bf16)
        back = exchange(back)
        if l == local - 1:
            stay, away, back = lax.optimization_barrier((stay, away, back))
            shares.append([stay, swap(away, outer[-1], sizes)])
        backs.append(back)
    joined, backs[-1] = lax.optimization_barrier((joined, backs[-1]))
    joined = exchange(joined)
    grad_tokens, *halves = backward(
        core,
        tokens,
        cotangent,
        cols,
        qkv,
        mixed,
        early(cols, qkv, lse, backs[:-1], cap),
        first,
        routed,
        gates,
        cap,
        packed,
        backs[-1],
        local,
        labels,
    )
    sums = []
    for keep, away in (halves[:2], halves[2:]):
        sums.append((keep, swap(away, sibling, sizes)))
    left = [list(order_of_hops), list(order_of_hops)]
    paths = [routes_one[::-1], routes_two[::-1]]
    share = output = None
    for turn, hops in enumerate(zip(*paths)):
        lengths = [own << (len(have) - 1 - have.index(hop)) for have, hop in zip(left, hops)]
        sums = stage(sums, lengths, [own_bit(hop) for hop in hops])
        sums = [(stay, swap(away, hop, sizes)) for (stay, away), hop in zip(sums, hops)]
        for have, hop in zip(left, hops):
            have.remove(hop)
        if turn == 0:
            for l in range(local):
                share = share_out(shares[l], share, l, local, depth)
            grad_tokens = with_layout_constraint(grad_tokens, Layout(major_to_minor=(1, 0, 2)))
            beside = [grad_tokens, *share]
        elif turn == 1:
            output = combine(first, cols, gates, joined, local)
            beside = [output]
        else:
            continue
        one, two, *beside = lax.optimization_barrier((sums[0][1], sums[1][1], *beside))
        sums = [(sums[0][0], one), (sums[1][0], two)]
        if turn == 0:
            grad_tokens, *share = beside
        else:
            output = beside[0]
    one, two = sums
    share_back, share_in, share_bias = share
    grad_qkv, grad_out, grad_router, *small = dense_out(one, two, labels, owners)
    return (
        output,
        grad_tokens,
        small[0].reshape(own),
        small[1].reshape(own),
        grad_qkv,
        grad_out,
        small[2].reshape(own),
        small[3].reshape(own),
        small[4].reshape(own),
        grad_router.T,
        share_in,
        share_bias[:, 0, :hidden],
        share_back,
        share_bias[:, 1, :depth],
    )


def solution(mesh):
    rows = P(BOTH, None)
    line = P(BOTH)
    tall = P(BOTH, None, None)
    deep = P("expert", "group", None)
    flat = P("expert", "group")
    groups, owners = mesh.shape["group"], mesh.shape["expert"]
    return jax.shard_map(
        functools.partial(per_device, groups, owners),
        mesh=mesh,
        in_specs=(
            tall,
            tall,
            tall,
            rows,
            line,
            line,
            rows,
            rows,
            line,
            line,
            line,
            rows,
            deep,
            flat,
            deep,
            flat,
        ),
        out_specs=(
            tall,
            tall,
            line,
            line,
            rows,
            rows,
            line,
            line,
            line,
            rows,
            deep,
            flat,
            deep,
            flat,
        ),
        check_vma=False,
    )
```
